32 devices in a mesh: dp: 8 (over y, x, core), tensor: 4 (over z).
Axes of the slice: x: 2, y: 2, z: 4, core: 2. Of those that a mesh axis runs over, the one named last changes fastest.
Arguments:
- tokens: bfloat16 [8192, 1536], P(('dp', 'tensor')), may hold values from -6 to 6
- expert_ids: int32 [8192, 4], P('dp'), may hold values from 0 to 31, all different within a row; in each aligned block of 1024 rows (0 to 1023, 1024 to 2047, ...) at most 256 rows name the same one
- route_weights: float32 [8192, 4], P('dp'), may hold values from 0.1 to 0.4
- attn_gain: bfloat16 [1536], P('dp'), may hold values from 0.5 to 1.5
- q_weight: bfloat16 [1536, 1536], P('dp', 'tensor'), may hold values from -0.21875 to 0.21875
- k_weight: bfloat16 [1536, 256], P('dp'), may hold values from -0.21875 to 0.21875
- v_weight: bfloat16 [1536, 256], P('dp'), may hold values from -0.15625 to 0.15625
- o_weight: bfloat16 [1536, 1536], P('dp', 'tensor'), may hold values from -0.875 to 0.875
- moe_gain: bfloat16 [1536], P('dp'), may hold values from 0.5 to 1.5
- gate_weight: bfloat16 [1536, 32, 768], P('dp', None, 'tensor'), may hold values from -0.15625 to 0.15625
- up_weight: bfloat16 [1536, 32, 768], P('dp', None, 'tensor'), may hold values from -0.15625 to 0.15625
- down_weight: bfloat16 [1536, 32, 768], P('dp', None, 'tensor'), may hold values from -0.4375 to 0.4375
- cotangent: float32 [8192, 1536], P(('dp', 'tensor')), may hold values from -6 to 6
Outputs:
- output: bfloat16 [8192, 1536], P(('dp', 'tensor'))
- tokens_grad: float32 [8192, 1536], P(('dp', 'tensor'))
- attn_gain_grad: float32 [1536], P('dp')
- q_grad: float32 [1536, 1536], P('dp', 'tensor')
- k_grad: float32 [1536, 256], P('dp')
- v_grad: float32 [1536, 256], P('dp')
- o_grad: float32 [1536, 1536], P('dp', 'tensor')
- moe_gain_grad: float32 [1536], P('dp')
- gate_grad: float32 [1536, 32, 768], P('dp', None, 'tensor')
- up_grad: float32 [1536, 32, 768], P('dp', None, 'tensor')
- down_grad: float32 [1536, 32, 768], P('dp', None, 'tensor')
The draws below stay inside these ranges and needn't reach their ends.
Inputs may be any that keep to these rules, and one draw needn't show every extreme that they name: `expert_ids`: each row names 4 different experts. Among the 1024 rows of one index of dp no expert is named more than 256 times, and in some index of dp an expert is named exactly 256 times.
All inputs are finite; a program needn't handle non-finite values.
Results may differ from the reference program's by a relative error of at most 0.023.
Values may be sent and summed in bfloat16 or wider, within the bound.
A program may use at most 192 MiB of HBM per device.

```python
import math
import jax
import jax.numpy as jnp
import numpy as np
from jax import lax

D = 1536
HEADS = 12
KV = 2
HD = 128
FF = 768
EXPERTS = 32
TOPK = 4
SEQ = 1024
BLOCK = 256
QROWS = 512
GROUP = 2
ROWS = 1024
TOKENS = 8192
CAP = 256
QH = 3


def level_of(stream_key, shape, pieces, smallest, high):
    level, own = 1.0, jax.random.fold_in(stream_key, 6)
    for axis_at, blocks in pieces:
        steps = jnp.exp(jax.random.uniform(jax.random.fold_in(own, axis_at), (blocks,), jnp.float32, smallest / len(pieces), high / len(pieces)))
        level = level * jnp.repeat(steps, shape[axis_at] // blocks).reshape([-1 if axis == axis_at else 1 for axis in range(len(shape))])
    return level


def routed_block(own_key, own, number, rows, number_of, top, limit, lean):
    sequence = jax.random.permutation(own_key, number_of)
    crowded, ordinary = shares(number_of, rows * top, limit, lean, True), shares(number_of, rows * top, limit, lean, False)
    places = jnp.arange(number_of)

    def named(lengths, offset_by):
        used = int((lengths > 0).sum())
        fixed = max(1, used // 4)
        shifted = fixed + (places - fixed + offset_by * (used - fixed)) % max(1, number_of - fixed)
        return jnp.zeros((number_of,), jnp.int32).at[sequence[jnp.where(places < fixed, places, shifted)]].set(jnp.asarray(lengths, jnp.int32))

    lengths = jnp.where(number % 4 == 0, named(crowded, number // 4), named(ordinary, number - number // 4 - 1))
    mixed = jax.random.permutation(jax.random.fold_in(own, 3), number_of)
    giver, sink = mixed[0:number_of // 2 * 2:2], mixed[1:number_of // 2 * 2:2]
    slack = jnp.minimum(lengths[giver] - 1, limit - lengths[sink]) // 2
    slack = jnp.where((giver == sequence[0]) | (sink == sequence[0]) | (lengths[sink] == 0), 0, jnp.maximum(slack, 0))
    shifted = jax.random.randint(jax.random.fold_in(own, 4), (number_of // 2,), 0, 1 << 20) % (slack + 1)
    lengths = lengths.at[giver].add(-shifted).at[sink].add(shifted)
    labels = jnp.searchsorted(jnp.cumsum(lengths), jnp.arange(rows * top), side="right").astype(jnp.int32)
    table = labels.reshape(top, rows).T
    table = table[jax.random.permutation(jax.random.fold_in(own, 1), rows)]
    offset_by = jax.random.randint(jax.random.fold_in(own, 2), (rows, 1), 0, top)
    return jnp.take_along_axis(table, (jnp.arange(top)[None, :] + offset_by) % top, axis=1)


def shares(count, total, most, slope, full):
    loads = [(1 << 20) // math.isqrt(rank ** slope) + 1 for rank in range(1, count + 1)]
    largest = most if full else min(most, max(-(-total // count), total * loads[0] // sum(loads)))
    least = 1 if total - largest >= count - 1 else 0
    given, spare = [largest] + [least] * (count - 1), total - largest - least * (count - 1)
    while spare > 0:
        candidates = [i for i in range(1, count) if given[i] < largest] or [i for i in range(1, count) if given[i] < most]
        mass, remaining = sum([loads[i] for i in candidates]), spare
        for i in candidates:
            more = min(most - given[i], max(1, remaining * loads[i] // mass), spare)
            given[i] = given[i] + more
            spare = spare - more
    return np.array(given)


def gaussian(stream_key, shape, spread, reach, shards=(), kind=jnp.bfloat16):
    loudness = level_of(stream_key, shape, shards, -0.22, 0.18) if shards else 1.0
    entries = jax.random.normal(stream_key, shape, jnp.float32) * spread * loudness
    return jnp.minimum(jnp.maximum(entries, -reach), reach).astype(kind)


def setup_inputs(seed: int = 0) -> dict:
    splits = jax.random.split(jax.random.key(seed), 14)
    tokens = gaussian(splits[0], (TOKENS, D), 1.0, 6.0, ((0, 32),))
    expert_ids_keys = jax.random.split(jax.random.fold_in(splits[1], 1), TOKENS // ROWS)
    expert_ids_turns = jax.random.permutation(jax.random.fold_in(splits[1], 3), TOKENS // ROWS)
    expert_ids = jax.vmap(lambda own, number: routed_block(jax.random.fold_in(splits[1], 2), own, number, ROWS, EXPERTS, TOPK, CAP, 1))(expert_ids_keys, expert_ids_turns).reshape((TOKENS, TOPK))
    route_weights = jnp.clip(jnp.exp(math.log(0.4) - 1.3862944 * jax.random.uniform(splits[2], (TOKENS, TOPK), jnp.float32) ** level_of(splits[2], (TOKENS, TOPK), ((0, 8),), -0.2, 0.2)), 0.1, 0.4)
    attn_gain = jnp.clip(1.0 + 0.1 * jax.random.normal(splits[3], (D,), jnp.float32), 0.5, 1.5).astype(jnp.bfloat16)
    q_weight = gaussian(splits[4], (D, HEADS * HD), (D // 2) ** -0.5, 0.21875, ((0, 8), (1, 4)))
    k_weight = gaussian(splits[5], (D, KV * HD), (D // 2) ** -0.5, 0.21875, ((0, 8),))
    v_weight = gaussian(splits[6], (D, KV * HD), D ** -0.5, 0.15625, ((0, 8),))
    o_weight = gaussian(splits[7], (D, HEADS * HD), (HEADS * HD // 32) ** -0.5, 0.875, ((0, 8), (1, 4)))
    moe_gain = jnp.clip(1.0 + 0.1 * jax.random.normal(splits[8], (D,), jnp.float32), 0.5, 1.5).astype(jnp.bfloat16)
    gate_weight = gaussian(splits[9], (D, EXPERTS, FF), D ** -0.5, 0.15625, ((0, 8), (2, 4)))
    up_weight = gaussian(splits[10], (D, EXPERTS, FF), D ** -0.5, 0.15625, ((0, 8), (2, 4)))
    down_weight = gaussian(splits[11], (D, EXPERTS, FF), (FF // 4) ** -0.5, 0.4375, ((0, 8), (2, 4)))
    cotangent = gaussian(splits[12], (TOKENS, D), 1.0, 6.0, ((0, 32),), jnp.float32)
    return dict(tokens=tokens, expert_ids=expert_ids, route_weights=route_weights, attn_gain=attn_gain, q_weight=q_weight, k_weight=k_weight, v_weight=v_weight, o_weight=o_weight, moe_gain=moe_gain, gate_weight=gate_weight, up_weight=up_weight, down_weight=down_weight, cotangent=cotangent)


@jax.custom_vjp
def low(v):
    return lax.optimization_barrier(v.astype(jnp.bfloat16)).astype(jnp.float32)

@jax.custom_vjp
def low_back(v):
    return v

def low_keep(v):
    return (low(v), None)

def low_pass(kept, grad):
    return (grad,)

def back_keep(v):
    return (v, None)

def back_low(kept, grad):
    return (low(grad),)
low.defvjp(low_keep, low_pass)
low_back.defvjp(back_keep, back_low)
eps = 1e-06
rope_base = 1000000.0
highest = lax.Precision.HIGHEST

def matmul(left_side, right_side):
    return jnp.dot(left_side, right_side, precision=highest, preferred_element_type=jnp.float32)

def rms_norm(values, norm_weight):
    return values * lax.rsqrt(lax.optimization_barrier(jnp.mean(values * values, axis=-1, keepdims=True)) + eps) * norm_weight

def rope_tables(row_count):
    half_size = HD // 2
    positions = (jnp.arange(row_count) % SEQ).astype(jnp.float32)
    frequency = rope_base ** (-(jnp.arange(half_size).astype(jnp.float32) * 2.0 / HD))
    angles = positions[:, None] * frequency[None, :]
    return (jnp.cos(angles), jnp.sin(angles))

def rotate(values, cos_table, sin_table):
    half_size = values.shape[-1] // 2
    first_half = values[..., :half_size]
    second_half = values[..., half_size:]
    return jnp.concatenate([first_half * cos_table - second_half * sin_table, second_half * cos_table + first_half * sin_table], axis=-1)

def slot_table(id_rows, weight_rows):
    row_count = id_rows.shape[0]
    flattened = id_rows.reshape(-1)
    one_hot = (flattened[:, None] == jnp.arange(EXPERTS, dtype=jnp.int32)[None, :]).astype(jnp.int32)
    before = jnp.cumsum(one_hot, axis=0) - one_hot
    ranking = lax.optimization_barrier(jnp.sum(before * one_hot, axis=1))
    slot_index = flattened * CAP + ranking
    owners = jnp.arange(row_count * TOPK, dtype=jnp.int32) // TOPK
    table = jnp.full((EXPERTS * CAP,), row_count, jnp.int32).at[slot_index].set(owners)
    slot_gates = jnp.zeros((EXPERTS * CAP,), weight_rows.dtype).at[slot_index].set(weight_rows.reshape(-1))
    return (table, slot_gates)

def attend(queries, keys_rot, values):
    row_count = queries.shape[0]
    seq_blocks = SEQ // QROWS
    head_scale = HD ** (-0.5)

    def one_block(block_index):
        q_rows = lax.dynamic_slice_in_dim(queries, block_index * QROWS, QROWS, 0)
        seq_start = block_index // seq_blocks * SEQ
        k_rows = lax.dynamic_slice_in_dim(keys_rot, seq_start, SEQ, 0)
        v_rows = lax.dynamic_slice_in_dim(values, seq_start, SEQ, 0)
        q_place = block_index % seq_blocks * QROWS + jnp.arange(QROWS, dtype=jnp.int32)
        k_place = jnp.arange(SEQ, dtype=jnp.int32)
        allowed = k_place[None, :] // BLOCK <= q_place[:, None] // BLOCK
        scores = jnp.einsum('qhd,kd->hqk', q_rows, k_rows, precision=highest) * head_scale
        scores = low_back(scores)
        scores = jnp.where(allowed[None], scores, -1e+30)
        row_peak = lax.optimization_barrier(jnp.max(scores, axis=-1, keepdims=True))
        exp_scores = jnp.exp(scores - row_peak)
        probs_low = low(exp_scores / lax.optimization_barrier(jnp.sum(exp_scores, axis=-1, keepdims=True)))
        mixed_heads = jnp.einsum('hqk,kd->qhd', probs_low, v_rows, precision=highest)
        return mixed_heads.reshape(QROWS, -1)
    outputs = lax.map(jax.checkpoint(one_block), jnp.arange(row_count // QROWS, dtype=jnp.int32))
    return outputs.reshape(row_count, -1)

def experts_forward(second_normalized, table, slot_gates, gate_weight, up_weight, down_weight):
    row_count = second_normalized.shape[0]
    padded = jnp.concatenate([second_normalized, jnp.zeros((1, D), second_normalized.dtype)], axis=0)

    def one_group(running, group_id):
        token_index = lax.dynamic_slice_in_dim(table, group_id * GROUP * CAP, GROUP * CAP, 0)
        gate_part = lax.dynamic_slice_in_dim(slot_gates, group_id * GROUP * CAP, GROUP * CAP, 0)
        inputs = jnp.take(padded, token_index, axis=0).reshape(GROUP, CAP, D)
        gate_block = lax.dynamic_slice_in_dim(gate_weight, group_id * GROUP, GROUP, 1)
        up_block = lax.dynamic_slice_in_dim(up_weight, group_id * GROUP, GROUP, 1)
        down_block = lax.dynamic_slice_in_dim(down_weight, group_id * GROUP, GROUP, 1)
        gate_value = low_back(jnp.einsum('gcd,dgf->gcf', inputs, gate_block, precision=highest))
        up_value = low_back(jnp.einsum('gcd,dgf->gcf', inputs, up_block, precision=highest))
        activated = low(jax.nn.silu(gate_value) * up_value)
        result = low_back(jnp.einsum('gcf,dgf->gcd', activated, down_block, precision=highest))
        weighted = (result * gate_part.reshape(GROUP, CAP, 1)).reshape(GROUP * CAP, D)
        return (running.at[token_index].add(weighted), None)
    running, unused = lax.scan(jax.checkpoint(one_group), jnp.zeros((row_count + 1, D), jnp.float32), jnp.arange(EXPERTS // GROUP, dtype=jnp.int32))
    return running[:row_count]

def layer(x_rows, params, table, slot_gates):
    attn_gain, q_weight, k_weight, v_weight, o_weight, moe_gain, gate_weight, up_weight, down_weight = params
    first_normalized = low(rms_norm(x_rows, attn_gain))
    cos_table, sin_table = rope_tables(x_rows.shape[0])
    width = QH * HD
    branch = jnp.zeros_like(x_rows)
    for member in range(HEADS // QH):
        kv_head = member * QH * KV // HEADS
        q_cols = q_weight[:, member * width:(member + 1) * width]
        queries = low_back(matmul(first_normalized, q_cols)).reshape(-1, QH, HD)
        queries = low(rotate(queries, cos_table[:, None, :], sin_table[:, None, :]))
        keys_pre = low_back(matmul(first_normalized, k_weight[:, kv_head * HD:(kv_head + 1) * HD]))
        keys_rot = low(rotate(keys_pre, cos_table, sin_table))
        values = low(low_back(matmul(first_normalized, v_weight[:, kv_head * HD:(kv_head + 1) * HD])))
        mixed_heads = low(low_back(attend(queries, keys_rot, values)))
        branch = branch + matmul(mixed_heads, o_weight[:, member * width:(member + 1) * width].T)
    residual_state = x_rows + low_back(branch)
    second_normalized = low(rms_norm(residual_state, moe_gain))
    moe_branch = low_back(experts_forward(second_normalized, table, slot_gates, gate_weight, up_weight, down_weight))
    return residual_state + moe_branch

def reference(tokens, expert_ids, route_weights, attn_gain, q_weight, k_weight, v_weight, o_weight, moe_gain, gate_weight, up_weight, down_weight, cotangent):
    weights = tuple((weight_arr.astype(jnp.float32) for weight_arr in (attn_gain, q_weight, k_weight, v_weight, o_weight, moe_gain, gate_weight, up_weight, down_weight)))
    index_count = tokens.shape[0] // ROWS
    x_all = tokens.astype(jnp.float32).reshape(index_count, ROWS, D)
    id_all = expert_ids.reshape(index_count, ROWS, TOPK)
    route_all = route_weights.reshape(index_count, ROWS, TOPK)
    cot_all = cotangent.reshape(index_count, ROWS, D)

    def one_index(grads, packed):
        x_rows, id_rows, route_rows, cot_rows = packed
        table, slot_gates = slot_table(id_rows, route_rows)

        def forward(x_in, *params):
            return layer(x_in, params, table, slot_gates)
        result, pullback = jax.vjp(forward, x_rows, *weights)
        back = pullback(cot_rows)
        grads = tuple((running + extra for running, extra in zip(grads, back[1:])))
        return (grads, (result, back[0]))
    init = tuple((jnp.zeros_like(weight_arr) for weight_arr in weights))
    grads, (outputs, input_grads) = lax.scan(one_index, init, (x_all, id_all, route_all, cot_all))
    return (outputs.reshape(-1, D).astype(jnp.bfloat16), input_grads.reshape(-1, D), grads[0], grads[1], grads[2], grads[3], grads[4], grads[5], grads[6], grads[7], grads[8])
```

```python
import jax
import jax.numpy as jnp
from jax import lax
from jax.experimental import pallas as pl
from jax.experimental.pallas import tpu as pltpu
from jax.sharding import PartitionSpec as P

KV = 2
HD = 128
EXPERTS = 32
TOPK = 4
SEQ = 1024
BLOCK = 256
CAP = 256
TAIL = 64
CALL_PAIRS = 4

eps = 1e-06
rope_base = 1000000.0
negative = -1e30
bf16 = jnp.bfloat16
f32 = jnp.float32


def nn(a, b):
    return jnp.dot(a, b, preferred_element_type=f32)


def nt(a, b):
    return lax.dot_general(a, b, (((1,), (1,)), ((), ())), preferred_element_type=f32)


def tn(a, b):
    return lax.dot_general(a, b, (((0,), (0,)), ((), ())), preferred_element_type=f32)


def rope_tables(positions):
    half = HD // 2
    frequency = rope_base ** (-(jnp.arange(half).astype(f32) * 2.0 / HD))
    angles = positions.astype(f32)[:, None] * frequency[None, :]
    return jnp.cos(angles), jnp.sin(angles)


def rotate(values, cos_table, sin_table):
    rows = values.shape[0]
    heads = values.reshape(rows, -1, 2, HD // 2)
    a, b = heads[:, :, 0], heads[:, :, 1]
    cos_table, sin_table = cos_table[:, None], sin_table[:, None]
    turned = jnp.stack([a * cos_table - b * sin_table, b * cos_table + a * sin_table], axis=2)
    return turned.reshape(rows, -1)


def rms_pieces(x):
    inverse = lax.rsqrt(jnp.mean(x * x, axis=-1, keepdims=True) + eps)
    return inverse, x * inverse


def rms_backward(grad, unit, inverse, gain):
    u = grad * gain
    back = inverse * (u - unit * jnp.mean(u * unit, axis=-1, keepdims=True))
    return back, jnp.sum(grad * unit, axis=0)


def probabilities(q, k, first_row):
    rows, keys = q.shape[0], k.shape[0]
    scores = nt(q, k) * (HD**-0.5)
    q_block = (first_row + lax.broadcasted_iota(jnp.int32, (rows, keys), 0)) // BLOCK
    k_block = lax.broadcasted_iota(jnp.int32, (rows, keys), 1) // BLOCK
    scores = jnp.where(k_block <= q_block, scores, negative)
    raised = jnp.exp(scores - jnp.max(scores, axis=-1, keepdims=True))
    return raised / jnp.sum(raised, axis=-1, keepdims=True)


def attend_forward(first_row, q, k, v):
    rows, width = q.shape
    heads = width // HD
    shared = heads // KV

    def kernel(first_ref, q_ref, k_ref, v_ref, o_ref):
        p = probabilities(q_ref[...], k_ref[...], first_ref[0]).astype(bf16)
        o_ref[...] = nn(p, v_ref[...]).astype(bf16)

    per_head = pl.BlockSpec((rows, HD), lambda h, f: (0, h))
    per_kv = pl.BlockSpec((k.shape[0], HD), lambda h, f: (0, h // shared))
    return pl.pallas_call(
        kernel,
        grid_spec=pltpu.PrefetchScalarGridSpec(
            num_scalar_prefetch=1,
            grid=(heads,),
            in_specs=[per_head, per_kv, per_kv],
            out_specs=per_head,
        ),
        out_shape=jax.ShapeDtypeStruct((rows, width), bf16),
        compiler_params=pltpu.CompilerParams(vmem_limit_bytes=32 * 2**20),
        cost_estimate=pl.CostEstimate(
            flops=4 * rows * width * k.shape[0],
            bytes_accessed=4 * rows * width,
            transcendentals=rows * heads * k.shape[0],
        ),
        name="attend",
    )(first_row, q, k, v)


def attend_backward(first_row, q, k, v, do):
    rows, width = q.shape
    keys = k.shape[0]
    heads = width // HD
    shared = heads // KV

    def kernel(first_ref, q_ref, k_ref, v_ref, do_ref, dq_ref, dk_ref, dv_ref):
        q_now, k_now, v_now, do_now = q_ref[...], k_ref[...], v_ref[...], do_ref[...]
        p = probabilities(q_now, k_now, first_ref[0])
        dp = nt(do_now, v_now)
        ds = (p * (dp - jnp.sum(p * dp, axis=-1, keepdims=True))).astype(bf16)
        dq_ref[...] = nn(ds, k_now) * (HD**-0.5)
        dk = tn(ds, q_now) * (HD**-0.5)
        dv = tn(p.astype(bf16), do_now)
        head = pl.program_id(0)

        @pl.when(lax.rem(head, shared) == 0)
        def _():
            dk_ref[...] = dk
            dv_ref[...] = dv

        @pl.when(lax.rem(head, shared) != 0)
        def _():
            dk_ref[...] += dk
            dv_ref[...] += dv

    per_head = pl.BlockSpec((rows, HD), lambda h, f: (0, h))
    per_kv = pl.BlockSpec((keys, HD), lambda h, f: (0, h // shared))
    return pl.pallas_call(
        kernel,
        grid_spec=pltpu.PrefetchScalarGridSpec(
            num_scalar_prefetch=1,
            grid=(heads,),
            in_specs=[per_head, per_kv, per_kv, per_head],
            out_specs=[per_head, per_kv, per_kv],
        ),
        out_shape=[
            jax.ShapeDtypeStruct((rows, width), f32),
            jax.ShapeDtypeStruct((keys, KV * HD), f32),
            jax.ShapeDtypeStruct((keys, KV * HD), f32),
        ],
        compiler_params=pltpu.CompilerParams(vmem_limit_bytes=32 * 2**20),
        cost_estimate=pl.CostEstimate(
            flops=10 * rows * width * keys,
            bytes_accessed=8 * rows * width,
            transcendentals=rows * heads * keys,
        ),
        name="attend_back",
    )(first_row, q, k, v, do)


def expert_call(first, rank_cols, rank_rows, weight_rows, x, gy, pieces, sums, out_count):
    rows, width = x.shape
    subs, per_sub = len(pieces), len(pieces[0])
    sub_pairs, height, lanes = pieces[0][0].shape
    pairs = subs * sub_pairs
    blocks = 6
    tile = 2 * width // blocks
    per_out = per_sub // out_count
    flat = [piece for sub in pieces for piece in sub]
    half = lanes // 3

    def kernel(first_ref, rank_c, rank_r, weight_r, x_ref, gy_ref, *rest):
        w_hbm = rest[: len(flat)]
        sums_in = rest[len(flat)]
        grads = rest[len(flat) + 1 : len(flat) + 1 + out_count]
        sums_out = rest[len(flat) + 1 + out_count]
        w_buf, y_buf, pick_buf, sems = rest[len(flat) + 2 + out_count :]
        step = pl.program_id(0)

        def copies(pair, slot, sub):
            return [
                pltpu.make_async_copy(
                    w_hbm[sub * per_sub + k].at[pair - sub * sub_pairs],
                    w_buf.at[slot, pl.ds(k * height, height)],
                    sems.at[slot, k],
                )
                for k in range(per_sub)
            ]

        def start(pair):
            slot = lax.rem(pair, 2)
            for sub in range(subs):

                @pl.when((pair >= sub * sub_pairs) & (pair < (sub + 1) * sub_pairs))
                def _():
                    for copy in copies(pair, slot, sub):
                        copy.start()

        def put(at, value):
            for n in range(out_count):
                for m in range(per_out):
                    row = (m * out_count + n) * height
                    grads[n][m, 0, :, at : at + value.shape[1]] = value[row : row + height]

        @pl.when(step == 0)
        def _():
            start(step)

        @pl.when(step + 1 < pairs)
        def _():
            start(step + 1)

        @pl.when(step < pairs)
        def _():
            slot = lax.rem(step, 2)
            for copy in copies(0, slot, 0):
                copy.wait()
            w = w_buf.at[slot]
            low_half = lax.broadcasted_iota(jnp.int32, (CAP, HD), 1) < TAIL
            tails = []
            for q in range(2):
                e = 2 * step + q
                column = (lax.broadcasted_iota(jnp.int32, (HD, CAP), 0) == first_ref[0] + e).astype(bf16)
                rank = nn(rank_c[...], column)
                slot_of = lax.broadcasted_iota(jnp.int32, (rows, CAP), 1).astype(f32)
                at = pl.ds(pl.multiple_of(e * CAP, CAP), CAP)
                pick_buf[:, at] = (rank == slot_of).astype(bf16)
                hit = lax.broadcasted_iota(jnp.int32, (CAP, rows), 0) == rank_r[q]
                pick = hit.astype(bf16)
                weight = jnp.sum(jnp.where(hit, weight_r[q], 0.0), axis=1, keepdims=True)
                xe = nn(pick, x_ref[...]).astype(bf16)
                deo = (nn(pick, gy_ref[...]) * weight).astype(bf16)
                gate_up = slice(q * half, (q + 1) * half)
                down = slice(2 * half + q * HD, 2 * half + (q + 1) * HD)
                down_tail = slice(2 * half + 2 * HD, lanes)
                gu = nn(xe, w[:, gate_up])
                d0 = nn(deo, w[:, down])
                d1 = nn(deo, w[:, down_tail])
                if q == 1:
                    d1 = pltpu.roll(d1, TAIL, 1)
                tail = gu[:, 2 * HD :]

                def unit(gate, up, dact):
                    sig = jax.nn.sigmoid(gate)
                    silu = gate * sig
                    return silu * up, dact * up * sig * (1.0 + gate * (1.0 - sig)), dact * silu

                a0, dg0, du0 = unit(gu[:, :HD], gu[:, HD : 2 * HD], d0)
                a1, dg1, du1 = unit(tail, pltpu.roll(tail, TAIL, 1), d1)
                a1 = jnp.where(low_half, a1, 0.0)
                if q == 1:
                    a1 = pltpu.roll(a1, TAIL, 1)
                dgu1 = jnp.where(low_half, dg1, pltpu.roll(du1, TAIL, 1))
                a0, a1 = a0.astype(bf16), a1.astype(bf16)
                dgu = jnp.concatenate([dg0.astype(bf16), du0.astype(bf16), dgu1.astype(bf16)], axis=1)
                eo = nt(a0, w[:, down]) + nt(a1, w[:, down_tail])
                y_buf[at, :width] = (eo * weight).astype(bf16)
                y_buf[at, width:] = nt(dgu, w[:, gate_up]).astype(bf16)
                put(q * half, tn(xe, dgu).astype(bf16))
                put(2 * half + q * HD, tn(deo, a0).astype(bf16))
                tails.append((deo, a1))
            put(2 * half + 2 * HD, (tn(*tails[0]) + tn(*tails[1])).astype(bf16))

        @pl.when(step >= pairs)
        def _():
            at = pl.ds(pl.multiple_of((step - pairs) * tile, tile), tile)
            sums_out[...] = sums_in[...] + nn(pick_buf[...], y_buf[:, at])

    def held(step):
        return jnp.minimum(step, pairs - 1)

    def block(step, _):
        return (0, jnp.maximum(step - pairs, 0))

    once = pl.Buffered(1)
    whole = pl.BlockSpec((rows, width), lambda s, f: (0, 0), pipeline_mode=once)
    routes = pl.BlockSpec((2, 1, rows), lambda s, f: (f[0] // 2 + held(s), 0, 0))
    grad_shape = (per_out, pairs, height, lanes)
    return pl.pallas_call(
        kernel,
        grid_spec=pltpu.PrefetchScalarGridSpec(
            num_scalar_prefetch=1,
            grid=(pairs + blocks,),
            in_specs=[
                pl.BlockSpec((rows, HD), lambda s, f: (0, 0), pipeline_mode=once),
                routes,
                routes,
                whole,
                whole,
            ]
            + [pl.BlockSpec(memory_space=pl.ANY)] * len(flat)
            + [pl.BlockSpec((rows, tile), block)],
            out_specs=[
                pl.BlockSpec((per_out, 1, height, lanes), lambda s, f: (0, held(s), 0, 0))
            ]
            * out_count
            + [pl.BlockSpec((rows, tile), block)],
            scratch_shapes=[
                pltpu.VMEM((2, width, lanes), bf16),
                pltpu.VMEM((2 * pairs * CAP, 2 * width), bf16),
                pltpu.VMEM((rows, 2 * pairs * CAP), bf16),
                pltpu.SemaphoreType.DMA((2, per_sub)),
            ],
        ),
        out_shape=[jax.ShapeDtypeStruct(grad_shape, bf16)] * out_count
        + [jax.ShapeDtypeStruct((rows, 2 * width), f32)],
        compiler_params=pltpu.CompilerParams(vmem_limit_bytes=60 * 2**20),
        cost_estimate=pl.CostEstimate(
            flops=pairs * 2 * CAP * width * (4 * rows * 2 + 18 * lanes // 6),
            bytes_accessed=8 * rows * width * 3,
            transcendentals=0,
        ),
        name="experts",
    )(first, rank_cols, rank_rows, weight_rows, x, gy, *flat, sums)


def pack(gate, up, down):
    def pair(a, b):
        return jnp.concatenate([a[..., :HD], b[..., :HD], a[..., HD:], b[..., HD:]], axis=-1)

    gate, up, down = (jnp.transpose(w, (1, 0, 2)) for w in (gate, up, down))
    gate_up = pair(gate, up)
    return jnp.concatenate([gate_up[0::2], gate_up[1::2], pair(down[0::2], down[1::2])], axis=-1)


def unpack(packed):
    n, height, lanes = packed.shape
    third = lanes // 3

    def halves(both):
        tail = third // 2 - HD
        a = jnp.concatenate([both[..., :HD], both[..., 2 * HD : 2 * HD + tail]], axis=-1)
        b = jnp.concatenate([both[..., HD : 2 * HD], both[..., 2 * HD + tail :]], axis=-1)
        return a, b

    def experts(even, odd):
        both = jnp.stack([even, odd], axis=1).reshape(2 * n, height, third // 2)
        return jnp.transpose(both, (1, 0, 2))

    gate0, up0 = halves(packed[..., :third])
    gate1, up1 = halves(packed[..., third : 2 * third])
    down0, down1 = halves(packed[..., 2 * third :])
    return experts(gate0, gate1), experts(up0, up1), experts(down0, down1)


def flip(value, bit):
    count = lax.axis_size("dp")
    return lax.ppermute(value, "dp", [(i, i ^ bit) for i in range(count)])


def relative(values, me):
    rows, width = values.shape
    blocks = values.reshape(rows, 2, 2, 2 * (width // 8))
    for axis, bit in ((1, 4), (2, 2)):
        blocks = jnp.where((me & bit) != 0, jnp.flip(blocks, axis), blocks)
    cut = width // 8
    swapped = jnp.concatenate([blocks[..., cut:], blocks[..., :cut]], axis=-1)
    blocks = jnp.where((me & 1) != 0, swapped, blocks)
    return blocks.reshape(rows, width)


def gather_pieces(own, turn):
    from_x, from_y = flip(own, 2), flip(own, 4)
    diagonal = flip(from_x, 4) if turn % 2 == 0 else flip(from_y, 2)
    even = [own, from_x, from_y, diagonal]
    odd = [flip(piece, 1) for piece in even]
    return [piece for both in zip(even, odd) for piece in both]


def scatter_pieces(even, odd):
    other = flip(odd, 1)
    cut = even.shape[1] // 2
    first, second = slice(0, cut), slice(cut, None)

    def both(m, part):
        return even[m, part].astype(f32) + other[m, part].astype(f32)

    via_x = flip(both(3, first).astype(bf16), 2)
    via_y = flip(both(3, second).astype(bf16), 4)
    x_parts = [flip(both(1, first).astype(bf16), 2), flip((both(1, second) + via_y.astype(f32)).astype(bf16), 2)]
    y_parts = [flip((both(2, first) + via_x.astype(f32)).astype(bf16), 4), flip(both(2, second).astype(bf16), 4)]
    return jnp.concatenate(
        [
            both(0, part) + x_parts[i].astype(f32) + y_parts[i].astype(f32)
            for i, part in enumerate((first, second))
        ],
        axis=0,
    )


def body(
    tokens,
    expert_ids,
    route_weights,
    attn_gain,
    q_weight,
    k_weight,
    v_weight,
    o_weight,
    moe_gain,
    gate_weight,
    up_weight,
    down_weight,
    cotangent,
):
    members = lax.axis_size("tensor")
    member = lax.axis_index("tensor")
    devices = lax.axis_size("dp")
    me = lax.axis_index("dp")
    own_rows, width = tokens.shape
    rows = own_rows * members
    by_bits = devices == 8
    pairs = EXPERTS // 2
    calls = pairs // CALL_PAIRS
    sub_pairs = CALL_PAIRS // 2

    packed = [
        pack(*(w[:, 2 * sub_pairs * i : 2 * sub_pairs * (i + 1)] for w in (gate_weight, up_weight, down_weight)))
        for i in range(2 * calls)
    ]
    if by_bits:
        gathered = [gather_pieces(own, i) for i, own in enumerate(packed)]
    else:
        gathered = [[lax.all_gather(own, "dp", axis=1, tiled=True)] for own in packed]

    gain_one = lax.all_gather(attn_gain, "dp", axis=0, tiled=True).astype(f32)
    gain_two = lax.all_gather(moe_gain, "dp", axis=0, tiled=True).astype(f32)
    kv_full = lax.all_gather(jnp.concatenate([k_weight, v_weight], axis=1), "dp", axis=0, tiled=True)
    q_full = lax.all_gather(lax.all_gather(q_weight, "dp", axis=0, tiled=True), "tensor", axis=0)
    o_full = lax.all_gather(lax.all_gather(o_weight, "dp", axis=0, tiled=True), "tensor", axis=0)
    kv_width = k_weight.shape[1]

    lanes = jnp.arange(EXPERTS, dtype=jnp.int32)
    named = expert_ids[:, :, None] == lanes
    member_of = jnp.any(named, axis=1)
    weight_of = jnp.sum(jnp.where(named, route_weights[:, :, None], 0.0), axis=1)
    earlier = jnp.arange(rows)[:, None] > jnp.arange(rows)[None, :]
    rank = jnp.where(member_of, nn(earlier.astype(bf16), member_of.astype(bf16)), -1.0)
    rank_cols = jnp.pad(rank, ((0, 0), (0, HD - EXPERTS)), constant_values=-1.0).astype(bf16)
    rank_rows = rank.T.astype(jnp.int32).reshape(EXPERTS, 1, rows)
    weight_rows = weight_of.T.reshape(EXPERTS, 1, rows)

    grad_low = cotangent.astype(bf16)
    if by_bits:
        grad_low = relative(grad_low, me)
    grad_all = lax.all_gather(grad_low, "tensor", axis=0, tiled=True)

    x = tokens.astype(f32)
    inverse_one, unit_one = rms_pieces(x)
    normed_one = (unit_one * gain_one).astype(bf16)
    first_row = (member * own_rows).reshape(1)
    cos_table, sin_table = rope_tables(member * own_rows + jnp.arange(own_rows, dtype=jnp.int32))
    kv_own = nn(normed_one, kv_full)
    kv_own = jnp.concatenate(
        [rotate(kv_own[:, :kv_width], cos_table, sin_table), kv_own[:, kv_width:]], axis=1
    ).astype(bf16)
    kv_all = lax.all_gather(kv_own, "tensor", axis=0, tiled=True)
    keys, values = kv_all[:, :kv_width], kv_all[:, kv_width:]
    queries = jnp.concatenate([nn(normed_one, q_full[t]) for t in range(members)], axis=1)
    queries = rotate(queries, cos_table, sin_table).astype(bf16)
    mixed = attend_forward(first_row, queries, keys, values)
    part = width // members
    branch = sum(nt(mixed[:, t * part : (t + 1) * part], o_full[t]) for t in range(members))
    hidden = x + branch
    inverse_two, unit_two = rms_pieces(hidden)
    normed_two = (unit_two * gain_two).astype(bf16)
    if by_bits:
        normed_two = relative(normed_two, me)
    rows_all = lax.all_gather(normed_two, "tensor", axis=0, tiled=True)

    sums = jnp.zeros((rows, 2 * width), f32)
    shares = []
    for call in range(calls):
        *grads, sums = expert_call(
            jnp.full((1,), 2 * CALL_PAIRS * call, jnp.int32),
            rank_cols,
            rank_rows,
            weight_rows,
            rows_all,
            grad_all,
            gathered[2 * call : 2 * call + 2],
            sums,
            2 if by_bits else 1,
        )
        if by_bits:
            shares.append(unpack(scatter_pieces(*grads)))
        else:
            shares.append(
                unpack(lax.psum_scatter(grads[0][0], "dp", scatter_dimension=1, tiled=True).astype(f32))
            )
    gate_out, up_out, down_out = (jnp.concatenate(parts, axis=1) for parts in zip(*shares))

    low_sums = sums.astype(bf16)
    normed_grad = lax.psum_scatter(low_sums[:, width:], "tensor", scatter_dimension=0, tiled=True).astype(f32)
    moe_own = lax.psum_scatter(low_sums[:, :width], "tensor", scatter_dimension=0, tiled=True).astype(f32)
    if by_bits:
        normed_grad, moe_own = relative(normed_grad, me), relative(moe_own, me)
    output = (hidden + moe_own).astype(bf16)

    back_two, gain_two_part = rms_backward(normed_grad, unit_two, inverse_two, gain_two)
    hidden_grad = cotangent + back_two
    hidden_low = hidden_grad.astype(bf16)
    mixed_grad = jnp.concatenate([nn(hidden_low, o_full[t]) for t in range(members)], axis=1).astype(bf16)
    o_part = jnp.stack([tn(hidden_low, mixed[:, t * part : (t + 1) * part]) for t in range(members)])
    dq, dk, dv = attend_backward(first_row, queries, keys, values, mixed_grad)
    kv_grad = lax.psum_scatter(
        jnp.concatenate([dk, dv], axis=1).astype(bf16), "tensor", scatter_dimension=0, tiled=True
    ).astype(f32)
    dq_low = rotate(dq, cos_table, -sin_table).astype(bf16)
    kv_low = jnp.concatenate(
        [rotate(kv_grad[:, :kv_width], cos_table, -sin_table), kv_grad[:, kv_width:]], axis=1
    ).astype(bf16)
    normed_one_grad = nt(kv_low, kv_full) + sum(
        nt(dq_low[:, t * part : (t + 1) * part], q_full[t]) for t in range(members)
    )
    back_one, gain_one_part = rms_backward(normed_one_grad, unit_one, inverse_one, gain_one)
    tokens_grad = hidden_grad + back_one
    q_part = jnp.stack([tn(normed_one, dq_low[:, t * part : (t + 1) * part]) for t in range(members)])
    kv_part = tn(normed_one, kv_low)

    def shared(values):
        summed = lax.psum_scatter(values.astype(bf16), "tensor", scatter_dimension=0, tiled=False)
        return lax.psum_scatter(summed, "dp", scatter_dimension=0, tiled=True).astype(f32)

    q_grad, o_grad = shared(q_part), shared(o_part)
    small = jnp.concatenate([kv_part, gain_one_part[:, None], gain_two_part[:, None]], axis=1)
    small = lax.psum_scatter(small, "dp", scatter_dimension=0, tiled=True)
    small = lax.psum(small.astype(bf16), "tensor").astype(f32)
    return (
        output,
        tokens_grad,
        small[:, 2 * kv_width],
        q_grad,
        small[:, :kv_width],
        small[:, kv_width : 2 * kv_width],
        o_grad,
        small[:, 2 * kv_width + 1],
        gate_out,
        up_out,
        down_out,
    )


def solution(mesh):
    rows = P(("dp", "tensor"), None)
    experts = P("dp", None, "tensor")
    square = P("dp", "tensor")
    tall = P("dp", None)
    return jax.shard_map(
        body,
        mesh=mesh,
        in_specs=(
            rows, tall, tall, P("dp"), square, tall, tall, square, P("dp"), experts, experts, experts, rows
        ),
        out_specs=(rows, rows, P("dp"), square, tall, tall, square, P("dp"), experts, experts, experts),
        check_vma=False,
    )
```

```python
import jax
import jax.numpy as jnp
from jax import lax
from jax.experimental import pallas as pl
from jax.experimental.pallas import tpu as pltpu
from jax.sharding import PartitionSpec as P

KV = 2
HD = 128
EXPERTS = 32
TOPK = 4
SEQ = 1024
BLOCK = 256
CAP = 256
TAIL = 64
CALL_PAIRS = 4

eps = 1e-06
rope_base = 1000000.0
negative = -1e30
bf16 = jnp.bfloat16
f32 = jnp.float32


def nn(a, b):
    return jnp.dot(a, b, preferred_element_type=f32)


def nt(a, b):
    return lax.dot_general(a, b, (((1,), (1,)), ((), ())), preferred_element_type=f32)


def tn(a, b):
    return lax.dot_general(a, b, (((0,), (0,)), ((), ())), preferred_element_type=f32)


def rope_tables(positions):
    half = HD // 2
    frequency = rope_base ** (-(jnp.arange(half).astype(f32) * 2.0 / HD))
    angles = positions.astype(f32)[:, None] * frequency[None, :]
    return jnp.cos(angles), jnp.sin(angles)


def rotate(values, cos_table, sin_table):
    rows = values.shape[0]
    heads = values.reshape(rows, -1, 2, HD // 2)
    a, b = heads[:, :, 0], heads[:, :, 1]
    cos_table, sin_table = cos_table[:, None], sin_table[:, None]
    turned = jnp.stack([a * cos_table - b * sin_table, b * cos_table + a * sin_table], axis=2)
    return turned.reshape(rows, -1)


def rms_pieces(x):
    inverse = lax.rsqrt(jnp.mean(x * x, axis=-1, keepdims=True) + eps)
    return inverse, x * inverse


def rms_backward(grad, unit, inverse, gain):
    u = grad * gain
    back = inverse * (u - unit * jnp.mean(u * unit, axis=-1, keepdims=True))
    return back, jnp.sum(grad * unit, axis=0)


def probabilities(q, k, first_row):
    rows, keys = q.shape[0], k.shape[0]
    scores = nt(q, k) * (HD**-0.5)
    q_block = (first_row + lax.broadcasted_iota(jnp.int32, (rows, keys), 0)) // BLOCK
    k_block = lax.broadcasted_iota(jnp.int32, (rows, keys), 1) // BLOCK
    scores = jnp.where(k_block <= q_block, scores, negative)
    raised = jnp.exp(scores - jnp.max(scores, axis=-1, keepdims=True))
    return raised / jnp.sum(raised, axis=-1, keepdims=True)


def attend_forward(first_row, q, k, v):
    rows, width = q.shape
    heads = width // HD
    shared = heads // KV

    def kernel(first_ref, q_ref, k_ref, v_ref, o_ref):
        p = probabilities(q_ref[...], k_ref[...], first_ref[0]).astype(bf16)
        o_ref[...] = nn(p, v_ref[...]).astype(bf16)

    per_head = pl.BlockSpec((rows, HD), lambda h, f: (0, h))
    per_kv = pl.BlockSpec((k.shape[0], HD), lambda h, f: (0, h // shared))
    return pl.pallas_call(
        kernel,
        grid_spec=pltpu.PrefetchScalarGridSpec(
            num_scalar_prefetch=1,
            grid=(heads,),
            in_specs=[per_head, per_kv, per_kv],
            out_specs=per_head,
        ),
        out_shape=jax.ShapeDtypeStruct((rows, width), bf16),
        compiler_params=pltpu.CompilerParams(vmem_limit_bytes=32 * 2**20),
        cost_estimate=pl.CostEstimate(
            flops=4 * rows * width * k.shape[0],
            bytes_accessed=4 * rows * width,
            transcendentals=rows * heads * k.shape[0],
        ),
        name="attend",
    )(first_row, q, k, v)


def attend_backward(first_row, q, k, v, do):
    rows, width = q.shape
    keys = k.shape[0]
    heads = width // HD
    shared = heads // KV

    def kernel(first_ref, q_ref, k_ref, v_ref, do_ref, dq_ref, dk_ref, dv_ref):
        q_now, k_now, v_now, do_now = q_ref[...], k_ref[...], v_ref[...], do_ref[...]
        p = probabilities(q_now, k_now, first_ref[0])
        dp = nt(do_now, v_now)
        ds = (p * (dp - jnp.sum(p * dp, axis=-1, keepdims=True))).astype(bf16)
        dq_ref[...] = nn(ds, k_now) * (HD**-0.5)
        dk = tn(ds, q_now) * (HD**-0.5)
        dv = tn(p.astype(bf16), do_now)
        head = pl.program_id(0)

        @pl.when(lax.rem(head, shared) == 0)
        def _():
            dk_ref[...] = dk
            dv_ref[...] = dv

        @pl.when(lax.rem(head, shared) != 0)
        def _():
            dk_ref[...] += dk
            dv_ref[...] += dv

    per_head = pl.BlockSpec((rows, HD), lambda h, f: (0, h))
    per_kv = pl.BlockSpec((keys, HD), lambda h, f: (0, h // shared))
    return pl.pallas_call(
        kernel,
        grid_spec=pltpu.PrefetchScalarGridSpec(
            num_scalar_prefetch=1,
            grid=(heads,),
            in_specs=[per_head, per_kv, per_kv, per_head],
            out_specs=[per_head, per_kv, per_kv],
        ),
        out_shape=[
            jax.ShapeDtypeStruct((rows, width), f32),
            jax.ShapeDtypeStruct((keys, KV * HD), f32),
            jax.ShapeDtypeStruct((keys, KV * HD), f32),
        ],
        compiler_params=pltpu.CompilerParams(vmem_limit_bytes=32 * 2**20),
        cost_estimate=pl.CostEstimate(
            flops=10 * rows * width * keys,
            bytes_accessed=8 * rows * width,
            transcendentals=rows * heads * keys,
        ),
        name="attend_back",
    )(first_row, q, k, v, do)


def after(value, waits):
    if not waits:
        return value

    def kernel(*refs):
        del refs

    anywhere = pl.BlockSpec(memory_space=pl.ANY)
    return pl.pallas_call(
        kernel,
        in_specs=[anywhere] * (1 + len(waits)),
        out_specs=anywhere,
        out_shape=jax.ShapeDtypeStruct(value.shape, value.dtype),
        input_output_aliases={0: 0},
        name="after",
    )(value, *waits)


def sibling():
    me = lax.axis_index("dp")
    return me + 1 - 2 * lax.rem(me, 2)


def expert_call(rank_cols, rank_rows, weight_rows, x, gy, pieces, sums, exchange):
    rows, width = x.shape
    subs, count = len(pieces), len(pieces[0])
    height, lanes = pieces[0][0][0].shape[1:]
    pairs = rank_rows.shape[0] // 2
    sub_pairs = pairs // subs
    blocks = 12
    tile = 2 * width // blocks
    flat = []
    place = []
    for sub in pieces:
        place.append([])
        for array, begin in sub:
            known = [i for i, other in enumerate(flat) if other is array]
            if not known:
                flat.append(array)
            place[-1].append((known[0] if known else len(flat) - 1, begin))
    third = lanes // 3
    stride = 2 if exchange else 1

    def kernel(rank_c, rank_r, weight_r, x_ref, gy_ref, *rest):
        w_hbm = rest[: len(flat)]
        rest = rest[len(flat) :]
        sums_in, rest = rest[0], rest[1:]
        grad_out, sums_out, w_buf, y_buf, pick_buf, local_sem = rest[:6]
        step = pl.program_id(0)
        if exchange:
            kept, leaving, arriving, push_sem, pull_sem, send_sem, recv_sem, w_free, g_free = rest[6:]
            other = {"dp": sibling()}

        def weights(pair, slot, sub):
            found = []
            for k in range(count):
                array, begin = place[sub][k]
                source = w_hbm[array].at[pair - sub * sub_pairs + begin]
                target = w_buf.at[slot, pl.ds(stride * k * height, height)]
                found.append(pltpu.make_async_copy(source, target, local_sem.at[slot, k]))
                if exchange:
                    target = w_buf.at[slot, pl.ds((stride * k + 1) * height, height)]
                    found.append(
                        pltpu.make_async_remote_copy(
                            src_ref=source,
                            dst_ref=target,
                            send_sem=push_sem.at[slot, k],
                            recv_sem=pull_sem.at[slot, k],
                            device_id=other,
                            device_id_type=pl.DeviceIdType.MESH,
                        )
                    )
            return found

        def start(pair):
            slot = lax.rem(pair, 2)
            for sub in range(subs):

                @pl.when((pair >= sub * sub_pairs) & (pair < (sub + 1) * sub_pairs))
                def _():
                    for copy in weights(pair, slot, sub):
                        copy.start()

        def leave(slot):
            return pltpu.make_async_remote_copy(
                src_ref=leaving.at[slot],
                dst_ref=arriving.at[slot],
                send_sem=send_sem.at[slot],
                recv_sem=recv_sem.at[slot],
                device_id=other,
                device_id_type=pl.DeviceIdType.MESH,
            )

        def put(at, value, slot):
            for k in range(count):
                for parity in range(stride):
                    row = (stride * k + parity) * height
                    part = value[row : row + height].astype(bf16)
                    span = slice(at, at + value.shape[1])
                    if not exchange:
                        grad_out[k, 0, :, span] = part
                    elif parity == 0:
                        kept[slot, k, :, span] = part
                    else:
                        leaving[slot, k, :, span] = part

        def signal(sem):
            pl.semaphore_signal(sem, inc=1, device_id=other, device_id_type=pl.DeviceIdType.MESH)

        def finish(pair):
            slot = lax.rem(pair, 2)
            leave(slot).wait()
            for k in range(count):
                both = kept[slot, k].astype(f32) + arriving[slot, k].astype(f32)
                grad_out[k, 0] = both.astype(bf16)

        @pl.when(step == 0)
        def _():
            if exchange:
                barrier = pltpu.get_barrier_semaphore()
                signal(barrier)
                pl.semaphore_wait(barrier, 1)
            start(step)

        if exchange:

            @pl.when((step >= 1) & (step + 1 < pairs))
            def _():
                signal(w_free)
                pl.semaphore_wait(w_free, 1)

        @pl.when(step + 1 < pairs)
        def _():
            start(step + 1)

        @pl.when(step < pairs)
        def _():
            slot = lax.rem(step, 2)
            for copy in weights(0, slot, 0):
                copy.wait()
            w = w_buf.at[slot]
            low_half = lax.broadcasted_iota(jnp.int32, (CAP, HD), 1) < TAIL
            tails = []
            for q in range(2):
                e = 2 * step + q
                column = (lax.broadcasted_iota(jnp.int32, (HD, CAP), 0) == e).astype(bf16)
                rank = nn(rank_c[...], column)
                slot_of = lax.broadcasted_iota(jnp.int32, (rows, CAP), 1).astype(f32)
                at = pl.ds(pl.multiple_of(e * CAP, CAP), CAP)
                pick_buf[:, at] = (rank == slot_of).astype(bf16)
                hit = lax.broadcasted_iota(jnp.int32, (CAP, rows), 0) == rank_r[q]
                pick = hit.astype(bf16)
                weight = jnp.sum(jnp.where(hit, weight_r[q], 0.0), axis=1, keepdims=True)
                xe = nn(pick, x_ref[...]).astype(bf16)
                deo = (nn(pick, gy_ref[...]) * weight).astype(bf16)
                gate_up = slice(q * third, (q + 1) * third)
                down = slice(2 * third + q * HD, 2 * third + (q + 1) * HD)
                down_tail = slice(2 * third + 2 * HD, lanes)
                gu = nn(xe, w[:, gate_up])
                d0 = nn(deo, w[:, down])
                d1 = nn(deo, w[:, down_tail])
                if q == 1:
                    d1 = pltpu.roll(d1, TAIL, 1)
                tail = gu[:, 2 * HD :]

                def unit(gate, up, dact):
                    sig = jax.nn.sigmoid(gate)
                    silu = gate * sig
                    return silu * up, dact * up * sig * (1.0 + gate * (1.0 - sig)), dact * silu

                a0, dg0, du0 = unit(gu[:, :HD], gu[:, HD : 2 * HD], d0)
                a1, dg1, du1 = unit(tail, pltpu.roll(tail, TAIL, 1), d1)
                a1 = jnp.where(low_half, a1, 0.0)
                if q == 1:
                    a1 = pltpu.roll(a1, TAIL, 1)
                dgu1 = jnp.where(low_half, dg1, pltpu.roll(du1, TAIL, 1))
                a0, a1 = a0.astype(bf16), a1.astype(bf16)
                dgu = jnp.concatenate([dg0.astype(bf16), du0.astype(bf16), dgu1.astype(bf16)], axis=1)
                eo = nt(a0, w[:, down]) + nt(a1, w[:, down_tail])
                y_buf[at, :width] = (eo * weight).astype(bf16)
                y_buf[at, width:] = nt(dgu, w[:, gate_up]).astype(bf16)
                put(q * third, tn(xe, dgu), slot)
                put(2 * third + q * HD, tn(deo, a0), slot)
                tails.append((deo, a1))
            put(2 * third + 2 * HD, tn(*tails[0]) + tn(*tails[1]), slot)

        if exchange:

            @pl.when((step >= 1) & (step <= pairs))
            def _():
                finish(step - 1)

            @pl.when((step >= 1) & (step + 1 < pairs))
            def _():
                signal(g_free)

            @pl.when((step >= 2) & (step < pairs))
            def _():
                pl.semaphore_wait(g_free, 1)

            @pl.when(step < pairs)
            def _():
                leave(lax.rem(step, 2)).start()

        @pl.when(step >= pairs)
        def _():
            at = pl.ds(pl.multiple_of((step - pairs) * tile, tile), tile)
            sums_out[...] = sums_in[...] + nn(pick_buf[...], y_buf[:, at])

    def held(step):
        return jnp.minimum(step, pairs - 1)

    def behind(step):
        return jnp.clip(step - 1, 0, pairs - 1) if exchange else held(step)

    def block(step):
        return (0, jnp.maximum(step - pairs, 0))

    once = pl.Buffered(1)
    whole = pl.BlockSpec((rows, width), lambda s: (0, 0), pipeline_mode=once)
    routes = pl.BlockSpec((2, 1, rows), lambda s: (held(s), 0, 0))
    anywhere = pl.BlockSpec(memory_space=pl.ANY)
    dma = pltpu.SemaphoreType.DMA
    traded = [
        pltpu.VMEM((2, count, height, lanes), bf16),
        pltpu.VMEM((2, count, height, lanes), bf16),
        pltpu.VMEM((2, count, height, lanes), bf16),
        dma((2, count)),
        dma((2, count)),
        dma((2,)),
        dma((2,)),
        pltpu.SemaphoreType.REGULAR,
        pltpu.SemaphoreType.REGULAR,
    ]
    remote = dict(collective_id=1, has_side_effects=True) if exchange else {}
    return pl.pallas_call(
        kernel,
        grid=(pairs + blocks,),
        in_specs=[pl.BlockSpec((rows, HD), lambda s: (0, 0), pipeline_mode=once), routes, routes, whole, whole]
        + [anywhere] * len(flat)
        + [pl.BlockSpec((rows, tile), block)],
        out_specs=[
            pl.BlockSpec((count, 1, height, lanes), lambda s: (0, behind(s), 0, 0)),
            pl.BlockSpec((rows, tile), block),
        ],
        scratch_shapes=[
            pltpu.VMEM((2, width, lanes), bf16),
            pltpu.VMEM((2 * pairs * CAP, 2 * width), bf16),
            pltpu.VMEM((rows, 2 * pairs * CAP), bf16),
            dma((2, count)),
        ]
        + (traded if exchange else []),
        out_shape=[
            jax.ShapeDtypeStruct((count, pairs, height, lanes), bf16),
            jax.ShapeDtypeStruct((rows, 2 * width), f32),
        ],
        compiler_params=pltpu.CompilerParams(vmem_limit_bytes=62 * 10**6, **remote),
        cost_estimate=pl.CostEstimate(
            flops=pairs * 4 * CAP * width * (4 * rows * 2 + 18 * lanes // 6),
            bytes_accessed=8 * rows * width * 3,
            transcendentals=0,
        ),
        name="experts",
    )(rank_cols, rank_rows, weight_rows, x, gy, *flat, sums)


def pack(gate, up, down):
    def pair(a, b):
        return jnp.concatenate([a[..., :HD], b[..., :HD], a[..., HD:], b[..., HD:]], axis=-1)

    gate, up, down = (jnp.transpose(w, (1, 0, 2)) for w in (gate, up, down))
    gate_up = pair(gate, up)
    return jnp.concatenate([gate_up[0::2], gate_up[1::2], pair(down[0::2], down[1::2])], axis=-1)


def unpack(packed):
    n, height, lanes = packed.shape
    third = lanes // 3

    def halves(both):
        tail = third // 2 - HD
        a = jnp.concatenate([both[..., :HD], both[..., 2 * HD : 2 * HD + tail]], axis=-1)
        b = jnp.concatenate([both[..., HD : 2 * HD], both[..., 2 * HD + tail :]], axis=-1)
        return a, b

    def experts(even, odd):
        both = jnp.stack([even, odd], axis=1).reshape(2 * n, height, third // 2)
        return jnp.transpose(both, (1, 0, 2))

    gate0, up0 = halves(packed[..., :third])
    gate1, up1 = halves(packed[..., third : 2 * third])
    down0, down1 = halves(packed[..., 2 * third :])
    return experts(gate0, gate1), experts(up0, up1), experts(down0, down1)


def flip(value, bit):
    count = lax.axis_size("dp")
    return lax.ppermute(value, "dp", [(i, i ^ bit) for i in range(count)])


def relative(values, me):
    rows, width = values.shape
    blocks = values.reshape(rows, 2, 2, 2 * (width // 8))
    for axis, bit in ((1, 4), (2, 2)):
        blocks = jnp.where((me & bit) != 0, jnp.flip(blocks, axis), blocks)
    cut = width // 8
    swapped = jnp.concatenate([blocks[..., cut:], blocks[..., :cut]], axis=-1)
    blocks = jnp.where((me & 1) != 0, swapped, blocks)
    return blocks.reshape(rows, width)


def gather_step(waiting, arrived):
    to_x = ([arrived[1][half_of(arrived[1])[1]]] if arrived else []) + ([waiting] if waiting is not None else [])
    to_y = ([arrived[0][half_of(arrived[0])[0]]] if arrived else []) + ([waiting] if waiting is not None else [])
    return flip(jnp.concatenate(to_x), 2), flip(jnp.concatenate(to_y), 4)


def half_of(chunk):
    cut = chunk.shape[0] // 2
    return slice(0, cut), slice(cut, None)


def scatter_step(chunk, before):
    to_x, to_y = [], []
    if before is not None:
        blocks, via_x, via_y = before
        first, second = half_of(blocks[0])
        to_x += [blocks[1, first], add(blocks[1, second], via_y)]
        to_y += [add(blocks[2, first], via_x), blocks[2, second]]
    if chunk is not None:
        first, second = half_of(chunk[0])
        to_x.append(chunk[3, first])
        to_y.append(chunk[3, second])
    return flip(jnp.concatenate(to_x), 2), flip(jnp.concatenate(to_y), 4)


def before_of(chunks, moved, call):
    if call == 0:
        return None
    cut = CALL_PAIRS // 2
    return chunks[call - 1], moved[call - 1][0][-cut:], moved[call - 1][1][-cut:]


def add(a, b):
    return (a.astype(f32) + b.astype(f32)).astype(bf16)


def body(
    tokens,
    expert_ids,
    route_weights,
    attn_gain,
    q_weight,
    k_weight,
    v_weight,
    o_weight,
    moe_gain,
    gate_weight,
    up_weight,
    down_weight,
    cotangent,
):
    members = lax.axis_size("tensor")
    member = lax.axis_index("tensor")
    devices = lax.axis_size("dp")
    me = lax.axis_index("dp")
    own_rows, width = tokens.shape
    rows = own_rows * members
    by_bits = devices == 8
    pairs = EXPERTS // 2
    calls = pairs // CALL_PAIRS
    sub_pairs = CALL_PAIRS // 2

    packed = [
        pack(*(w[:, 2 * CALL_PAIRS * i : 2 * CALL_PAIRS * (i + 1)] for w in (gate_weight, up_weight, down_weight)))
        for i in range(calls)
    ]
    if by_bits:
        steps = [gather_step(packed[0], None)]
        for i in range(calls):
            arrived = tuple(got[-CALL_PAIRS:] for got in steps[i])
            steps.append(gather_step(packed[i + 1] if i + 1 < calls else None, arrived))
        gathered = []
        for i in range(calls):
            from_x, from_y = (got[-CALL_PAIRS:] for got in steps[i])
            second, first = (got[:sub_pairs] for got in steps[i + 1])
            gathered.append(
                [
                    [(packed[i], 0), (from_x, 0), (from_y, 0), (first, 0)],
                    [(packed[i], sub_pairs), (from_x, sub_pairs), (from_y, sub_pairs), (second, 0)],
                ]
            )
    else:
        gathered = [[[(lax.all_gather(own, "dp", axis=1, tiled=True), 0)]] for own in packed]

    gain_one = lax.all_gather(attn_gain, "dp", axis=0, tiled=True).astype(f32)
    gain_two = lax.all_gather(moe_gain, "dp", axis=0, tiled=True).astype(f32)
    kv_full = lax.all_gather(jnp.concatenate([k_weight, v_weight], axis=1), "dp", axis=0, tiled=True)
    q_full = lax.all_gather(lax.all_gather(q_weight, "dp", axis=0, tiled=True), "tensor", axis=0)
    o_full = lax.all_gather(lax.all_gather(o_weight, "dp", axis=0, tiled=True), "tensor", axis=0)
    kv_width = k_weight.shape[1]

    lanes = jnp.arange(EXPERTS, dtype=jnp.int32)
    named = expert_ids[:, :, None] == lanes
    member_of = jnp.any(named, axis=1)
    weight_of = jnp.sum(jnp.where(named, route_weights[:, :, None], 0.0), axis=1)
    earlier = jnp.arange(rows)[:, None] > jnp.arange(rows)[None, :]
    rank = jnp.where(member_of, nn(earlier.astype(bf16), member_of.astype(bf16)), -1.0)
    rank_cols = jnp.pad(rank, ((0, 0), (0, HD)), constant_values=-1.0).astype(bf16)
    rank_rows = rank.T.astype(jnp.int32).reshape(EXPERTS, 1, rows)
    weight_rows = weight_of.T.reshape(EXPERTS, 1, rows)

    grad_low = cotangent.astype(bf16)
    if by_bits:
        grad_low = relative(grad_low, me)
    grad_all = lax.all_gather(grad_low, "tensor", axis=0, tiled=True)

    x = tokens.astype(f32)
    inverse_one, unit_one = rms_pieces(x)
    normed_one = (unit_one * gain_one).astype(bf16)
    first_row = (member * own_rows).reshape(1)
    cos_table, sin_table = rope_tables(member * own_rows + jnp.arange(own_rows, dtype=jnp.int32))
    kv_own = nn(normed_one, kv_full)
    kv_own = jnp.concatenate(
        [rotate(kv_own[:, :kv_width], cos_table, sin_table), kv_own[:, kv_width:]], axis=1
    ).astype(bf16)
    kv_all = lax.all_gather(kv_own, "tensor", axis=0, tiled=True)
    keys, values = kv_all[:, :kv_width], kv_all[:, kv_width:]
    queries = jnp.concatenate([nn(normed_one, q_full[t]) for t in range(members)], axis=1)
    queries = rotate(queries, cos_table, sin_table).astype(bf16)
    mixed = attend_forward(after(first_row, steps[0] if by_bits else ()), queries, keys, values)
    part = width // members
    branch = sum(nt(mixed[:, t * part : (t + 1) * part], o_full[t]) for t in range(members))
    hidden = x + branch
    inverse_two, unit_two = rms_pieces(hidden)
    normed_two = (unit_two * gain_two).astype(bf16)
    if by_bits:
        normed_two = relative(normed_two, me)
    rows_all = lax.all_gather(normed_two, "tensor", axis=0, tiled=True)

    sums = jnp.zeros((rows, 2 * width), f32)
    chunks, moved = [], []
    for call in range(calls):
        some = slice(2 * CALL_PAIRS * call, 2 * CALL_PAIRS * (call + 1))
        columns = slice(2 * CALL_PAIRS * call, 2 * CALL_PAIRS * call + HD)
        grads, sums = expert_call(
            rank_cols[:, columns],
            after(rank_rows[some], moved[call - 2] if by_bits and call >= 2 else ()),
            weight_rows[some],
            rows_all,
            grad_all,
            gathered[call],
            sums,
            by_bits,
        )
        chunks.append(grads)
        if by_bits:
            moved.append(scatter_step(grads, before_of(chunks, moved, call)))
    if by_bits:
        moved.append(scatter_step(None, before_of(chunks, moved, calls)))
        shares = []
        for call in range(calls):
            from_x, from_y = (got[:CALL_PAIRS].astype(f32) for got in moved[call + 1])
            shares.append(unpack(chunks[call][0].astype(f32) + from_x + from_y))
    else:
        shares = [
            unpack(lax.psum_scatter(grads[0], "dp", scatter_dimension=1, tiled=True).astype(f32))
            for grads in chunks
        ]
    gate_out, up_out, down_out = (jnp.concatenate(parts, axis=1) for parts in zip(*shares))

    low_sums = sums.astype(bf16)
    normed_grad = lax.psum_scatter(low_sums[:, width:], "tensor", scatter_dimension=0, tiled=True).astype(f32)
    moe_own = lax.psum_scatter(low_sums[:, :width], "tensor", scatter_dimension=0, tiled=True).astype(f32)
    if by_bits:
        normed_grad, moe_own = relative(normed_grad, me), relative(moe_own, me)
    output = (hidden + moe_own).astype(bf16)

    back_two, gain_two_part = rms_backward(normed_grad, unit_two, inverse_two, gain_two)
    hidden_grad = cotangent + back_two
    hidden_low = hidden_grad.astype(bf16)
    mixed_grad = jnp.concatenate([nn(hidden_low, o_full[t]) for t in range(members)], axis=1).astype(bf16)
    o_part = jnp.stack([tn(hidden_low, mixed[:, t * part : (t + 1) * part]) for t in range(members)])
    dq, dk, dv = attend_backward(
        after(first_row, moved[calls - 2] if by_bits else ()), queries, keys, values, mixed_grad
    )
    kv_grad = lax.psum_scatter(
        jnp.concatenate([dk, dv], axis=1).astype(bf16), "tensor", scatter_dimension=0, tiled=True
    ).astype(f32)
    dq_low = rotate(dq, cos_table, -sin_table).astype(bf16)
    kv_low = jnp.concatenate(
        [rotate(kv_grad[:, :kv_width], cos_table, -sin_table), kv_grad[:, kv_width:]], axis=1
    ).astype(bf16)
    normed_one_grad = nt(kv_low, kv_full) + sum(
        nt(dq_low[:, t * part : (t + 1) * part], q_full[t]) for t in range(members)
    )
    back_one, gain_one_part = rms_backward(normed_one_grad, unit_one, inverse_one, gain_one)
    tokens_grad = hidden_grad + back_one
    q_part = jnp.stack([tn(normed_one, dq_low[:, t * part : (t + 1) * part]) for t in range(members)])
    kv_part = tn(normed_one, kv_low)

    def shared(values):
        summed = lax.psum_scatter(values.astype(bf16), "tensor", scatter_dimension=0, tiled=False)
        return lax.psum_scatter(summed, "dp", scatter_dimension=0, tiled=True).astype(f32)

    q_grad, o_grad = shared(q_part), shared(o_part)
    small = jnp.concatenate([kv_part, gain_one_part[:, None], gain_two_part[:, None]], axis=1)
    small = lax.psum_scatter(small, "dp", scatter_dimension=0, tiled=True)
    small = lax.psum(small.astype(bf16), "tensor").astype(f32)
    return (
        output,
        tokens_grad,
        small[:, 2 * kv_width],
        q_grad,
        small[:, :kv_width],
        small[:, kv_width : 2 * kv_width],
        o_grad,
        small[:, 2 * kv_width + 1],
        gate_out,
        up_out,
        down_out,
    )


def solution(mesh):
    rows = P(("dp", "tensor"), None)
    experts = P("dp", None, "tensor")
    square = P("dp", "tensor")
    tall = P("dp", None)
    return jax.shard_map(
        body,
        mesh=mesh,
        in_specs=(
            rows, tall, tall, P("dp"), square, tall, tall, square, P("dp"), experts, experts, experts, rows
        ),
        out_specs=(rows, rows, P("dp"), square, tall, tall, square, P("dp"), experts, experts, experts),
        check_vma=False,
    )
```

```python
import jax
import jax.numpy as jnp
from jax import lax
from jax.experimental import pallas as pl
from jax.experimental.pallas import tpu as pltpu
from jax.sharding import PartitionSpec as P

KV = 2
HD = 128
EXPERTS = 32
TOPK = 4
SEQ = 1024
BLOCK = 256
CAP = 256
TAIL = 64
CALL_PAIRS = 4

eps = 1e-06
rope_base = 1000000.0
negative = -1e30
bf16 = jnp.bfloat16
f32 = jnp.float32


def nn(a, b):
    return jnp.dot(a, b, preferred_element_type=f32)


def nt(a, b):
    return lax.dot_general(a, b, (((1,), (1,)), ((), ())), preferred_element_type=f32)


def tn(a, b):
    return lax.dot_general(a, b, (((0,), (0,)), ((), ())), preferred_element_type=f32)


def rope_tables(positions):
    half = HD // 2
    frequency = rope_base ** (-(jnp.arange(half).astype(f32) * 2.0 / HD))
    angles = positions.astype(f32)[:, None] * frequency[None, :]
    return jnp.cos(angles), jnp.sin(angles)


def rotate(values, cos_table, sin_table):
    rows = values.shape[0]
    heads = values.reshape(rows, -1, 2, HD // 2)
    a, b = heads[:, :, 0], heads[:, :, 1]
    cos_table, sin_table = cos_table[:, None], sin_table[:, None]
    turned = jnp.stack([a * cos_table - b * sin_table, b * cos_table + a * sin_table], axis=2)
    return turned.reshape(rows, -1)


def rms_pieces(x):
    inverse = lax.rsqrt(jnp.mean(x * x, axis=-1, keepdims=True) + eps)
    return inverse, x * inverse


def rms_backward(grad, unit, inverse, gain):
    u = grad * gain
    back = inverse * (u - unit * jnp.mean(u * unit, axis=-1, keepdims=True))
    return back, jnp.sum(grad * unit, axis=0)


def probabilities(q, k, first_row):
    rows, keys = q.shape[0], k.shape[0]
    scores = nt(q, k) * (HD**-0.5)
    q_block = (first_row + lax.broadcasted_iota(jnp.int32, (rows, keys), 0)) // BLOCK
    k_block = lax.broadcasted_iota(jnp.int32, (rows, keys), 1) // BLOCK
    scores = jnp.where(k_block <= q_block, scores, negative)
    raised = jnp.exp(scores - jnp.max(scores, axis=-1, keepdims=True))
    return raised / jnp.sum(raised, axis=-1, keepdims=True)


def attend_forward(first_row, q, k, v):
    rows, width = q.shape
    heads = width // HD
    shared = heads // KV

    def kernel(first_ref, q_ref, k_ref, v_ref, o_ref):
        p = probabilities(q_ref[...], k_ref[...], first_ref[0]).astype(bf16)
        o_ref[...] = nn(p, v_ref[...]).astype(bf16)

    per_head = pl.BlockSpec((rows, HD), lambda h, f: (0, h))
    per_kv = pl.BlockSpec((k.shape[0], HD), lambda h, f: (0, h // shared))
    return pl.pallas_call(
        kernel,
        grid_spec=pltpu.PrefetchScalarGridSpec(
            num_scalar_prefetch=1,
            grid=(heads,),
            in_specs=[per_head, per_kv, per_kv],
            out_specs=per_head,
        ),
        out_shape=jax.ShapeDtypeStruct((rows, width), bf16),
        compiler_params=pltpu.CompilerParams(vmem_limit_bytes=32 * 2**20),
        cost_estimate=pl.CostEstimate(
            flops=4 * rows * width * k.shape[0],
            bytes_accessed=4 * rows * width,
            transcendentals=rows * heads * k.shape[0],
        ),
        name="attend",
    )(first_row, q, k, v)


def attend_backward(first_row, q, k, v, do):
    rows, width = q.shape
    keys = k.shape[0]
    heads = width // HD
    shared = heads // KV

    def kernel(first_ref, q_ref, k_ref, v_ref, do_ref, dq_ref, dk_ref, dv_ref):
        q_now, k_now, v_now, do_now = q_ref[...], k_ref[...], v_ref[...], do_ref[...]
        p = probabilities(q_now, k_now, first_ref[0])
        dp = nt(do_now, v_now)
        ds = (p * (dp - jnp.sum(p * dp, axis=-1, keepdims=True))).astype(bf16)
        dq_ref[...] = nn(ds, k_now) * (HD**-0.5)
        dk = tn(ds, q_now) * (HD**-0.5)
        dv = tn(p.astype(bf16), do_now)
        head = pl.program_id(0)

        @pl.when(lax.rem(head, shared) == 0)
        def _():
            dk_ref[...] = dk
            dv_ref[...] = dv

        @pl.when(lax.rem(head, shared) != 0)
        def _():
            dk_ref[...] += dk
            dv_ref[...] += dv

    per_head = pl.BlockSpec((rows, HD), lambda h, f: (0, h))
    per_kv = pl.BlockSpec((keys, HD), lambda h, f: (0, h // shared))
    return pl.pallas_call(
        kernel,
        grid_spec=pltpu.PrefetchScalarGridSpec(
            num_scalar_prefetch=1,
            grid=(heads,),
            in_specs=[per_head, per_kv, per_kv, per_head],
            out_specs=[per_head, per_kv, per_kv],
        ),
        out_shape=[
            jax.ShapeDtypeStruct((rows, width), f32),
            jax.ShapeDtypeStruct((keys, KV * HD), f32),
            jax.ShapeDtypeStruct((keys, KV * HD), f32),
        ],
        compiler_params=pltpu.CompilerParams(vmem_limit_bytes=32 * 2**20),
        cost_estimate=pl.CostEstimate(
            flops=10 * rows * width * keys,
            bytes_accessed=8 * rows * width,
            transcendentals=rows * heads * keys,
        ),
        name="attend_back",
    )(first_row, q, k, v, do)


def after(value, waits):
    if not waits:
        return value

    def kernel(*refs):
        del refs

    anywhere = pl.BlockSpec(memory_space=pl.ANY)
    return pl.pallas_call(
        kernel,
        in_specs=[anywhere] * (1 + len(waits)),
        out_specs=anywhere,
        out_shape=jax.ShapeDtypeStruct(value.shape, value.dtype),
        input_output_aliases={0: 0},
        name="after",
    )(value, *waits)


def sibling():
    me = lax.axis_index("dp")
    return me + 1 - 2 * lax.rem(me, 2)


def expert_call(rank_cols, rank_rows, weight_rows, x, gy, pieces, sums, exchange):
    rows, width = x.shape
    subs, count = len(pieces), len(pieces[0])
    height, lanes = pieces[0][0][0].shape[1:]
    pairs = rank_rows.shape[0] // 2
    sub_pairs = pairs // subs
    blocks = 12
    tile = 2 * width // blocks
    flat = []
    place = []
    for sub in pieces:
        place.append([])
        for array, begin in sub:
            known = [i for i, other in enumerate(flat) if other is array]
            if not known:
                flat.append(array)
            place[-1].append((known[0] if known else len(flat) - 1, begin))
    third = lanes // 3
    stride = 2 if exchange else 1

    def kernel(rank_c, rank_r, weight_r, x_ref, gy_ref, *rest):
        w_hbm = rest[: len(flat)]
        rest = rest[len(flat) :]
        sums_in, rest = rest[0], rest[1:]
        grad_out, sums_out, w_buf, y_buf, pick_buf, local_sem = rest[:6]
        step = pl.program_id(0)
        if exchange:
            kept, leaving, arriving, push_sem, pull_sem, send_sem, recv_sem, w_free, g_free = rest[6:]
            other = {"dp": sibling()}

        def weights(pair, slot, sub):
            found = []
            for k in range(count):
                array, begin = place[sub][k]
                source = w_hbm[array].at[pair - sub * sub_pairs + begin]
                target = w_buf.at[slot, pl.ds(stride * k * height, height)]
                found.append(pltpu.make_async_copy(source, target, local_sem.at[slot, k]))
                if exchange:
                    target = w_buf.at[slot, pl.ds((stride * k + 1) * height, height)]
                    found.append(
                        pltpu.make_async_remote_copy(
                            src_ref=source,
                            dst_ref=target,
                            send_sem=push_sem.at[slot, k],
                            recv_sem=pull_sem.at[slot, k],
                            device_id=other,
                            device_id_type=pl.DeviceIdType.MESH,
                        )
                    )
            return found

        def start(pair):
            slot = lax.rem(pair, 2)
            for sub in range(subs):

                @pl.when((pair >= sub * sub_pairs) & (pair < (sub + 1) * sub_pairs))
                def _():
                    for copy in weights(pair, slot, sub):
                        copy.start()

        def leave(slot):
            return pltpu.make_async_remote_copy(
                src_ref=leaving.at[slot],
                dst_ref=arriving.at[slot],
                send_sem=send_sem.at[slot],
                recv_sem=recv_sem.at[slot],
                device_id=other,
                device_id_type=pl.DeviceIdType.MESH,
            )

        def put(at, value, slot):
            for k in range(count):
                for parity in range(stride):
                    row = (stride * k + parity) * height
                    part = value[row : row + height].astype(bf16)
                    span = slice(at, at + value.shape[1])
                    if not exchange:
                        grad_out[k, 0, :, span] = part
                    elif parity == 0:
                        kept[slot, k, :, span] = part
                    else:
                        leaving[slot, k, :, span] = part

        def signal(sem):
            pl.semaphore_signal(sem, inc=1, device_id=other, device_id_type=pl.DeviceIdType.MESH)

        def finish(pair):
            slot = lax.rem(pair, 2)
            leave(slot).wait()
            for k in range(count):
                both = kept[slot, k].astype(f32) + arriving[slot, k].astype(f32)
                grad_out[k, 0] = both.astype(bf16)

        @pl.when(step == 0)
        def _():
            if exchange:
                barrier = pltpu.get_barrier_semaphore()
                signal(barrier)
                pl.semaphore_wait(barrier, 1)
            start(step)

        if exchange:

            @pl.when((step >= 1) & (step + 1 < pairs))
            def _():
                signal(w_free)
                pl.semaphore_wait(w_free, 1)

        @pl.when(step + 1 < pairs)
        def _():
            start(step + 1)

        @pl.when(step < pairs)
        def _():
            slot = lax.rem(step, 2)
            for copy in weights(0, slot, 0):
                copy.wait()
            w = w_buf.at[slot]
            low_half = lax.broadcasted_iota(jnp.int32, (CAP, HD), 1) < TAIL
            tails = []
            for q in range(2):
                e = 2 * step + q
                column = (lax.broadcasted_iota(jnp.int32, (HD, CAP), 0) == e).astype(bf16)
                rank = nn(rank_c[...], column)
                slot_of = lax.broadcasted_iota(jnp.int32, (rows, CAP), 1).astype(f32)
                at = pl.ds(pl.multiple_of(e * CAP, CAP), CAP)
                pick_buf[:, at] = (rank == slot_of).astype(bf16)
                hit = lax.broadcasted_iota(jnp.int32, (CAP, rows), 0) == rank_r[q]
                pick = hit.astype(bf16)
                weight = jnp.sum(jnp.where(hit, weight_r[q], 0.0), axis=1, keepdims=True)
                xe = nn(pick, x_ref[...]).astype(bf16)
                deo = (nn(pick, gy_ref[...]) * weight).astype(bf16)
                gate_up = slice(q * third, (q + 1) * third)
                down = slice(2 * third + q * HD, 2 * third + (q + 1) * HD)
                down_tail = slice(2 * third + 2 * HD, lanes)
                gu = nn(xe, w[:, gate_up])
                d0 = nn(deo, w[:, down])
                d1 = nn(deo, w[:, down_tail])
                if q == 1:
                    d1 = pltpu.roll(d1, TAIL, 1)
                tail = gu[:, 2 * HD :]

                def unit(gate, up, dact):
                    sig = jax.nn.sigmoid(gate)
                    silu = gate * sig
                    return silu * up, dact * up * sig * (1.0 + gate * (1.0 - sig)), dact * silu

                a0, dg0, du0 = unit(gu[:, :HD], gu[:, HD : 2 * HD], d0)
                a1, dg1, du1 = unit(tail, pltpu.roll(tail, TAIL, 1), d1)
                a1 = jnp.where(low_half, a1, 0.0)
                if q == 1:
                    a1 = pltpu.roll(a1, TAIL, 1)
                dgu1 = jnp.where(low_half, dg1, pltpu.roll(du1, TAIL, 1))
                a0, a1 = a0.astype(bf16), a1.astype(bf16)
                dgu = jnp.concatenate([dg0.astype(bf16), du0.astype(bf16), dgu1.astype(bf16)], axis=1)
                eo = nt(a0, w[:, down]) + nt(a1, w[:, down_tail])
                y_buf[at, :width] = (eo * weight).astype(bf16)
                y_buf[at, width:] = nt(dgu, w[:, gate_up]).astype(bf16)
                put(q * third, tn(xe, dgu), slot)
                put(2 * third + q * HD, tn(deo, a0), slot)
                tails.append((deo, a1))
            put(2 * third + 2 * HD, tn(*tails[0]) + tn(*tails[1]), slot)

        if exchange:

            @pl.when((step >= 1) & (step <= pairs))
            def _():
                finish(step - 1)

            @pl.when((step >= 1) & (step + 1 < pairs))
            def _():
                signal(g_free)

            @pl.when((step >= 2) & (step < pairs))
            def _():
                pl.semaphore_wait(g_free, 1)

            @pl.when(step < pairs)
            def _():
                leave(lax.rem(step, 2)).start()

        @pl.when(step >= pairs)
        def _():
            at = pl.ds(pl.multiple_of((step - pairs) * tile, tile), tile)
            sums_out[...] = sums_in[...] + nn(pick_buf[...], y_buf[:, at])

    def held(step):
        return jnp.minimum(step, pairs - 1)

    def behind(step):
        return jnp.clip(step - 1, 0, pairs - 1) if exchange else held(step)

    def block(step):
        return (0, jnp.maximum(step - pairs, 0))

    once = pl.Buffered(1)
    whole = pl.BlockSpec((rows, width), lambda s: (0, 0), pipeline_mode=once)
    routes = pl.BlockSpec((2, 1, rows), lambda s: (held(s), 0, 0))
    anywhere = pl.BlockSpec(memory_space=pl.ANY)
    dma = pltpu.SemaphoreType.DMA
    traded = [
        pltpu.VMEM((2, count, height, lanes), bf16),
        pltpu.VMEM((2, count, height, lanes), bf16),
        pltpu.VMEM((2, count, height, lanes), bf16),
        dma((2, count)),
        dma((2, count)),
        dma((2,)),
        dma((2,)),
        pltpu.SemaphoreType.REGULAR,
        pltpu.SemaphoreType.REGULAR,
    ]
    remote = dict(collective_id=1, has_side_effects=True) if exchange else {}
    return pl.pallas_call(
        kernel,
        grid=(pairs + blocks,),
        in_specs=[pl.BlockSpec((rows, HD), lambda s: (0, 0), pipeline_mode=once), routes, routes, whole, whole]
        + [anywhere] * len(flat)
        + [pl.BlockSpec((rows, tile), block)],
        out_specs=[
            pl.BlockSpec((count, 1, height, lanes), lambda s: (0, behind(s), 0, 0)),
            pl.BlockSpec((rows, tile), block),
        ],
        scratch_shapes=[
            pltpu.VMEM((2, width, lanes), bf16),
            pltpu.VMEM((2 * pairs * CAP, 2 * width), bf16),
            pltpu.VMEM((rows, 2 * pairs * CAP), bf16),
            dma((2, count)),
        ]
        + (traded if exchange else []),
        out_shape=[
            jax.ShapeDtypeStruct((count, pairs, height, lanes), bf16),
            jax.ShapeDtypeStruct((rows, 2 * width), f32),
        ],
        compiler_params=pltpu.CompilerParams(vmem_limit_bytes=62 * 10**6, **remote),
        cost_estimate=pl.CostEstimate(
            flops=pairs * 4 * CAP * width * (4 * rows * 2 + 18 * lanes // 6),
            bytes_accessed=8 * rows * width * 3,
            transcendentals=0,
        ),
        name="experts",
    )(rank_cols, rank_rows, weight_rows, x, gy, *flat, sums)


def remote(source, target, send_sem, recv_sem, device):
    return pltpu.make_async_remote_copy(
        src_ref=source,
        dst_ref=target,
        send_sem=send_sem,
        recv_sem=recv_sem,
        device_id=device,
        device_id_type=pl.DeviceIdType.MESH,
    )


def chip_neighbours():
    me = lax.axis_index("dp")
    return me + 2 - 4 * lax.rem(me // 2, 2), me + 4 - 8 * lax.rem(me // 4, 2)


def meet(members, chips):
    barrier = pltpu.get_barrier_semaphore()
    z = lax.axis_index("tensor")

    def signal(device):
        pl.semaphore_signal(barrier, inc=1, device_id=device, device_id_type=pl.DeviceIdType.MESH)

    @pl.when(z > 0)
    def _():
        signal({"tensor": z - 1})

    @pl.when(z < members - 1)
    def _():
        signal({"tensor": z + 1})

    if chips:
        for other in (*chip_neighbours(), sibling()):
            signal({"dp": other})
    inner = jnp.where((z > 0) & (z < members - 1), 1, 0)
    pl.semaphore_wait(barrier, 1 + inner + (3 if chips else 0))


class LineGather:
    def __init__(self, members, at, send, recv):
        self.members, self.at, self.send, self.recv = members, at, send, recv

    def copies(self, hop):
        z, last = lax.axis_index("tensor"), self.members - 1
        up, down = z - hop + 1, z + hop - 1

        def copy(block, way, device):
            return lambda: remote(
                self.at(block), self.at(block), self.send.at[way, hop - 1], self.recv.at[way, hop - 1], {"tensor": device}
            )

        return (
            ((up >= 0) & (z < last), copy(up, 0, z + 1)),
            ((down <= last) & (z > 0), copy(down, 1, z - 1)),
        ), (
            (z - hop >= 0, copy(z - hop, 0, z)),
            (z + hop <= last, copy(z + hop, 1, z)),
        )

    def start(self, hop):
        for present, copy in self.copies(hop)[0]:

            @pl.when(present)
            def _():
                copy().start()

    def arrive(self, hop):
        for present, copy in self.copies(hop)[1]:

            @pl.when(present)
            def _():
                copy().wait_recv()

    def close(self):
        for hop in range(1, self.members):
            for present, copy in self.copies(hop)[0]:

                @pl.when(present)
                def _():
                    copy().wait_send()


class LineSum:
    def __init__(self, members, part, leaving, arriving, send, recv):
        self.members, self.part, self.leaving, self.arriving = members, part, leaving, arriving
        self.send, self.recv = send, recv

    def copy(self, way, hop, device):
        return remote(
            self.leaving.at[way],
            self.arriving.at[way, hop - 1],
            self.send.at[way, hop - 1],
            self.recv.at[way, hop - 1],
            {"tensor": device},
        )

    def ways(self, hop):
        z, last = lax.axis_index("tensor"), self.members - 1
        return (
            (0, z - hop >= 0, z - hop, z < last, z - 1, (z < last) & (z + 1 - hop >= 0)),
            (1, z + hop <= last, z + hop, z > 0, z + 1, (z > 0) & (z - 1 + hop <= last)),
        )

    def start(self, hop):
        if hop + 1 < self.members:
            self.leave(hop + 1)
        for way, present, block, behind, device, _ in self.ways(hop):

            @pl.when(present)
            def _():
                self.leaving[way] = self.part(block).astype(bf16)

            if hop + 1 < self.members:

                @pl.when(present & behind)
                def _():
                    both = self.part(block).astype(f32) + self.arriving[way, hop].astype(f32)
                    self.leaving[way] = both.astype(bf16)

            @pl.when(present)
            def _():
                self.copy(way, hop, device).start()

    def arrive(self, hop):
        for way, _, _, _, device, present in self.ways(hop):

            @pl.when(present)
            def _():
                self.copy(way, hop, device).wait_recv()

    def total(self, out):
        z, last = lax.axis_index("tensor"), self.members - 1
        out[...] = self.part(z).astype(f32)
        for way, present in ((0, z < last), (1, z > 0)):

            @pl.when(present)
            def _():
                out[...] += self.arriving[way, 0].astype(f32)

    def leave(self, hop):
        for way, present, _, _, device, _ in self.ways(hop):

            @pl.when(present)
            def _():
                self.copy(way, hop, device).wait_send()

    def close(self):
        self.leave(1)


def swap_blocks(values):
    me = lax.axis_index("dp")
    chip = values.shape[1] // 4
    four = [values[:, i * chip : (i + 1) * chip] for i in range(4)]
    y_side, x_side, core_side = lax.rem(me // 4, 2) == 1, lax.rem(me // 2, 2) == 1, lax.rem(me, 2) == 1
    four = [jnp.where(y_side, four[i ^ 2], four[i]) for i in range(4)]
    four = [jnp.where(x_side, four[i ^ 1], four[i]) for i in range(4)]
    four = [jnp.where(core_side, pltpu.roll(part, chip // 2, 1), part) for part in four]
    return jnp.concatenate(four, axis=1)


def in_vmem(count):
    return [pl.BlockSpec(memory_space=pltpu.VMEM)] * count


def gather_small(square, tall, cotangent, members, devices):
    height = square.shape[0]
    own_rows, width = cotangent.shape
    dma = pltpu.SemaphoreType.DMA
    cut = square.shape[1] // 2

    def kernel(square_ref, tall_ref, cot_ref, square_all, tall_all, grad_all, *sems):
        line_send, line_recv, grad_send, grad_recv, chip_send, chip_recv, core_send, core_recv = sems
        me, z = lax.axis_index("dp"), lax.axis_index("tensor")
        x_side, y_side = chip_neighbours()
        core = sibling()
        meet(members, True)

        def rows(device):
            return pl.ds(pl.multiple_of(device * height, 16), height)

        square_all[z, rows(me), :] = square_ref[...]
        tall_all[rows(me), :] = tall_ref[...]
        line = LineGather(members, lambda block: square_all.at[block, rows(me)], line_send, line_recv)
        group = LineGather(
            members,
            lambda block: grad_all.at[pl.ds(pl.multiple_of(block * own_rows, 16), own_rows)],
            grad_send,
            grad_recv,
        )

        def chip(index, source, device):
            return remote(source, source, chip_send.at[index], chip_recv.at[index], {"dp": device})

        def across(index, source):
            return remote(source, source, core_send.at[index], core_recv.at[index], {"dp": core})

        def tall_at(device):
            return tall_all.at[rows(device)]

        def square_at(device, half=None):
            lanes = slice(None) if half is None else slice(half * cut, (half + 1) * cut)
            return square_all.at[:, rows(device), lanes]

        line.start(1)
        near = [chip(0, tall_at(me), x_side), chip(1, tall_at(me), y_side)]
        for copy in near:
            copy.start()
        grad_all[pl.ds(pl.multiple_of(z * own_rows, 16), own_rows), :] = swap_blocks(cot_ref[...]).astype(bf16)
        for hop in range(1, members):
            line.arrive(hop)
            if hop + 1 < members:
                line.start(hop + 1)
        near += [chip(2, square_at(me), x_side), chip(3, square_at(me), y_side)]
        for copy in near[2:]:
            copy.start()
        group.start(1)
        trades = [across(0, tall_at(me)), across(1, square_at(me))]
        for copy in trades:
            copy.start()
        chip(0, tall_at(x_side), x_side).wait_recv()
        chip(1, tall_at(y_side), y_side).wait_recv()
        diagonal = x_side + y_side - me
        far = [chip(4, tall_at(x_side), y_side)]
        far[0].start()
        trades += [across(2, tall_at(x_side)), across(3, tall_at(y_side))]
        for copy in trades[2:]:
            copy.start()
        group.arrive(1)
        if members > 2:
            group.start(2)
        chip(2, square_at(x_side), x_side).wait_recv()
        chip(3, square_at(y_side), y_side).wait_recv()
        far += [chip(5, square_at(x_side, 0), y_side), chip(6, square_at(y_side, 1), x_side)]
        for copy in far[1:]:
            copy.start()
        trades += [across(4, square_at(x_side)), across(5, square_at(y_side))]
        for copy in trades[4:]:
            copy.start()
        chip(4, tall_at(diagonal), y_side).wait_recv()
        trades.append(across(6, tall_at(diagonal)))
        trades[-1].start()
        for hop in range(2, members - 1):
            group.arrive(hop)
            group.start(hop + 1)
        chip(5, square_at(diagonal, 0), y_side).wait_recv()
        chip(6, square_at(diagonal, 1), x_side).wait_recv()
        trades.append(across(7, square_at(diagonal)))
        trades[-1].start()
        theirs = [core, core, x_side, y_side, x_side, y_side, diagonal, diagonal]
        for index, device in enumerate(theirs):
            there = device if index < 2 else device + core - me
            source = square_at(there) if index in (1, 4, 5, 7) else tall_at(there)
            across(index, source).wait_recv()
        if members > 2:
            group.arrive(members - 1)
        for copy in near + far + trades:
            copy.wait_send()
        line.close()
        group.close()

    return pl.pallas_call(
        kernel,
        in_specs=in_vmem(3),
        out_specs=in_vmem(3),
        out_shape=[
            jax.ShapeDtypeStruct((members, devices * height, square.shape[1]), bf16),
            jax.ShapeDtypeStruct((devices * height, tall.shape[1]), bf16),
            jax.ShapeDtypeStruct((members * own_rows, width), bf16),
        ],
        scratch_shapes=[dma((2, members - 1))] * 4 + [dma((7,))] * 2 + [dma((8,))] * 2,
        compiler_params=pltpu.CompilerParams(collective_id=2, has_side_effects=True, vmem_limit_bytes=40 * 2**20),
        cost_estimate=pl.CostEstimate(flops=8 * 10**10, bytes_accessed=10**7, transcendentals=0),
        name="gather_small",
    )(square, tall, cotangent)


def turn(values, cosine, sine):
    return values * cosine + pltpu.roll(values, HD // 2, 1) * sine


def gain_rows(tall_ref, kv):
    return jnp.transpose(tall_ref[:, kv:].astype(f32))


def attention_front(tokens, square, tall, cosine, sine, members):
    own_rows, width = tokens.shape
    rows = own_rows * members
    kv = 2 * KV * HD
    heads = width // HD
    per_kv = heads // KV
    part = width // members
    dma = pltpu.SemaphoreType.DMA

    def kernel(x_ref, square_ref, tall_ref, cos_ref, sin_ref, *rest):
        normed_ref, q_ref, kv_all, mixed_ref, hidden_ref, rows_all = rest[:6]
        kv_send, kv_recv, row_send, row_recv = rest[6:]
        z = lax.axis_index("tensor")

        def block_of(ref):
            return lambda block: ref.at[pl.ds(pl.multiple_of(block * own_rows, 16), own_rows)]

        own = pl.ds(pl.multiple_of(z * own_rows, 16), own_rows)
        kv_line = LineGather(members, block_of(kv_all), kv_send, kv_recv)
        row_line = LineGather(members, block_of(rows_all), row_send, row_recv)
        gains = gain_rows(tall_ref, kv)
        x = x_ref[...].astype(f32)
        normed_ref[...] = (rms_pieces(x)[1] * gains[0:1]).astype(bf16)
        cosine, sine = cos_ref[...], sin_ref[...]
        made = nn(normed_ref[...], tall_ref[:, :kv])
        for head in range(KV):
            span = slice(head * HD, (head + 1) * HD)
            kv_all[own, span] = turn(made[:, span], cosine, sine).astype(bf16)
        kv_all[own, KV * HD :] = made[:, KV * HD :].astype(bf16)
        meet(members, False)
        kv_line.start(1)
        for t in range(members):
            made = nn(normed_ref[...], square_ref[t, :, :part])
            for head in range(part // HD):
                span = slice(head * HD, (head + 1) * HD)
                q_ref[:, t * part + head * HD : t * part + (head + 1) * HD] = turn(
                    made[:, span], cosine, sine
                ).astype(bf16)
            if 1 <= t + 1 < members:
                kv_line.arrive(t + 1)
                if t + 2 < members:
                    kv_line.start(t + 2)
        first = z * own_rows

        @pl.loop(0, heads)
        def _(head):
            span = pl.ds(pl.multiple_of(head * HD, HD), HD)
            key_span = pl.ds(pl.multiple_of(head // per_kv * HD, HD), HD)
            value_span = pl.ds(pl.multiple_of((KV + head // per_kv) * HD, HD), HD)
            p = probabilities(q_ref[:, span], kv_all[:, key_span], first).astype(bf16)
            mixed_ref[:, span] = nn(p, kv_all[:, value_span]).astype(bf16)

        hidden = x_ref[...].astype(f32)
        for t in range(members):
            hidden += nt(mixed_ref[:, t * part : (t + 1) * part], square_ref[t, :, part:])
        hidden_ref[...] = hidden
        normed = rms_pieces(hidden)[1] * gains[1:2]
        rows_all[own, :] = swap_blocks(normed).astype(bf16)
        for hop in range(1, members):
            row_line.start(hop)
            row_line.arrive(hop)
        kv_line.close()
        row_line.close()

    return pl.pallas_call(
        kernel,
        in_specs=in_vmem(5),
        out_specs=in_vmem(6),
        out_shape=[
            jax.ShapeDtypeStruct((own_rows, width), bf16),
            jax.ShapeDtypeStruct((own_rows, width), bf16),
            jax.ShapeDtypeStruct((rows, kv), bf16),
            jax.ShapeDtypeStruct((own_rows, width), bf16),
            jax.ShapeDtypeStruct((own_rows, width), f32),
            jax.ShapeDtypeStruct((rows, width), bf16),
        ],
        scratch_shapes=[dma((2, members - 1))] * 4,
        compiler_params=pltpu.CompilerParams(collective_id=3, has_side_effects=True, vmem_limit_bytes=56 * 2**20),
        cost_estimate=pl.CostEstimate(flops=10**11, bytes_accessed=10**7, transcendentals=0),
        name="attention_front",
    )(tokens, square, tall, cosine, sine)


def attention_back(sums, cotangent, hidden, tokens, normed, q, kv_all, mixed, square, tall, cosine, sine, members):
    own_rows, width = tokens.shape
    rows = own_rows * members
    kv = 2 * KV * HD
    heads = width // HD
    per_kv = heads // KV
    part = width // members
    dma = pltpu.SemaphoreType.DMA

    def kernel(sums_ref, cot_ref, hidden_ref, x_ref, normed_ref, q_ref, kv_ref, mixed_ref, square_ref, tall_ref, *rest):
        cos_ref, sin_ref = rest[:2]
        out_ref, grad_ref, parts = rest[2:5]
        do_ref, dq_ref, dkv_ref, total, kv_total, stage, tall_part = rest[5:12]
        back_leave, back_arrive, moe_leave, moe_arrive, kv_leave, kv_arrive = rest[12:18]
        back_send, back_recv, moe_send, moe_recv, kv_send, kv_recv, stage_sem = rest[18:]
        z = lax.axis_index("tensor")

        def block(ref, span):
            return lambda b: ref[pl.ds(pl.multiple_of(b * own_rows, 16), own_rows), span]

        back = LineSum(members, block(sums_ref, slice(width, 2 * width)), back_leave, back_arrive, back_send, back_recv)
        moe = LineSum(members, block(sums_ref, slice(0, width)), moe_leave, moe_arrive, moe_send, moe_recv)
        pairs = LineSum(members, block(dkv_ref, slice(None)), kv_leave, kv_arrive, kv_send, kv_recv)
        meet(members, False)
        gains = gain_rows(tall_ref, kv)
        cosine, sine = cos_ref[...], sin_ref[...]
        last = members - 1
        stored = []

        def store(value, at):
            slot = len(stored) % 2
            if len(stored) >= 2:
                stored[-2].wait()
            stage[slot] = value.astype(bf16)
            copy = pltpu.make_async_copy(stage.at[slot], parts.at[:, at : at + part], stage_sem.at[slot])
            copy.start()
            stored.append(copy)

        for hop in range(last, 0, -1):
            back.start(hop)
            back.arrive(hop)
        moe.start(last)
        back.total(total)
        normed_grad = swap_blocks(total[...])
        inverse, unit = rms_pieces(hidden_ref[...])
        by_hidden, gain_two = rms_backward(normed_grad, unit, inverse, gains[1:2])
        grad_ref[...] = cot_ref[...] + by_hidden
        low = grad_ref[...].astype(bf16)
        for t in range(members):
            span = slice(t * part, (t + 1) * part)
            do_ref[:, span] = nn(low, square_ref[t, :, part:]).astype(bf16)
            store(tn(low, mixed_ref[:, span]), width + t * part)
        moe.arrive(last)
        if last > 1:
            moe.start(last - 1)
        dkv_ref[...] = jnp.zeros_like(dkv_ref)
        first = z * own_rows

        @pl.loop(0, heads)
        def _(head):
            span = pl.ds(pl.multiple_of(head * HD, HD), HD)
            key_span = pl.ds(pl.multiple_of(head // per_kv * HD, HD), HD)
            value_span = pl.ds(pl.multiple_of((KV + head // per_kv) * HD, HD), HD)
            q_now, k_now, do_now = q_ref[:, span], kv_ref[:, key_span], do_ref[:, span]
            p = probabilities(q_now, k_now, first)
            dp = nt(do_now, kv_ref[:, value_span])
            ds = (p * (dp - jnp.sum(p * dp, axis=-1, keepdims=True))).astype(bf16)
            dq_ref[:, span] = turn(nn(ds, k_now) * (HD**-0.5), cosine, -sine).astype(bf16)
            dkv_ref[:, key_span] += tn(ds, q_now) * (HD**-0.5)
            dkv_ref[:, value_span] += tn(p.astype(bf16), do_now)

        pairs.start(last)
        for t in range(members):
            span = slice(t * part, (t + 1) * part)
            store(tn(normed_ref[...], dq_ref[:, span]), t * part)
        for hop in range(last, 0, -1):
            if hop < last:
                pairs.start(hop)
            pairs.arrive(hop)
        for hop in range(last - 1, 0, -1):
            moe.arrive(hop)
            if hop > 1:
                moe.start(hop - 1)
        pairs.total(kv_total)
        low_kv = [
            turn(kv_total[:, head * HD : (head + 1) * HD], cosine, -sine).astype(bf16) for head in range(KV)
        ] + [kv_total[:, KV * HD :].astype(bf16)]
        low_kv = jnp.concatenate(low_kv, axis=1)
        normed_grad = nt(low_kv, tall_ref[:, :kv])
        for t in range(members):
            normed_grad += nt(dq_ref[:, t * part : (t + 1) * part], square_ref[t, :, :part])
        inverse, unit = rms_pieces(x_ref[...].astype(f32))
        by_tokens, gain_one = rms_backward(normed_grad, unit, inverse, gains[0:1])
        grad_ref[...] += by_tokens
        tall_part[:, :kv] = tn(normed_ref[...], low_kv).astype(bf16)
        row = lax.broadcasted_iota(jnp.int32, (HD, width), 0)
        both = jnp.where(row == 0, gain_one[None], jnp.where(row == 1, gain_two[None], 0.0))
        tall_part[:, kv:] = jnp.transpose(both).astype(bf16)
        tall_copy = pltpu.make_async_copy(tall_part, parts.at[:, 2 * width :], stage_sem.at[2])
        tall_copy.start()
        moe.total(total)
        out_ref[...] = (hidden_ref[...] + swap_blocks(total[...])).astype(bf16)
        for line in (back, moe, pairs):
            line.close()
        for copy in (*stored[-2:], tall_copy):
            copy.wait()

    hops = (2, members - 1)
    return pl.pallas_call(
        kernel,
        in_specs=in_vmem(12),
        out_specs=in_vmem(2) + [pl.BlockSpec(memory_space=pl.ANY)],
        out_shape=[
            jax.ShapeDtypeStruct((own_rows, width), bf16),
            jax.ShapeDtypeStruct((own_rows, width), f32),
            jax.ShapeDtypeStruct((width, 2 * width + tall.shape[1]), bf16),
        ],
        scratch_shapes=[
            pltpu.VMEM((own_rows, width), bf16),
            pltpu.VMEM((own_rows, width), bf16),
            pltpu.VMEM((rows, kv), f32),
            pltpu.VMEM((own_rows, width), f32),
            pltpu.VMEM((own_rows, kv), f32),
            pltpu.VMEM((2, width, part), bf16),
            pltpu.VMEM(tall.shape, bf16),
        ]
        + [pltpu.VMEM((2, own_rows, width), bf16), pltpu.VMEM((*hops, own_rows, width), bf16)] * 2
        + [pltpu.VMEM((2, own_rows, kv), bf16), pltpu.VMEM((*hops, own_rows, kv), bf16)]
        + [dma(hops)] * 6
        + [dma((3,))],
        compiler_params=pltpu.CompilerParams(collective_id=4, has_side_effects=True, vmem_limit_bytes=62 * 10**6),
        cost_estimate=pl.CostEstimate(flops=10**11, bytes_accessed=10**7, transcendentals=0),
        name="attention_back",
    )(sums, cotangent, hidden, tokens, normed, q, kv_all, mixed, square, tall, cosine, sine)


def reduce_small(parts, members, devices):
    width = parts.shape[0]
    height = width // devices
    lanes = parts.shape[1]
    tall = lanes - 2 * width
    part = width // members
    half = height // 2
    dma = pltpu.SemaphoreType.DMA

    def kernel(parts_ref, square_out, tall_out, own, theirs, leave, arrive, blocks, line_leave, line_arrive, tall_all, *sems):
        own_sem, core_send, core_recv, chip_send, chip_recv, line_send, line_recv, tall_send, tall_recv = sems
        me, z = lax.axis_index("dp"), lax.axis_index("tensor")
        x_side, y_side = chip_neighbours()
        core = sibling()
        chips = [me, x_side, y_side, x_side + y_side - me]
        meet(members, True)

        def rows(device):
            return parts_ref.at[pl.ds(pl.multiple_of(device * height, 16), height)]

        def trade(m):
            return remote(rows(chips[m] + core - me), theirs.at[m], core_send.at[m], core_recv.at[m], {"dp": core})

        def keep(m):
            return pltpu.make_async_copy(rows(chips[m]), own.at[m], own_sem.at[m])

        for m in (3, 2, 1, 0):
            trade(m).start()
            keep(m).start()

        def both(m, span):
            return own[m, span].astype(f32) + theirs[m, span].astype(f32)

        def chip(index, source, target, device):
            return remote(source, target, chip_send.at[index], chip_recv.at[index], {"dp": device})

        first, second = slice(0, half), slice(half, height)
        far = [
            chip(0, leave.at[0, first], arrive.at[0, first], x_side),
            chip(1, leave.at[0, second], arrive.at[0, second], y_side),
        ]
        near = [chip(2, leave.at[1], arrive.at[1], x_side), chip(3, leave.at[2], arrive.at[2], y_side)]
        for m in (3, 2, 1, 0):
            trade(m).wait()
            keep(m).wait()
            if m == 3:
                for copy, span in zip(far, (first, second)):
                    leave[0, span] = both(3, span).astype(bf16)
                    copy.start()
        for copy in far:
            copy.wait()
        leave[1, first] = both(1, first).astype(bf16)
        leave[1, second] = (both(1, second) + arrive[0, second].astype(f32)).astype(bf16)
        near[0].start()
        leave[2, first] = (both(2, first) + arrive[0, first].astype(f32)).astype(bf16)
        leave[2, second] = both(2, second).astype(bf16)
        near[1].start()
        for copy in near:
            copy.wait()

        def total(span):
            return (
                own[0, :, span].astype(f32)
                + theirs[0, :, span].astype(f32)
                + arrive[1, :, span].astype(f32)
                + arrive[2, :, span].astype(f32)
            )

        tall_all[z] = total(slice(2 * width, lanes)).astype(bf16)
        for t in range(members):
            blocks[t, :, :part] = total(slice(t * part, (t + 1) * part))
            blocks[t, :, part:] = total(slice(width + t * part, width + (t + 1) * part))
        line = LineSum(members, lambda b: blocks[b], line_leave, line_arrive, line_send, line_recv)
        group = LineGather(members, lambda b: tall_all.at[b], tall_send, tall_recv)
        for hop in range(1, members):
            line.start(members - hop)
            group.start(hop)
            line.arrive(members - hop)
            group.arrive(hop)
        line.total(square_out)
        summed = tall_all[0].astype(f32)
        for t in range(1, members):
            summed += tall_all[t].astype(f32)
        tall_out[...] = summed
        line.close()
        group.close()

    hops = (2, members - 1)
    return pl.pallas_call(
        kernel,
        in_specs=[pl.BlockSpec(memory_space=pl.ANY)],
        out_specs=in_vmem(2),
        out_shape=[
            jax.ShapeDtypeStruct((height, 2 * part), f32),
            jax.ShapeDtypeStruct((height, tall), f32),
        ],
        scratch_shapes=[
            pltpu.VMEM((4, height, lanes), bf16),
            pltpu.VMEM((4, height, lanes), bf16),
            pltpu.VMEM((3, height, lanes), bf16),
            pltpu.VMEM((3, height, lanes), bf16),
            pltpu.VMEM((members, height, 2 * part), f32),
            pltpu.VMEM((2, height, 2 * part), bf16),
            pltpu.VMEM((*hops, height, 2 * part), bf16),
            pltpu.VMEM((members, height, tall), bf16),
            dma((4,)),
            dma((4,)),
            dma((4,)),
            dma((4,)),
            dma((4,)),
        ]
        + [dma(hops)] * 4,
        compiler_params=pltpu.CompilerParams(collective_id=5, has_side_effects=True, vmem_limit_bytes=48 * 2**20),
        cost_estimate=pl.CostEstimate(flops=8 * 10**10, bytes_accessed=10**7, transcendentals=0),
        name="reduce_small",
    )(parts)


def pack(gate, up, down):
    def pair(a, b):
        return jnp.concatenate([a[..., :HD], b[..., :HD], a[..., HD:], b[..., HD:]], axis=-1)

    gate, up, down = (jnp.transpose(w, (1, 0, 2)) for w in (gate, up, down))
    gate_up = pair(gate, up)
    return jnp.concatenate([gate_up[0::2], gate_up[1::2], pair(down[0::2], down[1::2])], axis=-1)


def unpack(packed):
    n, height, lanes = packed.shape
    third = lanes // 3

    def halves(both):
        tail = third // 2 - HD
        a = jnp.concatenate([both[..., :HD], both[..., 2 * HD : 2 * HD + tail]], axis=-1)
        b = jnp.concatenate([both[..., HD : 2 * HD], both[..., 2 * HD + tail :]], axis=-1)
        return a, b

    def experts(even, odd):
        both = jnp.stack([even, odd], axis=1).reshape(2 * n, height, third // 2)
        return jnp.transpose(both, (1, 0, 2))

    gate0, up0 = halves(packed[..., :third])
    gate1, up1 = halves(packed[..., third : 2 * third])
    down0, down1 = halves(packed[..., 2 * third :])
    return experts(gate0, gate1), experts(up0, up1), experts(down0, down1)


def flip(value, bit):
    count = lax.axis_size("dp")
    return lax.ppermute(value, "dp", [(i, i ^ bit) for i in range(count)])


def gather_step(fresh, arrived):
    to_x = [from_y[half_of(from_y)[1]] for _, from_y in arrived] + fresh
    to_y = [from_x[half_of(from_x)[0]] for from_x, _ in arrived] + fresh
    return flip(jnp.concatenate(to_x), 2), flip(jnp.concatenate(to_y), 4)


def gather_chunks(packed):
    size = packed[0].shape[0]
    cut = size // 2
    fresh, steps, near, far = [[packed[0], packed[1]], *([p] for p in packed[2:]), []], [], [], []
    arrived = []
    for chunks in fresh:
        got = gather_step(chunks, arrived)
        steps.append(got)
        for i in range(len(arrived)):
            far.append(tuple(side[cut * i : cut * (i + 1)] for side in got))
        begin = cut * len(arrived)
        arrived = [
            tuple(side[begin + size * i : begin + size * (i + 1)] for side in got) for i in range(len(chunks))
        ]
        near += arrived
    gathered = []
    for own, (from_x, from_y), (second, first) in zip(packed, near, far):
        gathered.append(
            [
                [(own, 0), (from_x, 0), (from_y, 0), (first, 0)],
                [(own, cut), (from_x, cut), (from_y, cut), (second, 0)],
            ]
        )
    return gathered, steps


def half_of(chunk):
    cut = chunk.shape[0] // 2
    return slice(0, cut), slice(cut, None)


def scatter_step(chunk, before):
    to_x, to_y = [], []
    if before is not None:
        blocks, via_x, via_y = before
        first, second = half_of(blocks[0])
        to_x += [blocks[1, first], add(blocks[1, second], via_y)]
        to_y += [add(blocks[2, first], via_x), blocks[2, second]]
    if chunk is not None:
        first, second = half_of(chunk[0])
        to_x.append(chunk[3, first])
        to_y.append(chunk[3, second])
    return flip(jnp.concatenate(to_x), 2), flip(jnp.concatenate(to_y), 4)


def before_of(chunks, moved, call):
    if call == 0:
        return None
    cut = CALL_PAIRS // 2
    return chunks[call - 1], moved[call - 1][0][-cut:], moved[call - 1][1][-cut:]


def add(a, b):
    return (a.astype(f32) + b.astype(f32)).astype(bf16)


def routes_of(expert_ids, route_weights):
    rows = expert_ids.shape[0]
    lanes = jnp.arange(EXPERTS, dtype=jnp.int32)
    named = expert_ids[:, :, None] == lanes
    member_of = jnp.any(named, axis=1)
    weight_of = jnp.sum(jnp.where(named, route_weights[:, :, None], 0.0), axis=1)
    earlier = jnp.arange(rows)[:, None] > jnp.arange(rows)[None, :]
    rank = jnp.where(member_of, nn(earlier.astype(bf16), member_of.astype(bf16)), -1.0)
    rank_cols = jnp.pad(rank, ((0, 0), (0, HD)), constant_values=-1.0).astype(bf16)
    rank_rows = rank.T.astype(jnp.int32).reshape(EXPERTS, 1, rows)
    weight_rows = weight_of.T.reshape(EXPERTS, 1, rows)
    return rank_cols, rank_rows, weight_rows


def body_anywhere(
    tokens,
    expert_ids,
    route_weights,
    attn_gain,
    q_weight,
    k_weight,
    v_weight,
    o_weight,
    moe_gain,
    gate_weight,
    up_weight,
    down_weight,
    cotangent,
):
    members = lax.axis_size("tensor")
    member = lax.axis_index("tensor")
    own_rows, width = tokens.shape
    rows = own_rows * members
    pairs = EXPERTS // 2
    calls = pairs // CALL_PAIRS

    packed = [
        pack(*(w[:, 2 * CALL_PAIRS * i : 2 * CALL_PAIRS * (i + 1)] for w in (gate_weight, up_weight, down_weight)))
        for i in range(calls)
    ]
    gathered = [[[(lax.all_gather(own, "dp", axis=1, tiled=True), 0)]] for own in packed]

    gain_one = lax.all_gather(attn_gain, "dp", axis=0, tiled=True).astype(f32)
    gain_two = lax.all_gather(moe_gain, "dp", axis=0, tiled=True).astype(f32)
    kv_full = lax.all_gather(jnp.concatenate([k_weight, v_weight], axis=1), "dp", axis=0, tiled=True)
    q_full = lax.all_gather(lax.all_gather(q_weight, "dp", axis=0, tiled=True), "tensor", axis=0)
    o_full = lax.all_gather(lax.all_gather(o_weight, "dp", axis=0, tiled=True), "tensor", axis=0)
    kv_width = k_weight.shape[1]

    rank_cols, rank_rows, weight_rows = routes_of(expert_ids, route_weights)

    grad_low = cotangent.astype(bf16)
    grad_all = lax.all_gather(grad_low, "tensor", axis=0, tiled=True)

    x = tokens.astype(f32)
    inverse_one, unit_one = rms_pieces(x)
    normed_one = (unit_one * gain_one).astype(bf16)
    first_row = (member * own_rows).reshape(1)
    cos_table, sin_table = rope_tables(member * own_rows + jnp.arange(own_rows, dtype=jnp.int32))
    kv_own = nn(normed_one, kv_full)
    kv_own = jnp.concatenate(
        [rotate(kv_own[:, :kv_width], cos_table, sin_table), kv_own[:, kv_width:]], axis=1
    ).astype(bf16)
    kv_all = lax.all_gather(kv_own, "tensor", axis=0, tiled=True)
    keys, values = kv_all[:, :kv_width], kv_all[:, kv_width:]
    queries = jnp.concatenate([nn(normed_one, q_full[t]) for t in range(members)], axis=1)
    queries = rotate(queries, cos_table, sin_table).astype(bf16)
    mixed = attend_forward(first_row, queries, keys, values)
    part = width // members
    branch = sum(nt(mixed[:, t * part : (t + 1) * part], o_full[t]) for t in range(members))
    hidden = x + branch
    inverse_two, unit_two = rms_pieces(hidden)
    normed_two = (unit_two * gain_two).astype(bf16)
    rows_all = lax.all_gather(normed_two, "tensor", axis=0, tiled=True)

    sums = jnp.zeros((rows, 2 * width), f32)
    chunks = []
    for call in range(calls):
        some = slice(2 * CALL_PAIRS * call, 2 * CALL_PAIRS * (call + 1))
        columns = slice(2 * CALL_PAIRS * call, 2 * CALL_PAIRS * call + HD)
        grads, sums = expert_call(
            rank_cols[:, columns],
            rank_rows[some],
            weight_rows[some],
            rows_all,
            grad_all,
            gathered[call],
            sums,
            False,
        )
        chunks.append(grads)
    shares = [
        unpack(lax.psum_scatter(grads[0], "dp", scatter_dimension=1, tiled=True).astype(f32)) for grads in chunks
    ]
    gate_out, up_out, down_out = (jnp.concatenate(parts, axis=1) for parts in zip(*shares))

    low_sums = sums.astype(bf16)
    normed_grad = lax.psum_scatter(low_sums[:, width:], "tensor", scatter_dimension=0, tiled=True).astype(f32)
    moe_own = lax.psum_scatter(low_sums[:, :width], "tensor", scatter_dimension=0, tiled=True).astype(f32)
    output = (hidden + moe_own).astype(bf16)

    back_two, gain_two_part = rms_backward(normed_grad, unit_two, inverse_two, gain_two)
    hidden_grad = cotangent + back_two
    hidden_low = hidden_grad.astype(bf16)
    mixed_grad = jnp.concatenate([nn(hidden_low, o_full[t]) for t in range(members)], axis=1).astype(bf16)
    o_part = jnp.stack([tn(hidden_low, mixed[:, t * part : (t + 1) * part]) for t in range(members)])
    dq, dk, dv = attend_backward(first_row, queries, keys, values, mixed_grad)
    kv_grad = lax.psum_scatter(
        jnp.concatenate([dk, dv], axis=1).astype(bf16), "tensor", scatter_dimension=0, tiled=True
    ).astype(f32)
    dq_low = rotate(dq, cos_table, -sin_table).astype(bf16)
    kv_low = jnp.concatenate(
        [rotate(kv_grad[:, :kv_width], cos_table, -sin_table), kv_grad[:, kv_width:]], axis=1
    ).astype(bf16)
    normed_one_grad = nt(kv_low, kv_full) + sum(
        nt(dq_low[:, t * part : (t + 1) * part], q_full[t]) for t in range(members)
    )
    back_one, gain_one_part = rms_backward(normed_one_grad, unit_one, inverse_one, gain_one)
    tokens_grad = hidden_grad + back_one
    q_part = jnp.stack([tn(normed_one, dq_low[:, t * part : (t + 1) * part]) for t in range(members)])
    kv_part = tn(normed_one, kv_low)

    def shared(values):
        summed = lax.psum_scatter(values.astype(bf16), "tensor", scatter_dimension=0, tiled=False)
        return lax.psum_scatter(summed, "dp", scatter_dimension=0, tiled=True).astype(f32)

    q_grad, o_grad = shared(q_part), shared(o_part)
    small = jnp.concatenate([kv_part, gain_one_part[:, None], gain_two_part[:, None]], axis=1)
    small = lax.psum_scatter(small, "dp", scatter_dimension=0, tiled=True)
    small = lax.psum(small.astype(bf16), "tensor").astype(f32)
    return (
        output,
        tokens_grad,
        small[:, 2 * kv_width],
        q_grad,
        small[:, :kv_width],
        small[:, kv_width : 2 * kv_width],
        o_grad,
        small[:, 2 * kv_width + 1],
        gate_out,
        up_out,
        down_out,
    )

def body_by_chips(
    tokens,
    expert_ids,
    route_weights,
    attn_gain,
    q_weight,
    k_weight,
    v_weight,
    o_weight,
    moe_gain,
    gate_weight,
    up_weight,
    down_weight,
    cotangent,
):
    members = lax.axis_size("tensor")
    member = lax.axis_index("tensor")
    devices = lax.axis_size("dp")
    own_rows, width = tokens.shape
    rows = own_rows * members
    calls = EXPERTS // 2 // CALL_PAIRS
    kv_width = k_weight.shape[1]

    packed = [
        pack(*(w[:, 2 * CALL_PAIRS * i : 2 * CALL_PAIRS * (i + 1)] for w in (gate_weight, up_weight, down_weight)))
        for i in range(calls)
    ]
    gathered, steps = gather_chunks(packed)
    square = jnp.concatenate([q_weight, o_weight], axis=1)
    gains = jnp.stack([attn_gain, moe_gain], axis=1)
    tall = jnp.concatenate([k_weight, v_weight, jnp.pad(gains, ((0, 0), (0, HD - 2)))], axis=1)
    tall = after(tall, packed[:2])
    square_all, tall_all, grad_all = gather_small(square, tall, cotangent, members, devices)

    rank_cols, rank_rows, weight_rows = routes_of(expert_ids, route_weights)
    cos_table, sin_table = rope_tables(member * own_rows + jnp.arange(own_rows, dtype=jnp.int32))
    cosine = jnp.concatenate([cos_table, cos_table], axis=1)
    sine = after(jnp.concatenate([-sin_table, sin_table], axis=1), steps[0])
    normed_one, queries, kv_all, mixed, hidden, rows_all = attention_front(
        tokens, square_all, tall_all, cosine, sine, members
    )

    sums = jnp.zeros((rows, 2 * width), f32)
    chunks, moved = [], []
    for call in range(calls):
        some = slice(2 * CALL_PAIRS * call, 2 * CALL_PAIRS * (call + 1))
        columns = slice(2 * CALL_PAIRS * call, 2 * CALL_PAIRS * call + HD)
        grads, sums = expert_call(
            rank_cols[:, columns],
            after(rank_rows[some], moved[call - 2] if call >= 2 else ()),
            weight_rows[some],
            rows_all,
            grad_all,
            gathered[call],
            sums,
            True,
        )
        chunks.append(grads)
        moved.append(scatter_step(grads, before_of(chunks, moved, call)))
    moved.append(scatter_step(None, before_of(chunks, moved, calls)))

    output, tokens_grad, parts = attention_back(
        sums.astype(bf16),
        cotangent,
        hidden,
        tokens,
        normed_one,
        queries,
        kv_all,
        mixed,
        square_all,
        tall_all,
        cosine,
        after(sine, moved[calls - 2]),
        members,
    )
    square_grad, tall_grad = reduce_small(parts, members, devices)
    shares = []
    for call in range(calls):
        from_x, from_y = (got[:CALL_PAIRS].astype(f32) for got in moved[call + 1])
        shares.append(unpack(chunks[call][0].astype(f32) + from_x + from_y))
    gate_out, up_out, down_out = (jnp.concatenate(blocks, axis=1) for blocks in zip(*shares))
    part = width // members
    return (
        output,
        tokens_grad,
        tall_grad[:, 2 * kv_width],
        square_grad[:, :part],
        tall_grad[:, :kv_width],
        tall_grad[:, kv_width : 2 * kv_width],
        square_grad[:, part:],
        tall_grad[:, 2 * kv_width + 1],
        gate_out,
        up_out,
        down_out,
    )


def solution(mesh):
    rows = P(("dp", "tensor"), None)
    experts = P("dp", None, "tensor")
    square = P("dp", "tensor")
    tall = P("dp", None)
    return jax.shard_map(
        body_by_chips if mesh.shape["dp"] == 8 else body_anywhere,
        mesh=mesh,
        in_specs=(
            rows, tall, tall, P("dp"), square, tall, tall, square, P("dp"), experts, experts, experts, rows
        ),
        out_specs=(rows, rows, P("dp"), square, tall, tall, square, P("dp"), experts, experts, experts),
        check_vma=False,
    )
```

```python
import jax
import jax.numpy as jnp
import numpy as np
from jax import lax
from jax.experimental import pallas as pl
from jax.experimental.pallas import tpu as pltpu
from jax.sharding import PartitionSpec as P

KV = 2
HD = 128
EXPERTS = 32
TOPK = 4
SEQ = 1024
BLOCK = 256
CAP = 256
TAIL = 64
CALL_PAIRS = 4

eps = 1e-06
rope_base = 1000000.0
negative = -1e30
bf16 = jnp.bfloat16
f32 = jnp.float32


def nn(a, b):
    return jnp.dot(a, b, preferred_element_type=f32)


def nt(a, b):
    return lax.dot_general(a, b, (((1,), (1,)), ((), ())), preferred_element_type=f32)


def tn(a, b):
    return lax.dot_general(a, b, (((0,), (0,)), ((), ())), preferred_element_type=f32)


def rope_tables(positions):
    half = HD // 2
    frequency = rope_base ** (-(jnp.arange(half).astype(f32) * 2.0 / HD))
    angles = positions.astype(f32)[:, None] * frequency[None, :]
    return jnp.cos(angles), jnp.sin(angles)


def rotate(values, cos_table, sin_table):
    rows = values.shape[0]
    heads = values.reshape(rows, -1, 2, HD // 2)
    a, b = heads[:, :, 0], heads[:, :, 1]
    cos_table, sin_table = cos_table[:, None], sin_table[:, None]
    turned = jnp.stack([a * cos_table - b * sin_table, b * cos_table + a * sin_table], axis=2)
    return turned.reshape(rows, -1)


def rms_pieces(x):
    inverse = lax.rsqrt(jnp.mean(x * x, axis=-1, keepdims=True) + eps)
    return inverse, x * inverse


def rms_backward(grad, unit, inverse, gain):
    u = grad * gain
    back = inverse * (u - unit * jnp.mean(u * unit, axis=-1, keepdims=True))
    return back, jnp.sum(grad * unit, axis=0)


def probabilities(q, k, first_row):
    rows, keys = q.shape[0], k.shape[0]
    scores = nt(q, k) * (HD**-0.5)
    q_block = (first_row + lax.broadcasted_iota(jnp.int32, (rows, keys), 0)) // BLOCK
    k_block = lax.broadcasted_iota(jnp.int32, (rows, keys), 1) // BLOCK
    scores = jnp.where(k_block <= q_block, scores, negative)
    raised = jnp.exp(scores - jnp.max(scores, axis=-1, keepdims=True))
    return raised / jnp.sum(raised, axis=-1, keepdims=True)


def attend_forward(first_row, q, k, v):
    rows, width = q.shape
    heads = width // HD
    shared = heads // KV

    def kernel(first_ref, q_ref, k_ref, v_ref, o_ref):
        p = probabilities(q_ref[...], k_ref[...], first_ref[0]).astype(bf16)
        o_ref[...] = nn(p, v_ref[...]).astype(bf16)

    per_head = pl.BlockSpec((rows, HD), lambda h, f: (0, h))
    per_kv = pl.BlockSpec((k.shape[0], HD), lambda h, f: (0, h // shared))
    return pl.pallas_call(
        kernel,
        grid_spec=pltpu.PrefetchScalarGridSpec(
            num_scalar_prefetch=1,
            grid=(heads,),
            in_specs=[per_head, per_kv, per_kv],
            out_specs=per_head,
        ),
        out_shape=jax.ShapeDtypeStruct((rows, width), bf16),
        compiler_params=pltpu.CompilerParams(vmem_limit_bytes=32 * 2**20),
        cost_estimate=pl.CostEstimate(
            flops=4 * rows * width * k.shape[0],
            bytes_accessed=4 * rows * width,
            transcendentals=rows * heads * k.shape[0],
        ),
        name="attend",
    )(first_row, q, k, v)


def attend_backward(first_row, q, k, v, do):
    rows, width = q.shape
    keys = k.shape[0]
    heads = width // HD
    shared = heads // KV

    def kernel(first_ref, q_ref, k_ref, v_ref, do_ref, dq_ref, dk_ref, dv_ref):
        q_now, k_now, v_now, do_now = q_ref[...], k_ref[...], v_ref[...], do_ref[...]
        p = probabilities(q_now, k_now, first_ref[0])
        dp = nt(do_now, v_now)
        ds = (p * (dp - jnp.sum(p * dp, axis=-1, keepdims=True))).astype(bf16)
        dq_ref[...] = nn(ds, k_now) * (HD**-0.5)
        dk = tn(ds, q_now) * (HD**-0.5)
        dv = tn(p.astype(bf16), do_now)
        head = pl.program_id(0)

        @pl.when(lax.rem(head, shared) == 0)
        def _():
            dk_ref[...] = dk
            dv_ref[...] = dv

        @pl.when(lax.rem(head, shared) != 0)
        def _():
            dk_ref[...] += dk
            dv_ref[...] += dv

    per_head = pl.BlockSpec((rows, HD), lambda h, f: (0, h))
    per_kv = pl.BlockSpec((keys, HD), lambda h, f: (0, h // shared))
    return pl.pallas_call(
        kernel,
        grid_spec=pltpu.PrefetchScalarGridSpec(
            num_scalar_prefetch=1,
            grid=(heads,),
            in_specs=[per_head, per_kv, per_kv, per_head],
            out_specs=[per_head, per_kv, per_kv],
        ),
        out_shape=[
            jax.ShapeDtypeStruct((rows, width), f32),
            jax.ShapeDtypeStruct((keys, KV * HD), f32),
            jax.ShapeDtypeStruct((keys, KV * HD), f32),
        ],
        compiler_params=pltpu.CompilerParams(vmem_limit_bytes=32 * 2**20),
        cost_estimate=pl.CostEstimate(
            flops=10 * rows * width * keys,
            bytes_accessed=8 * rows * width,
            transcendentals=rows * heads * keys,
        ),
        name="attend_back",
    )(first_row, q, k, v, do)


def after(value, waits):
    if not waits:
        return value

    def kernel(*refs):
        del refs

    anywhere = pl.BlockSpec(memory_space=pl.ANY)
    return pl.pallas_call(
        kernel,
        in_specs=[anywhere] * (1 + len(waits)),
        out_specs=anywhere,
        out_shape=jax.ShapeDtypeStruct(value.shape, value.dtype),
        input_output_aliases={0: 0},
        name="after",
    )(value, *waits)


def sibling():
    me = lax.axis_index("dp")
    return me + 1 - 2 * lax.rem(me, 2)


def expert_call(rank_cols, routes, x, gy, pieces, sums, exchange):
    rows, width = x.shape
    subs, count = len(pieces), len(pieces[0])
    height, lanes = pieces[0][0][0].shape[1:]
    pairs = routes.shape[0] // 2
    sub_pairs = pairs // subs
    blocks = 12
    tile = 2 * width // blocks
    flat = []
    place = []
    for sub in pieces:
        place.append([])
        for array, begin in sub:
            known = [i for i, other in enumerate(flat) if other is array]
            if not known:
                flat.append(array)
            place[-1].append((known[0] if known else len(flat) - 1, begin))
    third = lanes // 3
    stride = 2 if exchange else 1

    def kernel(rank_c, routes_ref, x_ref, gy_ref, *rest):
        w_hbm = rest[: len(flat)]
        rest = rest[len(flat) :]
        sums_in, rest = rest[0], rest[1:]
        grad_out, sums_out, w_buf, y_buf, pick_buf, local_sem = rest[:6]
        step = pl.program_id(0)
        if exchange:
            kept, leaving, arriving, push_sem, pull_sem, send_sem, recv_sem, w_free, g_free = rest[6:]
            other = {"dp": sibling()}

        def weights(pair, slot, sub):
            found = []
            for k in range(count):
                array, begin = place[sub][k]
                source = w_hbm[array].at[pair - sub * sub_pairs + begin]
                target = w_buf.at[slot, pl.ds(stride * k * height, height)]
                found.append(pltpu.make_async_copy(source, target, local_sem.at[slot, k]))
                if exchange:
                    target = w_buf.at[slot, pl.ds((stride * k + 1) * height, height)]
                    found.append(
                        pltpu.make_async_remote_copy(
                            src_ref=source,
                            dst_ref=target,
                            send_sem=push_sem.at[slot, k],
                            recv_sem=pull_sem.at[slot, k],
                            device_id=other,
                            device_id_type=pl.DeviceIdType.MESH,
                        )
                    )
            return found

        def start(pair):
            slot = lax.rem(pair, 2)
            for sub in range(subs):

                @pl.when((pair >= sub * sub_pairs) & (pair < (sub + 1) * sub_pairs))
                def _():
                    for copy in weights(pair, slot, sub):
                        copy.start()

        def leave(slot):
            return pltpu.make_async_remote_copy(
                src_ref=leaving.at[slot],
                dst_ref=arriving.at[slot],
                send_sem=send_sem.at[slot],
                recv_sem=recv_sem.at[slot],
                device_id=other,
                device_id_type=pl.DeviceIdType.MESH,
            )

        def put(at, value, slot):
            for k in range(count):
                for parity in range(stride):
                    row = (stride * k + parity) * height
                    part = value[row : row + height].astype(bf16)
                    span = slice(at, at + value.shape[1])
                    if not exchange:
                        grad_out[k, 0, :, span] = part
                    elif parity == 0:
                        kept[slot, k, :, span] = part
                    else:
                        leaving[slot, k, :, span] = part

        def signal(sem):
            pl.semaphore_signal(sem, inc=1, device_id=other, device_id_type=pl.DeviceIdType.MESH)

        def finish(pair):
            slot = lax.rem(pair, 2)
            leave(slot).wait()
            for k in range(count):
                both = kept[slot, k].astype(f32) + arriving[slot, k].astype(f32)
                grad_out[k, 0] = both.astype(bf16)

        @pl.when(step == 0)
        def _():
            if exchange:
                barrier = pltpu.get_barrier_semaphore()
                signal(barrier)
                pl.semaphore_wait(barrier, 1)
            start(step)

        if exchange:

            @pl.when((step >= 1) & (step + 1 < pairs))
            def _():
                signal(w_free)
                pl.semaphore_wait(w_free, 1)

        @pl.when(step + 1 < pairs)
        def _():
            start(step + 1)

        @pl.when(step < pairs)
        def _():
            slot = lax.rem(step, 2)
            for copy in weights(0, slot, 0):
                copy.wait()
            w = w_buf.at[slot]
            low_half = lax.broadcasted_iota(jnp.int32, (CAP, HD), 1) < TAIL
            tails = []
            for q in range(2):
                e = 2 * step + q
                column = (lax.broadcasted_iota(jnp.int32, (HD, CAP), 0) == e).astype(bf16)
                rank = nn(rank_c[...], column)
                slot_of = lax.broadcasted_iota(jnp.int32, (rows, CAP), 1).astype(f32)
                at = pl.ds(pl.multiple_of(e * CAP, CAP), CAP)
                pick_buf[:, at] = (rank == slot_of).astype(bf16)
                hit = lax.broadcasted_iota(jnp.int32, (CAP, rows), 0).astype(f32) == routes_ref[q, 0:1]
                pick = hit.astype(bf16)
                weight = jnp.sum(jnp.where(hit, routes_ref[q, 1:2], 0.0), axis=1, keepdims=True)
                xe = nn(pick, x_ref[...]).astype(bf16)
                deo = (nn(pick, gy_ref[...]) * weight).astype(bf16)
                gate_up = slice(q * third, (q + 1) * third)
                down = slice(2 * third + q * HD, 2 * third + (q + 1) * HD)
                down_tail = slice(2 * third + 2 * HD, lanes)
                gu = nn(xe, w[:, gate_up])
                d0 = nn(deo, w[:, down])
                d1 = nn(deo, w[:, down_tail])
                if q == 1:
                    d1 = pltpu.roll(d1, TAIL, 1)
                tail = gu[:, 2 * HD :]

                def unit(gate, up, dact):
                    sig = jax.nn.sigmoid(gate)
                    silu = gate * sig
                    return silu * up, dact * up * sig * (1.0 + gate * (1.0 - sig)), dact * silu

                a0, dg0, du0 = unit(gu[:, :HD], gu[:, HD : 2 * HD], d0)
                a1, dg1, du1 = unit(tail, pltpu.roll(tail, TAIL, 1), d1)
                a1 = jnp.where(low_half, a1, 0.0)
                if q == 1:
                    a1 = pltpu.roll(a1, TAIL, 1)
                dgu1 = jnp.where(low_half, dg1, pltpu.roll(du1, TAIL, 1))
                a0, a1 = a0.astype(bf16), a1.astype(bf16)
                dgu = jnp.concatenate([dg0.astype(bf16), du0.astype(bf16), dgu1.astype(bf16)], axis=1)
                eo = nt(a0, w[:, down]) + nt(a1, w[:, down_tail])
                y_buf[at, :width] = (eo * weight).astype(bf16)
                y_buf[at, width:] = nt(dgu, w[:, gate_up]).astype(bf16)
                put(q * third, tn(xe, dgu), slot)
                put(2 * third + q * HD, tn(deo, a0), slot)
                tails.append((deo, a1))
            put(2 * third + 2 * HD, tn(*tails[0]) + tn(*tails[1]), slot)

        if exchange:

            @pl.when((step >= 1) & (step <= pairs))
            def _():
                finish(step - 1)

            @pl.when((step >= 1) & (step + 1 < pairs))
            def _():
                signal(g_free)

            @pl.when((step >= 2) & (step < pairs))
            def _():
                pl.semaphore_wait(g_free, 1)

            @pl.when(step < pairs)
            def _():
                leave(lax.rem(step, 2)).start()

        @pl.when(step >= pairs)
        def _():
            at = pl.ds(pl.multiple_of((step - pairs) * tile, tile), tile)
            sums_out[...] = sums_in[...] + nn(pick_buf[...], y_buf[:, at])

    def held(step):
        return jnp.minimum(step, pairs - 1)

    def behind(step):
        return jnp.clip(step - 1, 0, pairs - 1) if exchange else held(step)

    def block(step):
        return (0, jnp.maximum(step - pairs, 0))

    once = pl.Buffered(1)
    whole = pl.BlockSpec((rows, width), lambda s: (0, 0), pipeline_mode=once)
    of_pair = pl.BlockSpec((2, 2, rows), lambda s: (held(s), 0, 0))
    anywhere = pl.BlockSpec(memory_space=pl.ANY)
    dma = pltpu.SemaphoreType.DMA
    traded = [
        pltpu.VMEM((2, count, height, lanes), bf16),
        pltpu.VMEM((2, count, height, lanes), bf16),
        pltpu.VMEM((2, count, height, lanes), bf16),
        dma((2, count)),
        dma((2, count)),
        dma((2,)),
        dma((2,)),
        pltpu.SemaphoreType.REGULAR,
        pltpu.SemaphoreType.REGULAR,
    ]
    remote = dict(collective_id=1, has_side_effects=True) if exchange else {}
    return pl.pallas_call(
        kernel,
        grid=(pairs + blocks,),
        in_specs=[pl.BlockSpec((rows, HD), lambda s: (0, 0), pipeline_mode=once), of_pair, whole, whole]
        + [anywhere] * len(flat)
        + [pl.BlockSpec((rows, tile), block)],
        out_specs=[
            pl.BlockSpec((count, 1, height, lanes), lambda s: (0, behind(s), 0, 0)),
            pl.BlockSpec((rows, tile), block),
        ],
        scratch_shapes=[
            pltpu.VMEM((2, width, lanes), bf16),
            pltpu.VMEM((2 * pairs * CAP, 2 * width), bf16),
            pltpu.VMEM((rows, 2 * pairs * CAP), bf16),
            dma((2, count)),
        ]
        + (traded if exchange else []),
        out_shape=[
            jax.ShapeDtypeStruct((count, pairs, height, lanes), bf16),
            jax.ShapeDtypeStruct((rows, 2 * width), f32),
        ],
        compiler_params=pltpu.CompilerParams(vmem_limit_bytes=62 * 10**6, **remote),
        cost_estimate=pl.CostEstimate(
            flops=pairs * 4 * CAP * width * (4 * rows * 2 + 18 * lanes // 6),
            bytes_accessed=8 * rows * width * 3,
            transcendentals=0,
        ),
        name="experts",
    )(rank_cols, routes, x, gy, *flat, sums)


def remote(source, target, send_sem, recv_sem, device):
    return pltpu.make_async_remote_copy(
        src_ref=source,
        dst_ref=target,
        send_sem=send_sem,
        recv_sem=recv_sem,
        device_id=device,
        device_id_type=pl.DeviceIdType.MESH,
    )


def chip_neighbours():
    me = lax.axis_index("dp")
    return me + 2 - 4 * lax.rem(me // 2, 2), me + 4 - 8 * lax.rem(me // 4, 2)


def meet(members, core):
    barrier = pltpu.get_barrier_semaphore()
    z = lax.axis_index("tensor")

    def signal(device):
        pl.semaphore_signal(barrier, inc=1, device_id=device, device_id_type=pl.DeviceIdType.MESH)

    @pl.when(z > 0)
    def _():
        signal({"tensor": z - 1})

    @pl.when(z < members - 1)
    def _():
        signal({"tensor": z + 1})

    for other in (*chip_neighbours(), *([sibling()] if core else [])):
        signal({"dp": other})
    inner = jnp.where((z > 0) & (z < members - 1), 1, 0)
    pl.semaphore_wait(barrier, 3 + inner + (1 if core else 0))


class LineGather:
    def __init__(self, members, at, send, recv):
        self.members, self.at, self.send, self.recv = members, at, send, recv

    def copies(self, hop):
        z, last = lax.axis_index("tensor"), self.members - 1
        up, down = z - hop + 1, z + hop - 1

        def copy(block, way, device):
            return lambda: remote(
                self.at(block), self.at(block), self.send.at[way, hop - 1], self.recv.at[way, hop - 1], {"tensor": device}
            )

        return (
            ((up >= 0) & (z < last), copy(up, 0, z + 1)),
            ((down <= last) & (z > 0), copy(down, 1, z - 1)),
        ), (
            (z - hop >= 0, copy(z - hop, 0, z)),
            (z + hop <= last, copy(z + hop, 1, z)),
        )

    def start(self, hop):
        for present, copy in self.copies(hop)[0]:

            @pl.when(present)
            def _():
                copy().start()

    def arrive(self, hop):
        for present, copy in self.copies(hop)[1]:

            @pl.when(present)
            def _():
                copy().wait_recv()

    def close(self):
        for hop in range(1, self.members):
            for present, copy in self.copies(hop)[0]:

                @pl.when(present)
                def _():
                    copy().wait_send()


class LineSum:
    def __init__(self, members, part, leaving, arriving, send, recv):
        self.members, self.part, self.leaving, self.arriving = members, part, leaving, arriving
        self.send, self.recv = send, recv

    def copy(self, way, hop, device):
        return remote(
            self.leaving.at[way],
            self.arriving.at[way, hop - 1],
            self.send.at[way, hop - 1],
            self.recv.at[way, hop - 1],
            {"tensor": device},
        )

    def ways(self, hop):
        z, last = lax.axis_index("tensor"), self.members - 1
        return (
            (0, z - hop >= 0, z - hop, z < last, z - 1, (z < last) & (z + 1 - hop >= 0)),
            (1, z + hop <= last, z + hop, z > 0, z + 1, (z > 0) & (z - 1 + hop <= last)),
        )

    def start(self, hop):
        if hop + 1 < self.members:
            self.leave(hop + 1)
        for way, present, block, behind, device, _ in self.ways(hop):

            @pl.when(present)
            def _():
                self.leaving[way] = self.part(block).astype(bf16)

            if hop + 1 < self.members:

                @pl.when(present & behind)
                def _():
                    both = self.part(block).astype(f32) + self.arriving[way, hop].astype(f32)
                    self.leaving[way] = both.astype(bf16)

            @pl.when(present)
            def _():
                self.copy(way, hop, device).start()

    def arrive(self, hop):
        for way, _, _, _, device, present in self.ways(hop):

            @pl.when(present)
            def _():
                self.copy(way, hop, device).wait_recv()

    def total(self, out):
        z, last = lax.axis_index("tensor"), self.members - 1
        out[...] = self.part(z).astype(f32)
        for way, present in ((0, z < last), (1, z > 0)):

            @pl.when(present)
            def _():
                out[...] += self.arriving[way, 0].astype(f32)

    def leave(self, hop):
        for way, present, _, _, device, _ in self.ways(hop):

            @pl.when(present)
            def _():
                self.copy(way, hop, device).wait_send()

    def close(self):
        self.leave(1)


def swap_blocks(values):
    me = lax.axis_index("dp")
    chip = values.shape[1] // 4
    four = [values[:, i * chip : (i + 1) * chip] for i in range(4)]
    y_side, x_side, core_side = lax.rem(me // 4, 2) == 1, lax.rem(me // 2, 2) == 1, lax.rem(me, 2) == 1
    four = [jnp.where(y_side, four[i ^ 2], four[i]) for i in range(4)]
    four = [jnp.where(x_side, four[i ^ 1], four[i]) for i in range(4)]
    four = [jnp.where(core_side, pltpu.roll(part, chip // 2, 1), part) for part in four]
    return jnp.concatenate(four, axis=1)


def in_vmem(count):
    return [pl.BlockSpec(memory_space=pltpu.VMEM)] * count


def pack_chunk(gate, up, down, begin):
    gate, up, down = (
        jnp.swapaxes(w[:, begin : begin + 2 * CALL_PAIRS, :], 0, 1) for w in (gate, up, down)
    )

    def pair(a, b):
        return [a[:, :HD], b[:, :HD], jnp.concatenate([a[:, HD:], b[:, HD:]], axis=1)]

    return [
        jnp.concatenate(
            pair(gate[e], up[e]) + pair(gate[e + 1], up[e + 1]) + pair(down[e], down[e + 1]), axis=1
        )
        for e in range(0, 2 * CALL_PAIRS, 2)
    ]


def gather_small(
    q_weight, o_weight, k_weight, v_weight, gains, cotangent, ids, route_weights, gate, up, down, members, devices
):
    height, part = q_weight.shape
    own_rows, width = cotangent.shape
    rows = own_rows * members
    kv = k_weight.shape[1]
    tall = 2 * kv + HD
    lanes = 9 * HD
    calls = EXPERTS // 2 // CALL_PAIRS
    dma = pltpu.SemaphoreType.DMA
    cut = part

    def kernel(*refs):
        q_ref, o_ref, k_ref, v_ref, gains_ref, cot_ref, ids_ref, weights_ref, gate_ref, up_ref, down_ref = refs[:11]
        square_all, tall_all, grad_all = refs[11:14]
        rank_cols, routes, packed = (refs[14 + calls * i : 14 + calls * (i + 1)] for i in range(3))
        from_x, from_y = refs[14 + 3 * calls : 16 + 3 * calls]
        sems = refs[16 + 3 * calls :]
        line_send, line_recv, grad_send, grad_recv, chip_send, chip_recv, core_send, core_recv = sems
        me, z = lax.axis_index("dp"), lax.axis_index("tensor")
        x_side, y_side = chip_neighbours()
        core = sibling()

        def rows_of(device):
            return pl.ds(pl.multiple_of(device * height, 16), height)

        def pack(call):
            chunk = pack_chunk(gate_ref, up_ref, down_ref, 2 * CALL_PAIRS * call)
            for pair, value in enumerate(chunk):
                packed[call][pair] = value

        def chip(index, source, device, target=None):
            target = source if target is None else target
            return remote(source, target, chip_send.at[index], chip_recv.at[index], {"dp": device})

        def across(index, source):
            return remote(source, source, core_send.at[index], core_recv.at[index], {"dp": core})

        def tall_at(device):
            return tall_all.at[rows_of(device)]

        def square_at(device, half=None):
            span = slice(None) if half is None else slice(half * cut, (half + 1) * cut)
            return square_all.at[:, rows_of(device), span]

        square_all[z, rows_of(me), :part] = q_ref[...]
        square_all[z, rows_of(me), part:] = o_ref[...]
        tall_all[rows_of(me), :kv] = k_ref[...]
        tall_all[rows_of(me), kv : 2 * kv] = v_ref[...]
        tall_all[rows_of(me), 2 * kv :] = gains_ref[...]
        line = LineGather(members, lambda block: square_all.at[block, rows_of(me)], line_send, line_recv)
        group = LineGather(
            members,
            lambda block: grad_all.at[pl.ds(pl.multiple_of(block * own_rows, 16), own_rows)],
            grad_send,
            grad_recv,
        )
        meet(members, True)
        line.start(1)
        near = [chip(0, tall_at(me), x_side), chip(1, tall_at(me), y_side)]
        for copy in near:
            copy.start()
        pack(0)
        chunk = [chip(7, packed[0], x_side, from_x), chip(8, packed[0], y_side, from_y)]
        for copy in chunk:
            copy.start()
        grad_all[pl.ds(pl.multiple_of(z * own_rows, 16), own_rows), :] = swap_blocks(cot_ref[...]).astype(bf16)
        for hop in range(1, members):
            line.arrive(hop)
            if hop + 1 < members:
                line.start(hop + 1)
        near += [chip(2, square_at(me), x_side), chip(3, square_at(me), y_side)]
        for copy in near[2:]:
            copy.start()
        group.start(1)
        trades = [across(0, tall_at(me)), across(1, square_at(me))]
        for copy in trades:
            copy.start()
        chip(0, tall_at(x_side), x_side).wait_recv()
        chip(1, tall_at(y_side), y_side).wait_recv()
        diagonal = x_side + y_side - me
        far = [chip(4, tall_at(x_side), y_side)]
        far[0].start()
        trades += [across(2, tall_at(x_side)), across(3, tall_at(y_side))]
        for copy in trades[2:]:
            copy.start()

        lane = lax.broadcasted_iota(jnp.int32, (rows, HD), 1)
        weight = jnp.zeros((rows, HD), f32)
        named = jnp.zeros((rows, HD), f32)
        for route in range(ids_ref.shape[1]):
            here = ids_ref[:, route : route + 1] == lane
            named = jnp.where(here, 1.0, named)
            weight = jnp.where(here, weights_ref[:, route : route + 1], weight)
        row = lax.broadcasted_iota(jnp.int32, (rows, rows), 0)
        earlier = (row > lax.broadcasted_iota(jnp.int32, (rows, rows), 1)).astype(bf16)
        rank = jnp.where(named > 0.0, nn(earlier, named.astype(bf16)), -1.0)
        by_rank, by_weight = jnp.transpose(rank), jnp.transpose(weight)
        for call in range(calls):
            turned = rank if call == 0 else pltpu.roll(rank, HD - 2 * CALL_PAIRS * call, 1)
            rank_cols[call][...] = turned.astype(bf16)
            for e in range(2 * CALL_PAIRS):
                at = 2 * CALL_PAIRS * call + e
                routes[call][e, 0:1, :] = by_rank[at : at + 1]
                routes[call][e, 1:2, :] = by_weight[at : at + 1]
        for call in range(1, calls):
            pack(call)

        group.arrive(1)
        if members > 2:
            group.start(2)
        chip(2, square_at(x_side), x_side).wait_recv()
        chip(3, square_at(y_side), y_side).wait_recv()
        far += [chip(5, square_at(x_side, 0), y_side), chip(6, square_at(y_side, 1), x_side)]
        for copy in far[1:]:
            copy.start()
        trades += [across(4, square_at(x_side)), across(5, square_at(y_side))]
        for copy in trades[4:]:
            copy.start()
        chip(4, tall_at(diagonal), y_side).wait_recv()
        trades.append(across(6, tall_at(diagonal)))
        trades[-1].start()
        for hop in range(2, members - 1):
            group.arrive(hop)
            group.start(hop + 1)
        chip(5, square_at(diagonal, 0), y_side).wait_recv()
        chip(6, square_at(diagonal, 1), x_side).wait_recv()
        trades.append(across(7, square_at(diagonal)))
        trades[-1].start()
        theirs = [core, core, x_side, y_side, x_side, y_side, diagonal, diagonal]
        for index, device in enumerate(theirs):
            there = device if index < 2 else device + core - me
            source = square_at(there) if index in (1, 4, 5, 7) else tall_at(there)
            across(index, source).wait_recv()
        if members > 2:
            group.arrive(members - 1)
        for copy in chunk:
            copy.wait()
        for copy in near + far + trades:
            copy.wait_send()
        line.close()
        group.close()

    chunk_shape = jax.ShapeDtypeStruct((CALL_PAIRS, height, lanes), bf16)
    return pl.pallas_call(
        kernel,
        in_specs=in_vmem(11),
        out_specs=in_vmem(3 + 3 * calls) + [pl.BlockSpec(memory_space=pl.ANY)] * 2,
        out_shape=[
            jax.ShapeDtypeStruct((members, devices * height, 2 * part), bf16),
            jax.ShapeDtypeStruct((devices * height, tall), bf16),
            jax.ShapeDtypeStruct((rows, width), bf16),
        ]
        + [jax.ShapeDtypeStruct((rows, HD), bf16)] * calls
        + [jax.ShapeDtypeStruct((2 * CALL_PAIRS, 2, rows), f32)] * calls
        + [chunk_shape] * (calls + 2),
        scratch_shapes=[dma((2, members - 1))] * 4 + [dma((9,))] * 2 + [dma((8,))] * 2,
        compiler_params=pltpu.CompilerParams(collective_id=2, has_side_effects=True, vmem_limit_bytes=56 * 2**20),
        cost_estimate=pl.CostEstimate(flops=8 * 10**10, bytes_accessed=10**7, transcendentals=0),
        name="gather_small",
    )(q_weight, o_weight, k_weight, v_weight, gains, cotangent, ids, route_weights, gate, up, down)


def turn(values, cosine, sine):
    return values * cosine + pltpu.roll(values, HD // 2, 1) * sine


def gain_rows(tall_ref, kv):
    return jnp.transpose(tall_ref[:, kv:].astype(f32))


def attention_front(tokens, square, tall, cosine, sine, packed, near, members):
    own_rows, width = tokens.shape
    rows = own_rows * members
    kv = 2 * KV * HD
    heads = width // HD
    per_kv = heads // KV
    part = width // members
    dma = pltpu.SemaphoreType.DMA

    def kernel(x_ref, square_ref, tall_ref, cos_ref, sin_ref, *rest):
        chunks, rest = rest[:count], rest[count:]
        normed_ref, q_ref, kv_all, mixed_ref, hidden_ref, rows_all, sums_ref = rest[:7]
        landed, rest = rest[7 : 5 + 2 * count], rest[5 + 2 * count :]
        blank, kv_send, kv_recv, row_send, row_recv, chip_send, chip_recv, blank_sem = rest
        z = lax.axis_index("tensor")
        x_side, y_side = chip_neighbours()
        meet(members, False)
        pairs = chunks[0].shape[0]
        first, second = slice(0, pairs // 2), slice(pairs // 2, pairs)
        moves = [(chunks[0].at[first], y_side), (chunks[1].at[second], x_side)]
        for chunk in chunks[2:]:
            moves += [(chunk, x_side), (chunk, y_side)]
        moves = [
            remote(source, landed[i], chip_send.at[i], chip_recv.at[i], {"dp": device})
            for i, (source, device) in enumerate(moves)
        ]
        for copy in moves:
            copy.start()
        blank[...] = jnp.zeros_like(blank)
        fills = [
            pltpu.make_async_copy(blank, sums_ref.at[b * own_rows : (b + 1) * own_rows, s * width : (s + 1) * width], blank_sem.at[b, s])
            for b in range(members)
            for s in range(2)
        ]
        for copy in fills:
            copy.start()

        def block_of(ref):
            return lambda block: ref.at[pl.ds(pl.multiple_of(block * own_rows, 16), own_rows)]

        own = pl.ds(pl.multiple_of(z * own_rows, 16), own_rows)
        kv_line = LineGather(members, block_of(kv_all), kv_send, kv_recv)
        row_line = LineGather(members, block_of(rows_all), row_send, row_recv)
        gains = gain_rows(tall_ref, kv)
        x = x_ref[...].astype(f32)
        normed_ref[...] = (rms_pieces(x)[1] * gains[0:1]).astype(bf16)
        cosine, sine = cos_ref[own], sin_ref[own]
        made = nn(normed_ref[...], tall_ref[:, :kv])
        for head in range(KV):
            span = slice(head * HD, (head + 1) * HD)
            kv_all[own, span] = turn(made[:, span], cosine, sine).astype(bf16)
        kv_all[own, KV * HD :] = made[:, KV * HD :].astype(bf16)
        kv_line.start(1)
        for t in range(members):
            made = nn(normed_ref[...], square_ref[t, :, :part])
            for head in range(part // HD):
                span = slice(head * HD, (head + 1) * HD)
                q_ref[:, t * part + head * HD : t * part + (head + 1) * HD] = turn(
                    made[:, span], cosine, sine
                ).astype(bf16)
            if 1 <= t + 1 < members:
                kv_line.arrive(t + 1)
                if t + 2 < members:
                    kv_line.start(t + 2)
        first_row = z * own_rows

        @pl.loop(0, heads)
        def _(head):
            span = pl.ds(pl.multiple_of(head * HD, HD), HD)
            key_span = pl.ds(pl.multiple_of(head // per_kv * HD, HD), HD)
            value_span = pl.ds(pl.multiple_of((KV + head // per_kv) * HD, HD), HD)
            p = probabilities(q_ref[:, span], kv_all[:, key_span], first_row).astype(bf16)
            mixed_ref[:, span] = nn(p, kv_all[:, value_span]).astype(bf16)

        hidden = x_ref[...].astype(f32)
        for t in range(members):
            hidden += nt(mixed_ref[:, t * part : (t + 1) * part], square_ref[t, :, part:])
        hidden_ref[...] = hidden
        normed = rms_pieces(hidden)[1] * gains[1:2]
        rows_all[own, :] = swap_blocks(normed).astype(bf16)
        for hop in range(1, members):
            row_line.start(hop)
            row_line.arrive(hop)
        kv_line.close()
        row_line.close()
        for copy in moves:
            copy.wait()
        for copy in fills:
            copy.wait()

    count = 2 + len(packed)
    anywhere = pl.BlockSpec(memory_space=pl.ANY)
    size, height, lanes = near[0].shape
    return pl.pallas_call(
        kernel,
        in_specs=in_vmem(5) + [anywhere] * count,
        out_specs=in_vmem(6) + [anywhere] * (1 + 2 + 2 * len(packed)),
        out_shape=[
            jax.ShapeDtypeStruct((own_rows, width), bf16),
            jax.ShapeDtypeStruct((own_rows, width), bf16),
            jax.ShapeDtypeStruct((rows, kv), bf16),
            jax.ShapeDtypeStruct((own_rows, width), bf16),
            jax.ShapeDtypeStruct((own_rows, width), f32),
            jax.ShapeDtypeStruct((rows, width), bf16),
            jax.ShapeDtypeStruct((rows, 2 * width), f32),
        ]
        + [jax.ShapeDtypeStruct((size // 2, height, lanes), bf16)] * 2
        + [jax.ShapeDtypeStruct((size, height, lanes), bf16)] * (2 * len(packed)),
        scratch_shapes=[pltpu.VMEM((own_rows, width), f32)]
        + [dma((2, members - 1))] * 4
        + [dma((2 + 2 * len(packed),))] * 2
        + [dma((members, 2))],
        compiler_params=pltpu.CompilerParams(collective_id=3, has_side_effects=True, vmem_limit_bytes=56 * 2**20),
        cost_estimate=pl.CostEstimate(flops=10**11, bytes_accessed=10**7, transcendentals=0),
        name="attention_front",
    )(tokens, square, tall, cosine, sine, *near, *packed)


def attention_back(
    sums, cotangent, hidden, tokens, normed, q, kv_all, mixed, square, tall, cosine, sine, last_chunk, to_x, to_y, members
):
    own_rows, width = tokens.shape
    rows = own_rows * members
    kv = 2 * KV * HD
    heads = width // HD
    per_kv = heads // KV
    part = width // members
    dma = pltpu.SemaphoreType.DMA

    def kernel(sums_ref, cot_ref, hidden_ref, x_ref, normed_ref, q_ref, kv_ref, mixed_ref, square_ref, tall_ref, *rest):
        cos_ref, sin_ref, chunk, to_x_ref, to_y_ref = rest[:5]
        grad_ref, parts, x_before, y_before, x_last, y_last = rest[5:11]
        do_ref, dq_ref, dkv_ref, total, kv_total, stage, tall_part, back_part = rest[11:19]
        back_leave, back_arrive, kv_leave, kv_arrive = rest[19:23]
        back_send, back_recv, kv_send, kv_recv, stage_sem, part_sem = rest[23:29]
        through, added, added_sem, chip_send, chip_recv = rest[29:]
        z = lax.axis_index("tensor")
        x_side, y_side = chip_neighbours()
        first, second = slice(0, size // 2), slice(size // 2, size)

        def chip(index, source, target, device):
            return remote(source, target, chip_send.at[index], chip_recv.at[index], {"dp": device})

        loads = [
            pltpu.make_async_copy(
                sums_ref.at[b * own_rows : (b + 1) * own_rows, width:], back_part.at[b], part_sem.at[b]
            )
            for b in range(members)
        ] + [
            pltpu.make_async_copy(chunk.at[1, second], added.at[0], added_sem.at[0]),
            pltpu.make_async_copy(chunk.at[2, first], added.at[1], added_sem.at[1]),
        ]
        for copy in loads:
            copy.start()
        meet(members, False)
        moves = [
            chip(0, chunk.at[3, first], through.at[0], x_side),
            chip(1, chunk.at[3, second], through.at[1], y_side),
            chip(2, to_x_ref, x_before, x_side),
            chip(3, to_y_ref, y_before, y_side),
            chip(4, chunk.at[1, first], x_last.at[first], x_side),
            chip(5, chunk.at[2, second], y_last.at[second], y_side),
            chip(6, added.at[0], x_last.at[second], x_side),
            chip(7, added.at[1], y_last.at[first], y_side),
        ]
        for copy in moves[:6]:
            copy.start()
        own = pl.ds(pl.multiple_of(z * own_rows, 16), own_rows)
        for copy in loads:
            copy.wait()

        def block(ref, span):
            return lambda b: ref[pl.ds(pl.multiple_of(b * own_rows, 16), own_rows), span]

        back = LineSum(members, lambda b: back_part[b], back_leave, back_arrive, back_send, back_recv)
        pairs = LineSum(members, block(dkv_ref, slice(None)), kv_leave, kv_arrive, kv_send, kv_recv)
        gains = gain_rows(tall_ref, kv)
        cosine, sine = cos_ref[own], sin_ref[own]
        last = members - 1
        stored = []

        def store(value, at):
            slot = len(stored) % 2
            if len(stored) >= 2:
                stored[-2].wait()
            stage[slot] = value.astype(bf16)
            copy = pltpu.make_async_copy(stage.at[slot], parts.at[:, at : at + part], stage_sem.at[slot])
            copy.start()
            stored.append(copy)

        for hop in range(last, 0, -1):
            back.start(hop)
            back.arrive(hop)
        back.total(total)
        normed_grad = swap_blocks(total[...])
        inverse, unit = rms_pieces(hidden_ref[...])
        by_hidden, gain_two = rms_backward(normed_grad, unit, inverse, gains[1:2])
        grad_ref[...] = cot_ref[...] + by_hidden
        low = grad_ref[...].astype(bf16)
        for t in range(members):
            span = slice(t * part, (t + 1) * part)
            do_ref[:, span] = nn(low, square_ref[t, :, part:]).astype(bf16)
            store(tn(low, mixed_ref[:, span]), width + t * part)
        dkv_ref[...] = jnp.zeros_like(dkv_ref)
        first_row = z * own_rows

        @pl.loop(0, heads)
        def _(head):
            span = pl.ds(pl.multiple_of(head * HD, HD), HD)
            key_span = pl.ds(pl.multiple_of(head // per_kv * HD, HD), HD)
            value_span = pl.ds(pl.multiple_of((KV + head // per_kv) * HD, HD), HD)
            q_now, k_now, do_now = q_ref[:, span], kv_ref[:, key_span], do_ref[:, span]
            p = probabilities(q_now, k_now, first_row)
            dp = nt(do_now, kv_ref[:, value_span])
            ds = (p * (dp - jnp.sum(p * dp, axis=-1, keepdims=True))).astype(bf16)
            dq_ref[:, span] = turn(nn(ds, k_now) * (HD**-0.5), cosine, -sine).astype(bf16)
            dkv_ref[:, key_span] += tn(ds, q_now) * (HD**-0.5)
            dkv_ref[:, value_span] += tn(p.astype(bf16), do_now)

        pairs.start(last)
        for i, copy in enumerate(moves[:2]):
            copy.wait()
            added[1 - i] = (added[1 - i].astype(f32) + through[i].astype(f32)).astype(bf16)
            moves[7 - i].start()
        for t in range(members):
            span = slice(t * part, (t + 1) * part)
            store(tn(normed_ref[...], dq_ref[:, span]), t * part)
        for hop in range(last, 0, -1):
            if hop < last:
                pairs.start(hop)
            pairs.arrive(hop)
        pairs.total(kv_total)
        low_kv = [
            turn(kv_total[:, head * HD : (head + 1) * HD], cosine, -sine).astype(bf16) for head in range(KV)
        ] + [kv_total[:, KV * HD :].astype(bf16)]
        low_kv = jnp.concatenate(low_kv, axis=1)
        normed_grad = nt(low_kv, tall_ref[:, :kv])
        for t in range(members):
            normed_grad += nt(dq_ref[:, t * part : (t + 1) * part], square_ref[t, :, :part])
        inverse, unit = rms_pieces(x_ref[...].astype(f32))
        by_tokens, gain_one = rms_backward(normed_grad, unit, inverse, gains[0:1])
        grad_ref[...] += by_tokens
        tall_part[:, :kv] = tn(normed_ref[...], low_kv).astype(bf16)
        row = lax.broadcasted_iota(jnp.int32, (HD, width), 0)
        both = jnp.where(row == 0, gain_one[None], jnp.where(row == 1, gain_two[None], 0.0))
        tall_part[:, kv:] = jnp.transpose(both).astype(bf16)
        tall_copy = pltpu.make_async_copy(tall_part, parts.at[:, 2 * width :], stage_sem.at[2])
        tall_copy.start()
        for line in (back, pairs):
            line.close()
        for copy in (*stored[-2:], tall_copy, *moves[2:]):
            copy.wait()

    hops = (2, members - 1)
    anywhere = pl.BlockSpec(memory_space=pl.ANY)
    size, height, lanes = to_x.shape
    halves = (2, size // 2, height, lanes)
    return pl.pallas_call(
        kernel,
        in_specs=[anywhere] + in_vmem(11) + [anywhere] * 3,
        out_specs=in_vmem(1) + [anywhere] * 5,
        out_shape=[
            jax.ShapeDtypeStruct((own_rows, width), f32),
            jax.ShapeDtypeStruct((width, 2 * width + tall.shape[1]), bf16),
        ]
        + [jax.ShapeDtypeStruct((size, height, lanes), bf16)] * 4,
        scratch_shapes=[
            pltpu.VMEM((own_rows, width), bf16),
            pltpu.VMEM((own_rows, width), bf16),
            pltpu.VMEM((rows, kv), f32),
            pltpu.VMEM((own_rows, width), f32),
            pltpu.VMEM((own_rows, kv), f32),
            pltpu.VMEM((2, width, part), bf16),
            pltpu.VMEM(tall.shape, bf16),
            pltpu.VMEM((members, own_rows, width), f32),
            pltpu.VMEM((2, own_rows, width), bf16),
            pltpu.VMEM((*hops, own_rows, width), bf16),
            pltpu.VMEM((2, own_rows, kv), bf16),
            pltpu.VMEM((*hops, own_rows, kv), bf16),
        ]
        + [dma(hops)] * 4
        + [dma((3,)), dma((members,)), pltpu.VMEM(halves, bf16), pltpu.VMEM(halves, bf16), dma((2,)), dma((8,)), dma((8,))],
        compiler_params=pltpu.CompilerParams(collective_id=4, has_side_effects=True, vmem_limit_bytes=62 * 10**6),
        cost_estimate=pl.CostEstimate(flops=10**11, bytes_accessed=10**7, transcendentals=0),
        name="attention_back",
    )(
        sums, cotangent, hidden, tokens, normed, q, kv_all, mixed, square, tall, cosine, sine, last_chunk, to_x, to_y
    )


def reduce_small(parts, sums, hidden, members, devices):
    own_rows = hidden.shape[0]
    width = parts.shape[0]
    height = width // devices
    lanes = parts.shape[1]
    tall = lanes - 2 * width
    part = width // members
    half = height // 2
    dma = pltpu.SemaphoreType.DMA

    def kernel(parts_ref, sums_ref, hidden_ref, out_ref, square_out, tall_out, *rest):
        own, theirs, leave, arrive, blocks, line_leave, line_arrive, tall_all = rest[:8]
        moe_part, moe_leave, moe_arrive, total_ref = rest[8:12]
        own_sem, core_send, core_recv, chip_send, chip_recv, line_send, line_recv, tall_send, tall_recv = rest[12:21]
        moe_send, moe_recv, part_sem = rest[21:]
        me, z = lax.axis_index("dp"), lax.axis_index("tensor")
        x_side, y_side = chip_neighbours()
        core = sibling()
        chips = [me, x_side, y_side, x_side + y_side - me]
        loads = [
            pltpu.make_async_copy(
                sums_ref.at[b * own_rows : (b + 1) * own_rows, :width], moe_part.at[b], part_sem.at[b]
            )
            for b in range(members)
        ]
        for copy in loads:
            copy.start()
        meet(members, True)
        moe = LineSum(members, lambda b: moe_part[b], moe_leave, moe_arrive, moe_send, moe_recv)
        last = members - 1

        def rows(device):
            return parts_ref.at[pl.ds(pl.multiple_of(device * height, 16), height)]

        def trade(m):
            return remote(rows(chips[m] + core - me), theirs.at[m], core_send.at[m], core_recv.at[m], {"dp": core})

        def keep(m):
            return pltpu.make_async_copy(rows(chips[m]), own.at[m], own_sem.at[m])

        for m in (3, 2, 1, 0):
            trade(m).start()
            keep(m).start()
        for copy in loads:
            copy.wait()
        moe.start(last)

        def both(m, span):
            return own[m, span].astype(f32) + theirs[m, span].astype(f32)

        def chip(index, source, target, device):
            return remote(source, target, chip_send.at[index], chip_recv.at[index], {"dp": device})

        first, second = slice(0, half), slice(half, height)
        far = [
            chip(0, leave.at[0, first], arrive.at[0, first], x_side),
            chip(1, leave.at[0, second], arrive.at[0, second], y_side),
        ]
        near = [chip(2, leave.at[1], arrive.at[1], x_side), chip(3, leave.at[2], arrive.at[2], y_side)]
        for m in (3, 2, 1, 0):
            trade(m).wait()
            keep(m).wait()
            if m == 3:
                for copy, span in zip(far, (first, second)):
                    leave[0, span] = both(3, span).astype(bf16)
                    copy.start()
        for copy in far:
            copy.wait()
        moe.arrive(last)
        if last > 1:
            moe.start(last - 1)
        leave[1, first] = both(1, first).astype(bf16)
        leave[1, second] = (both(1, second) + arrive[0, second].astype(f32)).astype(bf16)
        near[0].start()
        leave[2, first] = (both(2, first) + arrive[0, first].astype(f32)).astype(bf16)
        leave[2, second] = both(2, second).astype(bf16)
        near[1].start()
        for hop in range(last - 1, 0, -1):
            moe.arrive(hop)
            if hop > 1:
                moe.start(hop - 1)
        moe.total(total_ref)
        out_ref[...] = (hidden_ref[...] + swap_blocks(total_ref[...])).astype(bf16)
        for copy in near:
            copy.wait()

        def total(span):
            return (
                own[0, :, span].astype(f32)
                + theirs[0, :, span].astype(f32)
                + arrive[1, :, span].astype(f32)
                + arrive[2, :, span].astype(f32)
            )

        tall_all[z] = total(slice(2 * width, lanes)).astype(bf16)
        for t in range(members):
            blocks[t, :, :part] = total(slice(t * part, (t + 1) * part))
            blocks[t, :, part:] = total(slice(width + t * part, width + (t + 1) * part))
        line = LineSum(members, lambda b: blocks[b], line_leave, line_arrive, line_send, line_recv)
        group = LineGather(members, lambda b: tall_all.at[b], tall_send, tall_recv)
        for hop in range(1, members):
            line.start(members - hop)
            group.start(hop)
            line.arrive(members - hop)
            group.arrive(hop)
        line.total(square_out)
        summed = tall_all[0].astype(f32)
        for t in range(1, members):
            summed += tall_all[t].astype(f32)
        tall_out[...] = summed
        line.close()
        group.close()
        moe.close()

    hops = (2, members - 1)
    return pl.pallas_call(
        kernel,
        in_specs=[pl.BlockSpec(memory_space=pl.ANY)] * 2 + in_vmem(1),
        out_specs=in_vmem(3),
        out_shape=[
            jax.ShapeDtypeStruct((own_rows, width), bf16),
            jax.ShapeDtypeStruct((height, 2 * part), f32),
            jax.ShapeDtypeStruct((height, tall), f32),
        ],
        scratch_shapes=[
            pltpu.VMEM((4, height, lanes), bf16),
            pltpu.VMEM((4, height, lanes), bf16),
            pltpu.VMEM((3, height, lanes), bf16),
            pltpu.VMEM((3, height, lanes), bf16),
            pltpu.VMEM((members, height, 2 * part), f32),
            pltpu.VMEM((2, height, 2 * part), bf16),
            pltpu.VMEM((*hops, height, 2 * part), bf16),
            pltpu.VMEM((members, height, tall), bf16),
            pltpu.VMEM((members, own_rows, width), f32),
            pltpu.VMEM((2, own_rows, width), bf16),
            pltpu.VMEM((*hops, own_rows, width), bf16),
            pltpu.VMEM((own_rows, width), f32),
            dma((4,)),
            dma((4,)),
            dma((4,)),
            dma((4,)),
            dma((4,)),
        ]
        + [dma(hops)] * 6
        + [dma((members,))],
        compiler_params=pltpu.CompilerParams(collective_id=5, has_side_effects=True, vmem_limit_bytes=60 * 2**20),
        cost_estimate=pl.CostEstimate(flops=8 * 10**10, bytes_accessed=10**7, transcendentals=0),
        name="reduce_small",
    )(parts, sums, hidden)


def unpack_all(chunks, from_x, from_y):
    calls = len(chunks)
    _, pairs, height, lanes = chunks[0].shape
    units = lanes // 6
    tail = units - HD
    step = 48 if height % 48 == 0 else height

    def kernel(*refs):
        gate, up, down = refs[3 * calls :]
        for call in range(calls):
            own, by_x, by_y = refs[3 * call : 3 * call + 3]
            found = [[], [], []]
            for pair in range(pairs):
                value = own[0, pair].astype(f32) + by_x[pair].astype(f32) + by_y[pair].astype(f32)
                tiles = [value[:, i * HD : (i + 1) * HD] for i in range(9)]
                for i, (a, b) in enumerate(((0, 1), (3, 4), (6, 7))):
                    ends = tiles[a - a % 3 + 2]
                    left = jnp.concatenate([tiles[a], ends[:, :tail]], axis=1)
                    right = jnp.concatenate([tiles[b], ends[:, tail:]], axis=1)
                    if i < 2:
                        found[0].append(left)
                        found[1].append(right)
                    else:
                        found[2] += [left, right]
            for out, values in zip((gate, up, down), found):
                out[:, 2 * pairs * call : 2 * pairs * (call + 1), :] = jnp.swapaxes(jnp.stack(values), 0, 1)

    chunk = pl.BlockSpec((1, pairs, step, lanes), lambda i: (0, 0, i, 0))
    other = pl.BlockSpec((pairs, step, lanes), lambda i: (0, i, 0))
    shape = (height, 2 * pairs * calls, units)
    return pl.pallas_call(
        kernel,
        grid=(height // step,),
        in_specs=[chunk, other, other] * calls,
        out_specs=[pl.BlockSpec((step, *shape[1:]), lambda i: (i, 0, 0))] * 3,
        out_shape=[jax.ShapeDtypeStruct(shape, f32)] * 3,
        compiler_params=pltpu.CompilerParams(vmem_limit_bytes=48 * 2**20),
        name="unpack",
    )(*(array for call in zip(chunks, from_x, from_y) for array in call))


def pack(gate, up, down):
    def pair(a, b):
        return jnp.concatenate([a[..., :HD], b[..., :HD], a[..., HD:], b[..., HD:]], axis=-1)

    gate, up, down = (jnp.transpose(w, (1, 0, 2)) for w in (gate, up, down))
    gate_up = pair(gate, up)
    return jnp.concatenate([gate_up[0::2], gate_up[1::2], pair(down[0::2], down[1::2])], axis=-1)


def unpack(packed):
    n, height, lanes = packed.shape
    third = lanes // 3

    def halves(both):
        tail = third // 2 - HD
        a = jnp.concatenate([both[..., :HD], both[..., 2 * HD : 2 * HD + tail]], axis=-1)
        b = jnp.concatenate([both[..., HD : 2 * HD], both[..., 2 * HD + tail :]], axis=-1)
        return a, b

    def experts(even, odd):
        both = jnp.stack([even, odd], axis=1).reshape(2 * n, height, third // 2)
        return jnp.transpose(both, (1, 0, 2))

    gate0, up0 = halves(packed[..., :third])
    gate1, up1 = halves(packed[..., third : 2 * third])
    down0, down1 = halves(packed[..., 2 * third :])
    return experts(gate0, gate1), experts(up0, up1), experts(down0, down1)


def flip(value, bit):
    count = lax.axis_size("dp")
    return lax.ppermute(value, "dp", [(i, i ^ bit) for i in range(count)])


def half_of(chunk):
    cut = chunk.shape[0] // 2
    return slice(0, cut), slice(cut, None)


def scatter_step(chunk, before):
    to_x, to_y = [], []
    if before is not None:
        blocks, via_x, via_y = before
        first, second = half_of(blocks[0])
        to_x += [blocks[1, first], add(blocks[1, second], via_y)]
        to_y += [add(blocks[2, first], via_x), blocks[2, second]]
    if chunk is not None:
        first, second = half_of(chunk[0])
        to_x.append(chunk[3, first])
        to_y.append(chunk[3, second])
    return flip(jnp.concatenate(to_x), 2), flip(jnp.concatenate(to_y), 4)


def before_of(chunks, moved, call):
    if call == 0:
        return None
    cut = CALL_PAIRS // 2
    return chunks[call - 1], moved[call - 1][0][-cut:], moved[call - 1][1][-cut:]


def add(a, b):
    return (a.astype(f32) + b.astype(f32)).astype(bf16)


def routes_of(expert_ids, route_weights):
    rows = expert_ids.shape[0]
    lanes = jnp.arange(EXPERTS, dtype=jnp.int32)
    named = expert_ids[:, :, None] == lanes
    member_of = jnp.any(named, axis=1)
    weight_of = jnp.sum(jnp.where(named, route_weights[:, :, None], 0.0), axis=1)
    earlier = jnp.arange(rows)[:, None] > jnp.arange(rows)[None, :]
    rank = jnp.where(member_of, nn(earlier.astype(bf16), member_of.astype(bf16)), -1.0)
    rank_cols = jnp.pad(rank, ((0, 0), (0, HD)), constant_values=-1.0).astype(bf16)
    return rank_cols, jnp.stack([rank.T, weight_of.T], axis=1)


def body_anywhere(
    tokens,
    expert_ids,
    route_weights,
    attn_gain,
    q_weight,
    k_weight,
    v_weight,
    o_weight,
    moe_gain,
    gate_weight,
    up_weight,
    down_weight,
    cotangent,
):
    members = lax.axis_size("tensor")
    member = lax.axis_index("tensor")
    own_rows, width = tokens.shape
    rows = own_rows * members
    pairs = EXPERTS // 2
    calls = pairs // CALL_PAIRS

    packed = [
        pack(*(w[:, 2 * CALL_PAIRS * i : 2 * CALL_PAIRS * (i + 1)] for w in (gate_weight, up_weight, down_weight)))
        for i in range(calls)
    ]
    gathered = [[[(lax.all_gather(own, "dp", axis=1, tiled=True), 0)]] for own in packed]

    gain_one = lax.all_gather(attn_gain, "dp", axis=0, tiled=True).astype(f32)
    gain_two = lax.all_gather(moe_gain, "dp", axis=0, tiled=True).astype(f32)
    kv_full = lax.all_gather(jnp.concatenate([k_weight, v_weight], axis=1), "dp", axis=0, tiled=True)
    q_full = lax.all_gather(lax.all_gather(q_weight, "dp", axis=0, tiled=True), "tensor", axis=0)
    o_full = lax.all_gather(lax.all_gather(o_weight, "dp", axis=0, tiled=True), "tensor", axis=0)
    kv_width = k_weight.shape[1]

    rank_cols, routes = routes_of(expert_ids, route_weights)

    grad_low = cotangent.astype(bf16)
    grad_all = lax.all_gather(grad_low, "tensor", axis=0, tiled=True)

    x = tokens.astype(f32)
    inverse_one, unit_one = rms_pieces(x)
    normed_one = (unit_one * gain_one).astype(bf16)
    first_row = (member * own_rows).reshape(1)
    cos_table, sin_table = rope_tables(member * own_rows + jnp.arange(own_rows, dtype=jnp.int32))
    kv_own = nn(normed_one, kv_full)
    kv_own = jnp.concatenate(
        [rotate(kv_own[:, :kv_width], cos_table, sin_table), kv_own[:, kv_width:]], axis=1
    ).astype(bf16)
    kv_all = lax.all_gather(kv_own, "tensor", axis=0, tiled=True)
    keys, values = kv_all[:, :kv_width], kv_all[:, kv_width:]
    queries = jnp.concatenate([nn(normed_one, q_full[t]) for t in range(members)], axis=1)
    queries = rotate(queries, cos_table, sin_table).astype(bf16)
    mixed = attend_forward(first_row, queries, keys, values)
    part = width // members
    branch = sum(nt(mixed[:, t * part : (t + 1) * part], o_full[t]) for t in range(members))
    hidden = x + branch
    inverse_two, unit_two = rms_pieces(hidden)
    normed_two = (unit_two * gain_two).astype(bf16)
    rows_all = lax.all_gather(normed_two, "tensor", axis=0, tiled=True)

    sums = jnp.zeros((rows, 2 * width), f32)
    chunks = []
    for call in range(calls):
        some = slice(2 * CALL_PAIRS * call, 2 * CALL_PAIRS * (call + 1))
        columns = slice(2 * CALL_PAIRS * call, 2 * CALL_PAIRS * call + HD)
        grads, sums = expert_call(
            rank_cols[:, columns],
            routes[some],
            rows_all,
            grad_all,
            gathered[call],
            sums,
            False,
        )
        chunks.append(grads)
    shares = [
        unpack(lax.psum_scatter(grads[0], "dp", scatter_dimension=1, tiled=True).astype(f32)) for grads in chunks
    ]
    gate_out, up_out, down_out = (jnp.concatenate(parts, axis=1) for parts in zip(*shares))

    low_sums = sums.astype(bf16)
    normed_grad = lax.psum_scatter(low_sums[:, width:], "tensor", scatter_dimension=0, tiled=True).astype(f32)
    moe_own = lax.psum_scatter(low_sums[:, :width], "tensor", scatter_dimension=0, tiled=True).astype(f32)
    output = (hidden + moe_own).astype(bf16)

    back_two, gain_two_part = rms_backward(normed_grad, unit_two, inverse_two, gain_two)
    hidden_grad = cotangent + back_two
    hidden_low = hidden_grad.astype(bf16)
    mixed_grad = jnp.concatenate([nn(hidden_low, o_full[t]) for t in range(members)], axis=1).astype(bf16)
    o_part = jnp.stack([tn(hidden_low, mixed[:, t * part : (t + 1) * part]) for t in range(members)])
    dq, dk, dv = attend_backward(first_row, queries, keys, values, mixed_grad)
    kv_grad = lax.psum_scatter(
        jnp.concatenate([dk, dv], axis=1).astype(bf16), "tensor", scatter_dimension=0, tiled=True
    ).astype(f32)
    dq_low = rotate(dq, cos_table, -sin_table).astype(bf16)
    kv_low = jnp.concatenate(
        [rotate(kv_grad[:, :kv_width], cos_table, -sin_table), kv_grad[:, kv_width:]], axis=1
    ).astype(bf16)
    normed_one_grad = nt(kv_low, kv_full) + sum(
        nt(dq_low[:, t * part : (t + 1) * part], q_full[t]) for t in range(members)
    )
    back_one, gain_one_part = rms_backward(normed_one_grad, unit_one, inverse_one, gain_one)
    tokens_grad = hidden_grad + back_one
    q_part = jnp.stack([tn(normed_one, dq_low[:, t * part : (t + 1) * part]) for t in range(members)])
    kv_part = tn(normed_one, kv_low)

    def shared(values):
        summed = lax.psum_scatter(values.astype(bf16), "tensor", scatter_dimension=0, tiled=False)
        return lax.psum_scatter(summed, "dp", scatter_dimension=0, tiled=True).astype(f32)

    q_grad, o_grad = shared(q_part), shared(o_part)
    small = jnp.concatenate([kv_part, gain_one_part[:, None], gain_two_part[:, None]], axis=1)
    small = lax.psum_scatter(small, "dp", scatter_dimension=0, tiled=True)
    small = lax.psum(small.astype(bf16), "tensor").astype(f32)
    return (
        output,
        tokens_grad,
        small[:, 2 * kv_width],
        q_grad,
        small[:, :kv_width],
        small[:, kv_width : 2 * kv_width],
        o_grad,
        small[:, 2 * kv_width + 1],
        gate_out,
        up_out,
        down_out,
    )

def body_by_chips(
    tokens,
    expert_ids,
    route_weights,
    attn_gain,
    q_weight,
    k_weight,
    v_weight,
    o_weight,
    moe_gain,
    gate_weight,
    up_weight,
    down_weight,
    cotangent,
):
    members = lax.axis_size("tensor")
    member = lax.axis_index("tensor")
    devices = lax.axis_size("dp")
    own_rows, width = tokens.shape
    rows = own_rows * members
    calls = EXPERTS // 2 // CALL_PAIRS
    kv_width = k_weight.shape[1]

    gains = jnp.pad(jnp.stack([attn_gain, moe_gain], axis=1), ((0, 0), (0, HD - 2)))
    small = gather_small(
        q_weight,
        o_weight,
        k_weight,
        v_weight,
        gains,
        cotangent,
        expert_ids,
        route_weights,
        gate_weight,
        up_weight,
        down_weight,
        members,
        devices,
    )
    square_all, tall_all, grad_all = small[:3]
    rank_cols, routes, packed = (small[3 + calls * i : 3 + calls * (i + 1)] for i in range(3))
    near = [tuple(small[3 + 3 * calls :])]
    cosine, sine = doubled_tables(rows)
    normed_one, queries, kv_all, mixed, hidden, rows_all, sums, *landed = attention_front(
        tokens, square_all, tall_all, cosine, sine, packed[1:-1], near[0], members
    )
    far = [(landed[1], landed[0])]
    near += [tuple(landed[2 * i : 2 * i + 2]) for i in range(1, calls - 1)]
    cut = CALL_PAIRS // 2
    chunks, moved = [], []
    for call in range(calls):
        if call == 0:
            to_x = [from_y[cut:] for _, from_y in near[1:]] + [packed[-1]]
            to_y = [from_x[:cut] for from_x, _ in near[1:]] + [packed[-1]]
            got = flip(jnp.concatenate(to_x), 2), flip(jnp.concatenate(to_y), 4)
        elif call == 1:
            far += [tuple(side[cut * i : cut * (i + 1)] for side in got) for i in range(calls - 2)]
            near.append(tuple(side[cut * (calls - 2) :] for side in got))
            far.append((flip(near[-1][1][cut:], 2), flip(near[-1][0][:cut], 4)))
        (from_x, from_y), (second, first) = near[call], far[call]
        own = packed[call]
        grads, sums = expert_call(
            rank_cols[call],
            after(routes[call], moved[call - 2] if call >= 2 else ()),
            rows_all,
            grad_all,
            [
                [(own, 0), (from_x, 0), (from_y, 0), (first, 0)],
                [(own, cut), (from_x, cut), (from_y, cut), (second, 0)],
            ],
            sums,
            True,
        )
        chunks.append(grads)
        if call + 1 < calls:
            moved.append(scatter_step(grads, before_of(chunks, moved, call)))

    blocks, via_x, via_y = before_of(chunks, moved, calls - 1)
    to_x = jnp.concatenate([blocks[1, :cut], add(blocks[1, cut:], via_y)])
    to_y = jnp.concatenate([add(blocks[2, :cut], via_x), blocks[2, cut:]])
    tokens_grad, parts, x_before, y_before, x_last, y_last = attention_back(
        sums,
        cotangent,
        hidden,
        tokens,
        normed_one,
        queries,
        kv_all,
        mixed,
        square_all,
        tall_all,
        cosine,
        sine,
        chunks[-1],
        to_x,
        to_y,
        members,
    )
    output, square_grad, tall_grad = reduce_small(parts, sums, hidden, members, devices)
    gate_out, up_out, down_out = unpack_all(
        chunks,
        [got[0] for got in moved[1:]] + [x_before, x_last],
        [got[1] for got in moved[1:]] + [y_before, y_last],
    )
    part = width // members
    return (
        output,
        tokens_grad,
        tall_grad[:, 2 * kv_width],
        square_grad[:, :part],
        tall_grad[:, :kv_width],
        tall_grad[:, kv_width : 2 * kv_width],
        square_grad[:, part:],
        tall_grad[:, 2 * kv_width + 1],
        gate_out,
        up_out,
        down_out,
    )


def doubled_tables(rows):
    half = HD // 2
    frequency = np.float32(rope_base) ** -(np.arange(half, dtype=np.float32) * np.float32(2.0 / HD))
    angles = (np.arange(rows) % SEQ).astype(np.float32)[:, None] * frequency
    cosine, sine = np.cos(angles), np.sin(angles)
    return jnp.asarray(np.concatenate([cosine, cosine], axis=1)), jnp.asarray(np.concatenate([-sine, sine], axis=1))


def solution(mesh):
    rows = P(("dp", "tensor"), None)
    experts = P("dp", None, "tensor")
    square = P("dp", "tensor")
    tall = P("dp", None)
    return jax.shard_map(
        body_by_chips if mesh.shape["dp"] == 8 else body_anywhere,
        mesh=mesh,
        in_specs=(
            rows, tall, tall, P("dp"), square, tall, tall, square, P("dp"), experts, experts, experts, rows
        ),
        out_specs=(rows, rows, P("dp"), square, tall, tall, square, P("dp"), experts, experts, experts),
        check_vma=False,
    )
```

```python
import jax
import jax.numpy as jnp
import numpy as np
from jax import lax
from jax.experimental import pallas as pl
from jax.experimental.pallas import tpu as pltpu
from jax.sharding import PartitionSpec as P

KV = 2
HD = 128
EXPERTS = 32
TOPK = 4
SEQ = 1024
BLOCK = 256
CAP = 256
TAIL = 64
CALL_PAIRS = 4

eps = 1e-06
rope_base = 1000000.0
negative = -1e30
bf16 = jnp.bfloat16
f32 = jnp.float32


def nn(a, b):
    return jnp.dot(a, b, preferred_element_type=f32)


def nt(a, b):
    return lax.dot_general(a, b, (((1,), (1,)), ((), ())), preferred_element_type=f32)


def tn(a, b):
    return lax.dot_general(a, b, (((0,), (0,)), ((), ())), preferred_element_type=f32)


def rope_tables(positions):
    half = HD // 2
    frequency = rope_base ** (-(jnp.arange(half).astype(f32) * 2.0 / HD))
    angles = positions.astype(f32)[:, None] * frequency[None, :]
    return jnp.cos(angles), jnp.sin(angles)


def rotate(values, cos_table, sin_table):
    rows = values.shape[0]
    heads = values.reshape(rows, -1, 2, HD // 2)
    a, b = heads[:, :, 0], heads[:, :, 1]
    cos_table, sin_table = cos_table[:, None], sin_table[:, None]
    turned = jnp.stack([a * cos_table - b * sin_table, b * cos_table + a * sin_table], axis=2)
    return turned.reshape(rows, -1)


def rms_pieces(x):
    inverse = lax.rsqrt(jnp.mean(x * x, axis=-1, keepdims=True) + eps)
    return inverse, x * inverse


def rms_backward(grad, unit, inverse, gain):
    u = grad * gain
    back = inverse * (u - unit * jnp.mean(u * unit, axis=-1, keepdims=True))
    return back, jnp.sum(grad * unit, axis=0)


def probabilities(q, k, first_row):
    rows, keys = q.shape[0], k.shape[0]
    scores = nt(q, k) * (HD**-0.5)
    q_block = (first_row + lax.broadcasted_iota(jnp.int32, (rows, keys), 0)) // BLOCK
    k_block = lax.broadcasted_iota(jnp.int32, (rows, keys), 1) // BLOCK
    scores = jnp.where(k_block <= q_block, scores, negative)
    raised = jnp.exp(scores - jnp.max(scores, axis=-1, keepdims=True))
    return raised / jnp.sum(raised, axis=-1, keepdims=True)


def attend_forward(first_row, q, k, v):
    rows, width = q.shape
    heads = width // HD
    shared = heads // KV

    def kernel(first_ref, q_ref, k_ref, v_ref, o_ref):
        p = probabilities(q_ref[...], k_ref[...], first_ref[0]).astype(bf16)
        o_ref[...] = nn(p, v_ref[...]).astype(bf16)

    per_head = pl.BlockSpec((rows, HD), lambda h, f: (0, h))
    per_kv = pl.BlockSpec((k.shape[0], HD), lambda h, f: (0, h // shared))
    return pl.pallas_call(
        kernel,
        grid_spec=pltpu.PrefetchScalarGridSpec(
            num_scalar_prefetch=1,
            grid=(heads,),
            in_specs=[per_head, per_kv, per_kv],
            out_specs=per_head,
        ),
        out_shape=jax.ShapeDtypeStruct((rows, width), bf16),
        compiler_params=pltpu.CompilerParams(vmem_limit_bytes=32 * 2**20),
        cost_estimate=pl.CostEstimate(
            flops=4 * rows * width * k.shape[0],
            bytes_accessed=4 * rows * width,
            transcendentals=rows * heads * k.shape[0],
        ),
        name="attend",
    )(first_row, q, k, v)


def attend_backward(first_row, q, k, v, do):
    rows, width = q.shape
    keys = k.shape[0]
    heads = width // HD
    shared = heads // KV

    def kernel(first_ref, q_ref, k_ref, v_ref, do_ref, dq_ref, dk_ref, dv_ref):
        q_now, k_now, v_now, do_now = q_ref[...], k_ref[...], v_ref[...], do_ref[...]
        p = probabilities(q_now, k_now, first_ref[0])
        dp = nt(do_now, v_now)
        ds = (p * (dp - jnp.sum(p * dp, axis=-1, keepdims=True))).astype(bf16)
        dq_ref[...] = nn(ds, k_now) * (HD**-0.5)
        dk = tn(ds, q_now) * (HD**-0.5)
        dv = tn(p.astype(bf16), do_now)
        head = pl.program_id(0)

        @pl.when(lax.rem(head, shared) == 0)
        def _():
            dk_ref[...] = dk
            dv_ref[...] = dv

        @pl.when(lax.rem(head, shared) != 0)
        def _():
            dk_ref[...] += dk
            dv_ref[...] += dv

    per_head = pl.BlockSpec((rows, HD), lambda h, f: (0, h))
    per_kv = pl.BlockSpec((keys, HD), lambda h, f: (0, h // shared))
    return pl.pallas_call(
        kernel,
        grid_spec=pltpu.PrefetchScalarGridSpec(
            num_scalar_prefetch=1,
            grid=(heads,),
            in_specs=[per_head, per_kv, per_kv, per_head],
            out_specs=[per_head, per_kv, per_kv],
        ),
        out_shape=[
            jax.ShapeDtypeStruct((rows, width), f32),
            jax.ShapeDtypeStruct((keys, KV * HD), f32),
            jax.ShapeDtypeStruct((keys, KV * HD), f32),
        ],
        compiler_params=pltpu.CompilerParams(vmem_limit_bytes=32 * 2**20),
        cost_estimate=pl.CostEstimate(
            flops=10 * rows * width * keys,
            bytes_accessed=8 * rows * width,
            transcendentals=rows * heads * keys,
        ),
        name="attend_back",
    )(first_row, q, k, v, do)


def sibling():
    me = lax.axis_index("dp")
    return me + 1 - 2 * lax.rem(me, 2)


def pair_of_experts(expert, place, w, rank_c, routes_ref, x_ref, gy_ref, y_buf, pick_buf, put):
    rows, width = x_ref.shape
    lanes = w.shape[1]
    third = lanes // 3
    low_half = lax.broadcasted_iota(jnp.int32, (CAP, HD), 1) < TAIL
    slot_of = lax.broadcasted_iota(jnp.int32, (rows, CAP), 1).astype(f32)
    slot_at = lax.broadcasted_iota(jnp.int32, (CAP, rows), 0).astype(f32)
    gate_up = [slice(q * third, (q + 1) * third) for q in range(2)]
    down = [slice(2 * third + q * HD, 2 * third + (q + 2) * HD) for q in range(2)]

    def place_of(q):
        return pl.ds(pl.multiple_of((place + q) * CAP, CAP), CAP)

    def rows_of(q):
        hit = slot_at == routes_ref[q, 0:1]
        weight = jnp.sum(jnp.where(hit, routes_ref[q, 1:2], 0.0), axis=1, keepdims=True)
        pick = hit.astype(bf16)
        return nn(pick, x_ref[...]).astype(bf16), (nn(pick, gy_ref[...]) * weight).astype(bf16), weight

    def picked(q):
        column = (lax.broadcasted_iota(jnp.int32, (HD, CAP), 0) == expert + q).astype(bf16)
        pick_buf[:, place_of(q)] = (nn(rank_c[...], column) == slot_of).astype(bf16)

    def unit(gate, up, dact):
        sig = jax.nn.sigmoid(gate)
        silu = gate * sig
        return silu * up, dact * up * sig * (1.0 + gate * (1.0 - sig)), dact * silu

    def middle(q, gu, dact):
        tail = gu[:, 2 * HD :]
        if q == 0:
            d0, d1 = dact[:, :HD], dact[:, HD:]
        else:
            d0, d1 = dact[:, HD:], pltpu.roll(dact[:, :HD], TAIL, 1)
        a0, dg0, du0 = unit(gu[:, :HD], gu[:, HD : 2 * HD], d0)
        a1, dg1, du1 = unit(tail, pltpu.roll(tail, TAIL, 1), d1)
        a1 = jnp.where(low_half, a1, 0.0)
        dgu1 = jnp.where(low_half, dg1, pltpu.roll(du1, TAIL, 1))
        act = [a0, a1] if q == 0 else [pltpu.roll(a1, TAIL, 1), a0]
        act = jnp.concatenate([part.astype(bf16) for part in act], axis=1)
        return act, jnp.concatenate([part.astype(bf16) for part in (dg0, du0, dgu1)], axis=1)

    def ends(q, xe, deo, weight, act, dgu):
        y_buf[place_of(q), :width] = (nt(act, w[:, down[q]]) * weight).astype(bf16)
        y_buf[place_of(q), width:] = nt(dgu, w[:, gate_up[q]]).astype(bf16)
        put(q * third, tn(xe, dgu))
        grad = tn(deo, act)
        put(2 * third + 2 * q * HD, grad[:, :HD] if q == 0 else grad[:, HD:])
        return grad[:, HD:] if q == 0 else grad[:, :HD]

    xe0, deo0, weight0 = rows_of(0)
    first = nn(xe0, w[:, gate_up[0]]), nn(deo0, w[:, down[0]])
    xe1, deo1, weight1 = rows_of(1)
    act0, dgu0 = middle(0, *first)
    second = nn(xe1, w[:, gate_up[1]]), nn(deo1, w[:, down[1]])
    picked(0)
    tail0 = ends(0, xe0, deo0, weight0, act0, dgu0)
    act1, dgu1 = middle(1, *second)
    picked(1)
    tail1 = ends(1, xe1, deo1, weight1, act1, dgu1)
    put(2 * third + HD, tail0 + tail1)


def expert_call(rank_cols, routes, x, gy, weights, sums):
    rows, width = x.shape
    pairs, _, lanes = weights.shape
    blocks = 6
    tile = 2 * width // blocks

    def kernel(rank_c, routes_ref, x_ref, gy_ref, w_ref, sums_in, grad_out, sums_out, y_buf, pick_buf):
        step = pl.program_id(0)

        def put(at, value):
            grad_out[0, :, at : at + value.shape[1]] = value.astype(bf16)

        @pl.when(step < pairs)
        def _():
            pair_of_experts(2 * step, 2 * step, w_ref.at[0], rank_c, routes_ref, x_ref, gy_ref, y_buf, pick_buf, put)

        @pl.when(step >= pairs)
        def _():
            at = pl.ds(pl.multiple_of((step - pairs) * tile, tile), tile)
            sums_out[...] = sums_in[...] + nn(pick_buf[...], y_buf[:, at])

    def held(step):
        return jnp.minimum(step, pairs - 1)

    def block(step):
        return (0, jnp.maximum(step - pairs, 0))

    once = pl.Buffered(1)
    whole = pl.BlockSpec((rows, width), lambda s: (0, 0), pipeline_mode=once)
    of_pair = pl.BlockSpec((1, width, lanes), lambda s: (held(s), 0, 0))
    return pl.pallas_call(
        kernel,
        grid=(pairs + blocks,),
        in_specs=[
            pl.BlockSpec((rows, HD), lambda s: (0, 0), pipeline_mode=once),
            pl.BlockSpec((2, 2, rows), lambda s: (held(s), 0, 0)),
            whole,
            whole,
            of_pair,
            pl.BlockSpec((rows, tile), block),
        ],
        out_specs=[of_pair, pl.BlockSpec((rows, tile), block)],
        scratch_shapes=[pltpu.VMEM((2 * pairs * CAP, 2 * width), bf16), pltpu.VMEM((rows, 2 * pairs * CAP), bf16)],
        out_shape=[
            jax.ShapeDtypeStruct((pairs, width, lanes), bf16),
            jax.ShapeDtypeStruct((rows, 2 * width), f32),
        ],
        compiler_params=pltpu.CompilerParams(vmem_limit_bytes=62 * 10**6),
        name="experts",
    )(rank_cols, routes, x, gy, weights, sums)


def expert_pass(rank_cols, routes, x, gy, packed, near, far, members):
    rows, width = x.shape
    calls = len(packed)
    size, height, lanes = packed[0].shape
    half = size // 2
    pairs = calls * size
    blocks = 6
    tile = 2 * width // blocks
    period = size + blocks
    early = calls - 1
    dma = pltpu.SemaphoreType.DMA
    n_in = 4 + calls + 2 * early + 2

    def kernel(*refs):
        rank_c, routes_ref, x_ref, gy_ref = refs[:4]
        own = refs[4 : 4 + calls]
        near_in = refs[4 + calls : 4 + calls + 2 * early]
        far_in = refs[n_in - 2 : n_in]
        outs = refs[n_in:]
        sums_out, grads, x_last, y_last = outs[:4]
        far_out = outs[4 : 4 + 2 * early]
        plain_x, plain_y, added_x, added_y, via_x, via_y = outs[4 + 2 * early : 10 + 2 * early]
        scratch = outs[10 + 2 * early :]
        w_buf, y_buf, pick_buf, total, kept, leaving, arriving, load_buf, add_buf = scratch[:9]
        local_sem, push_sem, pull_sem, send_sem, recv_sem, keep_sem, load_sem, add_sem = scratch[9:17]
        chip_send, chip_recv, cross_send, cross_recv, straight_send, straight_recv, w_free, g_free = scratch[17:]
        step = pl.program_id(0)
        call, phase = step // period, lax.rem(step, period)
        pair = call * size + phase
        x_side, y_side = chip_neighbours()
        other = {"dp": sibling()}
        near_x = [near_in[2 * i] for i in range(early)] + [x_last]
        near_y = [near_in[2 * i + 1] for i in range(early)] + [y_last]
        far_all = [far_in, *(far_out[2 * i : 2 * i + 2] for i in range(early))]

        def chip(index, source, target, device):
            return remote(source, target, chip_send.at[index], chip_recv.at[index], {"dp": device})

        forward = []
        for i in range(early):
            forward.append(chip(2 * i, near_x[i + 1].at[:half], far_out[2 * i], y_side))
            forward.append(chip(2 * i + 1, near_y[i + 1].at[half:], far_out[2 * i + 1], x_side))
        fresh = [
            chip(2 * early, own[-1], x_last, x_side),
            chip(2 * early + 1, own[-1], y_last, y_side),
        ]

        def weights(now, slot, sub):
            chunk, side = sub // 2, sub % 2
            sources = [own[chunk], near_x[chunk], near_y[chunk], far_all[chunk][side]]
            begins = [chunk * size] * 3 + [chunk * size + side * half]
            found = []
            for k, (source, begin) in enumerate(zip(sources, begins)):
                source = source.at[now - begin]
                mine = w_buf.at[slot, pl.ds(2 * k * height, height)]
                found.append(pltpu.make_async_copy(source, mine, local_sem.at[slot, k]))
                theirs = w_buf.at[slot, pl.ds((2 * k + 1) * height, height)]
                found.append(remote(source, theirs, push_sem.at[slot, k], pull_sem.at[slot, k], other))
            return found

        def start(now):
            slot = lax.rem(now, 2)
            for sub in range(2 * calls):

                @pl.when((now >= sub * half) & (now < (sub + 1) * half))
                def _():
                    if sub >= 2:

                        @pl.when(now == sub * half)
                        def _():
                            forward[sub - 2].wait_recv()

                    for copy in weights(now, slot, sub):
                        copy.start()

        def leave(slot):
            return remote(leaving.at[slot], arriving.at[slot], send_sem.at[slot], recv_sem.at[slot], other)

        def keep(now):
            slot = lax.rem(now, 2)
            return pltpu.make_async_copy(kept.at[slot], grads.at[:, now], keep_sem.at[slot])

        def crossing(now, first):
            at = now // size * half + lax.rem(now, size) - (0 if first else half)
            sems = cross_send.at[now], cross_recv.at[now]
            if first:
                return remote(grads.at[3, now], via_x.at[at], *sems, {"dp": x_side})
            return remote(grads.at[3, now], via_y.at[at], *sems, {"dp": y_side})

        def straight(now, first):
            at = now // size * half + lax.rem(now, size) - (0 if first else half)
            sems = straight_send.at[now], straight_recv.at[now]
            if first:
                return remote(grads.at[1, now], plain_x.at[at], *sems, {"dp": x_side})
            return remote(grads.at[2, now], plain_y.at[at], *sems, {"dp": y_side})

        def by_half(now, do):
            for first in (True, False):

                @pl.when((lax.rem(now, size) < half) if first else (lax.rem(now, size) >= half))
                def _():
                    do(first)

        def scatter(now):
            def both(first):
                crossing(now, first).start()
                straight(now, first).start()

            by_half(now, both)

        def finish(now):
            slot = lax.rem(now, 2)
            leave(slot).wait()
            for k in range(4):
                kept[slot, k] = (kept[slot, k].astype(f32) + arriving[slot, k].astype(f32)).astype(bf16)
            keep(now).start()

        def signal(sem):
            pl.semaphore_signal(sem, inc=1, device_id=other, device_id_type=pl.DeviceIdType.MESH)

        def put(at, value):
            slot = lax.rem(pair, 2)
            for k in range(4):
                for parity, target in enumerate((kept, leaving)):
                    row = (2 * k + parity) * height
                    target[slot, k, :, at : at + value.shape[1]] = value[row : row + height].astype(bf16)

        def loads(now):
            at = now // size * half + lax.rem(now, half)

            def copies(first):
                via, block = (via_x, 2) if first else (via_y, 1)
                return (
                    pltpu.make_async_copy(via.at[at], load_buf.at[0], load_sem.at[0]),
                    pltpu.make_async_copy(grads.at[block, now], load_buf.at[1], load_sem.at[1]),
                )

            return copies

        def stores(now, first):
            at = now // size * half + lax.rem(now, half)
            return pltpu.make_async_copy(add_buf, (added_y if first else added_x).at[at], add_sem)

        @pl.when(step == 0)
        def _():
            barrier = pltpu.get_barrier_semaphore()
            for device in (x_side, y_side, sibling()):
                pl.semaphore_signal(barrier, inc=1, device_id={"dp": device}, device_id_type=pl.DeviceIdType.MESH)
            pl.semaphore_wait(barrier, 3)
            start(step)
            for copy in (*forward[:2], *fresh, *forward[2 : 2 * early - 2]):
                copy.start()

        @pl.when(phase < size)
        def _():
            @pl.when((pair >= 1) & (pair + 1 < pairs))
            def _():
                signal(w_free)
                pl.semaphore_wait(w_free, 1)

            @pl.when(pair == size + 1)
            def _():
                for copy in fresh:
                    copy.wait_recv()
                for copy in forward[2 * early - 2 :]:
                    copy.start()

            @pl.when(pair + 1 < pairs)
            def _():
                start(pair + 1)

            @pl.when(pair >= 2)
            def _():
                keep(pair - 2).wait()

            @pl.when((pair >= 2) & (pair - 2 < early * size))
            def _():
                scatter(pair - 2)

            slot = lax.rem(pair, 2)
            for copy in weights(0, slot, 0):
                copy.wait()
            pair_of_experts(
                2 * pair, 2 * phase, w_buf.at[slot], rank_c, routes_ref, x_ref, gy_ref, y_buf, pick_buf, put
            )

        @pl.when((phase >= 1) & (phase <= size))
        def _():
            finish(pair - 1)

            @pl.when(pair + 1 < pairs)
            def _():
                signal(g_free)

        @pl.when(phase < size)
        def _():
            @pl.when(pair >= 2)
            def _():
                pl.semaphore_wait(g_free, 1)

            leave(lax.rem(pair, 2)).start()

        @pl.when(phase >= size)
        def _():
            block = phase - size
            at = pl.ds(pl.multiple_of(block * tile, tile), tile)
            made = nn(pick_buf[...], y_buf[:, at])

            @pl.when(call == 0)
            def _():
                total[:, at] = made.astype(bf16)

            @pl.when((call > 0) & (call < calls - 1))
            def _():
                total[:, at] = (made + total[:, at].astype(f32)).astype(bf16)

            @pl.when(call == calls - 1)
            def _():
                sums_out[...] = (made + total[:, at].astype(f32)).astype(bf16)

            before = (call - 1) * size + block

            @pl.when((call > 0) & (block >= 2) & (block < size + 2))
            def _():
                by_half(before - 2, lambda first: stores(before - 2, first).wait())

            @pl.when((call > 0) & (block >= 1) & (block < size + 1))
            def _():
                def add_to(first):
                    for copy in loads(before - 1)(first):
                        copy.wait()
                    add_buf[...] = (load_buf[0].astype(f32) + load_buf[1].astype(f32)).astype(bf16)
                    stores(before - 1, first).start()

                by_half(before - 1, add_to)

            @pl.when((call > 0) & (block < size))
            def _():
                def load(first):
                    crossing(before, first).wait_recv()
                    for copy in loads(before)(first):
                        copy.start()

                by_half(before, load)

        @pl.when(step == calls * period - 1)
        def _():
            for now in (pairs - 2, pairs - 1):
                keep(now).wait()
            for copy in (*forward, *fresh):
                copy.wait_send()
            for now in range(early * size):
                first = now % size < half
                crossing(now, first).wait_send()
                straight(now, first).wait()

    def held(step):
        return step // period * size + jnp.minimum(lax.rem(step, period), size - 1)

    def block(step):
        return (0, jnp.where(step >= (calls - 1) * period + size, step - (calls - 1) * period - size, 0))

    once = pl.Buffered(1)
    whole = pl.BlockSpec((rows, width), lambda s: (0, 0), pipeline_mode=once)
    anywhere = pl.BlockSpec(memory_space=pl.ANY)
    some = jax.ShapeDtypeStruct((early * half, height, lanes), bf16)
    regular = pltpu.SemaphoreType.REGULAR
    return pl.pallas_call(
        kernel,
        grid=(calls * period,),
        in_specs=[
            pl.BlockSpec((rows, HD), lambda s: (0, 0), pipeline_mode=once),
            pl.BlockSpec((2, 2, rows), lambda s: (held(s), 0, 0)),
            whole,
            whole,
        ]
        + [anywhere] * (n_in - 4),
        out_specs=[pl.BlockSpec((rows, tile), block)] + [anywhere] * (9 + 2 * early),
        out_shape=[
            jax.ShapeDtypeStruct((rows, 2 * width), bf16),
            jax.ShapeDtypeStruct((4, pairs, height, lanes), bf16),
        ]
        + [jax.ShapeDtypeStruct((size, height, lanes), bf16)] * 2
        + [jax.ShapeDtypeStruct((half, height, lanes), bf16)] * (2 * early)
        + [some] * 6,
        scratch_shapes=[
            pltpu.VMEM((2, width, lanes), bf16),
            pltpu.VMEM((2 * size * CAP, 2 * width), bf16),
            pltpu.VMEM((rows, 2 * size * CAP), bf16),
            pltpu.VMEM((rows, 2 * width), bf16),
            pltpu.VMEM((2, 4, height, lanes), bf16),
            pltpu.VMEM((2, 4, height, lanes), bf16),
            pltpu.VMEM((2, 4, height, lanes), bf16),
            pltpu.VMEM((2, height, lanes), bf16),
            pltpu.VMEM((height, lanes), bf16),
            dma((2, 4)),
            dma((2, 4)),
            dma((2, 4)),
            dma((2,)),
            dma((2,)),
            dma((2,)),
            dma((2,)),
            dma,
            dma((2 * early + 2,)),
            dma((2 * early + 2,)),
            dma((early * size,)),
            dma((early * size,)),
            dma((early * size,)),
            dma((early * size,)),
            regular,
            regular,
        ],
        compiler_params=pltpu.CompilerParams(
            vmem_limit_bytes=62 * 10**6, collective_id=1, has_side_effects=True
        ),
        cost_estimate=pl.CostEstimate(flops=2 * 10**11, bytes_accessed=10**8, transcendentals=0),
        name="experts",
    )(rank_cols, routes, x, gy, *packed, *(side for both in near for side in both), *far)


def remote(source, target, send_sem, recv_sem, device):
    return pltpu.make_async_remote_copy(
        src_ref=source,
        dst_ref=target,
        send_sem=send_sem,
        recv_sem=recv_sem,
        device_id=device,
        device_id_type=pl.DeviceIdType.MESH,
    )


def chip_neighbours():
    me = lax.axis_index("dp")
    return me + 2 - 4 * lax.rem(me // 2, 2), me + 4 - 8 * lax.rem(me // 4, 2)


def meet(members, core):
    barrier = pltpu.get_barrier_semaphore()
    z = lax.axis_index("tensor")

    def signal(device):
        pl.semaphore_signal(barrier, inc=1, device_id=device, device_id_type=pl.DeviceIdType.MESH)

    @pl.when(z > 0)
    def _():
        signal({"tensor": z - 1})

    @pl.when(z < members - 1)
    def _():
        signal({"tensor": z + 1})

    for other in (*chip_neighbours(), *([sibling()] if core else [])):
        signal({"dp": other})
    inner = jnp.where((z > 0) & (z < members - 1), 1, 0)
    pl.semaphore_wait(barrier, 3 + inner + (1 if core else 0))


class LineGather:
    def __init__(self, members, at, send, recv):
        self.members, self.at, self.send, self.recv = members, at, send, recv

    def copies(self, hop):
        z, last = lax.axis_index("tensor"), self.members - 1
        up, down = z - hop + 1, z + hop - 1

        def copy(block, way, device):
            return lambda: remote(
                self.at(block), self.at(block), self.send.at[way, hop - 1], self.recv.at[way, hop - 1], {"tensor": device}
            )

        return (
            ((up >= 0) & (z < last), copy(up, 0, z + 1)),
            ((down <= last) & (z > 0), copy(down, 1, z - 1)),
        ), (
            (z - hop >= 0, copy(z - hop, 0, z)),
            (z + hop <= last, copy(z + hop, 1, z)),
        )

    def start(self, hop):
        for present, copy in self.copies(hop)[0]:

            @pl.when(present)
            def _():
                copy().start()

    def arrive(self, hop):
        for present, copy in self.copies(hop)[1]:

            @pl.when(present)
            def _():
                copy().wait_recv()

    def close(self):
        for hop in range(1, self.members):
            for present, copy in self.copies(hop)[0]:

                @pl.when(present)
                def _():
                    copy().wait_send()


class LineSum:
    def __init__(self, members, part, leaving, arriving, send, recv):
        self.members, self.part, self.leaving, self.arriving = members, part, leaving, arriving
        self.send, self.recv = send, recv

    def copy(self, way, hop, device):
        return remote(
            self.leaving.at[way],
            self.arriving.at[way, hop - 1],
            self.send.at[way, hop - 1],
            self.recv.at[way, hop - 1],
            {"tensor": device},
        )

    def ways(self, hop):
        z, last = lax.axis_index("tensor"), self.members - 1
        return (
            (0, z - hop >= 0, z - hop, z < last, z - 1, (z < last) & (z + 1 - hop >= 0)),
            (1, z + hop <= last, z + hop, z > 0, z + 1, (z > 0) & (z - 1 + hop <= last)),
        )

    def start(self, hop):
        if hop + 1 < self.members:
            self.leave(hop + 1)
        for way, present, block, behind, device, _ in self.ways(hop):

            @pl.when(present)
            def _():
                self.leaving[way] = self.part(block).astype(bf16)

            if hop + 1 < self.members:

                @pl.when(present & behind)
                def _():
                    both = self.part(block).astype(f32) + self.arriving[way, hop].astype(f32)
                    self.leaving[way] = both.astype(bf16)

            @pl.when(present)
            def _():
                self.copy(way, hop, device).start()

    def arrive(self, hop):
        for way, _, _, _, device, present in self.ways(hop):

            @pl.when(present)
            def _():
                self.copy(way, hop, device).wait_recv()

    def total(self, out):
        z, last = lax.axis_index("tensor"), self.members - 1
        out[...] = self.part(z).astype(f32)
        for way, present in ((0, z < last), (1, z > 0)):

            @pl.when(present)
            def _():
                out[...] += self.arriving[way, 0].astype(f32)

    def leave(self, hop):
        for way, present, _, _, device, _ in self.ways(hop):

            @pl.when(present)
            def _():
                self.copy(way, hop, device).wait_send()

    def close(self):
        self.leave(1)


def swap_blocks(values):
    me = lax.axis_index("dp")
    chip = values.shape[1] // 4
    four = [values[:, i * chip : (i + 1) * chip] for i in range(4)]
    y_side, x_side, core_side = lax.rem(me // 4, 2) == 1, lax.rem(me // 2, 2) == 1, lax.rem(me, 2) == 1
    four = [jnp.where(y_side, four[i ^ 2], four[i]) for i in range(4)]
    four = [jnp.where(x_side, four[i ^ 1], four[i]) for i in range(4)]
    four = [jnp.where(core_side, pltpu.roll(part, chip // 2, 1), part) for part in four]
    return jnp.concatenate(four, axis=1)


def in_vmem(count):
    return [pl.BlockSpec(memory_space=pltpu.VMEM)] * count


def pack_chunk(gate, up, down, begin):
    gate, up, down = (
        jnp.swapaxes(w[:, begin : begin + 2 * CALL_PAIRS, :], 0, 1) for w in (gate, up, down)
    )

    def pair(a, b):
        return [a[:, :HD], b[:, :HD], jnp.concatenate([a[:, HD:], b[:, HD:]], axis=1)]

    def inner(a, b):
        a, b, tails = pair(a, b)
        return [a, tails, b]

    return [
        jnp.concatenate(
            pair(gate[e], up[e]) + pair(gate[e + 1], up[e + 1]) + inner(down[e], down[e + 1]), axis=1
        )
        for e in range(0, 2 * CALL_PAIRS, 2)
    ]


def gather_small(
    q_weight, o_weight, k_weight, v_weight, gains, cotangent, ids, route_weights, gate, up, down, members, devices
):
    height, part = q_weight.shape
    own_rows, width = cotangent.shape
    rows = own_rows * members
    kv = k_weight.shape[1]
    tall = 2 * kv + HD
    lanes = 9 * HD
    calls = EXPERTS // 2 // CALL_PAIRS
    dma = pltpu.SemaphoreType.DMA
    cut = part

    def kernel(*refs):
        q_ref, o_ref, k_ref, v_ref, gains_ref, cot_ref, ids_ref, weights_ref, gate_ref, up_ref, down_ref = refs[:11]
        square_all, tall_all, grad_all = refs[11:14]
        rank_cols, routes = refs[14:16]
        packed = refs[16 : 16 + calls]
        from_x, from_y = refs[16 + calls : 18 + calls]
        sems = refs[18 + calls :]
        line_send, line_recv, grad_send, grad_recv, chip_send, chip_recv, core_send, core_recv = sems
        me, z = lax.axis_index("dp"), lax.axis_index("tensor")
        x_side, y_side = chip_neighbours()
        core = sibling()

        def rows_of(device):
            return pl.ds(pl.multiple_of(device * height, 16), height)

        def pack(call):
            chunk = pack_chunk(gate_ref, up_ref, down_ref, 2 * CALL_PAIRS * call)
            for pair, value in enumerate(chunk):
                packed[call][pair] = value

        def chip(index, source, device, target=None):
            target = source if target is None else target
            return remote(source, target, chip_send.at[index], chip_recv.at[index], {"dp": device})

        def across(index, source):
            return remote(source, source, core_send.at[index], core_recv.at[index], {"dp": core})

        def tall_at(device):
            return tall_all.at[rows_of(device)]

        def square_at(device, half=None):
            span = slice(None) if half is None else slice(half * cut, (half + 1) * cut)
            return square_all.at[:, rows_of(device), span]

        square_all[z, rows_of(me), :part] = q_ref[...]
        square_all[z, rows_of(me), part:] = o_ref[...]
        tall_all[rows_of(me), :kv] = k_ref[...]
        tall_all[rows_of(me), kv : 2 * kv] = v_ref[...]
        tall_all[rows_of(me), 2 * kv :] = gains_ref[...]
        line = LineGather(members, lambda block: square_all.at[block, rows_of(me)], line_send, line_recv)
        group = LineGather(
            members,
            lambda block: grad_all.at[pl.ds(pl.multiple_of(block * own_rows, 16), own_rows)],
            grad_send,
            grad_recv,
        )
        meet(members, True)
        line.start(1)
        near = [chip(0, tall_at(me), x_side), chip(1, tall_at(me), y_side)]
        for copy in near:
            copy.start()
        pack(0)
        chunk = [chip(7, packed[0], x_side, from_x), chip(8, packed[0], y_side, from_y)]
        for copy in chunk:
            copy.start()
        grad_all[pl.ds(pl.multiple_of(z * own_rows, 16), own_rows), :] = swap_blocks(cot_ref[...]).astype(bf16)
        for hop in range(1, members):
            line.arrive(hop)
            if hop + 1 < members:
                line.start(hop + 1)
        near += [chip(2, square_at(me), x_side), chip(3, square_at(me), y_side)]
        for copy in near[2:]:
            copy.start()
        group.start(1)
        trades = [across(0, tall_at(me)), across(1, square_at(me))]
        for copy in trades:
            copy.start()
        chip(0, tall_at(x_side), x_side).wait_recv()
        chip(1, tall_at(y_side), y_side).wait_recv()
        diagonal = x_side + y_side - me
        far = [chip(4, tall_at(x_side), y_side)]
        far[0].start()
        trades += [across(2, tall_at(x_side)), across(3, tall_at(y_side))]
        for copy in trades[2:]:
            copy.start()

        expert = lax.broadcasted_iota(jnp.int32, (HD, rows), 0)
        weight = jnp.zeros((HD, rows), f32)
        named = jnp.zeros((HD, rows), f32)
        for route in range(ids_ref.shape[0]):
            here = ids_ref[route : route + 1, :] == expert
            named = jnp.where(here, 1.0, named)
            weight = jnp.where(here, weights_ref[route : route + 1, :], weight)
        row = lax.broadcasted_iota(jnp.int32, (rows, rows), 0)
        later = (row < lax.broadcasted_iota(jnp.int32, (rows, rows), 1)).astype(bf16)
        rank = jnp.where(named > 0.0, nn(named.astype(bf16), later), -1.0)
        rank_cols[...] = jnp.transpose(rank).astype(bf16)
        for e in range(EXPERTS):
            routes[e, 0:1, :] = rank[e : e + 1]
            routes[e, 1:2, :] = weight[e : e + 1]
        for call in range(1, calls):
            pack(call)

        group.arrive(1)
        if members > 2:
            group.start(2)
        chip(2, square_at(x_side), x_side).wait_recv()
        chip(3, square_at(y_side), y_side).wait_recv()
        far += [chip(5, square_at(x_side, 0), y_side), chip(6, square_at(y_side, 1), x_side)]
        for copy in far[1:]:
            copy.start()
        trades += [across(4, square_at(x_side)), across(5, square_at(y_side))]
        for copy in trades[4:]:
            copy.start()
        chip(4, tall_at(diagonal), y_side).wait_recv()
        trades.append(across(6, tall_at(diagonal)))
        trades[-1].start()
        for hop in range(2, members - 1):
            group.arrive(hop)
            group.start(hop + 1)
        chip(5, square_at(diagonal, 0), y_side).wait_recv()
        chip(6, square_at(diagonal, 1), x_side).wait_recv()
        trades.append(across(7, square_at(diagonal)))
        trades[-1].start()
        theirs = [core, core, x_side, y_side, x_side, y_side, diagonal, diagonal]
        for index, device in enumerate(theirs):
            there = device if index < 2 else device + core - me
            source = square_at(there) if index in (1, 4, 5, 7) else tall_at(there)
            across(index, source).wait_recv()
        if members > 2:
            group.arrive(members - 1)
        for copy in chunk:
            copy.wait()
        for copy in near + far + trades:
            copy.wait_send()
        line.close()
        group.close()

    chunk_shape = jax.ShapeDtypeStruct((CALL_PAIRS, height, lanes), bf16)
    return pl.pallas_call(
        kernel,
        in_specs=in_vmem(11),
        out_specs=in_vmem(5 + calls) + [pl.BlockSpec(memory_space=pl.ANY)] * 2,
        out_shape=[
            jax.ShapeDtypeStruct((members, devices * height, 2 * part), bf16),
            jax.ShapeDtypeStruct((devices * height, tall), bf16),
            jax.ShapeDtypeStruct((rows, width), bf16),
        ]
        + [jax.ShapeDtypeStruct((rows, HD), bf16), jax.ShapeDtypeStruct((EXPERTS, 2, rows), f32)]
        + [chunk_shape] * (calls + 2),
        scratch_shapes=[dma((2, members - 1))] * 4 + [dma((9,))] * 2 + [dma((8,))] * 2,
        compiler_params=pltpu.CompilerParams(collective_id=2, has_side_effects=True, vmem_limit_bytes=56 * 2**20),
        cost_estimate=pl.CostEstimate(flops=8 * 10**10, bytes_accessed=10**7, transcendentals=0),
        name="gather_small",
    )(q_weight, o_weight, k_weight, v_weight, gains, cotangent, ids, route_weights, gate, up, down)


def turn(values, cosine, sine):
    return values * cosine + pltpu.roll(values, HD // 2, 1) * sine


def gain_rows(tall_ref, kv):
    return jnp.transpose(tall_ref[:, kv:].astype(f32))


def attention_front(tokens, square, tall, cosine, sine, packed, near, members):
    own_rows, width = tokens.shape
    rows = own_rows * members
    kv = 2 * KV * HD
    heads = width // HD
    per_kv = heads // KV
    part = width // members
    dma = pltpu.SemaphoreType.DMA

    def kernel(x_ref, square_ref, tall_ref, cos_ref, sin_ref, *rest):
        chunks, rest = rest[:count], rest[count:]
        normed_ref, q_ref, kv_all, mixed_ref, hidden_ref, rows_all = rest[:6]
        landed, rest = rest[6 : 4 + 2 * count], rest[4 + 2 * count :]
        kv_send, kv_recv, row_send, row_recv, chip_send, chip_recv = rest
        z = lax.axis_index("tensor")
        x_side, y_side = chip_neighbours()
        meet(members, False)
        pairs = chunks[0].shape[0]
        first, second = slice(0, pairs // 2), slice(pairs // 2, pairs)
        moves = [(chunks[0].at[first], y_side), (chunks[1].at[second], x_side)]
        for chunk in chunks[2:]:
            moves += [(chunk, x_side), (chunk, y_side)]
        moves = [
            remote(source, landed[i], chip_send.at[i], chip_recv.at[i], {"dp": device})
            for i, (source, device) in enumerate(moves)
        ]
        for copy in moves:
            copy.start()
        def block_of(ref):
            return lambda block: ref.at[pl.ds(pl.multiple_of(block * own_rows, 16), own_rows)]

        own = pl.ds(pl.multiple_of(z * own_rows, 16), own_rows)
        kv_line = LineGather(members, block_of(kv_all), kv_send, kv_recv)
        row_line = LineGather(members, block_of(rows_all), row_send, row_recv)
        gains = gain_rows(tall_ref, kv)
        x = x_ref[...].astype(f32)
        normed_ref[...] = (rms_pieces(x)[1] * gains[0:1]).astype(bf16)
        cosine, sine = cos_ref[own], sin_ref[own]
        made = nn(normed_ref[...], tall_ref[:, :kv])
        for head in range(KV):
            span = slice(head * HD, (head + 1) * HD)
            kv_all[own, span] = turn(made[:, span], cosine, sine).astype(bf16)
        kv_all[own, KV * HD :] = made[:, KV * HD :].astype(bf16)
        kv_line.start(1)
        for t in range(members):
            made = nn(normed_ref[...], square_ref[t, :, :part])
            for head in range(part // HD):
                span = slice(head * HD, (head + 1) * HD)
                q_ref[:, t * part + head * HD : t * part + (head + 1) * HD] = turn(
                    made[:, span], cosine, sine
                ).astype(bf16)
            if 1 <= t + 1 < members:
                kv_line.arrive(t + 1)
                if t + 2 < members:
                    kv_line.start(t + 2)
        first_row = z * own_rows

        @pl.loop(0, heads)
        def _(head):
            span = pl.ds(pl.multiple_of(head * HD, HD), HD)
            key_span = pl.ds(pl.multiple_of(head // per_kv * HD, HD), HD)
            value_span = pl.ds(pl.multiple_of((KV + head // per_kv) * HD, HD), HD)
            p = probabilities(q_ref[:, span], kv_all[:, key_span], first_row).astype(bf16)
            mixed_ref[:, span] = nn(p, kv_all[:, value_span]).astype(bf16)

        hidden = x_ref[...].astype(f32)
        for t in range(members):
            hidden += nt(mixed_ref[:, t * part : (t + 1) * part], square_ref[t, :, part:])
        hidden_ref[...] = hidden
        normed = rms_pieces(hidden)[1] * gains[1:2]
        rows_all[own, :] = swap_blocks(normed).astype(bf16)
        for hop in range(1, members):
            row_line.start(hop)
            row_line.arrive(hop)
        kv_line.close()
        row_line.close()
        for copy in moves:
            copy.wait()

    count = 2 + len(packed)
    anywhere = pl.BlockSpec(memory_space=pl.ANY)
    size, height, lanes = near[0].shape
    return pl.pallas_call(
        kernel,
        in_specs=in_vmem(5) + [anywhere] * count,
        out_specs=in_vmem(6) + [anywhere] * (2 + 2 * len(packed)),
        out_shape=[
            jax.ShapeDtypeStruct((own_rows, width), bf16),
            jax.ShapeDtypeStruct((own_rows, width), bf16),
            jax.ShapeDtypeStruct((rows, kv), bf16),
            jax.ShapeDtypeStruct((own_rows, width), bf16),
            jax.ShapeDtypeStruct((own_rows, width), f32),
            jax.ShapeDtypeStruct((rows, width), bf16),
        ]
        + [jax.ShapeDtypeStruct((size // 2, height, lanes), bf16)] * 2
        + [jax.ShapeDtypeStruct((size, height, lanes), bf16)] * (2 * len(packed)),
        scratch_shapes=[dma((2, members - 1))] * 4 + [dma((2 + 2 * len(packed),))] * 2,
        compiler_params=pltpu.CompilerParams(collective_id=3, has_side_effects=True, vmem_limit_bytes=56 * 2**20),
        cost_estimate=pl.CostEstimate(flops=10**11, bytes_accessed=10**7, transcendentals=0),
        name="attention_front",
    )(tokens, square, tall, cosine, sine, *near, *packed)


def attention_back(
    sums, cotangent, hidden, tokens, normed, q, kv_all, mixed, square, tall, cosine, sine, grads, to_x, to_y, members
):
    own_rows, width = tokens.shape
    rows = own_rows * members
    kv = 2 * KV * HD
    heads = width // HD
    per_kv = heads // KV
    part = width // members
    dma = pltpu.SemaphoreType.DMA

    def kernel(sums_ref, cot_ref, hidden_ref, x_ref, normed_ref, q_ref, kv_ref, mixed_ref, square_ref, tall_ref, *rest):
        cos_ref, sin_ref, grads_ref, to_x_ref, to_y_ref = rest[:5]
        grad_ref, parts, x_before, y_before, x_last, y_last = rest[5:11]
        do_ref, dq_ref, dkv_ref, total, kv_total, stage, tall_part, back_part = rest[11:19]
        back_leave, back_arrive, kv_leave, kv_arrive = rest[19:23]
        back_send, back_recv, kv_send, kv_recv, stage_sem, part_sem = rest[23:29]
        through, added, added_sem, chip_send, chip_recv = rest[29:]
        z = lax.axis_index("tensor")
        x_side, y_side = chip_neighbours()
        first, second = slice(0, size // 2), slice(size // 2, size)

        def chunk(block, span):
            return grads_ref.at[block, pairs_before + span.start : pairs_before + span.stop]


        def chip(index, source, target, device):
            return remote(source, target, chip_send.at[index], chip_recv.at[index], {"dp": device})

        loads = [
            pltpu.make_async_copy(
                sums_ref.at[b * own_rows : (b + 1) * own_rows, width:], back_part.at[b], part_sem.at[b]
            )
            for b in range(members)
        ] + [
            pltpu.make_async_copy(chunk(1, second), added.at[0], added_sem.at[0]),
            pltpu.make_async_copy(chunk(2, first), added.at[1], added_sem.at[1]),
        ]
        for copy in loads:
            copy.start()
        meet(members, False)
        moves = [
            chip(0, chunk(3, first), through.at[0], x_side),
            chip(1, chunk(3, second), through.at[1], y_side),
            chip(2, to_x_ref, x_before, x_side),
            chip(3, to_y_ref, y_before, y_side),
            chip(4, chunk(1, first), x_last.at[first], x_side),
            chip(5, chunk(2, second), y_last.at[second], y_side),
            chip(6, added.at[0], x_last.at[second], x_side),
            chip(7, added.at[1], y_last.at[first], y_side),
        ]
        for copy in moves[:6]:
            copy.start()
        own = pl.ds(pl.multiple_of(z * own_rows, 16), own_rows)
        for copy in loads:
            copy.wait()

        def block(ref, span):
            return lambda b: ref[pl.ds(pl.multiple_of(b * own_rows, 16), own_rows), span]

        back = LineSum(members, lambda b: back_part[b], back_leave, back_arrive, back_send, back_recv)
        pairs = LineSum(members, block(dkv_ref, slice(None)), kv_leave, kv_arrive, kv_send, kv_recv)
        gains = gain_rows(tall_ref, kv)
        cosine, sine = cos_ref[own], sin_ref[own]
        last = members - 1
        stored = []

        def store(value, at):
            slot = len(stored) % 2
            if len(stored) >= 2:
                stored[-2].wait()
            stage[slot] = value.astype(bf16)
            copy = pltpu.make_async_copy(stage.at[slot], parts.at[:, at : at + part], stage_sem.at[slot])
            copy.start()
            stored.append(copy)

        for hop in range(last, 0, -1):
            back.start(hop)
            back.arrive(hop)
        back.total(total)
        normed_grad = swap_blocks(total[...])
        inverse, unit = rms_pieces(hidden_ref[...])
        by_hidden, gain_two = rms_backward(normed_grad, unit, inverse, gains[1:2])
        grad_ref[...] = cot_ref[...] + by_hidden
        low = grad_ref[...].astype(bf16)
        for t in range(members):
            span = slice(t * part, (t + 1) * part)
            do_ref[:, span] = nn(low, square_ref[t, :, part:]).astype(bf16)
            store(tn(low, mixed_ref[:, span]), width + t * part)
        dkv_ref[...] = jnp.zeros_like(dkv_ref)
        first_row = z * own_rows

        @pl.loop(0, heads)
        def _(head):
            span = pl.ds(pl.multiple_of(head * HD, HD), HD)
            key_span = pl.ds(pl.multiple_of(head // per_kv * HD, HD), HD)
            value_span = pl.ds(pl.multiple_of((KV + head // per_kv) * HD, HD), HD)
            q_now, k_now, do_now = q_ref[:, span], kv_ref[:, key_span], do_ref[:, span]
            p = probabilities(q_now, k_now, first_row)
            dp = nt(do_now, kv_ref[:, value_span])
            ds = (p * (dp - jnp.sum(p * dp, axis=-1, keepdims=True))).astype(bf16)
            dq_ref[:, span] = turn(nn(ds, k_now) * (HD**-0.5), cosine, -sine).astype(bf16)
            dkv_ref[:, key_span] += tn(ds, q_now) * (HD**-0.5)
            dkv_ref[:, value_span] += tn(p.astype(bf16), do_now)

        pairs.start(last)
        for i, copy in enumerate(moves[:2]):
            copy.wait()
            added[1 - i] = (added[1 - i].astype(f32) + through[i].astype(f32)).astype(bf16)
            moves[7 - i].start()
        for t in range(members):
            span = slice(t * part, (t + 1) * part)
            store(tn(normed_ref[...], dq_ref[:, span]), t * part)
        for hop in range(last, 0, -1):
            if hop < last:
                pairs.start(hop)
            pairs.arrive(hop)
        pairs.total(kv_total)
        low_kv = [
            turn(kv_total[:, head * HD : (head + 1) * HD], cosine, -sine).astype(bf16) for head in range(KV)
        ] + [kv_total[:, KV * HD :].astype(bf16)]
        low_kv = jnp.concatenate(low_kv, axis=1)
        normed_grad = nt(low_kv, tall_ref[:, :kv])
        for t in range(members):
            normed_grad += nt(dq_ref[:, t * part : (t + 1) * part], square_ref[t, :, :part])
        inverse, unit = rms_pieces(x_ref[...].astype(f32))
        by_tokens, gain_one = rms_backward(normed_grad, unit, inverse, gains[0:1])
        grad_ref[...] += by_tokens
        tall_part[:, :kv] = tn(normed_ref[...], low_kv).astype(bf16)
        row = lax.broadcasted_iota(jnp.int32, (HD, width), 0)
        both = jnp.where(row == 0, gain_one[None], jnp.where(row == 1, gain_two[None], 0.0))
        tall_part[:, kv:] = jnp.transpose(both).astype(bf16)
        tall_copy = pltpu.make_async_copy(tall_part, parts.at[:, 2 * width :], stage_sem.at[2])
        tall_copy.start()
        for line in (back, pairs):
            line.close()
        for copy in (*stored[-2:], tall_copy, *moves[2:]):
            copy.wait()

    hops = (2, members - 1)
    anywhere = pl.BlockSpec(memory_space=pl.ANY)
    _, height, lanes = to_x.shape
    size = CALL_PAIRS
    pairs_before = grads.shape[1] - size
    halves = (2, size // 2, height, lanes)
    return pl.pallas_call(
        kernel,
        in_specs=[anywhere] + in_vmem(11) + [anywhere] * 3,
        out_specs=in_vmem(1) + [anywhere] * 5,
        out_shape=[
            jax.ShapeDtypeStruct((own_rows, width), f32),
            jax.ShapeDtypeStruct((width, 2 * width + tall.shape[1]), bf16),
        ]
        + [jax.ShapeDtypeStruct(to_x.shape, bf16)] * 2
        + [jax.ShapeDtypeStruct((size, height, lanes), bf16)] * 2,
        scratch_shapes=[
            pltpu.VMEM((own_rows, width), bf16),
            pltpu.VMEM((own_rows, width), bf16),
            pltpu.VMEM((rows, kv), f32),
            pltpu.VMEM((own_rows, width), f32),
            pltpu.VMEM((own_rows, kv), f32),
            pltpu.VMEM((2, width, part), bf16),
            pltpu.VMEM(tall.shape, bf16),
            pltpu.VMEM((members, own_rows, width), bf16),
            pltpu.VMEM((2, own_rows, width), bf16),
            pltpu.VMEM((*hops, own_rows, width), bf16),
            pltpu.VMEM((2, own_rows, kv), bf16),
            pltpu.VMEM((*hops, own_rows, kv), bf16),
        ]
        + [dma(hops)] * 4
        + [dma((3,)), dma((members,)), pltpu.VMEM(halves, bf16), pltpu.VMEM(halves, bf16), dma((2,)), dma((8,)), dma((8,))],
        compiler_params=pltpu.CompilerParams(collective_id=4, has_side_effects=True, vmem_limit_bytes=62 * 10**6),
        cost_estimate=pl.CostEstimate(flops=10**11, bytes_accessed=10**7, transcendentals=0),
        name="attention_back",
    )(
        sums, cotangent, hidden, tokens, normed, q, kv_all, mixed, square, tall, cosine, sine, grads, to_x, to_y
    )


def reduce_small(parts, sums, hidden, members, devices):
    own_rows = hidden.shape[0]
    width = parts.shape[0]
    height = width // devices
    lanes = parts.shape[1]
    tall = lanes - 2 * width
    part = width // members
    half = height // 2
    dma = pltpu.SemaphoreType.DMA

    def kernel(parts_ref, sums_ref, hidden_ref, out_ref, square_out, tall_out, *rest):
        own, theirs, leave, arrive, blocks, line_leave, line_arrive, tall_all = rest[:8]
        moe_part, moe_leave, moe_arrive, total_ref = rest[8:12]
        own_sem, core_send, core_recv, chip_send, chip_recv, line_send, line_recv, tall_send, tall_recv = rest[12:21]
        moe_send, moe_recv, part_sem = rest[21:]
        me, z = lax.axis_index("dp"), lax.axis_index("tensor")
        x_side, y_side = chip_neighbours()
        core = sibling()
        chips = [me, x_side, y_side, x_side + y_side - me]
        loads = [
            pltpu.make_async_copy(
                sums_ref.at[b * own_rows : (b + 1) * own_rows, :width], moe_part.at[b], part_sem.at[b]
            )
            for b in range(members)
        ]
        for copy in loads:
            copy.start()
        meet(members, True)
        moe = LineSum(members, lambda b: moe_part[b], moe_leave, moe_arrive, moe_send, moe_recv)
        last = members - 1

        def rows(device):
            return parts_ref.at[pl.ds(pl.multiple_of(device * height, 16), height)]

        def trade(m):
            return remote(rows(chips[m] + core - me), theirs.at[m], core_send.at[m], core_recv.at[m], {"dp": core})

        def keep(m):
            return pltpu.make_async_copy(rows(chips[m]), own.at[m], own_sem.at[m])

        for m in (3, 2, 1, 0):
            trade(m).start()
            keep(m).start()
        for copy in loads:
            copy.wait()
        moe.start(last)

        def both(m, span):
            return own[m, span].astype(f32) + theirs[m, span].astype(f32)

        def chip(index, source, target, device):
            return remote(source, target, chip_send.at[index], chip_recv.at[index], {"dp": device})

        first, second = slice(0, half), slice(half, height)
        far = [
            chip(0, leave.at[0, first], arrive.at[0, first], x_side),
            chip(1, leave.at[0, second], arrive.at[0, second], y_side),
        ]
        near = [chip(2, leave.at[1], arrive.at[1], x_side), chip(3, leave.at[2], arrive.at[2], y_side)]
        for m in (3, 2, 1, 0):
            trade(m).wait()
            keep(m).wait()
            if m == 3:
                for copy, span in zip(far, (first, second)):
                    leave[0, span] = both(3, span).astype(bf16)
                    copy.start()
        for copy in far:
            copy.wait()
        moe.arrive(last)
        if last > 1:
            moe.start(last - 1)
        leave[1, first] = both(1, first).astype(bf16)
        leave[1, second] = (both(1, second) + arrive[0, second].astype(f32)).astype(bf16)
        near[0].start()
        leave[2, first] = (both(2, first) + arrive[0, first].astype(f32)).astype(bf16)
        leave[2, second] = both(2, second).astype(bf16)
        near[1].start()
        for hop in range(last - 1, 0, -1):
            moe.arrive(hop)
            if hop > 1:
                moe.start(hop - 1)
        moe.total(total_ref)
        out_ref[...] = (hidden_ref[...] + swap_blocks(total_ref[...])).astype(bf16)
        for copy in near:
            copy.wait()

        def total(span):
            return (
                own[0, :, span].astype(f32)
                + theirs[0, :, span].astype(f32)
                + arrive[1, :, span].astype(f32)
                + arrive[2, :, span].astype(f32)
            )

        tall_all[z] = total(slice(2 * width, lanes)).astype(bf16)
        for t in range(members):
            blocks[t, :, :part] = total(slice(t * part, (t + 1) * part))
            blocks[t, :, part:] = total(slice(width + t * part, width + (t + 1) * part))
        line = LineSum(members, lambda b: blocks[b], line_leave, line_arrive, line_send, line_recv)
        group = LineGather(members, lambda b: tall_all.at[b], tall_send, tall_recv)
        for hop in range(1, members):
            line.start(members - hop)
            group.start(hop)
            line.arrive(members - hop)
            group.arrive(hop)
        line.total(square_out)
        summed = tall_all[0].astype(f32)
        for t in range(1, members):
            summed += tall_all[t].astype(f32)
        tall_out[...] = summed
        line.close()
        group.close()
        moe.close()

    hops = (2, members - 1)
    return pl.pallas_call(
        kernel,
        in_specs=[pl.BlockSpec(memory_space=pl.ANY)] * 2 + in_vmem(1),
        out_specs=in_vmem(3),
        out_shape=[
            jax.ShapeDtypeStruct((own_rows, width), bf16),
            jax.ShapeDtypeStruct((height, 2 * part), f32),
            jax.ShapeDtypeStruct((height, tall), f32),
        ],
        scratch_shapes=[
            pltpu.VMEM((4, height, lanes), bf16),
            pltpu.VMEM((4, height, lanes), bf16),
            pltpu.VMEM((3, height, lanes), bf16),
            pltpu.VMEM((3, height, lanes), bf16),
            pltpu.VMEM((members, height, 2 * part), f32),
            pltpu.VMEM((2, height, 2 * part), bf16),
            pltpu.VMEM((*hops, height, 2 * part), bf16),
            pltpu.VMEM((members, height, tall), bf16),
            pltpu.VMEM((members, own_rows, width), bf16),
            pltpu.VMEM((2, own_rows, width), bf16),
            pltpu.VMEM((*hops, own_rows, width), bf16),
            pltpu.VMEM((own_rows, width), f32),
            dma((4,)),
            dma((4,)),
            dma((4,)),
            dma((4,)),
            dma((4,)),
        ]
        + [dma(hops)] * 6
        + [dma((members,))],
        compiler_params=pltpu.CompilerParams(collective_id=5, has_side_effects=True, vmem_limit_bytes=60 * 2**20),
        cost_estimate=pl.CostEstimate(flops=8 * 10**10, bytes_accessed=10**7, transcendentals=0),
        name="reduce_small",
    )(parts, sums, hidden)


def unpack_all(grads, plain, added, last):
    _, pairs, height, lanes = grads.shape
    half = CALL_PAIRS // 2
    units = lanes // 6
    tail = units - HD
    step = 48 if height % 48 == 0 else height
    others = (*plain, *added, *last)

    def kernel(own, plain_x, plain_y, added_x, added_y, last_x, last_y, gate, up, down):
        for call in range(pairs // CALL_PAIRS):
            found = [[], [], []]
            for turn in range(CALL_PAIRS):
                pair = call * CALL_PAIRS + turn
                at = call * half + turn % half
                if pair >= pairs - CALL_PAIRS:
                    by_x, by_y = last_x[turn], last_y[turn]
                elif turn < half:
                    by_x, by_y = plain_x[at], added_y[at]
                else:
                    by_x, by_y = added_x[at], plain_y[at]
                value = own[0, pair].astype(f32) + by_x.astype(f32) + by_y.astype(f32)
                tiles = [value[:, i * HD : (i + 1) * HD] for i in range(9)]
                for i, (a, b, both) in enumerate(((0, 1, 2), (3, 4, 5), (6, 8, 7))):
                    left = jnp.concatenate([tiles[a], tiles[both][:, :tail]], axis=1)
                    right = jnp.concatenate([tiles[b], tiles[both][:, tail:]], axis=1)
                    if i < 2:
                        found[0].append(left)
                        found[1].append(right)
                    else:
                        found[2] += [left, right]
            span = slice(2 * CALL_PAIRS * call, 2 * CALL_PAIRS * (call + 1))
            for out, values in zip((gate, up, down), found):
                out[:, span, :] = jnp.swapaxes(jnp.stack(values), 0, 1)

    shape = (height, 2 * pairs, units)
    return pl.pallas_call(
        kernel,
        grid=(height // step,),
        in_specs=[pl.BlockSpec((1, pairs, step, lanes), lambda i: (0, 0, i, 0))]
        + [pl.BlockSpec((other.shape[0], step, lanes), lambda i: (0, i, 0)) for other in others],
        out_specs=[pl.BlockSpec((step, *shape[1:]), lambda i: (i, 0, 0))] * 3,
        out_shape=[jax.ShapeDtypeStruct(shape, f32)] * 3,
        compiler_params=pltpu.CompilerParams(vmem_limit_bytes=48 * 2**20),
        name="unpack",
    )(grads, *others)


def pack(gate, up, down):
    def pair(a, b):
        return jnp.concatenate([a[..., :HD], b[..., :HD], a[..., HD:], b[..., HD:]], axis=-1)

    gate, up, down = (jnp.transpose(w, (1, 0, 2)) for w in (gate, up, down))
    gate_up = pair(gate, up)
    a, b = down[0::2], down[1::2]
    inner = jnp.concatenate([a[..., :HD], a[..., HD:], b[..., HD:], b[..., :HD]], axis=-1)
    return jnp.concatenate([gate_up[0::2], gate_up[1::2], inner], axis=-1)


def unpack(packed):
    n, height, lanes = packed.shape
    third = lanes // 3

    def halves(both):
        tail = third // 2 - HD
        a = jnp.concatenate([both[..., :HD], both[..., 2 * HD : 2 * HD + tail]], axis=-1)
        b = jnp.concatenate([both[..., HD : 2 * HD], both[..., 2 * HD + tail :]], axis=-1)
        return a, b

    def experts(even, odd):
        both = jnp.stack([even, odd], axis=1).reshape(2 * n, height, third // 2)
        return jnp.transpose(both, (1, 0, 2))

    gate0, up0 = halves(packed[..., :third])
    gate1, up1 = halves(packed[..., third : 2 * third])
    down0, down1 = packed[..., 2 * third : 2 * third + third // 2], packed[..., 2 * third + third // 2 :]
    tail = third // 2 - HD
    down1 = jnp.concatenate([down1[..., tail:], down1[..., :tail]], axis=-1)
    return experts(gate0, gate1), experts(up0, up1), experts(down0, down1)


def routes_of(expert_ids, route_weights):
    rows = expert_ids.shape[0]
    lanes = jnp.arange(EXPERTS, dtype=jnp.int32)
    named = expert_ids[:, :, None] == lanes
    member_of = jnp.any(named, axis=1)
    weight_of = jnp.sum(jnp.where(named, route_weights[:, :, None], 0.0), axis=1)
    earlier = jnp.arange(rows)[:, None] > jnp.arange(rows)[None, :]
    rank = jnp.where(member_of, nn(earlier.astype(bf16), member_of.astype(bf16)), -1.0)
    rank_cols = jnp.pad(rank, ((0, 0), (0, HD)), constant_values=-1.0).astype(bf16)
    return rank_cols, jnp.stack([rank.T, weight_of.T], axis=1)


def body_anywhere(
    tokens,
    expert_ids,
    route_weights,
    attn_gain,
    q_weight,
    k_weight,
    v_weight,
    o_weight,
    moe_gain,
    gate_weight,
    up_weight,
    down_weight,
    cotangent,
):
    members = lax.axis_size("tensor")
    member = lax.axis_index("tensor")
    own_rows, width = tokens.shape
    rows = own_rows * members
    pairs = EXPERTS // 2
    calls = pairs // CALL_PAIRS

    packed = [
        pack(*(w[:, 2 * CALL_PAIRS * i : 2 * CALL_PAIRS * (i + 1)] for w in (gate_weight, up_weight, down_weight)))
        for i in range(calls)
    ]
    gathered = [lax.all_gather(own, "dp", axis=1, tiled=True) for own in packed]

    gain_one = lax.all_gather(attn_gain, "dp", axis=0, tiled=True).astype(f32)
    gain_two = lax.all_gather(moe_gain, "dp", axis=0, tiled=True).astype(f32)
    kv_full = lax.all_gather(jnp.concatenate([k_weight, v_weight], axis=1), "dp", axis=0, tiled=True)
    q_full = lax.all_gather(lax.all_gather(q_weight, "dp", axis=0, tiled=True), "tensor", axis=0)
    o_full = lax.all_gather(lax.all_gather(o_weight, "dp", axis=0, tiled=True), "tensor", axis=0)
    kv_width = k_weight.shape[1]

    rank_cols, routes = routes_of(expert_ids, route_weights)

    grad_low = cotangent.astype(bf16)
    grad_all = lax.all_gather(grad_low, "tensor", axis=0, tiled=True)

    x = tokens.astype(f32)
    inverse_one, unit_one = rms_pieces(x)
    normed_one = (unit_one * gain_one).astype(bf16)
    first_row = (member * own_rows).reshape(1)
    cos_table, sin_table = rope_tables(member * own_rows + jnp.arange(own_rows, dtype=jnp.int32))
    kv_own = nn(normed_one, kv_full)
    kv_own = jnp.concatenate(
        [rotate(kv_own[:, :kv_width], cos_table, sin_table), kv_own[:, kv_width:]], axis=1
    ).astype(bf16)
    kv_all = lax.all_gather(kv_own, "tensor", axis=0, tiled=True)
    keys, values = kv_all[:, :kv_width], kv_all[:, kv_width:]
    queries = jnp.concatenate([nn(normed_one, q_full[t]) for t in range(members)], axis=1)
    queries = rotate(queries, cos_table, sin_table).astype(bf16)
    mixed = attend_forward(first_row, queries, keys, values)
    part = width // members
    branch = sum(nt(mixed[:, t * part : (t + 1) * part], o_full[t]) for t in range(members))
    hidden = x + branch
    inverse_two, unit_two = rms_pieces(hidden)
    normed_two = (unit_two * gain_two).astype(bf16)
    rows_all = lax.all_gather(normed_two, "tensor", axis=0, tiled=True)

    sums = jnp.zeros((rows, 2 * width), f32)
    chunks = []
    for call in range(calls):
        some = slice(2 * CALL_PAIRS * call, 2 * CALL_PAIRS * (call + 1))
        columns = slice(2 * CALL_PAIRS * call, 2 * CALL_PAIRS * call + HD)
        grads, sums = expert_call(
            rank_cols[:, columns],
            routes[some],
            rows_all,
            grad_all,
            gathered[call],
            sums,
        )
        chunks.append(grads)
    shares = [
        unpack(lax.psum_scatter(grads, "dp", scatter_dimension=1, tiled=True).astype(f32)) for grads in chunks
    ]
    gate_out, up_out, down_out = (jnp.concatenate(parts, axis=1) for parts in zip(*shares))

    low_sums = sums.astype(bf16)
    normed_grad = lax.psum_scatter(low_sums[:, width:], "tensor", scatter_dimension=0, tiled=True).astype(f32)
    moe_own = lax.psum_scatter(low_sums[:, :width], "tensor", scatter_dimension=0, tiled=True).astype(f32)
    output = (hidden + moe_own).astype(bf16)

    back_two, gain_two_part = rms_backward(normed_grad, unit_two, inverse_two, gain_two)
    hidden_grad = cotangent + back_two
    hidden_low = hidden_grad.astype(bf16)
    mixed_grad = jnp.concatenate([nn(hidden_low, o_full[t]) for t in range(members)], axis=1).astype(bf16)
    o_part = jnp.stack([tn(hidden_low, mixed[:, t * part : (t + 1) * part]) for t in range(members)])
    dq, dk, dv = attend_backward(first_row, queries, keys, values, mixed_grad)
    kv_grad = lax.psum_scatter(
        jnp.concatenate([dk, dv], axis=1).astype(bf16), "tensor", scatter_dimension=0, tiled=True
    ).astype(f32)
    dq_low = rotate(dq, cos_table, -sin_table).astype(bf16)
    kv_low = jnp.concatenate(
        [rotate(kv_grad[:, :kv_width], cos_table, -sin_table), kv_grad[:, kv_width:]], axis=1
    ).astype(bf16)
    normed_one_grad = nt(kv_low, kv_full) + sum(
        nt(dq_low[:, t * part : (t + 1) * part], q_full[t]) for t in range(members)
    )
    back_one, gain_one_part = rms_backward(normed_one_grad, unit_one, inverse_one, gain_one)
    tokens_grad = hidden_grad + back_one
    q_part = jnp.stack([tn(normed_one, dq_low[:, t * part : (t + 1) * part]) for t in range(members)])
    kv_part = tn(normed_one, kv_low)

    def shared(values):
        summed = lax.psum_scatter(values.astype(bf16), "tensor", scatter_dimension=0, tiled=False)
        return lax.psum_scatter(summed, "dp", scatter_dimension=0, tiled=True).astype(f32)

    q_grad, o_grad = shared(q_part), shared(o_part)
    small = jnp.concatenate([kv_part, gain_one_part[:, None], gain_two_part[:, None]], axis=1)
    small = lax.psum_scatter(small, "dp", scatter_dimension=0, tiled=True)
    small = lax.psum(small.astype(bf16), "tensor").astype(f32)
    return (
        output,
        tokens_grad,
        small[:, 2 * kv_width],
        q_grad,
        small[:, :kv_width],
        small[:, kv_width : 2 * kv_width],
        o_grad,
        small[:, 2 * kv_width + 1],
        gate_out,
        up_out,
        down_out,
    )

def body_by_chips(
    tokens,
    expert_ids,
    route_weights,
    attn_gain,
    q_weight,
    k_weight,
    v_weight,
    o_weight,
    moe_gain,
    gate_weight,
    up_weight,
    down_weight,
    cotangent,
):
    members = lax.axis_size("tensor")
    member = lax.axis_index("tensor")
    devices = lax.axis_size("dp")
    own_rows, width = tokens.shape
    rows = own_rows * members
    calls = EXPERTS // 2 // CALL_PAIRS
    kv_width = k_weight.shape[1]

    gains = jnp.pad(jnp.stack([attn_gain, moe_gain], axis=1), ((0, 0), (0, HD - 2)))
    small = gather_small(
        q_weight,
        o_weight,
        k_weight,
        v_weight,
        gains,
        cotangent,
        expert_ids.T,
        route_weights.T,
        gate_weight,
        up_weight,
        down_weight,
        members,
        devices,
    )
    square_all, tall_all, grad_all, rank_cols, routes = small[:5]
    packed, near = small[5 : 5 + calls], [tuple(small[5 + calls :])]
    cosine, sine = doubled_tables(rows)
    normed_one, queries, kv_all, mixed, hidden, rows_all, *landed = attention_front(
        tokens, square_all, tall_all, cosine, sine, packed[1:-1], near[0], members
    )
    near += [tuple(landed[2 * i : 2 * i + 2]) for i in range(1, calls - 1)]
    sums, grads, *others = expert_pass(
        rank_cols, routes, rows_all, grad_all, packed, near, landed[:2], members
    )
    plain, added = others[-6:-4], others[-4:-2]
    tokens_grad, parts, *moved = attention_back(
        sums,
        cotangent,
        hidden,
        tokens,
        normed_one,
        queries,
        kv_all,
        mixed,
        square_all,
        tall_all,
        cosine,
        sine,
        grads,
        *added,
        members,
    )
    output, square_grad, tall_grad = reduce_small(parts, sums, hidden, members, devices)
    gate_out, up_out, down_out = unpack_all(grads, plain, moved[:2], moved[2:])
    part = width // members
    return (
        output,
        tokens_grad,
        tall_grad[:, 2 * kv_width],
        square_grad[:, :part],
        tall_grad[:, :kv_width],
        tall_grad[:, kv_width : 2 * kv_width],
        square_grad[:, part:],
        tall_grad[:, 2 * kv_width + 1],
        gate_out,
        up_out,
        down_out,
    )


def doubled_tables(rows):
    half = HD // 2
    frequency = np.float32(rope_base) ** -(np.arange(half, dtype=np.float32) * np.float32(2.0 / HD))
    angles = (np.arange(rows) % SEQ).astype(np.float32)[:, None] * frequency
    cosine, sine = np.cos(angles), np.sin(angles)
    return jnp.asarray(np.concatenate([cosine, cosine], axis=1)), jnp.asarray(np.concatenate([-sine, sine], axis=1))


def solution(mesh):
    rows = P(("dp", "tensor"), None)
    experts = P("dp", None, "tensor")
    square = P("dp", "tensor")
    tall = P("dp", None)
    return jax.shard_map(
        body_by_chips if mesh.shape["dp"] == 8 else body_anywhere,
        mesh=mesh,
        in_specs=(
            rows, tall, tall, P("dp"), square, tall, tall, square, P("dp"), experts, experts, experts, rows
        ),
        out_specs=(rows, rows, P("dp"), square, tall, tall, square, P("dp"), experts, experts, experts),
        check_vma=False,
    )
```

```python
import jax
import jax.numpy as jnp
import numpy as np
from jax import lax
from jax.experimental import pallas as pl
from jax.experimental.pallas import tpu as pltpu
from jax.sharding import PartitionSpec as P

KV = 2
HD = 128
EXPERTS = 32
TOPK = 4
SEQ = 1024
BLOCK = 256
CAP = 256
TAIL = 64
CALL_PAIRS = 4

eps = 1e-06
rope_base = 1000000.0
negative = -1e30
bf16 = jnp.bfloat16
f32 = jnp.float32


def nn(a, b):
    return jnp.dot(a, b, preferred_element_type=f32)


def nt(a, b):
    return lax.dot_general(a, b, (((1,), (1,)), ((), ())), preferred_element_type=f32)


def tn(a, b):
    return lax.dot_general(a, b, (((0,), (0,)), ((), ())), preferred_element_type=f32)


def rope_tables(positions):
    half = HD // 2
    frequency = rope_base ** (-(jnp.arange(half).astype(f32) * 2.0 / HD))
    angles = positions.astype(f32)[:, None] * frequency[None, :]
    return jnp.cos(angles), jnp.sin(angles)


def rotate(values, cos_table, sin_table):
    rows = values.shape[0]
    heads = values.reshape(rows, -1, 2, HD // 2)
    a, b = heads[:, :, 0], heads[:, :, 1]
    cos_table, sin_table = cos_table[:, None], sin_table[:, None]
    turned = jnp.stack([a * cos_table - b * sin_table, b * cos_table + a * sin_table], axis=2)
    return turned.reshape(rows, -1)


def rms_pieces(x):
    inverse = lax.rsqrt(jnp.mean(x * x, axis=-1, keepdims=True) + eps)
    return inverse, x * inverse


def rms_backward(grad, unit, inverse, gain):
    u = grad * gain
    back = inverse * (u - unit * jnp.mean(u * unit, axis=-1, keepdims=True))
    return back, jnp.sum(grad * unit, axis=0)


def probabilities(q, k, first_row):
    rows, keys = q.shape[0], k.shape[0]
    scores = nt(q, k) * (HD**-0.5)
    q_block = (first_row + lax.broadcasted_iota(jnp.int32, (rows, keys), 0)) // BLOCK
    k_block = lax.broadcasted_iota(jnp.int32, (rows, keys), 1) // BLOCK
    scores = jnp.where(k_block <= q_block, scores, negative)
    raised = jnp.exp(scores - jnp.max(scores, axis=-1, keepdims=True))
    return raised / jnp.sum(raised, axis=-1, keepdims=True)


def attend_forward(first_row, q, k, v):
    rows, width = q.shape
    heads = width // HD
    shared = heads // KV

    def kernel(first_ref, q_ref, k_ref, v_ref, o_ref):
        p = probabilities(q_ref[...], k_ref[...], first_ref[0]).astype(bf16)
        o_ref[...] = nn(p, v_ref[...]).astype(bf16)

    per_head = pl.BlockSpec((rows, HD), lambda h, f: (0, h))
    per_kv = pl.BlockSpec((k.shape[0], HD), lambda h, f: (0, h // shared))
    return pl.pallas_call(
        kernel,
        grid_spec=pltpu.PrefetchScalarGridSpec(
            num_scalar_prefetch=1,
            grid=(heads,),
            in_specs=[per_head, per_kv, per_kv],
            out_specs=per_head,
        ),
        out_shape=jax.ShapeDtypeStruct((rows, width), bf16),
        compiler_params=pltpu.CompilerParams(vmem_limit_bytes=32 * 2**20),
        cost_estimate=pl.CostEstimate(
            flops=4 * rows * width * k.shape[0],
            bytes_accessed=4 * rows * width,
            transcendentals=rows * heads * k.shape[0],
        ),
        name="attend",
    )(first_row, q, k, v)


def attend_backward(first_row, q, k, v, do):
    rows, width = q.shape
    keys = k.shape[0]
    heads = width // HD
    shared = heads // KV

    def kernel(first_ref, q_ref, k_ref, v_ref, do_ref, dq_ref, dk_ref, dv_ref):
        q_now, k_now, v_now, do_now = q_ref[...], k_ref[...], v_ref[...], do_ref[...]
        p = probabilities(q_now, k_now, first_ref[0])
        dp = nt(do_now, v_now)
        ds = (p * (dp - jnp.sum(p * dp, axis=-1, keepdims=True))).astype(bf16)
        dq_ref[...] = nn(ds, k_now) * (HD**-0.5)
        dk = tn(ds, q_now) * (HD**-0.5)
        dv = tn(p.astype(bf16), do_now)
        head = pl.program_id(0)

        @pl.when(lax.rem(head, shared) == 0)
        def _():
            dk_ref[...] = dk
            dv_ref[...] = dv

        @pl.when(lax.rem(head, shared) != 0)
        def _():
            dk_ref[...] += dk
            dv_ref[...] += dv

    per_head = pl.BlockSpec((rows, HD), lambda h, f: (0, h))
    per_kv = pl.BlockSpec((keys, HD), lambda h, f: (0, h // shared))
    return pl.pallas_call(
        kernel,
        grid_spec=pltpu.PrefetchScalarGridSpec(
            num_scalar_prefetch=1,
            grid=(heads,),
            in_specs=[per_head, per_kv, per_kv, per_head],
            out_specs=[per_head, per_kv, per_kv],
        ),
        out_shape=[
            jax.ShapeDtypeStruct((rows, width), f32),
            jax.ShapeDtypeStruct((keys, KV * HD), f32),
            jax.ShapeDtypeStruct((keys, KV * HD), f32),
        ],
        compiler_params=pltpu.CompilerParams(vmem_limit_bytes=32 * 2**20),
        cost_estimate=pl.CostEstimate(
            flops=10 * rows * width * keys,
            bytes_accessed=8 * rows * width,
            transcendentals=rows * heads * keys,
        ),
        name="attend_back",
    )(first_row, q, k, v, do)


def sibling():
    me = lax.axis_index("dp")
    return me + 1 - 2 * lax.rem(me, 2)


def pair_of_experts(expert, place, w, rank_c, routes_ref, x_ref, gy_ref, y_buf, pick_buf, put):
    rows, width = x_ref.shape
    lanes = w.shape[1]
    third = lanes // 3
    low_half = lax.broadcasted_iota(jnp.int32, (CAP, HD), 1) < TAIL
    slot_of = lax.broadcasted_iota(jnp.int32, (rows, CAP), 1).astype(f32)
    slot_at = lax.broadcasted_iota(jnp.int32, (CAP, rows), 0).astype(f32)
    gate_up = [slice(q * third, (q + 1) * third) for q in range(2)]
    down = [slice(2 * third + q * HD, 2 * third + (q + 2) * HD) for q in range(2)]

    def place_of(q):
        return pl.ds(pl.multiple_of((place + q) * CAP, CAP), CAP)

    def rows_of(q):
        hit = slot_at == routes_ref[q, 0:1]
        weight = jnp.sum(jnp.where(hit, routes_ref[q, 1:2], 0.0), axis=1, keepdims=True)
        pick = hit.astype(bf16)
        return nn(pick, x_ref[...]).astype(bf16), (nn(pick, gy_ref[...]) * weight).astype(bf16), weight

    def picked(q):
        column = (lax.broadcasted_iota(jnp.int32, (HD, CAP), 0) == expert + q).astype(bf16)
        pick_buf[:, place_of(q)] = (nn(rank_c[...], column) == slot_of).astype(bf16)

    def unit(gate, up, dact):
        sig = jax.nn.sigmoid(gate)
        silu = gate * sig
        return silu * up, dact * up * sig * (1.0 + gate * (1.0 - sig)), dact * silu

    def middle(q, gu, dact):
        tail = gu[:, 2 * HD :]
        if q == 0:
            d0, d1 = dact[:, :HD], dact[:, HD:]
        else:
            d0, d1 = dact[:, HD:], pltpu.roll(dact[:, :HD], TAIL, 1)
        a0, dg0, du0 = unit(gu[:, :HD], gu[:, HD : 2 * HD], d0)
        a1, dg1, du1 = unit(tail, pltpu.roll(tail, TAIL, 1), d1)
        a1 = jnp.where(low_half, a1, 0.0)
        dgu1 = jnp.where(low_half, dg1, pltpu.roll(du1, TAIL, 1))
        act = [a0, a1] if q == 0 else [pltpu.roll(a1, TAIL, 1), a0]
        act = jnp.concatenate([part.astype(bf16) for part in act], axis=1)
        return act, jnp.concatenate([part.astype(bf16) for part in (dg0, du0, dgu1)], axis=1)

    def ends(q, xe, deo, weight, act, dgu):
        y_buf[place_of(q), :width] = (nt(act, w[:, down[q]]) * weight).astype(bf16)
        y_buf[place_of(q), width:] = nt(dgu, w[:, gate_up[q]]).astype(bf16)
        put(q * third, tn(xe, dgu))
        grad = tn(deo, act)
        put(2 * third + 2 * q * HD, grad[:, :HD] if q == 0 else grad[:, HD:])
        return grad[:, HD:] if q == 0 else grad[:, :HD]

    xe0, deo0, weight0 = rows_of(0)
    first = nn(xe0, w[:, gate_up[0]]), nn(deo0, w[:, down[0]])
    xe1, deo1, weight1 = rows_of(1)
    act0, dgu0 = middle(0, *first)
    second = nn(xe1, w[:, gate_up[1]]), nn(deo1, w[:, down[1]])
    picked(0)
    tail0 = ends(0, xe0, deo0, weight0, act0, dgu0)
    act1, dgu1 = middle(1, *second)
    picked(1)
    tail1 = ends(1, xe1, deo1, weight1, act1, dgu1)
    put(2 * third + HD, tail0 + tail1)


def expert_call(rank_cols, routes, x, gy, weights, sums):
    rows, width = x.shape
    pairs, _, lanes = weights.shape
    blocks = 6
    tile = 2 * width // blocks

    def kernel(rank_c, routes_ref, x_ref, gy_ref, w_ref, sums_in, grad_out, sums_out, y_buf, pick_buf):
        step = pl.program_id(0)

        def put(at, value):
            grad_out[0, :, at : at + value.shape[1]] = value.astype(bf16)

        @pl.when(step < pairs)
        def _():
            pair_of_experts(2 * step, 2 * step, w_ref.at[0], rank_c, routes_ref, x_ref, gy_ref, y_buf, pick_buf, put)

        @pl.when(step >= pairs)
        def _():
            at = pl.ds(pl.multiple_of((step - pairs) * tile, tile), tile)
            sums_out[...] = sums_in[...] + nn(pick_buf[...], y_buf[:, at])

    def held(step):
        return jnp.minimum(step, pairs - 1)

    def block(step):
        return (0, jnp.maximum(step - pairs, 0))

    once = pl.Buffered(1)
    whole = pl.BlockSpec((rows, width), lambda s: (0, 0), pipeline_mode=once)
    of_pair = pl.BlockSpec((1, width, lanes), lambda s: (held(s), 0, 0))
    return pl.pallas_call(
        kernel,
        grid=(pairs + blocks,),
        in_specs=[
            pl.BlockSpec((rows, HD), lambda s: (0, 0), pipeline_mode=once),
            pl.BlockSpec((2, 2, rows), lambda s: (held(s), 0, 0)),
            whole,
            whole,
            of_pair,
            pl.BlockSpec((rows, tile), block),
        ],
        out_specs=[of_pair, pl.BlockSpec((rows, tile), block)],
        scratch_shapes=[pltpu.VMEM((2 * pairs * CAP, 2 * width), bf16), pltpu.VMEM((rows, 2 * pairs * CAP), bf16)],
        out_shape=[
            jax.ShapeDtypeStruct((pairs, width, lanes), bf16),
            jax.ShapeDtypeStruct((rows, 2 * width), f32),
        ],
        compiler_params=pltpu.CompilerParams(vmem_limit_bytes=62 * 10**6),
        name="experts",
    )(rank_cols, routes, x, gy, weights, sums)


def expert_pass(rank_cols, routes, x, gy, packed, near, far, members):
    rows, width = x.shape
    calls = len(packed)
    size, height, lanes = packed[0].shape
    half = size // 2
    pairs = calls * size
    blocks = 6
    tile = 2 * width // blocks
    period = size + blocks
    early = calls - 1
    dma = pltpu.SemaphoreType.DMA
    known = len(near)
    unknown = calls - known
    n_in = 4 + calls + 2 * known + 2

    def kernel(*refs):
        rank_c, routes_ref, x_ref, gy_ref = refs[:4]
        own = refs[4 : 4 + calls]
        near_in = refs[4 + calls : n_in - 2]
        far_in = refs[n_in - 2 : n_in]
        outs = refs[n_in:]
        sums_out, grads = outs[:2]
        near_out, outs = outs[2 : 2 + 2 * unknown], outs[2 + 2 * unknown :]
        far_out = outs[: 2 * early]
        plain_x, plain_y, added_x, added_y, via_x, via_y = outs[2 * early : 6 + 2 * early]
        scratch = outs[6 + 2 * early :]
        w_buf, y_buf, pick_buf, total, kept, leaving, arriving, load_buf, add_buf = scratch[:9]
        local_sem, push_sem, pull_sem, send_sem, recv_sem, keep_sem, load_sem, add_sem = scratch[9:17]
        chip_send, chip_recv, cross_send, cross_recv, straight_send, straight_recv, w_free, g_free = scratch[17:]
        step = pl.program_id(0)
        call, phase = step // period, lax.rem(step, period)
        pair = call * size + phase
        x_side, y_side = chip_neighbours()
        other = {"dp": sibling()}
        near_all = (*near_in, *near_out)
        near_x, near_y = near_all[0::2], near_all[1::2]
        far_all = [far_in, *(far_out[2 * i : 2 * i + 2] for i in range(early))]

        def chip(index, source, target, device):
            return remote(source, target, chip_send.at[index], chip_recv.at[index], {"dp": device})

        forward = []
        for i in range(early):
            forward.append(chip(2 * i, near_x[i + 1].at[:half], far_out[2 * i], y_side))
            forward.append(chip(2 * i + 1, near_y[i + 1].at[half:], far_out[2 * i + 1], x_side))
        fresh = []
        for i in range(unknown):
            fresh.append(chip(2 * early + 2 * i, own[known + i], near_out[2 * i], x_side))
            fresh.append(chip(2 * early + 2 * i + 1, own[known + i], near_out[2 * i + 1], y_side))

        def weights(now, slot, sub):
            chunk, side = sub // 2, sub % 2
            sources = [own[chunk], near_x[chunk], near_y[chunk], far_all[chunk][side]]
            begins = [chunk * size] * 3 + [chunk * size + side * half]
            found = []
            for k, (source, begin) in enumerate(zip(sources, begins)):
                source = source.at[now - begin]
                mine = w_buf.at[slot, pl.ds(2 * k * height, height)]
                found.append(pltpu.make_async_copy(source, mine, local_sem.at[slot, k]))
                theirs = w_buf.at[slot, pl.ds((2 * k + 1) * height, height)]
                found.append(remote(source, theirs, push_sem.at[slot, k], pull_sem.at[slot, k], other))
            return found

        def start(now):
            slot = lax.rem(now, 2)
            for sub in range(2 * calls):

                @pl.when((now >= sub * half) & (now < (sub + 1) * half))
                def _():
                    if sub >= 2:

                        @pl.when(now == sub * half)
                        def _():
                            forward[sub - 2].wait_recv()

                    for copy in weights(now, slot, sub):
                        copy.start()

        def leave(slot):
            return remote(leaving.at[slot], arriving.at[slot], send_sem.at[slot], recv_sem.at[slot], other)

        def keep(now):
            slot = lax.rem(now, 2)
            return pltpu.make_async_copy(kept.at[slot], grads.at[:, now], keep_sem.at[slot])

        def crossing(now, first):
            at = now // size * half + lax.rem(now, size) - (0 if first else half)
            sems = cross_send.at[now], cross_recv.at[now]
            if first:
                return remote(grads.at[3, now], via_x.at[at], *sems, {"dp": x_side})
            return remote(grads.at[3, now], via_y.at[at], *sems, {"dp": y_side})

        def straight(now, first):
            at = now // size * half + lax.rem(now, size) - (0 if first else half)
            sems = straight_send.at[now], straight_recv.at[now]
            if first:
                return remote(grads.at[1, now], plain_x.at[at], *sems, {"dp": x_side})
            return remote(grads.at[2, now], plain_y.at[at], *sems, {"dp": y_side})

        def by_half(now, do):
            for first in (True, False):

                @pl.when((lax.rem(now, size) < half) if first else (lax.rem(now, size) >= half))
                def _():
                    do(first)

        def scatter(now):
            def both(first):
                crossing(now, first).start()
                straight(now, first).start()

            by_half(now, both)

        def finish(now):
            slot = lax.rem(now, 2)
            leave(slot).wait()
            for k in range(4):
                kept[slot, k] = (kept[slot, k].astype(f32) + arriving[slot, k].astype(f32)).astype(bf16)
            keep(now).start()

        def signal(sem):
            pl.semaphore_signal(sem, inc=1, device_id=other, device_id_type=pl.DeviceIdType.MESH)

        def put(at, value):
            slot = lax.rem(pair, 2)
            for k in range(4):
                for parity, target in enumerate((kept, leaving)):
                    row = (2 * k + parity) * height
                    target[slot, k, :, at : at + value.shape[1]] = value[row : row + height].astype(bf16)

        def loads(now):
            at = now // size * half + lax.rem(now, half)

            def copies(first):
                via, block = (via_x, 2) if first else (via_y, 1)
                return (
                    pltpu.make_async_copy(via.at[at], load_buf.at[0], load_sem.at[0]),
                    pltpu.make_async_copy(grads.at[block, now], load_buf.at[1], load_sem.at[1]),
                )

            return copies

        def stores(now, first):
            at = now // size * half + lax.rem(now, half)
            return pltpu.make_async_copy(add_buf, (added_y if first else added_x).at[at], add_sem)

        @pl.when(step == 0)
        def _():
            barrier = pltpu.get_barrier_semaphore()
            for device in (x_side, y_side, sibling()):
                pl.semaphore_signal(barrier, inc=1, device_id={"dp": device}, device_id_type=pl.DeviceIdType.MESH)
            pl.semaphore_wait(barrier, 3)
            start(step)
            for copy in forward[:2]:
                copy.start()

        @pl.when(phase < size)
        def _():
            @pl.when((pair >= 1) & (pair + 1 < pairs))
            def _():
                signal(w_free)
                pl.semaphore_wait(w_free, 1)

            @pl.when(pair == 1)
            def _():
                for copy in fresh:
                    copy.start()

            for i in range(1, known - 1):

                @pl.when(pair == 1 + i)
                def _():
                    for copy in forward[2 * i : 2 * i + 2]:
                        copy.start()

            @pl.when(pair == size + 2)
            def _():
                for copy in fresh:
                    copy.wait_recv()
                for copy in forward[2 * known - 2 :]:
                    copy.start()

            @pl.when(pair + 1 < pairs)
            def _():
                start(pair + 1)

            @pl.when(pair >= 2)
            def _():
                keep(pair - 2).wait()

            @pl.when((pair >= 2) & (pair - 2 < early * size))
            def _():
                scatter(pair - 2)

            slot = lax.rem(pair, 2)
            for copy in weights(0, slot, 0):
                copy.wait()
            pair_of_experts(
                2 * pair, 2 * phase, w_buf.at[slot], rank_c, routes_ref, x_ref, gy_ref, y_buf, pick_buf, put
            )

        @pl.when((phase >= 1) & (phase <= size))
        def _():
            finish(pair - 1)

            @pl.when(pair + 1 < pairs)
            def _():
                signal(g_free)

        @pl.when(phase < size)
        def _():
            @pl.when(pair >= 2)
            def _():
                pl.semaphore_wait(g_free, 1)

            leave(lax.rem(pair, 2)).start()

        @pl.when(phase >= size)
        def _():
            block = phase - size
            at = pl.ds(pl.multiple_of(block * tile, tile), tile)
            made = nn(pick_buf[...], y_buf[:, at])

            @pl.when(call == 0)
            def _():
                total[:, at] = made.astype(bf16)

            @pl.when((call > 0) & (call < calls - 1))
            def _():
                total[:, at] = (made + total[:, at].astype(f32)).astype(bf16)

            @pl.when(call == calls - 1)
            def _():
                sums_out[...] = (made + total[:, at].astype(f32)).astype(bf16)

            before = (call - 1) * size + block

            @pl.when((call > 0) & (block >= 2) & (block < size + 2))
            def _():
                by_half(before - 2, lambda first: stores(before - 2, first).wait())

            @pl.when((call > 0) & (block >= 1) & (block < size + 1))
            def _():
                def add_to(first):
                    for copy in loads(before - 1)(first):
                        copy.wait()
                    add_buf[...] = (load_buf[0].astype(f32) + load_buf[1].astype(f32)).astype(bf16)
                    stores(before - 1, first).start()

                by_half(before - 1, add_to)

            @pl.when((call > 0) & (block < size))
            def _():
                def load(first):
                    crossing(before, first).wait_recv()
                    for copy in loads(before)(first):
                        copy.start()

                by_half(before, load)

        @pl.when(step == calls * period - 1)
        def _():
            for now in (pairs - 2, pairs - 1):
                keep(now).wait()
            for copy in (*forward, *fresh):
                copy.wait_send()
            for now in range(early * size):
                first = now % size < half
                crossing(now, first).wait_send()
                straight(now, first).wait()

    def held(step):
        return step // period * size + jnp.minimum(lax.rem(step, period), size - 1)

    def block(step):
        return (0, jnp.where(step >= (calls - 1) * period + size, step - (calls - 1) * period - size, 0))

    once = pl.Buffered(1)
    whole = pl.BlockSpec((rows, width), lambda s: (0, 0), pipeline_mode=once)
    anywhere = pl.BlockSpec(memory_space=pl.ANY)
    some = jax.ShapeDtypeStruct((early * half, height, lanes), bf16)
    regular = pltpu.SemaphoreType.REGULAR
    return pl.pallas_call(
        kernel,
        grid=(calls * period,),
        in_specs=[
            pl.BlockSpec((rows, HD), lambda s: (0, 0), pipeline_mode=once),
            pl.BlockSpec((2, 2, rows), lambda s: (held(s), 0, 0)),
            whole,
            whole,
        ]
        + [anywhere] * (n_in - 4),
        out_specs=[pl.BlockSpec((rows, tile), block)] + [anywhere] * (7 + 2 * unknown + 2 * early),
        out_shape=[
            jax.ShapeDtypeStruct((rows, 2 * width), bf16),
            jax.ShapeDtypeStruct((4, pairs, height, lanes), bf16),
        ]
        + [jax.ShapeDtypeStruct((size, height, lanes), bf16)] * (2 * unknown)
        + [jax.ShapeDtypeStruct((half, height, lanes), bf16)] * (2 * early)
        + [some] * 6,
        scratch_shapes=[
            pltpu.VMEM((2, width, lanes), bf16),
            pltpu.VMEM((2 * size * CAP, 2 * width), bf16),
            pltpu.VMEM((rows, 2 * size * CAP), bf16),
            pltpu.VMEM((rows, 2 * width), bf16),
            pltpu.VMEM((2, 4, height, lanes), bf16),
            pltpu.VMEM((2, 4, height, lanes), bf16),
            pltpu.VMEM((2, 4, height, lanes), bf16),
            pltpu.VMEM((2, height, lanes), bf16),
            pltpu.VMEM((height, lanes), bf16),
            dma((2, 4)),
            dma((2, 4)),
            dma((2, 4)),
            dma((2,)),
            dma((2,)),
            dma((2,)),
            dma((2,)),
            dma,
            dma((2 * early + 2 * unknown,)),
            dma((2 * early + 2 * unknown,)),
            dma((early * size,)),
            dma((early * size,)),
            dma((early * size,)),
            dma((early * size,)),
            regular,
            regular,
        ],
        compiler_params=pltpu.CompilerParams(
            vmem_limit_bytes=62 * 10**6, collective_id=1, has_side_effects=True
        ),
        cost_estimate=pl.CostEstimate(flops=2 * 10**11, bytes_accessed=10**8, transcendentals=0),
        name="experts",
    )(rank_cols, routes, x, gy, *packed, *(side for both in near for side in both), *far)


def remote(source, target, send_sem, recv_sem, device):
    return pltpu.make_async_remote_copy(
        src_ref=source,
        dst_ref=target,
        send_sem=send_sem,
        recv_sem=recv_sem,
        device_id=device,
        device_id_type=pl.DeviceIdType.MESH,
    )


def chip_neighbours():
    me = lax.axis_index("dp")
    return me + 2 - 4 * lax.rem(me // 2, 2), me + 4 - 8 * lax.rem(me // 4, 2)


def meet(members, core):
    barrier = pltpu.get_barrier_semaphore()
    z = lax.axis_index("tensor")

    def signal(device):
        pl.semaphore_signal(barrier, inc=1, device_id=device, device_id_type=pl.DeviceIdType.MESH)

    @pl.when(z > 0)
    def _():
        signal({"tensor": z - 1})

    @pl.when(z < members - 1)
    def _():
        signal({"tensor": z + 1})

    for other in (*chip_neighbours(), *([sibling()] if core else [])):
        signal({"dp": other})
    inner = jnp.where((z > 0) & (z < members - 1), 1, 0)
    pl.semaphore_wait(barrier, 3 + inner + (1 if core else 0))


class LineGather:
    def __init__(self, members, at, send, recv):
        self.members, self.at, self.send, self.recv = members, at, send, recv

    def copies(self, hop):
        z, last = lax.axis_index("tensor"), self.members - 1
        up, down = z - hop + 1, z + hop - 1

        def copy(block, way, device):
            return lambda: remote(
                self.at(block), self.at(block), self.send.at[way, hop - 1], self.recv.at[way, hop - 1], {"tensor": device}
            )

        return (
            ((up >= 0) & (z < last), copy(up, 0, z + 1)),
            ((down <= last) & (z > 0), copy(down, 1, z - 1)),
        ), (
            (z - hop >= 0, copy(z - hop, 0, z)),
            (z + hop <= last, copy(z + hop, 1, z)),
        )

    def start(self, hop):
        for present, copy in self.copies(hop)[0]:

            @pl.when(present)
            def _():
                copy().start()

    def arrive(self, hop):
        for present, copy in self.copies(hop)[1]:

            @pl.when(present)
            def _():
                copy().wait_recv()

    def close(self):
        for hop in range(1, self.members):
            for present, copy in self.copies(hop)[0]:

                @pl.when(present)
                def _():
                    copy().wait_send()


class LineSum:
    def __init__(self, members, part, leaving, arriving, send, recv):
        self.members, self.part, self.leaving, self.arriving = members, part, leaving, arriving
        self.send, self.recv = send, recv

    def copy(self, way, hop, device):
        return remote(
            self.leaving.at[way],
            self.arriving.at[way, hop - 1],
            self.send.at[way, hop - 1],
            self.recv.at[way, hop - 1],
            {"tensor": device},
        )

    def ways(self, hop):
        z, last = lax.axis_index("tensor"), self.members - 1
        return (
            (0, z - hop >= 0, z - hop, z < last, z - 1, (z < last) & (z + 1 - hop >= 0)),
            (1, z + hop <= last, z + hop, z > 0, z + 1, (z > 0) & (z - 1 + hop <= last)),
        )

    def start(self, hop, begun=True):
        if hop + 1 < self.members and begun:
            self.leave(hop + 1)
        for way, present, block, behind, device, _ in self.ways(hop):

            @pl.when(present)
            def _():
                self.leaving[way] = self.part(block).astype(bf16)

            if hop + 1 < self.members:

                @pl.when(present & behind)
                def _():
                    both = self.part(block).astype(f32) + self.arriving[way, hop].astype(f32)
                    self.leaving[way] = both.astype(bf16)

            @pl.when(present)
            def _():
                self.copy(way, hop, device).start()

    def arrive(self, hop):
        for way, _, _, _, device, present in self.ways(hop):

            @pl.when(present)
            def _():
                self.copy(way, hop, device).wait_recv()

    def total(self, out):
        z, last = lax.axis_index("tensor"), self.members - 1
        out[...] = self.part(z).astype(f32)
        for way, present in ((0, z < last), (1, z > 0)):

            @pl.when(present)
            def _():
                out[...] += self.arriving[way, 0].astype(f32)

    def leave(self, hop):
        for way, present, _, _, device, _ in self.ways(hop):

            @pl.when(present)
            def _():
                self.copy(way, hop, device).wait_send()

    def close(self):
        self.leave(1)


def swap_blocks(values):
    me = lax.axis_index("dp")
    chip = values.shape[1] // 4
    four = [values[:, i * chip : (i + 1) * chip] for i in range(4)]
    y_side, x_side, core_side = lax.rem(me // 4, 2) == 1, lax.rem(me // 2, 2) == 1, lax.rem(me, 2) == 1
    four = [jnp.where(y_side, four[i ^ 2], four[i]) for i in range(4)]
    four = [jnp.where(x_side, four[i ^ 1], four[i]) for i in range(4)]
    four = [jnp.where(core_side, pltpu.roll(part, chip // 2, 1), part) for part in four]
    return jnp.concatenate(four, axis=1)


def in_vmem(count):
    return [pl.BlockSpec(memory_space=pltpu.VMEM)] * count


def pack_chunk(gate, up, down, begin):
    gate, up, down = (
        jnp.swapaxes(w[:, begin : begin + 2 * CALL_PAIRS, :], 0, 1) for w in (gate, up, down)
    )

    def pair(a, b):
        return [a[:, :HD], b[:, :HD], jnp.concatenate([a[:, HD:], b[:, HD:]], axis=1)]

    def inner(a, b):
        a, b, tails = pair(a, b)
        return [a, tails, b]

    return [
        jnp.concatenate(
            pair(gate[e], up[e]) + pair(gate[e + 1], up[e + 1]) + inner(down[e], down[e + 1]), axis=1
        )
        for e in range(0, 2 * CALL_PAIRS, 2)
    ]


def turn(values, cosine, sine):
    return values * cosine + pltpu.roll(values, HD // 2, 1) * sine


def front(
    tokens, q_weight, o_weight, k_weight, v_weight, gains, cosine, sine, cotangent, ids, route_weights, gate, up, down, members, devices
):
    height, part = q_weight.shape
    own_rows, width = cotangent.shape
    rows = own_rows * members
    kv = 2 * KV * HD
    tall = kv + HD
    lanes = 9 * HD
    calls = EXPERTS // 2 // CALL_PAIRS
    half = CALL_PAIRS // 2
    heads = width // HD
    per_kv = heads // KV
    last = members - 1
    dma = pltpu.SemaphoreType.DMA

    def kernel(*refs):
        x_ref, q_weight_ref, o_ref, k_ref, v_ref, gains_ref, cos_ref, sin_ref, cot_ref = refs[:9]
        ids_ref, weights_ref, gate_ref, up_ref, down_ref = refs[9:14]
        square_all, tall_all, grad_all, rank_cols, routes = refs[14:19]
        normed_ref, q_ref, kv_all, mixed_ref, hidden_ref, rows_all = refs[19:25]
        packed = refs[25 : 25 + calls]
        from_x, from_y, far_x, far_y, next_x, next_y = refs[25 + calls : 31 + calls]
        after, rest = refs[31 + calls : 25 + 3 * calls], refs[25 + 3 * calls :]
        line_send, line_recv, grad_send, grad_recv, kv_send, kv_recv, row_send, row_recv = rest[:8]
        chip_send, chip_recv, core_send, core_recv = rest[8:]
        me, z = lax.axis_index("dp"), lax.axis_index("tensor")
        x_side, y_side = chip_neighbours()
        diagonal = x_side + y_side - me
        core = sibling()

        def rows_of(device):
            return pl.ds(pl.multiple_of(device * height, 16), height)

        def block_of(ref):
            return lambda block: ref.at[pl.ds(pl.multiple_of(block * own_rows, 16), own_rows)]

        own = pl.ds(pl.multiple_of(z * own_rows, 16), own_rows)

        def pack(call):
            chunk = pack_chunk(gate_ref, up_ref, down_ref, 2 * CALL_PAIRS * call)
            for pair, value in enumerate(chunk):
                packed[call][pair] = value

        def chip(index, source, device, target=None):
            target = source if target is None else target
            return remote(source, target, chip_send.at[index], chip_recv.at[index], {"dp": device})

        def across(index, source):
            return remote(source, source, core_send.at[index], core_recv.at[index], {"dp": core})

        def tall_at(device):
            return tall_all.at[rows_of(device)]

        def square_at(device, side=None):
            span = slice(None) if side is None else slice(side * part, (side + 1) * part)
            return square_all.at[:, rows_of(device), span]

        trades = []

        def trade(index, source):
            trades.append(across(index, source))
            trades[-1].start()

        def there(index, device, of):
            across(index, of(core if device is None else device + core - me)).wait_recv()

        square_all[z, rows_of(me), :part] = q_weight_ref[...]
        square_all[z, rows_of(me), part:] = o_ref[...]
        tall_all[rows_of(me), : kv // 2] = k_ref[...]
        tall_all[rows_of(me), kv // 2 : kv] = v_ref[...]
        tall_all[rows_of(me), kv:] = gains_ref[...]
        line = LineGather(members, lambda block: square_all.at[block, rows_of(me)], line_send, line_recv)
        group = LineGather(members, block_of(grad_all), grad_send, grad_recv)
        kv_line = LineGather(members, block_of(kv_all), kv_send, kv_recv)
        row_line = LineGather(members, block_of(rows_all), row_send, row_recv)
        moves = [
            chip(0, tall_at(me), x_side),
            chip(1, tall_at(me), y_side),
            chip(2, packed[0].at[:half], x_side, from_x.at[:half]),
            chip(3, packed[0].at[:half], y_side, from_y.at[:half]),
            chip(4, square_at(me), x_side),
            chip(5, square_at(me), y_side),
            chip(6, packed[0].at[half:], x_side, from_x.at[half:]),
            chip(7, packed[0].at[half:], y_side, from_y.at[half:]),
            chip(8, tall_at(x_side), y_side),
            chip(9, square_at(x_side, 0), y_side),
            chip(10, square_at(y_side, 1), x_side),
            chip(11, from_x.at[:half], y_side, far_x),
            chip(12, from_y.at[half:], x_side, far_y),
            chip(13, packed[1], x_side, next_x),
            chip(14, packed[1], y_side, next_y),
        ]
        for i in range(2, calls - 1):
            moves.append(chip(11 + 2 * i, packed[i], x_side, after[2 * i - 4]))
            moves.append(chip(12 + 2 * i, packed[i], y_side, after[2 * i - 3]))
        meet(members, True)
        line.start(1)
        for copy in moves[:2]:
            copy.start()
        trade(0, tall_at(me))
        pack(0)
        for copy in moves[2:4]:
            copy.start()
        for index, device in ((0, x_side), (1, y_side)):
            chip(index, tall_at(device), device).wait_recv()
        moves[8].start()
        trade(2, tall_at(x_side))
        trade(3, tall_at(y_side))
        line.arrive(1)
        if last > 1:
            line.start(2)
        grad_all[own, :] = swap_blocks(cot_ref[...]).astype(bf16)
        chip(8, tall_at(diagonal), y_side).wait_recv()
        trade(6, tall_at(diagonal))
        for hop in range(2, members):
            line.arrive(hop)
            if hop < last:
                line.start(hop + 1)
        for copy in moves[4:6]:
            copy.start()
        trade(1, square_at(me))

        for index, device in ((0, None), (2, x_side), (3, y_side), (6, diagonal)):
            there(index, device, tall_at)
        gain_one, gain_two = (jnp.transpose(tall_all[:, kv:].astype(f32))[i : i + 1] for i in range(2))
        cosine, sine = cos_ref[own], sin_ref[own]
        normed_ref[...] = (rms_pieces(x_ref[...].astype(f32))[1] * gain_one).astype(bf16)
        made = nn(normed_ref[...], tall_all[:, :kv])
        for head in range(KV):
            span = slice(head * HD, (head + 1) * HD)
            kv_all[own, span] = turn(made[:, span], cosine, sine).astype(bf16)
        kv_all[own, KV * HD :] = made[:, KV * HD :].astype(bf16)
        kv_line.start(1)

        expert = lax.broadcasted_iota(jnp.int32, (HD, rows), 0)
        weight = jnp.zeros((HD, rows), f32)
        named = jnp.zeros((HD, rows), f32)
        for route in range(ids_ref.shape[0]):
            here = ids_ref[route : route + 1, :] == expert
            named = jnp.where(here, 1.0, named)
            weight = jnp.where(here, weights_ref[route : route + 1, :], weight)
        row = lax.broadcasted_iota(jnp.int32, (rows, rows), 0)
        later = (row < lax.broadcasted_iota(jnp.int32, (rows, rows), 1)).astype(bf16)
        rank = jnp.where(named > 0.0, nn(named.astype(bf16), later), -1.0)
        rank_cols[...] = jnp.transpose(rank).astype(bf16)
        for e in range(EXPERTS):
            routes[e, 0:1, :] = rank[e : e + 1]
            routes[e, 1:2, :] = weight[e : e + 1]
        for call in range(1, calls):
            kv_line_hop = call
            if kv_line_hop < members:
                kv_line.arrive(kv_line_hop)
                if kv_line_hop < last:
                    kv_line.start(kv_line_hop + 1)
            pack(call)
        for hop in range(calls, members):
            kv_line.arrive(hop)
            if hop < last:
                kv_line.start(hop + 1)
        group.start(1)

        for index, device in ((4, x_side), (5, y_side)):
            chip(index, square_at(device), device).wait_recv()
        for copy in moves[9:11]:
            copy.start()
        trade(4, square_at(x_side))
        trade(5, square_at(y_side))
        chip(9, square_at(diagonal, 0), y_side).wait_recv()
        chip(10, square_at(diagonal, 1), x_side).wait_recv()
        trade(7, square_at(diagonal))
        for copy in moves[2:4]:
            copy.wait_recv()
        for copy in (*moves[6:8], moves[11]):
            copy.start()
        group.arrive(1)
        if last > 1:
            group.start(2)
        for index, device in ((1, None), (4, x_side), (5, y_side), (7, diagonal)):
            there(index, device, square_at)

        for t in range(members):
            made = nn(normed_ref[...], square_all[t, :, :part])
            for head in range(part // HD):
                span = slice(head * HD, (head + 1) * HD)
                q_ref[:, t * part + head * HD : t * part + (head + 1) * HD] = turn(
                    made[:, span], cosine, sine
                ).astype(bf16)

        def attend(begin, end):
            @pl.loop(begin, end)
            def _(head):
                span = pl.ds(pl.multiple_of(head * HD, HD), HD)
                key_span = pl.ds(pl.multiple_of(head // per_kv * HD, HD), HD)
                value_span = pl.ds(pl.multiple_of((KV + head // per_kv) * HD, HD), HD)
                p = probabilities(q_ref[:, span], kv_all[:, key_span], z * own_rows).astype(bf16)
                mixed_ref[:, span] = nn(p, kv_all[:, value_span]).astype(bf16)

        for copy in moves[13:15]:
            copy.start()
        attend(0, heads // 2)
        for hop in range(2, members):
            group.arrive(hop)
            if hop < last:
                group.start(hop + 1)
            if hop == 2:
                attend(heads // 2, heads)
        if members <= 2:
            attend(heads // 2, heads)
        hidden = x_ref[...].astype(f32)
        for t in range(members):
            hidden += nt(mixed_ref[:, t * part : (t + 1) * part], square_all[t, :, part:])
        hidden_ref[...] = hidden
        rows_all[own, :] = swap_blocks(rms_pieces(hidden)[1] * gain_two).astype(bf16)
        for hop in range(1, members):
            row_line.start(hop)
            if hop == 1:
                for copy in moves[6:8]:
                    copy.wait_recv()
                for copy in (moves[12], *moves[15:]):
                    copy.start()
            row_line.arrive(hop)
        for copy in moves[11:]:
            copy.wait_recv()
        for copy in moves + trades:
            copy.wait_send()
        for each in (line, group, kv_line, row_line):
            each.close()

    chunk_shape = jax.ShapeDtypeStruct((CALL_PAIRS, height, lanes), bf16)
    half_shape = jax.ShapeDtypeStruct((half, height, lanes), bf16)
    low_rows = jax.ShapeDtypeStruct((own_rows, width), bf16)
    return pl.pallas_call(
        kernel,
        in_specs=in_vmem(14),
        out_specs=in_vmem(11 + calls) + [pl.BlockSpec(memory_space=pl.ANY)] * (2 * calls),
        out_shape=[
            jax.ShapeDtypeStruct((members, devices * height, 2 * part), bf16),
            jax.ShapeDtypeStruct((devices * height, tall), bf16),
            jax.ShapeDtypeStruct((rows, width), bf16),
            jax.ShapeDtypeStruct((rows, HD), bf16),
            jax.ShapeDtypeStruct((EXPERTS, 2, rows), f32),
            low_rows,
            low_rows,
            jax.ShapeDtypeStruct((rows, kv), bf16),
            low_rows,
            jax.ShapeDtypeStruct((own_rows, width), f32),
            jax.ShapeDtypeStruct((rows, width), bf16),
        ]
        + [chunk_shape] * (calls + 2)
        + [half_shape] * 2
        + [chunk_shape] * (2 * calls - 4),
        scratch_shapes=[dma((2, members - 1))] * 8 + [dma((9 + 2 * calls,))] * 2 + [dma((8,))] * 2,
        compiler_params=pltpu.CompilerParams(collective_id=2, has_side_effects=True, vmem_limit_bytes=62 * 10**6),
        cost_estimate=pl.CostEstimate(flops=2 * 10**11, bytes_accessed=10**7, transcendentals=0),
        name="front",
    )(
        tokens,
        q_weight,
        o_weight,
        k_weight,
        v_weight,
        gains,
        cosine,
        sine,
        cotangent,
        ids,
        route_weights,
        gate,
        up,
        down,
    )


def gain_rows(tall_ref, kv):
    return jnp.transpose(tall_ref[:, kv:].astype(f32))


def attention_back(
    sums, cotangent, hidden, tokens, normed, q, kv_all, mixed, square, tall, cosine, sine, grads, to_x, to_y, members
):
    own_rows, width = tokens.shape
    rows = own_rows * members
    kv = 2 * KV * HD
    heads = width // HD
    per_kv = heads // KV
    part = width // members
    dma = pltpu.SemaphoreType.DMA

    def kernel(sums_ref, cot_ref, hidden_ref, x_ref, normed_ref, q_ref, kv_ref, mixed_ref, square_ref, tall_ref, *rest):
        cos_ref, sin_ref, grads_ref, to_x_ref, to_y_ref = rest[:5]
        grad_ref, moe_out, parts, x_before, y_before, x_last, y_last = rest[5:12]
        do_ref, dq_ref, dkv_ref, total, kv_total, stage, tall_part, back_part = rest[12:20]
        back_leave, back_arrive, moe_leave, moe_arrive, kv_leave, kv_arrive = rest[20:26]
        back_send, back_recv, moe_send, moe_recv, kv_send, kv_recv, stage_sem, part_sem = rest[26:34]
        through, added, added_sem, chip_send, chip_recv = rest[34:]
        z = lax.axis_index("tensor")
        x_side, y_side = chip_neighbours()
        first, second = slice(0, size // 2), slice(size // 2, size)

        def chunk(block, span):
            return grads_ref.at[block, pairs_before + span.start : pairs_before + span.stop]


        def chip(index, source, target, device):
            return remote(source, target, chip_send.at[index], chip_recv.at[index], {"dp": device})

        def sums_of(begin):
            return [
                pltpu.make_async_copy(
                    sums_ref.at[b * own_rows : (b + 1) * own_rows, begin : begin + width], back_part.at[b], part_sem.at[b]
                )
                for b in range(members)
            ]

        loads = sums_of(width) + [
            pltpu.make_async_copy(chunk(1, second), added.at[0], added_sem.at[0]),
            pltpu.make_async_copy(chunk(2, first), added.at[1], added_sem.at[1]),
        ]
        for copy in loads:
            copy.start()
        meet(members, False)
        moves = [
            chip(0, chunk(3, first), through.at[0], x_side),
            chip(1, chunk(3, second), through.at[1], y_side),
            chip(2, to_x_ref, x_before, x_side),
            chip(3, to_y_ref, y_before, y_side),
            chip(4, chunk(1, first), x_last.at[first], x_side),
            chip(5, chunk(2, second), y_last.at[second], y_side),
            chip(6, added.at[0], x_last.at[second], x_side),
            chip(7, added.at[1], y_last.at[first], y_side),
        ]
        for copy in moves[:6]:
            copy.start()
        own = pl.ds(pl.multiple_of(z * own_rows, 16), own_rows)
        for copy in loads:
            copy.wait()

        def block(ref, span):
            return lambda b: ref[pl.ds(pl.multiple_of(b * own_rows, 16), own_rows), span]

        back = LineSum(members, lambda b: back_part[b], back_leave, back_arrive, back_send, back_recv)
        moe = LineSum(members, lambda b: back_part[b], moe_leave, moe_arrive, moe_send, moe_recv)
        pairs = LineSum(members, block(dkv_ref, slice(None)), kv_leave, kv_arrive, kv_send, kv_recv)
        gains = gain_rows(tall_ref, kv)
        cosine, sine = cos_ref[own], sin_ref[own]
        last = members - 1
        stored = []

        def store(value, at):
            slot = len(stored) % 2
            if len(stored) >= 2:
                stored[-2].wait()
            stage[slot] = value.astype(bf16)
            copy = pltpu.make_async_copy(stage.at[slot], parts.at[:, at : at + part], stage_sem.at[slot])
            copy.start()
            stored.append(copy)

        for hop in range(last, 0, -1):
            back.start(hop)
            back.arrive(hop)
        back.total(total)
        loads = sums_of(0)
        for copy in loads:
            copy.start()
        normed_grad = swap_blocks(total[...])
        inverse, unit = rms_pieces(hidden_ref[...])
        for copy in loads:
            copy.wait()
        if last > 1:
            moe.start(last)
        by_hidden, gain_two = rms_backward(normed_grad, unit, inverse, gains[1:2])
        grad_ref[...] = cot_ref[...] + by_hidden
        low = grad_ref[...].astype(bf16)
        for t in range(members):
            span = slice(t * part, (t + 1) * part)
            do_ref[:, span] = nn(low, square_ref[t, :, part:]).astype(bf16)
            store(tn(low, mixed_ref[:, span]), t * part)
        dkv_ref[...] = jnp.zeros_like(dkv_ref)
        first_row = z * own_rows

        def attend(begin, end):
            @pl.loop(begin, end)
            def _(head):
                span = pl.ds(pl.multiple_of(head * HD, HD), HD)
                key_span = pl.ds(pl.multiple_of(head // per_kv * HD, HD), HD)
                value_span = pl.ds(pl.multiple_of((KV + head // per_kv) * HD, HD), HD)
                q_now, k_now, do_now = q_ref[:, span], kv_ref[:, key_span], do_ref[:, span]
                p = probabilities(q_now, k_now, first_row)
                dp = nt(do_now, kv_ref[:, value_span])
                ds = (p * (dp - jnp.sum(p * dp, axis=-1, keepdims=True))).astype(bf16)
                dq_ref[:, span] = turn(nn(ds, k_now) * (HD**-0.5), cosine, -sine).astype(bf16)
                dkv_ref[:, key_span] += tn(ds, q_now) * (HD**-0.5)
                dkv_ref[:, value_span] += tn(p.astype(bf16), do_now)

        attend(0, heads // 3)
        if last > 1:
            moe.arrive(last)
            if last > 2:
                moe.start(last - 1)
        attend(heads // 3, heads)

        pairs.start(last)

        def query_part(t):
            store(tn(normed_ref[...], dq_ref[:, t * part : (t + 1) * part]), width + t * part)

        def normed_part(t):
            made = nt(dq_ref[:, t * part : (t + 1) * part], square_ref[t, :, :part])
            if t == 0:
                total[...] = made
            else:
                total[...] += made

        for i, copy in enumerate(moves[:2]):
            copy.wait()
            added[1 - i] = (added[1 - i].astype(f32) + through[i].astype(f32)).astype(bf16)
            moves[7 - i].start()
        work = [(do, t) for do in (query_part, normed_part) for t in range(members)]
        share = len(work) // last
        for hop in range(last, 0, -1):
            for do, t in work[: share if hop > 1 else None]:
                do(t)
            work = work[share:]
            pairs.arrive(hop)
            if hop > 1:
                pairs.start(hop - 1)
        for hop in range(last - 1, 1, -1):
            moe.arrive(hop)
            if hop > 2:
                moe.start(hop - 1)
        for way, present in ((0, (z < last) & (z >= 1)), (1, (z > 0) & (z + 1 <= last))):

            @pl.when(present)
            def _():
                moe_out[way] = moe_arrive[way, 1]

            @pl.when(jnp.logical_not(present))
            def _():
                moe_out[way] = jnp.zeros((own_rows, width), bf16)

        pairs.total(kv_total)
        low_kv = [
            turn(kv_total[:, head * HD : (head + 1) * HD], cosine, -sine).astype(bf16) for head in range(KV)
        ] + [kv_total[:, KV * HD :].astype(bf16)]
        low_kv = jnp.concatenate(low_kv, axis=1)
        normed_grad = total[...] + nt(low_kv, tall_ref[:, :kv])
        inverse, unit = rms_pieces(x_ref[...].astype(f32))
        by_tokens, gain_one = rms_backward(normed_grad, unit, inverse, gains[0:1])
        grad_ref[...] += by_tokens
        tall_part[:, :kv] = tn(normed_ref[...], low_kv).astype(bf16)
        row = lax.broadcasted_iota(jnp.int32, (HD, width), 0)
        both = jnp.where(row == 0, gain_one[None], jnp.where(row == 1, gain_two[None], 0.0))
        tall_part[:, kv:] = jnp.transpose(both).astype(bf16)
        tall_copy = pltpu.make_async_copy(tall_part, parts.at[:, 2 * width :], stage_sem.at[2])
        tall_copy.start()
        for line in (back, pairs):
            line.close()
        if last > 1:
            moe.leave(2)
        for copy in (*stored[-2:], tall_copy, *moves[2:]):
            copy.wait()

    hops = (2, members - 1)
    anywhere = pl.BlockSpec(memory_space=pl.ANY)
    _, height, lanes = to_x.shape
    size = CALL_PAIRS
    pairs_before = grads.shape[1] - size
    halves = (2, size // 2, height, lanes)
    return pl.pallas_call(
        kernel,
        in_specs=[anywhere] + in_vmem(11) + [anywhere] * 3,
        out_specs=in_vmem(2) + [anywhere] * 5,
        out_shape=[
            jax.ShapeDtypeStruct((own_rows, width), f32),
            jax.ShapeDtypeStruct((2, own_rows, width), bf16),
            jax.ShapeDtypeStruct((width, 2 * width + tall.shape[1]), bf16),
        ]
        + [jax.ShapeDtypeStruct(to_x.shape, bf16)] * 2
        + [jax.ShapeDtypeStruct((size, height, lanes), bf16)] * 2,
        scratch_shapes=[
            pltpu.VMEM((own_rows, width), bf16),
            pltpu.VMEM((own_rows, width), bf16),
            pltpu.VMEM((rows, kv), f32),
            pltpu.VMEM((own_rows, width), f32),
            pltpu.VMEM((own_rows, kv), f32),
            pltpu.VMEM((2, width, part), bf16),
            pltpu.VMEM(tall.shape, bf16),
            pltpu.VMEM((members, own_rows, width), bf16),
            pltpu.VMEM((2, own_rows, width), bf16),
            pltpu.VMEM((*hops, own_rows, width), bf16),
            pltpu.VMEM((2, own_rows, width), bf16),
            pltpu.VMEM((*hops, own_rows, width), bf16),
            pltpu.VMEM((2, own_rows, kv), bf16),
            pltpu.VMEM((*hops, own_rows, kv), bf16),
        ]
        + [dma(hops)] * 6
        + [dma((3,)), dma((members,)), pltpu.VMEM(halves, bf16), pltpu.VMEM(halves, bf16), dma((2,)), dma((8,)), dma((8,))],
        compiler_params=pltpu.CompilerParams(collective_id=4, has_side_effects=True, vmem_limit_bytes=62 * 10**6),
        cost_estimate=pl.CostEstimate(flops=10**11, bytes_accessed=10**7, transcendentals=0),
        name="attention_back",
    )(
        sums, cotangent, hidden, tokens, normed, q, kv_all, mixed, square, tall, cosine, sine, grads, to_x, to_y
    )


def reduce_small(parts, sums, moved, hidden, members, devices):
    own_rows = hidden.shape[0]
    width = parts.shape[0]
    height = width // devices
    lanes = parts.shape[1]
    tall = lanes - 2 * width
    kv = KV * HD
    part = width // members
    half = height // 2
    groups = (slice(0, width), slice(width, lanes))
    dma = pltpu.SemaphoreType.DMA

    def kernel(parts_ref, sums_ref, moved_ref, hidden_ref, out_ref, q_out, o_out, k_out, v_out, gains_out, *rest):
        own, theirs, leave, arrive, blocks, line_leave, line_arrive, tall_all, line_total = rest[:9]
        moe_part, moe_leave, moe_arrive, total_ref = rest[9:13]
        own_sem, core_send, core_recv, chip_send, chip_recv = rest[13:18]
        o_send, o_recv, q_send, q_recv, tall_send, tall_recv, moe_send, moe_recv, part_sem = rest[18:]
        me, z = lax.axis_index("dp"), lax.axis_index("tensor")
        x_side, y_side = chip_neighbours()
        core = sibling()
        chips = [me, x_side, y_side, x_side + y_side - me]
        loads = [
            pltpu.make_async_copy(
                sums_ref.at[b * own_rows : (b + 1) * own_rows, :width], moe_part.at[b], part_sem.at[b]
            )
            for b in range(members)
        ]
        for copy in loads:
            copy.start()

        def rows(device, span):
            return parts_ref.at[pl.ds(pl.multiple_of(device * height, 16), height), span]

        def trade(m, g):
            target = theirs.at[m, :, groups[g]]
            source = rows(chips[m] + core - me, groups[g])
            return remote(source, target, core_send.at[m, g], core_recv.at[m, g], {"dp": core})

        def keep(m, g):
            return pltpu.make_async_copy(rows(chips[m], groups[g]), own.at[m, :, groups[g]], own_sem.at[m, g])

        order = (3, 2, 1, 0)
        for g in range(2):
            for m in order:
                keep(m, g).start()
        meet(members, True)
        for g in range(2):
            for m in order:
                trade(m, g).start()
        moe = LineSum(members, lambda b: moe_part[b], moe_leave, moe_arrive, moe_send, moe_recv)
        if members > 2:
            for way in range(2):
                moe_arrive[way, 1] = moved_ref[way]
        for copy in loads:
            copy.wait()
        moe.start(1, False)

        def both(m, rows, lanes):
            return own[m, rows, lanes].astype(f32) + theirs[m, rows, lanes].astype(f32)

        def chip(index, g, slot, span, device):
            source, target = leave.at[slot, span, groups[g]], arrive.at[slot, span, groups[g]]
            return remote(source, target, chip_send.at[index, g], chip_recv.at[index, g], {"dp": device})

        first, second = slice(0, half), slice(half, height)
        every = slice(0, height)
        far = [[chip(0, g, 0, first, x_side), chip(1, g, 0, second, y_side)] for g in range(2)]
        near = [[chip(2, g, 1, every, x_side), chip(3, g, 2, every, y_side)] for g in range(2)]

        def ready(m, g):
            trade(m, g).wait()
            keep(m, g).wait()

        for g, span in enumerate(groups):
            ready(3, g)
            for copy, part_of in zip(far[g], (first, second)):
                leave[0, part_of, span] = both(3, part_of, span).astype(bf16)
                copy.start()
            for m in order[1:]:
                ready(m, g)
        for g, span in enumerate(groups):
            leave[1, first, span] = both(1, first, span).astype(bf16)
            leave[2, second, span] = both(2, second, span).astype(bf16)
            far[g][1].wait()
            leave[1, second, span] = (both(1, second, span) + arrive[0, second, span].astype(f32)).astype(bf16)
            near[g][0].start()
            far[g][0].wait()
            leave[2, first, span] = (both(2, first, span) + arrive[0, first, span].astype(f32)).astype(bf16)
            near[g][1].start()
        moe.arrive(1)
        moe.total(total_ref)
        out_ref[...] = (hidden_ref[...] + swap_blocks(total_ref[...])).astype(bf16)

        def total(span):
            return both(0, every, span) + arrive[1, :, span].astype(f32) + arrive[2, :, span].astype(f32)

        lines = [
            LineSum(members, lambda b, g=g: blocks[g, b], line_leave.at[g], line_arrive.at[g], send, recv)
            for g, (send, recv) in enumerate(((o_send, o_recv), (q_send, q_recv)))
        ]
        group = LineGather(members, lambda b: tall_all.at[b], tall_send, tall_recv)

        def hop_of(line, hop):
            line.arrive(hop)
            if hop > 1:
                line.start(hop - 1)

        last = members - 1
        for copy in near[0]:
            copy.wait()
        for t in range(members):
            blocks[0, t] = total(slice(t * part, (t + 1) * part))
        lines[0].start(last)
        for copy in near[1]:
            copy.wait()
        tall_all[z] = total(slice(2 * width, lanes)).astype(bf16)
        for t in range(members):
            blocks[1, t] = total(slice(width + t * part, width + (t + 1) * part))
        lines[1].start(last)
        group.start(1)
        for hop in range(last, 0, -1):
            hop_of(lines[0], hop)
            hop_of(lines[1], hop)
            group.arrive(members - hop)
            if hop > 1:
                group.start(members - hop + 1)
        lines[0].total(line_total)
        o_out[...] = line_total[...]
        lines[1].total(line_total)
        q_out[...] = line_total[...]
        summed = tall_all[0].astype(f32)
        for t in range(1, members):
            summed += tall_all[t].astype(f32)
        k_out[...] = summed[:, :kv]
        v_out[...] = summed[:, kv : 2 * kv]
        gains_out[...] = summed[:, 2 * kv :]
        for line in (*lines, group, moe):
            line.close()

    hops = (2, members - 1)
    return pl.pallas_call(
        kernel,
        in_specs=[pl.BlockSpec(memory_space=pl.ANY)] * 2 + in_vmem(2),
        out_specs=in_vmem(6),
        out_shape=[
            jax.ShapeDtypeStruct((own_rows, width), bf16),
            jax.ShapeDtypeStruct((height, part), f32),
            jax.ShapeDtypeStruct((height, part), f32),
            jax.ShapeDtypeStruct((height, kv), f32),
            jax.ShapeDtypeStruct((height, kv), f32),
            jax.ShapeDtypeStruct((height, tall - 2 * kv), f32),
        ],
        scratch_shapes=[
            pltpu.VMEM((4, height, lanes), bf16),
            pltpu.VMEM((4, height, lanes), bf16),
            pltpu.VMEM((3, height, lanes), bf16),
            pltpu.VMEM((3, height, lanes), bf16),
            pltpu.VMEM((2, members, height, part), f32),
            pltpu.VMEM((2, 2, height, part), bf16),
            pltpu.VMEM((2, *hops, height, part), bf16),
            pltpu.VMEM((members, height, tall), bf16),
            pltpu.VMEM((height, part), f32),
            pltpu.VMEM((members, own_rows, width), bf16),
            pltpu.VMEM((2, own_rows, width), bf16),
            pltpu.VMEM((*hops, own_rows, width), bf16),
            pltpu.VMEM((own_rows, width), f32),
            dma((4, 2)),
            dma((4, 2)),
            dma((4, 2)),
            dma((4, 2)),
            dma((4, 2)),
        ]
        + [dma(hops)] * 8
        + [dma((members,))],
        compiler_params=pltpu.CompilerParams(collective_id=5, has_side_effects=True, vmem_limit_bytes=60 * 2**20),
        cost_estimate=pl.CostEstimate(flops=8 * 10**10, bytes_accessed=10**7, transcendentals=0),
        name="reduce_small",
    )(parts, sums, moved, hidden)


def unpack_all(grads, plain, added, last):
    _, pairs, height, lanes = grads.shape
    half = CALL_PAIRS // 2
    units = lanes // 6
    tail = units - HD
    step = 48 if height % 48 == 0 else height
    others = (*plain, *added, *last)

    def kernel(own, plain_x, plain_y, added_x, added_y, last_x, last_y, gate, up, down):
        for call in range(pairs // CALL_PAIRS):
            found = [[], [], []]
            for turn in range(CALL_PAIRS):
                pair = call * CALL_PAIRS + turn
                at = call * half + turn % half
                if pair >= pairs - CALL_PAIRS:
                    by_x, by_y = last_x[turn], last_y[turn]
                elif turn < half:
                    by_x, by_y = plain_x[at], added_y[at]
                else:
                    by_x, by_y = added_x[at], plain_y[at]
                value = own[0, pair].astype(f32) + by_x.astype(f32) + by_y.astype(f32)
                tiles = [value[:, i * HD : (i + 1) * HD] for i in range(9)]
                for i, (a, b, both) in enumerate(((0, 1, 2), (3, 4, 5), (6, 8, 7))):
                    left = jnp.concatenate([tiles[a], tiles[both][:, :tail]], axis=1)
                    right = jnp.concatenate([tiles[b], tiles[both][:, tail:]], axis=1)
                    if i < 2:
                        found[0].append(left)
                        found[1].append(right)
                    else:
                        found[2] += [left, right]
            span = slice(2 * CALL_PAIRS * call, 2 * CALL_PAIRS * (call + 1))
            for out, values in zip((gate, up, down), found):
                out[:, span, :] = jnp.swapaxes(jnp.stack(values), 0, 1)

    shape = (height, 2 * pairs, units)
    return pl.pallas_call(
        kernel,
        grid=(height // step,),
        in_specs=[pl.BlockSpec((1, pairs, step, lanes), lambda i: (0, 0, i, 0))]
        + [pl.BlockSpec((other.shape[0], step, lanes), lambda i: (0, i, 0)) for other in others],
        out_specs=[pl.BlockSpec((step, *shape[1:]), lambda i: (i, 0, 0))] * 3,
        out_shape=[jax.ShapeDtypeStruct(shape, f32)] * 3,
        compiler_params=pltpu.CompilerParams(vmem_limit_bytes=48 * 2**20),
        name="unpack",
    )(grads, *others)


def pack(gate, up, down):
    def pair(a, b):
        return jnp.concatenate([a[..., :HD], b[..., :HD], a[..., HD:], b[..., HD:]], axis=-1)

    gate, up, down = (jnp.transpose(w, (1, 0, 2)) for w in (gate, up, down))
    gate_up = pair(gate, up)
    a, b = down[0::2], down[1::2]
    inner = jnp.concatenate([a[..., :HD], a[..., HD:], b[..., HD:], b[..., :HD]], axis=-1)
    return jnp.concatenate([gate_up[0::2], gate_up[1::2], inner], axis=-1)


def unpack(packed):
    n, height, lanes = packed.shape
    third = lanes // 3

    def halves(both):
        tail = third // 2 - HD
        a = jnp.concatenate([both[..., :HD], both[..., 2 * HD : 2 * HD + tail]], axis=-1)
        b = jnp.concatenate([both[..., HD : 2 * HD], both[..., 2 * HD + tail :]], axis=-1)
        return a, b

    def experts(even, odd):
        both = jnp.stack([even, odd], axis=1).reshape(2 * n, height, third // 2)
        return jnp.transpose(both, (1, 0, 2))

    gate0, up0 = halves(packed[..., :third])
    gate1, up1 = halves(packed[..., third : 2 * third])
    down0, down1 = packed[..., 2 * third : 2 * third + third // 2], packed[..., 2 * third + third // 2 :]
    tail = third // 2 - HD
    down1 = jnp.concatenate([down1[..., tail:], down1[..., :tail]], axis=-1)
    return experts(gate0, gate1), experts(up0, up1), experts(down0, down1)


def routes_of(expert_ids, route_weights):
    rows = expert_ids.shape[0]
    lanes = jnp.arange(EXPERTS, dtype=jnp.int32)
    named = expert_ids[:, :, None] == lanes
    member_of = jnp.any(named, axis=1)
    weight_of = jnp.sum(jnp.where(named, route_weights[:, :, None], 0.0), axis=1)
    earlier = jnp.arange(rows)[:, None] > jnp.arange(rows)[None, :]
    rank = jnp.where(member_of, nn(earlier.astype(bf16), member_of.astype(bf16)), -1.0)
    rank_cols = jnp.pad(rank, ((0, 0), (0, HD)), constant_values=-1.0).astype(bf16)
    return rank_cols, jnp.stack([rank.T, weight_of.T], axis=1)


def body_anywhere(
    tokens,
    expert_ids,
    route_weights,
    attn_gain,
    q_weight,
    k_weight,
    v_weight,
    o_weight,
    moe_gain,
    gate_weight,
    up_weight,
    down_weight,
    cotangent,
):
    members = lax.axis_size("tensor")
    member = lax.axis_index("tensor")
    own_rows, width = tokens.shape
    rows = own_rows * members
    pairs = EXPERTS // 2
    calls = pairs // CALL_PAIRS

    packed = [
        pack(*(w[:, 2 * CALL_PAIRS * i : 2 * CALL_PAIRS * (i + 1)] for w in (gate_weight, up_weight, down_weight)))
        for i in range(calls)
    ]
    gathered = [lax.all_gather(own, "dp", axis=1, tiled=True) for own in packed]

    gain_one = lax.all_gather(attn_gain, "dp", axis=0, tiled=True).astype(f32)
    gain_two = lax.all_gather(moe_gain, "dp", axis=0, tiled=True).astype(f32)
    kv_full = lax.all_gather(jnp.concatenate([k_weight, v_weight], axis=1), "dp", axis=0, tiled=True)
    q_full = lax.all_gather(lax.all_gather(q_weight, "dp", axis=0, tiled=True), "tensor", axis=0)
    o_full = lax.all_gather(lax.all_gather(o_weight, "dp", axis=0, tiled=True), "tensor", axis=0)
    kv_width = k_weight.shape[1]

    rank_cols, routes = routes_of(expert_ids, route_weights)

    grad_low = cotangent.astype(bf16)
    grad_all = lax.all_gather(grad_low, "tensor", axis=0, tiled=True)

    x = tokens.astype(f32)
    inverse_one, unit_one = rms_pieces(x)
    normed_one = (unit_one * gain_one).astype(bf16)
    first_row = (member * own_rows).reshape(1)
    cos_table, sin_table = rope_tables(member * own_rows + jnp.arange(own_rows, dtype=jnp.int32))
    kv_own = nn(normed_one, kv_full)
    kv_own = jnp.concatenate(
        [rotate(kv_own[:, :kv_width], cos_table, sin_table), kv_own[:, kv_width:]], axis=1
    ).astype(bf16)
    kv_all = lax.all_gather(kv_own, "tensor", axis=0, tiled=True)
    keys, values = kv_all[:, :kv_width], kv_all[:, kv_width:]
    queries = jnp.concatenate([nn(normed_one, q_full[t]) for t in range(members)], axis=1)
    queries = rotate(queries, cos_table, sin_table).astype(bf16)
    mixed = attend_forward(first_row, queries, keys, values)
    part = width // members
    branch = sum(nt(mixed[:, t * part : (t + 1) * part], o_full[t]) for t in range(members))
    hidden = x + branch
    inverse_two, unit_two = rms_pieces(hidden)
    normed_two = (unit_two * gain_two).astype(bf16)
    rows_all = lax.all_gather(normed_two, "tensor", axis=0, tiled=True)

    sums = jnp.zeros((rows, 2 * width), f32)
    chunks = []
    for call in range(calls):
        some = slice(2 * CALL_PAIRS * call, 2 * CALL_PAIRS * (call + 1))
        columns = slice(2 * CALL_PAIRS * call, 2 * CALL_PAIRS * call + HD)
        grads, sums = expert_call(
            rank_cols[:, columns],
            routes[some],
            rows_all,
            grad_all,
            gathered[call],
            sums,
        )
        chunks.append(grads)
    shares = [
        unpack(lax.psum_scatter(grads, "dp", scatter_dimension=1, tiled=True).astype(f32)) for grads in chunks
    ]
    gate_out, up_out, down_out = (jnp.concatenate(parts, axis=1) for parts in zip(*shares))

    low_sums = sums.astype(bf16)
    normed_grad = lax.psum_scatter(low_sums[:, width:], "tensor", scatter_dimension=0, tiled=True).astype(f32)
    moe_own = lax.psum_scatter(low_sums[:, :width], "tensor", scatter_dimension=0, tiled=True).astype(f32)
    output = (hidden + moe_own).astype(bf16)

    back_two, gain_two_part = rms_backward(normed_grad, unit_two, inverse_two, gain_two)
    hidden_grad = cotangent + back_two
    hidden_low = hidden_grad.astype(bf16)
    mixed_grad = jnp.concatenate([nn(hidden_low, o_full[t]) for t in range(members)], axis=1).astype(bf16)
    o_part = jnp.stack([tn(hidden_low, mixed[:, t * part : (t + 1) * part]) for t in range(members)])
    dq, dk, dv = attend_backward(first_row, queries, keys, values, mixed_grad)
    kv_grad = lax.psum_scatter(
        jnp.concatenate([dk, dv], axis=1).astype(bf16), "tensor", scatter_dimension=0, tiled=True
    ).astype(f32)
    dq_low = rotate(dq, cos_table, -sin_table).astype(bf16)
    kv_low = jnp.concatenate(
        [rotate(kv_grad[:, :kv_width], cos_table, -sin_table), kv_grad[:, kv_width:]], axis=1
    ).astype(bf16)
    normed_one_grad = nt(kv_low, kv_full) + sum(
        nt(dq_low[:, t * part : (t + 1) * part], q_full[t]) for t in range(members)
    )
    back_one, gain_one_part = rms_backward(normed_one_grad, unit_one, inverse_one, gain_one)
    tokens_grad = hidden_grad + back_one
    q_part = jnp.stack([tn(normed_one, dq_low[:, t * part : (t + 1) * part]) for t in range(members)])
    kv_part = tn(normed_one, kv_low)

    def shared(values):
        summed = lax.psum_scatter(values.astype(bf16), "tensor", scatter_dimension=0, tiled=False)
        return lax.psum_scatter(summed, "dp", scatter_dimension=0, tiled=True).astype(f32)

    q_grad, o_grad = shared(q_part), shared(o_part)
    small = jnp.concatenate([kv_part, gain_one_part[:, None], gain_two_part[:, None]], axis=1)
    small = lax.psum_scatter(small, "dp", scatter_dimension=0, tiled=True)
    small = lax.psum(small.astype(bf16), "tensor").astype(f32)
    return (
        output,
        tokens_grad,
        small[:, 2 * kv_width],
        q_grad,
        small[:, :kv_width],
        small[:, kv_width : 2 * kv_width],
        o_grad,
        small[:, 2 * kv_width + 1],
        gate_out,
        up_out,
        down_out,
    )

def body_by_chips(
    tokens,
    expert_ids,
    route_weights,
    attn_gain,
    q_weight,
    k_weight,
    v_weight,
    o_weight,
    moe_gain,
    gate_weight,
    up_weight,
    down_weight,
    cotangent,
):
    members = lax.axis_size("tensor")
    member = lax.axis_index("tensor")
    devices = lax.axis_size("dp")
    own_rows, width = tokens.shape
    rows = own_rows * members
    calls = EXPERTS // 2 // CALL_PAIRS

    gains = jnp.pad(jnp.stack([attn_gain, moe_gain], axis=1), ((0, 0), (0, HD - 2)))
    cosine, sine = doubled_tables(rows)
    square_all, tall_all, grad_all, rank_cols, routes, normed_one, queries, kv_all, mixed, hidden, rows_all, *chunks = front(
        tokens,
        q_weight,
        o_weight,
        k_weight,
        v_weight,
        gains,
        cosine,
        sine,
        cotangent,
        expert_ids.T,
        route_weights.T,
        gate_weight,
        up_weight,
        down_weight,
        members,
        devices,
    )
    packed, (from_x, from_y, far_x, far_y, *after) = chunks[:calls], chunks[calls:]
    near = [(from_x, from_y), *zip(after[0::2], after[1::2])]
    sums, grads, *others = expert_pass(
        rank_cols, routes, rows_all, grad_all, packed, near, (far_x, far_y), members
    )
    plain, added = others[-6:-4], others[-4:-2]
    tokens_grad, moe_moved, parts, *moved = attention_back(
        sums,
        cotangent,
        hidden,
        tokens,
        normed_one,
        queries,
        kv_all,
        mixed,
        square_all,
        tall_all,
        cosine,
        sine,
        grads,
        *added,
        members,
    )
    output, q_grad, o_grad, k_grad, v_grad, gain_grads = reduce_small(parts, sums, moe_moved, hidden, members, devices)
    gate_out, up_out, down_out = unpack_all(grads, plain, moved[:2], moved[2:])
    return (
        output,
        tokens_grad,
        gain_grads[:, 0],
        q_grad,
        k_grad,
        v_grad,
        o_grad,
        gain_grads[:, 1],
        gate_out,
        up_out,
        down_out,
    )


def doubled_tables(rows):
    half = HD // 2
    frequency = np.float32(rope_base) ** -(np.arange(half, dtype=np.float32) * np.float32(2.0 / HD))
    angles = (np.arange(rows) % SEQ).astype(np.float32)[:, None] * frequency
    cosine, sine = np.cos(angles), np.sin(angles)
    return jnp.asarray(np.concatenate([cosine, cosine], axis=1)), jnp.asarray(np.concatenate([-sine, sine], axis=1))


def solution(mesh):
    rows = P(("dp", "tensor"), None)
    experts = P("dp", None, "tensor")
    square = P("dp", "tensor")
    tall = P("dp", None)
    return jax.shard_map(
        body_by_chips if mesh.shape["dp"] == 8 else body_anywhere,
        mesh=mesh,
        in_specs=(
            rows, tall, tall, P("dp"), square, tall, tall, square, P("dp"), experts, experts, experts, rows
        ),
        out_specs=(rows, rows, P("dp"), square, tall, tall, square, P("dp"), experts, experts, experts),
        check_vma=False,
    )
```

```python
import jax
import jax.numpy as jnp
import numpy as np
from jax import lax
from jax.experimental import pallas as pl
from jax.experimental.pallas import tpu as pltpu
from jax.sharding import PartitionSpec as P

KV = 2
HD = 128
EXPERTS = 32
TOPK = 4
SEQ = 1024
BLOCK = 256
CAP = 256
TAIL = 64
CALL_PAIRS = 4
STRAIGHT = 2

eps = 1e-06
rope_base = 1000000.0
negative = -1e30
bf16 = jnp.bfloat16
f32 = jnp.float32


def nn(a, b):
    return jnp.dot(a, b, preferred_element_type=f32)


def nt(a, b):
    return lax.dot_general(a, b, (((1,), (1,)), ((), ())), preferred_element_type=f32)


def tn(a, b):
    return lax.dot_general(a, b, (((0,), (0,)), ((), ())), preferred_element_type=f32)


def rope_tables(positions):
    half = HD // 2
    frequency = rope_base ** (-(jnp.arange(half).astype(f32) * 2.0 / HD))
    angles = positions.astype(f32)[:, None] * frequency[None, :]
    return jnp.cos(angles), jnp.sin(angles)


def rotate(values, cos_table, sin_table):
    rows = values.shape[0]
    heads = values.reshape(rows, -1, 2, HD // 2)
    a, b = heads[:, :, 0], heads[:, :, 1]
    cos_table, sin_table = cos_table[:, None], sin_table[:, None]
    turned = jnp.stack([a * cos_table - b * sin_table, b * cos_table + a * sin_table], axis=2)
    return turned.reshape(rows, -1)


def rms_pieces(x):
    inverse = lax.rsqrt(jnp.mean(x * x, axis=-1, keepdims=True) + eps)
    return inverse, x * inverse


def rms_backward(grad, unit, inverse, gain):
    u = grad * gain
    back = inverse * (u - unit * jnp.mean(u * unit, axis=-1, keepdims=True))
    return back, jnp.sum(grad * unit, axis=0)


def probabilities(q, k, first_row):
    rows, keys = q.shape[0], k.shape[0]
    scores = nt(q, k) * (HD**-0.5)
    q_block = (first_row + lax.broadcasted_iota(jnp.int32, (rows, keys), 0)) // BLOCK
    k_block = lax.broadcasted_iota(jnp.int32, (rows, keys), 1) // BLOCK
    scores = jnp.where(k_block <= q_block, scores, negative)
    raised = jnp.exp(scores - jnp.max(scores, axis=-1, keepdims=True))
    return raised / jnp.sum(raised, axis=-1, keepdims=True)


def attend_forward(first_row, q, k, v):
    rows, width = q.shape
    heads = width // HD
    shared = heads // KV

    def kernel(first_ref, q_ref, k_ref, v_ref, o_ref):
        p = probabilities(q_ref[...], k_ref[...], first_ref[0]).astype(bf16)
        o_ref[...] = nn(p, v_ref[...]).astype(bf16)

    per_head = pl.BlockSpec((rows, HD), lambda h, f: (0, h))
    per_kv = pl.BlockSpec((k.shape[0], HD), lambda h, f: (0, h // shared))
    return pl.pallas_call(
        kernel,
        grid_spec=pltpu.PrefetchScalarGridSpec(
            num_scalar_prefetch=1,
            grid=(heads,),
            in_specs=[per_head, per_kv, per_kv],
            out_specs=per_head,
        ),
        out_shape=jax.ShapeDtypeStruct((rows, width), bf16),
        compiler_params=pltpu.CompilerParams(vmem_limit_bytes=32 * 2**20),
        cost_estimate=pl.CostEstimate(
            flops=4 * rows * width * k.shape[0],
            bytes_accessed=4 * rows * width,
            transcendentals=rows * heads * k.shape[0],
        ),
        name="attend",
    )(first_row, q, k, v)


def attend_backward(first_row, q, k, v, do):
    rows, width = q.shape
    keys = k.shape[0]
    heads = width // HD
    shared = heads // KV

    def kernel(first_ref, q_ref, k_ref, v_ref, do_ref, dq_ref, dk_ref, dv_ref):
        q_now, k_now, v_now, do_now = q_ref[...], k_ref[...], v_ref[...], do_ref[...]
        p = probabilities(q_now, k_now, first_ref[0])
        dp = nt(do_now, v_now)
        ds = (p * (dp - jnp.sum(p * dp, axis=-1, keepdims=True))).astype(bf16)
        dq_ref[...] = nn(ds, k_now) * (HD**-0.5)
        dk = tn(ds, q_now) * (HD**-0.5)
        dv = tn(p.astype(bf16), do_now)
        head = pl.program_id(0)

        @pl.when(lax.rem(head, shared) == 0)
        def _():
            dk_ref[...] = dk
            dv_ref[...] = dv

        @pl.when(lax.rem(head, shared) != 0)
        def _():
            dk_ref[...] += dk
            dv_ref[...] += dv

    per_head = pl.BlockSpec((rows, HD), lambda h, f: (0, h))
    per_kv = pl.BlockSpec((keys, HD), lambda h, f: (0, h // shared))
    return pl.pallas_call(
        kernel,
        grid_spec=pltpu.PrefetchScalarGridSpec(
            num_scalar_prefetch=1,
            grid=(heads,),
            in_specs=[per_head, per_kv, per_kv, per_head],
            out_specs=[per_head, per_kv, per_kv],
        ),
        out_shape=[
            jax.ShapeDtypeStruct((rows, width), f32),
            jax.ShapeDtypeStruct((keys, KV * HD), f32),
            jax.ShapeDtypeStruct((keys, KV * HD), f32),
        ],
        compiler_params=pltpu.CompilerParams(vmem_limit_bytes=32 * 2**20),
        cost_estimate=pl.CostEstimate(
            flops=10 * rows * width * keys,
            bytes_accessed=8 * rows * width,
            transcendentals=rows * heads * keys,
        ),
        name="attend_back",
    )(first_row, q, k, v, do)


def sibling():
    me = lax.axis_index("dp")
    return me + 1 - 2 * lax.rem(me, 2)


def pair_of_experts(expert, place, w, rank_c, routes_ref, x_ref, gy_ref, y_buf, pick_buf, put):
    rows, width = x_ref.shape
    lanes = w.shape[1]
    third = lanes // 3
    low_half = lax.broadcasted_iota(jnp.int32, (CAP, HD), 1) < TAIL
    slot_of = lax.broadcasted_iota(jnp.int32, (rows, CAP), 1).astype(f32)
    slot_at = lax.broadcasted_iota(jnp.int32, (CAP, rows), 0).astype(f32)
    gate_up = [slice(q * third, (q + 1) * third) for q in range(2)]
    down = [slice(2 * third + q * HD, 2 * third + (q + 2) * HD) for q in range(2)]

    def place_of(q):
        return pl.ds(pl.multiple_of((place + q) * CAP, CAP), CAP)

    def rows_of(q):
        hit = slot_at == routes_ref[q, 0:1]
        weight = jnp.sum(jnp.where(hit, routes_ref[q, 1:2], 0.0), axis=1, keepdims=True)
        pick = hit.astype(bf16)
        return nn(pick, x_ref[...]).astype(bf16), (nn(pick, gy_ref[...]) * weight).astype(bf16), weight

    def picked(q):
        column = (lax.broadcasted_iota(jnp.int32, (HD, CAP), 0) == expert + q).astype(bf16)
        pick_buf[:, place_of(q)] = (nn(rank_c[...], column) == slot_of).astype(bf16)

    def unit(gate, up, dact):
        sig = jax.nn.sigmoid(gate)
        silu = gate * sig
        return silu * up, dact * up * sig * (1.0 + gate * (1.0 - sig)), dact * silu

    def middle(q, gu, dact):
        tail = gu[:, 2 * HD :]
        if q == 0:
            d0, d1 = dact[:, :HD], dact[:, HD:]
        else:
            d0, d1 = dact[:, HD:], pltpu.roll(dact[:, :HD], TAIL, 1)
        a0, dg0, du0 = unit(gu[:, :HD], gu[:, HD : 2 * HD], d0)
        a1, dg1, du1 = unit(tail, pltpu.roll(tail, TAIL, 1), d1)
        a1 = jnp.where(low_half, a1, 0.0)
        dgu1 = jnp.where(low_half, dg1, pltpu.roll(du1, TAIL, 1))
        act = [a0, a1] if q == 0 else [pltpu.roll(a1, TAIL, 1), a0]
        act = jnp.concatenate([part.astype(bf16) for part in act], axis=1)
        return act, jnp.concatenate([part.astype(bf16) for part in (dg0, du0, dgu1)], axis=1)

    def ends(q, xe, deo, weight, act, dgu):
        y_buf[place_of(q), :width] = (nt(act, w[:, down[q]]) * weight).astype(bf16)
        y_buf[place_of(q), width:] = nt(dgu, w[:, gate_up[q]]).astype(bf16)
        put(q * third, tn(xe, dgu))
        grad = tn(deo, act)
        put(2 * third + 2 * q * HD, grad[:, :HD] if q == 0 else grad[:, HD:])
        return grad[:, HD:] if q == 0 else grad[:, :HD]

    xe0, deo0, weight0 = rows_of(0)
    first = nn(xe0, w[:, gate_up[0]]), nn(deo0, w[:, down[0]])
    xe1, deo1, weight1 = rows_of(1)
    act0, dgu0 = middle(0, *first)
    second = nn(xe1, w[:, gate_up[1]]), nn(deo1, w[:, down[1]])
    picked(0)
    tail0 = ends(0, xe0, deo0, weight0, act0, dgu0)
    act1, dgu1 = middle(1, *second)
    picked(1)
    tail1 = ends(1, xe1, deo1, weight1, act1, dgu1)
    put(2 * third + HD, tail0 + tail1)


def expert_call(rank_cols, routes, x, gy, weights, sums):
    rows, width = x.shape
    pairs, _, lanes = weights.shape
    blocks = 6
    tile = 2 * width // blocks

    def kernel(rank_c, routes_ref, x_ref, gy_ref, w_ref, sums_in, grad_out, sums_out, y_buf, pick_buf):
        step = pl.program_id(0)

        def put(at, value):
            grad_out[0, :, at : at + value.shape[1]] = value.astype(bf16)

        @pl.when(step < pairs)
        def _():
            pair_of_experts(2 * step, 2 * step, w_ref.at[0], rank_c, routes_ref, x_ref, gy_ref, y_buf, pick_buf, put)

        @pl.when(step >= pairs)
        def _():
            at = pl.ds(pl.multiple_of((step - pairs) * tile, tile), tile)
            sums_out[...] = sums_in[...] + nn(pick_buf[...], y_buf[:, at])

    def held(step):
        return jnp.minimum(step, pairs - 1)

    def block(step):
        return (0, jnp.maximum(step - pairs, 0))

    once = pl.Buffered(1)
    whole = pl.BlockSpec((rows, width), lambda s: (0, 0), pipeline_mode=once)
    of_pair = pl.BlockSpec((1, width, lanes), lambda s: (held(s), 0, 0))
    return pl.pallas_call(
        kernel,
        grid=(pairs + blocks,),
        in_specs=[
            pl.BlockSpec((rows, HD), lambda s: (0, 0), pipeline_mode=once),
            pl.BlockSpec((2, 2, rows), lambda s: (held(s), 0, 0)),
            whole,
            whole,
            of_pair,
            pl.BlockSpec((rows, tile), block),
        ],
        out_specs=[of_pair, pl.BlockSpec((rows, tile), block)],
        scratch_shapes=[pltpu.VMEM((2 * pairs * CAP, 2 * width), bf16), pltpu.VMEM((rows, 2 * pairs * CAP), bf16)],
        out_shape=[
            jax.ShapeDtypeStruct((pairs, width, lanes), bf16),
            jax.ShapeDtypeStruct((rows, 2 * width), f32),
        ],
        compiler_params=pltpu.CompilerParams(vmem_limit_bytes=62 * 10**6),
        name="experts",
    )(rank_cols, routes, x, gy, weights, sums)


def expert_pass(rank_cols, routes, x, gy, packed, near, far, members):
    rows, width = x.shape
    calls = len(packed)
    size, height, lanes = packed[0].shape
    half = size // 2
    pairs = calls * size
    blocks = 6
    tile = 2 * width // blocks
    period = size + blocks
    early = calls - 1
    dma = pltpu.SemaphoreType.DMA
    known = len(near)
    unknown = calls - known
    n_in = 4 + calls + 2 * known + 2

    def kernel(*refs):
        rank_c, routes_ref, x_ref, gy_ref = refs[:4]
        own = refs[4 : 4 + calls]
        near_in = refs[4 + calls : n_in - 2]
        far_in = refs[n_in - 2 : n_in]
        outs = refs[n_in:]
        sums_out, grads = outs[:2]
        near_out, outs = outs[2 : 2 + 2 * unknown], outs[2 + 2 * unknown :]
        far_out = outs[: 2 * early]
        plain_x, plain_y, added_x, added_y, via_x, via_y = outs[2 * early : 6 + 2 * early]
        scratch = outs[6 + 2 * early :]
        w_buf, y_buf, pick_buf, total, kept, leaving, arriving, load_buf, add_buf = scratch[:9]
        local_sem, push_sem, pull_sem, send_sem, recv_sem, keep_sem, load_sem, add_sem = scratch[9:17]
        chip_send, chip_recv, cross_send, cross_recv, straight_send, straight_recv, w_free, g_free = scratch[17:]
        step = pl.program_id(0)
        call, phase = step // period, lax.rem(step, period)
        pair = call * size + phase
        x_side, y_side = chip_neighbours()
        other = {"dp": sibling()}
        near_all = (*near_in, *near_out)
        near_x, near_y = near_all[0::2], near_all[1::2]
        far_all = [far_in, *(far_out[2 * i : 2 * i + 2] for i in range(early))]

        def chip(index, source, target, device):
            return remote(source, target, chip_send.at[index], chip_recv.at[index], {"dp": device})

        forward = []
        for i in range(early):
            forward.append(chip(2 * i, near_x[i + 1].at[:half], far_out[2 * i], y_side))
            forward.append(chip(2 * i + 1, near_y[i + 1].at[half:], far_out[2 * i + 1], x_side))
        fresh = []
        for i in range(unknown):
            fresh.append(chip(2 * early + 2 * i, own[known + i], near_out[2 * i], x_side))
            fresh.append(chip(2 * early + 2 * i + 1, own[known + i], near_out[2 * i + 1], y_side))

        def weights(now, slot, sub):
            chunk, side = sub // 2, sub % 2
            sources = [own[chunk], near_x[chunk], near_y[chunk], far_all[chunk][side]]
            begins = [chunk * size] * 3 + [chunk * size + side * half]
            found = []
            for k, (source, begin) in enumerate(zip(sources, begins)):
                source = source.at[now - begin]
                mine = w_buf.at[slot, pl.ds(2 * k * height, height)]
                found.append(pltpu.make_async_copy(source, mine, local_sem.at[slot, k]))
                theirs = w_buf.at[slot, pl.ds((2 * k + 1) * height, height)]
                found.append(remote(source, theirs, push_sem.at[slot, k], pull_sem.at[slot, k], other))
            return found

        def start(now):
            slot = lax.rem(now, 2)
            for sub in range(2 * calls):

                @pl.when((now >= sub * half) & (now < (sub + 1) * half))
                def _():
                    if sub >= 2:

                        @pl.when(now == sub * half)
                        def _():
                            forward[sub - 2].wait_recv()

                    for copy in weights(now, slot, sub):
                        copy.start()

        def leave(slot):
            return remote(leaving.at[slot], arriving.at[slot], send_sem.at[slot], recv_sem.at[slot], other)

        def keep(now):
            slot = lax.rem(now, 2)
            return pltpu.make_async_copy(kept.at[slot], grads.at[:, now], keep_sem.at[slot])

        def crossing(now, first):
            at = now // size * half + lax.rem(now, size) - (0 if first else half)
            sems = cross_send.at[now], cross_recv.at[now]
            if first:
                return remote(grads.at[3, now], via_x.at[at], *sems, {"dp": x_side})
            return remote(grads.at[3, now], via_y.at[at], *sems, {"dp": y_side})

        def straight(now, first):
            at = now // size * half + lax.rem(now, size) - (0 if first else half)
            sems = straight_send.at[now], straight_recv.at[now]
            if first:
                return remote(grads.at[1, now], plain_x.at[at], *sems, {"dp": x_side})
            return remote(grads.at[2, now], plain_y.at[at], *sems, {"dp": y_side})

        def by_half(now, do):
            for first in (True, False):

                @pl.when((lax.rem(now, size) < half) if first else (lax.rem(now, size) >= half))
                def _():
                    do(first)

        def scatter(now):
            by_half(now, lambda first: crossing(now, first).start())

        def finish(now):
            slot = lax.rem(now, 2)
            leave(slot).wait()
            for k in range(4):
                kept[slot, k] = (kept[slot, k].astype(f32) + arriving[slot, k].astype(f32)).astype(bf16)
            keep(now).start()

        def signal(sem):
            pl.semaphore_signal(sem, inc=1, device_id=other, device_id_type=pl.DeviceIdType.MESH)

        def put(at, value):
            slot = lax.rem(pair, 2)
            for k in range(4):
                for parity, target in enumerate((kept, leaving)):
                    row = (2 * k + parity) * height
                    target[slot, k, :, at : at + value.shape[1]] = value[row : row + height].astype(bf16)

        def loads(now):
            at = now // size * half + lax.rem(now, half)

            def copies(first):
                via, block = (via_x, 2) if first else (via_y, 1)
                return (
                    pltpu.make_async_copy(via.at[at], load_buf.at[0], load_sem.at[0]),
                    pltpu.make_async_copy(grads.at[block, now], load_buf.at[1], load_sem.at[1]),
                )

            return copies

        def stores(now, first):
            at = now // size * half + lax.rem(now, half)
            return pltpu.make_async_copy(add_buf, (added_y if first else added_x).at[at], add_sem)

        @pl.when(step == 0)
        def _():
            barrier = pltpu.get_barrier_semaphore()
            for device in (x_side, y_side, sibling()):
                pl.semaphore_signal(barrier, inc=1, device_id={"dp": device}, device_id_type=pl.DeviceIdType.MESH)
            pl.semaphore_wait(barrier, 3)
            start(step)
            for copy in forward[:2]:
                copy.start()

        @pl.when(phase < size)
        def _():
            @pl.when((pair >= 1) & (pair + 1 < pairs))
            def _():
                signal(w_free)
                pl.semaphore_wait(w_free, 1)

            for i in range(unknown):

                @pl.when(pair == (1 if i == 0 else i * size + 2))
                def _():
                    for copy in fresh[2 * i : 2 * i + 2]:
                        copy.start()

                @pl.when(pair == (i + 1) * size + i)
                def _():
                    for copy in fresh[2 * i : 2 * i + 2]:
                        copy.wait_recv()
                    begin = 2 * (known + i - 1)
                    for copy in forward[begin : begin + 2]:
                        copy.start()

            @pl.when(pair >= early * size)
            def _():
                for i in range(STRAIGHT):
                    now = pair - (early - i) * size
                    by_half(now, lambda first, now=now: straight(now, first).start())

            @pl.when(pair + 1 < pairs)
            def _():
                start(pair + 1)

            @pl.when(pair >= 2)
            def _():
                keep(pair - 2).wait()

            @pl.when((pair >= 2) & (pair - 2 < early * size))
            def _():
                scatter(pair - 2)

            slot = lax.rem(pair, 2)
            for copy in weights(0, slot, 0):
                copy.wait()
            pair_of_experts(
                2 * pair, 2 * phase, w_buf.at[slot], rank_c, routes_ref, x_ref, gy_ref, y_buf, pick_buf, put
            )

        @pl.when((phase >= 1) & (phase <= size))
        def _():
            finish(pair - 1)

            @pl.when(pair + 1 < pairs)
            def _():
                signal(g_free)

        @pl.when(phase < size)
        def _():
            @pl.when(pair >= 2)
            def _():
                pl.semaphore_wait(g_free, 1)

            leave(lax.rem(pair, 2)).start()

        @pl.when(phase >= size)
        def _():
            block = phase - size
            at = pl.ds(pl.multiple_of(block * tile, tile), tile)
            made = nn(pick_buf[...], y_buf[:, at])

            @pl.when(call == 0)
            def _():
                total[:, at] = made.astype(bf16)

            @pl.when((call > 0) & (call < calls - 1))
            def _():
                total[:, at] = (made + total[:, at].astype(f32)).astype(bf16)

            @pl.when(call == calls - 1)
            def _():
                sums_out[...] = (made + total[:, at].astype(f32)).astype(bf16)

            before = (call - 1) * size + block

            @pl.when((call > 0) & (block >= 2) & (block < size + 2))
            def _():
                by_half(before - 2, lambda first: stores(before - 2, first).wait())

            @pl.when((call > 0) & (block >= 1) & (block < size + 1))
            def _():
                def add_to(first):
                    for copy in loads(before - 1)(first):
                        copy.wait()
                    add_buf[...] = (load_buf[0].astype(f32) + load_buf[1].astype(f32)).astype(bf16)
                    stores(before - 1, first).start()

                by_half(before - 1, add_to)

            @pl.when((call > 0) & (block < size))
            def _():
                def load(first):
                    crossing(before, first).wait_recv()
                    for copy in loads(before)(first):
                        copy.start()

                by_half(before, load)

        @pl.when(step == calls * period - 1)
        def _():
            for now in (pairs - 2, pairs - 1):
                keep(now).wait()
            for copy in (*forward, *fresh):
                copy.wait_send()
            for now in range(early * size):
                first = now % size < half
                crossing(now, first).wait_send()
                if now < STRAIGHT * size:
                    straight(now, first).wait()

    def held(step):
        return step // period * size + jnp.minimum(lax.rem(step, period), size - 1)

    def block(step):
        return (0, jnp.where(step >= (calls - 1) * period + size, step - (calls - 1) * period - size, 0))

    once = pl.Buffered(1)
    whole = pl.BlockSpec((rows, width), lambda s: (0, 0), pipeline_mode=once)
    anywhere = pl.BlockSpec(memory_space=pl.ANY)
    some = jax.ShapeDtypeStruct((early * half, height, lanes), bf16)
    regular = pltpu.SemaphoreType.REGULAR
    return pl.pallas_call(
        kernel,
        grid=(calls * period,),
        in_specs=[
            pl.BlockSpec((rows, HD), lambda s: (0, 0), pipeline_mode=once),
            pl.BlockSpec((2, 2, rows), lambda s: (held(s), 0, 0)),
            whole,
            whole,
        ]
        + [anywhere] * (n_in - 4),
        out_specs=[pl.BlockSpec((rows, tile), block)] + [anywhere] * (7 + 2 * unknown + 2 * early),
        out_shape=[
            jax.ShapeDtypeStruct((rows, 2 * width), bf16),
            jax.ShapeDtypeStruct((4, pairs, height, lanes), bf16),
        ]
        + [jax.ShapeDtypeStruct((size, height, lanes), bf16)] * (2 * unknown)
        + [jax.ShapeDtypeStruct((half, height, lanes), bf16)] * (2 * early)
        + [jax.ShapeDtypeStruct((STRAIGHT * half, height, lanes), bf16)] * 2
        + [some] * 4,
        scratch_shapes=[
            pltpu.VMEM((2, width, lanes), bf16),
            pltpu.VMEM((2 * size * CAP, 2 * width), bf16),
            pltpu.VMEM((rows, 2 * size * CAP), bf16),
            pltpu.VMEM((rows, 2 * width), bf16),
            pltpu.VMEM((2, 4, height, lanes), bf16),
            pltpu.VMEM((2, 4, height, lanes), bf16),
            pltpu.VMEM((2, 4, height, lanes), bf16),
            pltpu.VMEM((2, height, lanes), bf16),
            pltpu.VMEM((height, lanes), bf16),
            dma((2, 4)),
            dma((2, 4)),
            dma((2, 4)),
            dma((2,)),
            dma((2,)),
            dma((2,)),
            dma((2,)),
            dma,
            dma((2 * early + 2 * unknown,)),
            dma((2 * early + 2 * unknown,)),
            dma((early * size,)),
            dma((early * size,)),
            dma((early * size,)),
            dma((early * size,)),
            regular,
            regular,
        ],
        compiler_params=pltpu.CompilerParams(
            vmem_limit_bytes=62 * 10**6, collective_id=1, has_side_effects=True
        ),
        cost_estimate=pl.CostEstimate(flops=2 * 10**11, bytes_accessed=10**8, transcendentals=0),
        name="experts",
    )(rank_cols, routes, x, gy, *packed, *(side for both in near for side in both), *far)


def remote(source, target, send_sem, recv_sem, device):
    return pltpu.make_async_remote_copy(
        src_ref=source,
        dst_ref=target,
        send_sem=send_sem,
        recv_sem=recv_sem,
        device_id=device,
        device_id_type=pl.DeviceIdType.MESH,
    )


def chip_neighbours():
    me = lax.axis_index("dp")
    return me + 2 - 4 * lax.rem(me // 2, 2), me + 4 - 8 * lax.rem(me // 4, 2)


def meet(members, core):
    barrier = pltpu.get_barrier_semaphore()
    z = lax.axis_index("tensor")

    def signal(device):
        pl.semaphore_signal(barrier, inc=1, device_id=device, device_id_type=pl.DeviceIdType.MESH)

    @pl.when(z > 0)
    def _():
        signal({"tensor": z - 1})

    @pl.when(z < members - 1)
    def _():
        signal({"tensor": z + 1})

    for other in (*chip_neighbours(), *([sibling()] if core else [])):
        signal({"dp": other})
    inner = jnp.where((z > 0) & (z < members - 1), 1, 0)
    pl.semaphore_wait(barrier, 3 + inner + (1 if core else 0))


class LineGather:
    def __init__(self, members, at, send, recv):
        self.members, self.at, self.send, self.recv = members, at, send, recv

    def copies(self, hop):
        z, last = lax.axis_index("tensor"), self.members - 1
        up, down = z - hop + 1, z + hop - 1

        def copy(block, way, device):
            return lambda: remote(
                self.at(block), self.at(block), self.send.at[way, hop - 1], self.recv.at[way, hop - 1], {"tensor": device}
            )

        return (
            ((up >= 0) & (z < last), copy(up, 0, z + 1)),
            ((down <= last) & (z > 0), copy(down, 1, z - 1)),
        ), (
            (z - hop >= 0, copy(z - hop, 0, z)),
            (z + hop <= last, copy(z + hop, 1, z)),
        )

    def start(self, hop):
        for present, copy in self.copies(hop)[0]:

            @pl.when(present)
            def _():
                copy().start()

    def arrive(self, hop):
        for present, copy in self.copies(hop)[1]:

            @pl.when(present)
            def _():
                copy().wait_recv()

    def close(self):
        for hop in range(1, self.members):
            for present, copy in self.copies(hop)[0]:

                @pl.when(present)
                def _():
                    copy().wait_send()


class LineSum:
    def __init__(self, members, part, leaving, arriving, send, recv):
        self.members, self.part, self.leaving, self.arriving = members, part, leaving, arriving
        self.send, self.recv = send, recv

    def copy(self, way, hop, device):
        return remote(
            self.leaving.at[way],
            self.arriving.at[way, hop - 1],
            self.send.at[way, hop - 1],
            self.recv.at[way, hop - 1],
            {"tensor": device},
        )

    def ways(self, hop):
        z, last = lax.axis_index("tensor"), self.members - 1
        return (
            (0, z - hop >= 0, z - hop, z < last, z - 1, (z < last) & (z + 1 - hop >= 0)),
            (1, z + hop <= last, z + hop, z > 0, z + 1, (z > 0) & (z - 1 + hop <= last)),
        )

    def start(self, hop, begun=True):
        if hop + 1 < self.members and begun:
            self.leave(hop + 1)
        for way, present, block, behind, device, _ in self.ways(hop):

            @pl.when(present)
            def _():
                self.leaving[way] = self.part(block).astype(bf16)

            if hop + 1 < self.members:

                @pl.when(present & behind)
                def _():
                    both = self.part(block).astype(f32) + self.arriving[way, hop].astype(f32)
                    self.leaving[way] = both.astype(bf16)

            @pl.when(present)
            def _():
                self.copy(way, hop, device).start()

    def arrive(self, hop):
        for way, _, _, _, device, present in self.ways(hop):

            @pl.when(present)
            def _():
                self.copy(way, hop, device).wait_recv()

    def total(self, out):
        z, last = lax.axis_index("tensor"), self.members - 1
        out[...] = self.part(z).astype(f32)
        for way, present in ((0, z < last), (1, z > 0)):

            @pl.when(present)
            def _():
                out[...] += self.arriving[way, 0].astype(f32)

    def leave(self, hop):
        for way, present, _, _, device, _ in self.ways(hop):

            @pl.when(present)
            def _():
                self.copy(way, hop, device).wait_send()

    def close(self):
        self.leave(1)


def swap_blocks(values):
    me = lax.axis_index("dp")
    chip = values.shape[1] // 4
    four = [values[:, i * chip : (i + 1) * chip] for i in range(4)]
    y_side, x_side, core_side = lax.rem(me // 4, 2) == 1, lax.rem(me // 2, 2) == 1, lax.rem(me, 2) == 1
    four = [jnp.where(y_side, four[i ^ 2], four[i]) for i in range(4)]
    four = [jnp.where(x_side, four[i ^ 1], four[i]) for i in range(4)]
    four = [jnp.where(core_side, pltpu.roll(part, chip // 2, 1), part) for part in four]
    return jnp.concatenate(four, axis=1)


def in_vmem(count):
    return [pl.BlockSpec(memory_space=pltpu.VMEM)] * count


def pack_chunk(gate, up, down, begin):
    gate, up, down = (
        jnp.swapaxes(w[:, begin : begin + 2 * CALL_PAIRS, :], 0, 1) for w in (gate, up, down)
    )

    def pair(a, b):
        return [a[:, :HD], b[:, :HD], jnp.concatenate([a[:, HD:], b[:, HD:]], axis=1)]

    def inner(a, b):
        a, b, tails = pair(a, b)
        return [a, tails, b]

    return [
        jnp.concatenate(
            pair(gate[e], up[e]) + pair(gate[e + 1], up[e + 1]) + inner(down[e], down[e + 1]), axis=1
        )
        for e in range(0, 2 * CALL_PAIRS, 2)
    ]


def turn(values, cosine, sine):
    return values * cosine + pltpu.roll(values, HD // 2, 1) * sine


def front(
    tokens, q_weight, o_weight, k_weight, v_weight, gains, cosine, sine, cotangent, ids, route_weights, gate, up, down, members, devices
):
    height, part = q_weight.shape
    own_rows, width = cotangent.shape
    rows = own_rows * members
    kv = 2 * KV * HD
    tall = kv + HD
    lanes = 9 * HD
    calls = EXPERTS // 2 // CALL_PAIRS
    half = CALL_PAIRS // 2
    heads = width // HD
    per_kv = heads // KV
    last = members - 1
    dma = pltpu.SemaphoreType.DMA

    def kernel(*refs):
        x_ref, q_weight_ref, o_ref, k_ref, v_ref, gains_ref, cos_ref, sin_ref, cot_ref = refs[:9]
        ids_ref, weights_ref, gate_ref, up_ref, down_ref = refs[9:14]
        square_all, tall_all, grad_all, rank_cols, routes = refs[14:19]
        normed_ref, q_ref, kv_all, mixed_ref, hidden_ref, rows_all = refs[19:25]
        packed = refs[25 : 25 + calls]
        from_x, from_y, far_x, far_y, next_x, next_y = refs[25 + calls : 31 + calls]
        rest = refs[31 + calls :]
        line_send, line_recv, grad_send, grad_recv, kv_send, kv_recv, row_send, row_recv = rest[:8]
        chip_send, chip_recv, core_send, core_recv = rest[8:]
        me, z = lax.axis_index("dp"), lax.axis_index("tensor")
        x_side, y_side = chip_neighbours()
        diagonal = x_side + y_side - me
        core = sibling()

        def rows_of(device):
            return pl.ds(pl.multiple_of(device * height, 16), height)

        def block_of(ref):
            return lambda block: ref.at[pl.ds(pl.multiple_of(block * own_rows, 16), own_rows)]

        own = pl.ds(pl.multiple_of(z * own_rows, 16), own_rows)

        def pack(call):
            chunk = pack_chunk(gate_ref, up_ref, down_ref, 2 * CALL_PAIRS * call)
            for pair, value in enumerate(chunk):
                packed[call][pair] = value

        def chip(index, source, device, target=None):
            target = source if target is None else target
            return remote(source, target, chip_send.at[index], chip_recv.at[index], {"dp": device})

        def across(index, source):
            return remote(source, source, core_send.at[index], core_recv.at[index], {"dp": core})

        def tall_at(device):
            return tall_all.at[rows_of(device)]

        def square_at(device, side=None):
            span = slice(None) if side is None else slice(side * part, (side + 1) * part)
            return square_all.at[:, rows_of(device), span]

        trades = []

        def trade(index, source):
            trades.append(across(index, source))
            trades[-1].start()

        def there(index, device, of):
            across(index, of(core if device is None else device + core - me)).wait_recv()

        square_all[z, rows_of(me), :part] = q_weight_ref[...]
        square_all[z, rows_of(me), part:] = o_ref[...]
        tall_all[rows_of(me), : kv // 2] = k_ref[...]
        tall_all[rows_of(me), kv // 2 : kv] = v_ref[...]
        tall_all[rows_of(me), kv:] = gains_ref[...]
        line = LineGather(members, lambda block: square_all.at[block, rows_of(me)], line_send, line_recv)
        group = LineGather(members, block_of(grad_all), grad_send, grad_recv)
        kv_line = LineGather(members, block_of(kv_all), kv_send, kv_recv)
        row_line = LineGather(members, block_of(rows_all), row_send, row_recv)
        moves = [
            chip(0, tall_at(me), x_side),
            chip(1, tall_at(me), y_side),
            chip(2, packed[0].at[:half], x_side, from_x.at[:half]),
            chip(3, packed[0].at[:half], y_side, from_y.at[:half]),
            chip(4, square_at(me), x_side),
            chip(5, square_at(me), y_side),
            chip(6, packed[0].at[half:], x_side, from_x.at[half:]),
            chip(7, packed[0].at[half:], y_side, from_y.at[half:]),
            chip(8, tall_at(x_side), y_side),
            chip(9, square_at(x_side, 0), y_side),
            chip(10, square_at(y_side, 1), x_side),
            chip(11, from_x.at[:half], y_side, far_x),
            chip(12, from_y.at[half:], x_side, far_y),
            chip(13, packed[1], x_side, next_x),
            chip(14, packed[1], y_side, next_y),
        ]
        meet(members, True)
        line.start(1)
        for copy in moves[:2]:
            copy.start()
        trade(0, tall_at(me))
        pack(0)
        for copy in moves[2:4]:
            copy.start()
        for index, device in ((0, x_side), (1, y_side)):
            chip(index, tall_at(device), device).wait_recv()
        moves[8].start()
        trade(2, tall_at(x_side))
        trade(3, tall_at(y_side))
        line.arrive(1)
        if last > 1:
            line.start(2)
        grad_all[own, :] = swap_blocks(cot_ref[...]).astype(bf16)
        chip(8, tall_at(diagonal), y_side).wait_recv()
        trade(6, tall_at(diagonal))
        for hop in range(2, members):
            line.arrive(hop)
            if hop < last:
                line.start(hop + 1)
        for copy in moves[4:6]:
            copy.start()
        trade(1, square_at(me))

        for index, device in ((0, None), (2, x_side), (3, y_side), (6, diagonal)):
            there(index, device, tall_at)
        gain_one, gain_two = (jnp.transpose(tall_all[:, kv:].astype(f32))[i : i + 1] for i in range(2))
        cosine, sine = cos_ref[own], sin_ref[own]
        normed_ref[...] = (rms_pieces(x_ref[...].astype(f32))[1] * gain_one).astype(bf16)
        made = nn(normed_ref[...], tall_all[:, :kv])
        for head in range(KV):
            span = slice(head * HD, (head + 1) * HD)
            kv_all[own, span] = turn(made[:, span], cosine, sine).astype(bf16)
        kv_all[own, KV * HD :] = made[:, KV * HD :].astype(bf16)
        kv_line.start(1)

        expert = lax.broadcasted_iota(jnp.int32, (HD, rows), 0)
        weight = jnp.zeros((HD, rows), f32)
        named = jnp.zeros((HD, rows), f32)
        for route in range(ids_ref.shape[0]):
            here = ids_ref[route : route + 1, :] == expert
            named = jnp.where(here, 1.0, named)
            weight = jnp.where(here, weights_ref[route : route + 1, :], weight)
        row = lax.broadcasted_iota(jnp.int32, (rows, rows), 0)
        later = (row < lax.broadcasted_iota(jnp.int32, (rows, rows), 1)).astype(bf16)
        rank = jnp.where(named > 0.0, nn(named.astype(bf16), later), -1.0)
        rank_cols[...] = jnp.transpose(rank).astype(bf16)
        for e in range(EXPERTS):
            routes[e, 0:1, :] = rank[e : e + 1]
            routes[e, 1:2, :] = weight[e : e + 1]
        for call in range(1, calls):
            kv_line_hop = call
            if kv_line_hop < members:
                kv_line.arrive(kv_line_hop)
                if kv_line_hop < last:
                    kv_line.start(kv_line_hop + 1)
            pack(call)
        for hop in range(calls, members):
            kv_line.arrive(hop)
            if hop < last:
                kv_line.start(hop + 1)
        group.start(1)

        for index, device in ((4, x_side), (5, y_side)):
            chip(index, square_at(device), device).wait_recv()
        for copy in moves[9:11]:
            copy.start()
        trade(4, square_at(x_side))
        trade(5, square_at(y_side))
        chip(9, square_at(diagonal, 0), y_side).wait_recv()
        chip(10, square_at(diagonal, 1), x_side).wait_recv()
        trade(7, square_at(diagonal))
        for copy in moves[2:4]:
            copy.wait_recv()
        for copy in (*moves[6:8], moves[11]):
            copy.start()
        group.arrive(1)
        if last > 1:
            group.start(2)
        for index, device in ((1, None), (4, x_side), (5, y_side), (7, diagonal)):
            there(index, device, square_at)

        for t in range(members):
            made = nn(normed_ref[...], square_all[t, :, :part])
            for head in range(part // HD):
                span = slice(head * HD, (head + 1) * HD)
                q_ref[:, t * part + head * HD : t * part + (head + 1) * HD] = turn(
                    made[:, span], cosine, sine
                ).astype(bf16)

        def attend(begin, end):
            @pl.loop(begin, end)
            def _(head):
                span = pl.ds(pl.multiple_of(head * HD, HD), HD)
                key_span = pl.ds(pl.multiple_of(head // per_kv * HD, HD), HD)
                value_span = pl.ds(pl.multiple_of((KV + head // per_kv) * HD, HD), HD)
                p = probabilities(q_ref[:, span], kv_all[:, key_span], z * own_rows).astype(bf16)
                mixed_ref[:, span] = nn(p, kv_all[:, value_span]).astype(bf16)

        for copy in moves[13:15]:
            copy.start()
        attend(0, heads // 2)
        for hop in range(2, members):
            group.arrive(hop)
            if hop < last:
                group.start(hop + 1)
            if hop == 2:
                attend(heads // 2, heads)
        if members <= 2:
            attend(heads // 2, heads)
        hidden = x_ref[...].astype(f32)
        for t in range(members):
            hidden += nt(mixed_ref[:, t * part : (t + 1) * part], square_all[t, :, part:])
        hidden_ref[...] = hidden
        rows_all[own, :] = swap_blocks(rms_pieces(hidden)[1] * gain_two).astype(bf16)
        for hop in range(1, members):
            row_line.start(hop)
            if hop == 1:
                for copy in moves[6:8]:
                    copy.wait_recv()
                moves[12].start()
            row_line.arrive(hop)
        for copy in moves[11:]:
            copy.wait_recv()
        for copy in moves + trades:
            copy.wait_send()
        for each in (line, group, kv_line, row_line):
            each.close()

    chunk_shape = jax.ShapeDtypeStruct((CALL_PAIRS, height, lanes), bf16)
    half_shape = jax.ShapeDtypeStruct((half, height, lanes), bf16)
    low_rows = jax.ShapeDtypeStruct((own_rows, width), bf16)
    return pl.pallas_call(
        kernel,
        in_specs=in_vmem(14),
        out_specs=in_vmem(11 + calls) + [pl.BlockSpec(memory_space=pl.ANY)] * 6,
        out_shape=[
            jax.ShapeDtypeStruct((members, devices * height, 2 * part), bf16),
            jax.ShapeDtypeStruct((devices * height, tall), bf16),
            jax.ShapeDtypeStruct((rows, width), bf16),
            jax.ShapeDtypeStruct((rows, HD), bf16),
            jax.ShapeDtypeStruct((EXPERTS, 2, rows), f32),
            low_rows,
            low_rows,
            jax.ShapeDtypeStruct((rows, kv), bf16),
            low_rows,
            jax.ShapeDtypeStruct((own_rows, width), f32),
            jax.ShapeDtypeStruct((rows, width), bf16),
        ]
        + [chunk_shape] * (calls + 2)
        + [half_shape] * 2
        + [chunk_shape] * 2,
        scratch_shapes=[dma((2, members - 1))] * 8 + [dma((15,))] * 2 + [dma((8,))] * 2,
        compiler_params=pltpu.CompilerParams(collective_id=2, has_side_effects=True, vmem_limit_bytes=62 * 10**6),
        cost_estimate=pl.CostEstimate(flops=2 * 10**11, bytes_accessed=10**7, transcendentals=0),
        name="front",
    )(
        tokens,
        q_weight,
        o_weight,
        k_weight,
        v_weight,
        gains,
        cosine,
        sine,
        cotangent,
        ids,
        route_weights,
        gate,
        up,
        down,
    )


def gain_rows(tall_ref, kv):
    return jnp.transpose(tall_ref[:, kv:].astype(f32))


def attention_back(
    sums, cotangent, hidden, tokens, normed, q, kv_all, mixed, square, tall, cosine, sine, grads, to_x, to_y, members
):
    own_rows, width = tokens.shape
    rows = own_rows * members
    kv = 2 * KV * HD
    heads = width // HD
    per_kv = heads // KV
    part = width // members
    dma = pltpu.SemaphoreType.DMA

    def kernel(sums_ref, cot_ref, hidden_ref, x_ref, normed_ref, q_ref, kv_ref, mixed_ref, square_ref, tall_ref, *rest):
        cos_ref, sin_ref, grads_ref, to_x_ref, to_y_ref = rest[:5]
        grad_ref, moe_out, parts, x_before, y_before, x_last, y_last, x_late, y_late = rest[5:14]
        do_ref, dq_ref, dkv_ref, total, kv_total, stage, tall_part, back_part = rest[14:22]
        back_leave, back_arrive, moe_leave, moe_arrive, kv_leave, kv_arrive = rest[22:28]
        back_send, back_recv, moe_send, moe_recv, kv_send, kv_recv, stage_sem, part_sem = rest[28:36]
        through, added, added_sem, chip_send, chip_recv = rest[36:]
        z = lax.axis_index("tensor")
        x_side, y_side = chip_neighbours()
        first, second = slice(0, size // 2), slice(size // 2, size)

        def chunk(block, span):
            return grads_ref.at[block, pairs_before + span.start : pairs_before + span.stop]


        def chip(index, source, target, device):
            return remote(source, target, chip_send.at[index], chip_recv.at[index], {"dp": device})

        def sums_of(begin):
            return [
                pltpu.make_async_copy(
                    sums_ref.at[b * own_rows : (b + 1) * own_rows, begin : begin + width], back_part.at[b], part_sem.at[b]
                )
                for b in range(members)
            ]

        loads = sums_of(width) + [
            pltpu.make_async_copy(chunk(1, second), added.at[0], added_sem.at[0]),
            pltpu.make_async_copy(chunk(2, first), added.at[1], added_sem.at[1]),
        ]
        for copy in loads:
            copy.start()
        meet(members, False)
        moves = [
            chip(0, chunk(3, first), through.at[0], x_side),
            chip(1, chunk(3, second), through.at[1], y_side),
            chip(2, to_x_ref.at[:soon], x_before, x_side),
            chip(3, to_y_ref.at[:soon], y_before, y_side),
            chip(4, chunk(1, first), x_last.at[first], x_side),
            chip(5, chunk(2, second), y_last.at[second], y_side),
            chip(6, added.at[0], x_last.at[second], x_side),
            chip(7, added.at[1], y_last.at[first], y_side),
        ]
        for i in range(late):
            begin, here = (i + STRAIGHT) * size, slice(i * size // 2, (i + 1) * size // 2)
            middle = begin + size // 2
            moves.append(chip(8 + 2 * i, grads_ref.at[1, begin:middle], x_late.at[here], x_side))
            moves.append(chip(9 + 2 * i, grads_ref.at[2, middle : begin + size], y_late.at[here], y_side))
        for copy in (*moves[:6], *moves[8:]):
            copy.start()
        own = pl.ds(pl.multiple_of(z * own_rows, 16), own_rows)
        for copy in loads:
            copy.wait()

        def block(ref, span):
            return lambda b: ref[pl.ds(pl.multiple_of(b * own_rows, 16), own_rows), span]

        back = LineSum(members, lambda b: back_part[b], back_leave, back_arrive, back_send, back_recv)
        moe = LineSum(members, lambda b: back_part[b], moe_leave, moe_arrive, moe_send, moe_recv)
        pairs = LineSum(members, block(dkv_ref, slice(None)), kv_leave, kv_arrive, kv_send, kv_recv)
        gains = gain_rows(tall_ref, kv)
        cosine, sine = cos_ref[own], sin_ref[own]
        last = members - 1
        stored = []

        def store(value, at):
            slot = len(stored) % 2
            if len(stored) >= 2:
                stored[-2].wait()
            stage[slot] = value.astype(bf16)
            copy = pltpu.make_async_copy(stage.at[slot], parts.at[:, at : at + part], stage_sem.at[slot])
            copy.start()
            stored.append(copy)

        for hop in range(last, 0, -1):
            back.start(hop)
            back.arrive(hop)
        back.total(total)
        loads = sums_of(0)
        for copy in loads:
            copy.start()
        normed_grad = swap_blocks(total[...])
        inverse, unit = rms_pieces(hidden_ref[...])
        for copy in loads:
            copy.wait()
        if last > 1:
            moe.start(last)
        by_hidden, gain_two = rms_backward(normed_grad, unit, inverse, gains[1:2])
        grad_ref[...] = cot_ref[...] + by_hidden
        low = grad_ref[...].astype(bf16)
        for t in range(members):
            span = slice(t * part, (t + 1) * part)
            do_ref[:, span] = nn(low, square_ref[t, :, part:]).astype(bf16)
            store(tn(low, mixed_ref[:, span]), t * part)
        dkv_ref[...] = jnp.zeros_like(dkv_ref)
        first_row = z * own_rows

        def attend(begin, end):
            @pl.loop(begin, end)
            def _(head):
                span = pl.ds(pl.multiple_of(head * HD, HD), HD)
                key_span = pl.ds(pl.multiple_of(head // per_kv * HD, HD), HD)
                value_span = pl.ds(pl.multiple_of((KV + head // per_kv) * HD, HD), HD)
                q_now, k_now, do_now = q_ref[:, span], kv_ref[:, key_span], do_ref[:, span]
                p = probabilities(q_now, k_now, first_row)
                dp = nt(do_now, kv_ref[:, value_span])
                ds = (p * (dp - jnp.sum(p * dp, axis=-1, keepdims=True))).astype(bf16)
                dq_ref[:, span] = turn(nn(ds, k_now) * (HD**-0.5), cosine, -sine).astype(bf16)
                dkv_ref[:, key_span] += tn(ds, q_now) * (HD**-0.5)
                dkv_ref[:, value_span] += tn(p.astype(bf16), do_now)

        attend(0, heads // 3)
        if last > 1:
            moe.arrive(last)
            if last > 2:
                moe.start(last - 1)
        attend(heads // 3, heads)

        pairs.start(last)

        def query_part(t):
            store(tn(normed_ref[...], dq_ref[:, t * part : (t + 1) * part]), width + t * part)

        def normed_part(t):
            made = nt(dq_ref[:, t * part : (t + 1) * part], square_ref[t, :, :part])
            if t == 0:
                total[...] = made
            else:
                total[...] += made

        for i, copy in enumerate(moves[:2]):
            copy.wait()
            added[1 - i] = (added[1 - i].astype(f32) + through[i].astype(f32)).astype(bf16)
            moves[7 - i].start()
        work = [(do, t) for do in (query_part, normed_part) for t in range(members)]
        share = len(work) // last
        for hop in range(last, 0, -1):
            for do, t in work[: share if hop > 1 else None]:
                do(t)
            work = work[share:]
            pairs.arrive(hop)
            if hop > 1:
                pairs.start(hop - 1)
        for hop in range(last - 1, 1, -1):
            moe.arrive(hop)
            if hop > 2:
                moe.start(hop - 1)
        for way, present in ((0, (z < last) & (z >= 1)), (1, (z > 0) & (z + 1 <= last))):

            @pl.when(present)
            def _():
                moe_out[way] = moe_arrive[way, 1]

            @pl.when(jnp.logical_not(present))
            def _():
                moe_out[way] = jnp.zeros((own_rows, width), bf16)

        pairs.total(kv_total)
        low_kv = [
            turn(kv_total[:, head * HD : (head + 1) * HD], cosine, -sine).astype(bf16) for head in range(KV)
        ] + [kv_total[:, KV * HD :].astype(bf16)]
        low_kv = jnp.concatenate(low_kv, axis=1)
        normed_grad = total[...] + nt(low_kv, tall_ref[:, :kv])
        inverse, unit = rms_pieces(x_ref[...].astype(f32))
        by_tokens, gain_one = rms_backward(normed_grad, unit, inverse, gains[0:1])
        grad_ref[...] += by_tokens
        tall_part[:, :kv] = tn(normed_ref[...], low_kv).astype(bf16)
        row = lax.broadcasted_iota(jnp.int32, (HD, width), 0)
        both = jnp.where(row == 0, gain_one[None], jnp.where(row == 1, gain_two[None], 0.0))
        tall_part[:, kv:] = jnp.transpose(both).astype(bf16)
        tall_copy = pltpu.make_async_copy(tall_part, parts.at[:, 2 * width :], stage_sem.at[2])
        tall_copy.start()
        for line in (back, pairs):
            line.close()
        if last > 1:
            moe.leave(2)
        for copy in (*stored[-2:], tall_copy, *moves[2:]):
            copy.wait()

    hops = (2, members - 1)
    anywhere = pl.BlockSpec(memory_space=pl.ANY)
    _, height, lanes = to_x.shape
    size = CALL_PAIRS
    pairs_before = grads.shape[1] - size
    late = pairs_before // size - STRAIGHT
    soon = to_x.shape[0] - size // 2
    halves = (2, size // 2, height, lanes)
    return pl.pallas_call(
        kernel,
        in_specs=[anywhere] + in_vmem(11) + [anywhere] * 3,
        out_specs=in_vmem(2) + [anywhere] * 7,
        out_shape=[
            jax.ShapeDtypeStruct((own_rows, width), f32),
            jax.ShapeDtypeStruct((2, own_rows, width), bf16),
            jax.ShapeDtypeStruct((width, 2 * width + tall.shape[1]), bf16),
        ]
        + [jax.ShapeDtypeStruct((soon, height, lanes), bf16)] * 2
        + [jax.ShapeDtypeStruct((size, height, lanes), bf16)] * 2
        + [jax.ShapeDtypeStruct((late * size // 2, height, lanes), bf16)] * 2,
        scratch_shapes=[
            pltpu.VMEM((own_rows, width), bf16),
            pltpu.VMEM((own_rows, width), bf16),
            pltpu.VMEM((rows, kv), f32),
            pltpu.VMEM((own_rows, width), f32),
            pltpu.VMEM((own_rows, kv), f32),
            pltpu.VMEM((2, width, part), bf16),
            pltpu.VMEM(tall.shape, bf16),
            pltpu.VMEM((members, own_rows, width), bf16),
            pltpu.VMEM((2, own_rows, width), bf16),
            pltpu.VMEM((*hops, own_rows, width), bf16),
            pltpu.VMEM((2, own_rows, width), bf16),
            pltpu.VMEM((*hops, own_rows, width), bf16),
            pltpu.VMEM((2, own_rows, kv), bf16),
            pltpu.VMEM((*hops, own_rows, kv), bf16),
        ]
        + [dma(hops)] * 6
        + [dma((3,)), dma((members,)), pltpu.VMEM(halves, bf16), pltpu.VMEM(halves, bf16), dma((2,)), dma((8 + 2 * late,)), dma((8 + 2 * late,))],
        compiler_params=pltpu.CompilerParams(collective_id=4, has_side_effects=True, vmem_limit_bytes=62 * 10**6),
        cost_estimate=pl.CostEstimate(flops=10**11, bytes_accessed=10**7, transcendentals=0),
        name="attention_back",
    )(
        sums, cotangent, hidden, tokens, normed, q, kv_all, mixed, square, tall, cosine, sine, grads, to_x, to_y
    )


def reduce_small(parts, sums, moved, hidden, to_x, to_y, members, devices):
    own_rows = hidden.shape[0]
    width = parts.shape[0]
    height = width // devices
    lanes = parts.shape[1]
    tall = lanes - 2 * width
    kv = KV * HD
    part = width // members
    half = height // 2
    groups = (slice(0, width), slice(width, lanes))
    begun = to_x.shape[0] - CALL_PAIRS // 2
    dma = pltpu.SemaphoreType.DMA

    def kernel(parts_ref, sums_ref, to_x_ref, to_y_ref, moved_ref, hidden_ref, *rest):
        out_ref, q_out, o_out, k_out, v_out, gains_out, x_end, y_end = rest[:8]
        rest = rest[8:]
        own, theirs, leave, arrive, blocks, line_leave, line_arrive, tall_all, line_total = rest[:9]
        moe_part, moe_leave, moe_arrive, total_ref = rest[9:13]
        own_sem, core_send, core_recv, chip_send, chip_recv = rest[13:18]
        o_send, o_recv, q_send, q_recv, tall_send, tall_recv, moe_send, moe_recv, part_sem, end_send, end_recv = rest[18:]
        me, z = lax.axis_index("dp"), lax.axis_index("tensor")
        x_side, y_side = chip_neighbours()
        core = sibling()
        chips = [me, x_side, y_side, x_side + y_side - me]
        loads = [
            pltpu.make_async_copy(
                sums_ref.at[b * own_rows : (b + 1) * own_rows, :width], moe_part.at[b], part_sem.at[b]
            )
            for b in range(members)
        ]
        for copy in loads:
            copy.start()

        def rows(device, span):
            return parts_ref.at[pl.ds(pl.multiple_of(device * height, 16), height), span]

        def trade(m, g):
            target = theirs.at[m, :, groups[g]]
            source = rows(chips[m] + core - me, groups[g])
            return remote(source, target, core_send.at[m, g], core_recv.at[m, g], {"dp": core})

        def keep(m, g):
            return pltpu.make_async_copy(rows(chips[m], groups[g]), own.at[m, :, groups[g]], own_sem.at[m, g])

        order = (3, 2, 1, 0)
        for g in range(2):
            for m in order:
                keep(m, g).start()
        meet(members, True)
        for g in range(2):
            for m in order:
                trade(m, g).start()
        moe = LineSum(members, lambda b: moe_part[b], moe_leave, moe_arrive, moe_send, moe_recv)
        if members > 2:
            for way in range(2):
                moe_arrive[way, 1] = moved_ref[way]
        for copy in loads:
            copy.wait()
        moe.start(1, False)

        def both(m, rows, lanes):
            return own[m, rows, lanes].astype(f32) + theirs[m, rows, lanes].astype(f32)

        def chip(index, g, slot, span, device):
            source, target = leave.at[slot, span, groups[g]], arrive.at[slot, span, groups[g]]
            return remote(source, target, chip_send.at[index, g], chip_recv.at[index, g], {"dp": device})

        first, second = slice(0, half), slice(half, height)
        every = slice(0, height)
        far = [[chip(0, g, 0, first, x_side), chip(1, g, 0, second, y_side)] for g in range(2)]
        near = [[chip(2, g, 1, every, x_side), chip(3, g, 2, every, y_side)] for g in range(2)]

        def ready(m, g):
            trade(m, g).wait()
            keep(m, g).wait()

        for g, span in enumerate(groups):
            ready(3, g)
            for copy, part_of in zip(far[g], (first, second)):
                leave[0, part_of, span] = both(3, part_of, span).astype(bf16)
                copy.start()
            for m in order[1:]:
                ready(m, g)
        for g, span in enumerate(groups):
            leave[1, first, span] = both(1, first, span).astype(bf16)
            leave[2, second, span] = both(2, second, span).astype(bf16)
            far[g][1].wait()
            leave[1, second, span] = (both(1, second, span) + arrive[0, second, span].astype(f32)).astype(bf16)
            near[g][0].start()
            far[g][0].wait()
            leave[2, first, span] = (both(2, first, span) + arrive[0, first, span].astype(f32)).astype(bf16)
            near[g][1].start()
        moe.arrive(1)
        moe.total(total_ref)
        out_ref[...] = (hidden_ref[...] + swap_blocks(total_ref[...])).astype(bf16)

        def total(span):
            return both(0, every, span) + arrive[1, :, span].astype(f32) + arrive[2, :, span].astype(f32)

        lines = [
            LineSum(members, lambda b, g=g: blocks[g, b], line_leave.at[g], line_arrive.at[g], send, recv)
            for g, (send, recv) in enumerate(((o_send, o_recv), (q_send, q_recv)))
        ]
        group = LineGather(members, lambda b: tall_all.at[b], tall_send, tall_recv)

        def hop_of(line, hop):
            line.arrive(hop)
            if hop > 1:
                line.start(hop - 1)

        last = members - 1
        for copy in near[0]:
            copy.wait()
        for t in range(members):
            blocks[0, t] = total(slice(t * part, (t + 1) * part))
        lines[0].start(last)
        for copy in near[1]:
            copy.wait()
        ends = [
            remote(source.at[begun:], target, end_send.at[i], end_recv.at[i], {"dp": device})
            for i, (source, target, device) in enumerate(((to_x_ref, x_end, x_side), (to_y_ref, y_end, y_side)))
        ]
        for copy in ends:
            copy.start()
        tall_all[z] = total(slice(2 * width, lanes)).astype(bf16)
        for t in range(members):
            blocks[1, t] = total(slice(width + t * part, width + (t + 1) * part))
        lines[1].start(last)
        group.start(1)
        for hop in range(last, 0, -1):
            hop_of(lines[0], hop)
            hop_of(lines[1], hop)
            group.arrive(members - hop)
            if hop > 1:
                group.start(members - hop + 1)
        lines[0].total(line_total)
        o_out[...] = line_total[...]
        lines[1].total(line_total)
        q_out[...] = line_total[...]
        summed = tall_all[0].astype(f32)
        for t in range(1, members):
            summed += tall_all[t].astype(f32)
        k_out[...] = summed[:, :kv]
        v_out[...] = summed[:, kv : 2 * kv]
        gains_out[...] = summed[:, 2 * kv :]
        for line in (*lines, group, moe):
            line.close()
        for copy in ends:
            copy.wait()

    hops = (2, members - 1)
    return pl.pallas_call(
        kernel,
        in_specs=[pl.BlockSpec(memory_space=pl.ANY)] * 4 + in_vmem(2),
        out_specs=in_vmem(6) + [pl.BlockSpec(memory_space=pl.ANY)] * 2,
        out_shape=[
            jax.ShapeDtypeStruct((own_rows, width), bf16),
            jax.ShapeDtypeStruct((height, part), f32),
            jax.ShapeDtypeStruct((height, part), f32),
            jax.ShapeDtypeStruct((height, kv), f32),
            jax.ShapeDtypeStruct((height, kv), f32),
            jax.ShapeDtypeStruct((height, tall - 2 * kv), f32),
        ]
        + [jax.ShapeDtypeStruct((CALL_PAIRS // 2, *to_x.shape[1:]), bf16)] * 2,
        scratch_shapes=[
            pltpu.VMEM((4, height, lanes), bf16),
            pltpu.VMEM((4, height, lanes), bf16),
            pltpu.VMEM((3, height, lanes), bf16),
            pltpu.VMEM((3, height, lanes), bf16),
            pltpu.VMEM((2, members, height, part), f32),
            pltpu.VMEM((2, 2, height, part), bf16),
            pltpu.VMEM((2, *hops, height, part), bf16),
            pltpu.VMEM((members, height, tall), bf16),
            pltpu.VMEM((height, part), f32),
            pltpu.VMEM((members, own_rows, width), bf16),
            pltpu.VMEM((2, own_rows, width), bf16),
            pltpu.VMEM((*hops, own_rows, width), bf16),
            pltpu.VMEM((own_rows, width), f32),
            dma((4, 2)),
            dma((4, 2)),
            dma((4, 2)),
            dma((4, 2)),
            dma((4, 2)),
        ]
        + [dma(hops)] * 8
        + [dma((members,)), dma((2,)), dma((2,))],
        compiler_params=pltpu.CompilerParams(collective_id=5, has_side_effects=True, vmem_limit_bytes=60 * 2**20),
        cost_estimate=pl.CostEstimate(flops=8 * 10**10, bytes_accessed=10**7, transcendentals=0),
        name="reduce_small",
    )(parts, sums, to_x, to_y, moved, hidden)


def unpack_all(grads, plain, added, last):
    _, pairs, height, lanes = grads.shape
    half = CALL_PAIRS // 2
    units = lanes // 6
    tail = units - HD
    step = 48 if height % 48 == 0 else height
    kinds = (*plain, *added, last[:1], last[1:])
    others = [array for kind in kinds for array in kind]

    def kernel(own, *refs):
        gate, up, down = refs[len(others) :]
        given = iter(refs)
        plain_x, plain_y, added_x, added_y, last_x, last_y = (
            [(ref, i) for _, ref in zip(kind, given) for i in range(ref.shape[0])] for kind in kinds
        )

        def of(kind, at):
            ref, i = kind[at]
            return ref[i].astype(f32)

        for call in range(pairs // CALL_PAIRS):
            found = [[], [], []]
            for turn in range(CALL_PAIRS):
                pair = call * CALL_PAIRS + turn
                at = call * half + turn % half
                if pair >= pairs - CALL_PAIRS:
                    by_x, by_y = of(last_x, turn), of(last_y, turn)
                elif turn < half:
                    by_x, by_y = of(plain_x, at), of(added_y, at)
                else:
                    by_x, by_y = of(added_x, at), of(plain_y, at)
                value = own[0, pair].astype(f32) + by_x + by_y
                tiles = [value[:, i * HD : (i + 1) * HD] for i in range(9)]
                for i, (a, b, both) in enumerate(((0, 1, 2), (3, 4, 5), (6, 8, 7))):
                    left = jnp.concatenate([tiles[a], tiles[both][:, :tail]], axis=1)
                    right = jnp.concatenate([tiles[b], tiles[both][:, tail:]], axis=1)
                    if i < 2:
                        found[0].append(left)
                        found[1].append(right)
                    else:
                        found[2] += [left, right]
            span = slice(2 * CALL_PAIRS * call, 2 * CALL_PAIRS * (call + 1))
            for out, values in zip((gate, up, down), found):
                out[:, span, :] = jnp.swapaxes(jnp.stack(values), 0, 1)

    shape = (height, 2 * pairs, units)
    return pl.pallas_call(
        kernel,
        grid=(height // step,),
        in_specs=[pl.BlockSpec((1, pairs, step, lanes), lambda i: (0, 0, i, 0))]
        + [pl.BlockSpec((other.shape[0], step, lanes), lambda i: (0, i, 0)) for other in others],
        out_specs=[pl.BlockSpec((step, *shape[1:]), lambda i: (i, 0, 0))] * 3,
        out_shape=[jax.ShapeDtypeStruct(shape, f32)] * 3,
        compiler_params=pltpu.CompilerParams(vmem_limit_bytes=48 * 2**20),
        name="unpack",
    )(grads, *others)


def pack(gate, up, down):
    def pair(a, b):
        return jnp.concatenate([a[..., :HD], b[..., :HD], a[..., HD:], b[..., HD:]], axis=-1)

    gate, up, down = (jnp.transpose(w, (1, 0, 2)) for w in (gate, up, down))
    gate_up = pair(gate, up)
    a, b = down[0::2], down[1::2]
    inner = jnp.concatenate([a[..., :HD], a[..., HD:], b[..., HD:], b[..., :HD]], axis=-1)
    return jnp.concatenate([gate_up[0::2], gate_up[1::2], inner], axis=-1)


def unpack(packed):
    n, height, lanes = packed.shape
    third = lanes // 3

    def halves(both):
        tail = third // 2 - HD
        a = jnp.concatenate([both[..., :HD], both[..., 2 * HD : 2 * HD + tail]], axis=-1)
        b = jnp.concatenate([both[..., HD : 2 * HD], both[..., 2 * HD + tail :]], axis=-1)
        return a, b

    def experts(even, odd):
        both = jnp.stack([even, odd], axis=1).reshape(2 * n, height, third // 2)
        return jnp.transpose(both, (1, 0, 2))

    gate0, up0 = halves(packed[..., :third])
    gate1, up1 = halves(packed[..., third : 2 * third])
    down0, down1 = packed[..., 2 * third : 2 * third + third // 2], packed[..., 2 * third + third // 2 :]
    tail = third // 2 - HD
    down1 = jnp.concatenate([down1[..., tail:], down1[..., :tail]], axis=-1)
    return experts(gate0, gate1), experts(up0, up1), experts(down0, down1)


def routes_of(expert_ids, route_weights):
    rows = expert_ids.shape[0]
    lanes = jnp.arange(EXPERTS, dtype=jnp.int32)
    named = expert_ids[:, :, None] == lanes
    member_of = jnp.any(named, axis=1)
    weight_of = jnp.sum(jnp.where(named, route_weights[:, :, None], 0.0), axis=1)
    earlier = jnp.arange(rows)[:, None] > jnp.arange(rows)[None, :]
    rank = jnp.where(member_of, nn(earlier.astype(bf16), member_of.astype(bf16)), -1.0)
    rank_cols = jnp.pad(rank, ((0, 0), (0, HD)), constant_values=-1.0).astype(bf16)
    return rank_cols, jnp.stack([rank.T, weight_of.T], axis=1)


def body_anywhere(
    tokens,
    expert_ids,
    route_weights,
    attn_gain,
    q_weight,
    k_weight,
    v_weight,
    o_weight,
    moe_gain,
    gate_weight,
    up_weight,
    down_weight,
    cotangent,
):
    members = lax.axis_size("tensor")
    member = lax.axis_index("tensor")
    own_rows, width = tokens.shape
    rows = own_rows * members
    pairs = EXPERTS // 2
    calls = pairs // CALL_PAIRS

    packed = [
        pack(*(w[:, 2 * CALL_PAIRS * i : 2 * CALL_PAIRS * (i + 1)] for w in (gate_weight, up_weight, down_weight)))
        for i in range(calls)
    ]
    gathered = [lax.all_gather(own, "dp", axis=1, tiled=True) for own in packed]

    gain_one = lax.all_gather(attn_gain, "dp", axis=0, tiled=True).astype(f32)
    gain_two = lax.all_gather(moe_gain, "dp", axis=0, tiled=True).astype(f32)
    kv_full = lax.all_gather(jnp.concatenate([k_weight, v_weight], axis=1), "dp", axis=0, tiled=True)
    q_full = lax.all_gather(lax.all_gather(q_weight, "dp", axis=0, tiled=True), "tensor", axis=0)
    o_full = lax.all_gather(lax.all_gather(o_weight, "dp", axis=0, tiled=True), "tensor", axis=0)
    kv_width = k_weight.shape[1]

    rank_cols, routes = routes_of(expert_ids, route_weights)

    grad_low = cotangent.astype(bf16)
    grad_all = lax.all_gather(grad_low, "tensor", axis=0, tiled=True)

    x = tokens.astype(f32)
    inverse_one, unit_one = rms_pieces(x)
    normed_one = (unit_one * gain_one).astype(bf16)
    first_row = (member * own_rows).reshape(1)
    cos_table, sin_table = rope_tables(member * own_rows + jnp.arange(own_rows, dtype=jnp.int32))
    kv_own = nn(normed_one, kv_full)
    kv_own = jnp.concatenate(
        [rotate(kv_own[:, :kv_width], cos_table, sin_table), kv_own[:, kv_width:]], axis=1
    ).astype(bf16)
    kv_all = lax.all_gather(kv_own, "tensor", axis=0, tiled=True)
    keys, values = kv_all[:, :kv_width], kv_all[:, kv_width:]
    queries = jnp.concatenate([nn(normed_one, q_full[t]) for t in range(members)], axis=1)
    queries = rotate(queries, cos_table, sin_table).astype(bf16)
    mixed = attend_forward(first_row, queries, keys, values)
    part = width // members
    branch = sum(nt(mixed[:, t * part : (t + 1) * part], o_full[t]) for t in range(members))
    hidden = x + branch
    inverse_two, unit_two = rms_pieces(hidden)
    normed_two = (unit_two * gain_two).astype(bf16)
    rows_all = lax.all_gather(normed_two, "tensor", axis=0, tiled=True)

    sums = jnp.zeros((rows, 2 * width), f32)
    chunks = []
    for call in range(calls):
        some = slice(2 * CALL_PAIRS * call, 2 * CALL_PAIRS * (call + 1))
        columns = slice(2 * CALL_PAIRS * call, 2 * CALL_PAIRS * call + HD)
        grads, sums = expert_call(
            rank_cols[:, columns],
            routes[some],
            rows_all,
            grad_all,
            gathered[call],
            sums,
        )
        chunks.append(grads)
    shares = [
        unpack(lax.psum_scatter(grads, "dp", scatter_dimension=1, tiled=True).astype(f32)) for grads in chunks
    ]
    gate_out, up_out, down_out = (jnp.concatenate(parts, axis=1) for parts in zip(*shares))

    low_sums = sums.astype(bf16)
    normed_grad = lax.psum_scatter(low_sums[:, width:], "tensor", scatter_dimension=0, tiled=True).astype(f32)
    moe_own = lax.psum_scatter(low_sums[:, :width], "tensor", scatter_dimension=0, tiled=True).astype(f32)
    output = (hidden + moe_own).astype(bf16)

    back_two, gain_two_part = rms_backward(normed_grad, unit_two, inverse_two, gain_two)
    hidden_grad = cotangent + back_two
    hidden_low = hidden_grad.astype(bf16)
    mixed_grad = jnp.concatenate([nn(hidden_low, o_full[t]) for t in range(members)], axis=1).astype(bf16)
    o_part = jnp.stack([tn(hidden_low, mixed[:, t * part : (t + 1) * part]) for t in range(members)])
    dq, dk, dv = attend_backward(first_row, queries, keys, values, mixed_grad)
    kv_grad = lax.psum_scatter(
        jnp.concatenate([dk, dv], axis=1).astype(bf16), "tensor", scatter_dimension=0, tiled=True
    ).astype(f32)
    dq_low = rotate(dq, cos_table, -sin_table).astype(bf16)
    kv_low = jnp.concatenate(
        [rotate(kv_grad[:, :kv_width], cos_table, -sin_table), kv_grad[:, kv_width:]], axis=1
    ).astype(bf16)
    normed_one_grad = nt(kv_low, kv_full) + sum(
        nt(dq_low[:, t * part : (t + 1) * part], q_full[t]) for t in range(members)
    )
    back_one, gain_one_part = rms_backward(normed_one_grad, unit_one, inverse_one, gain_one)
    tokens_grad = hidden_grad + back_one
    q_part = jnp.stack([tn(normed_one, dq_low[:, t * part : (t + 1) * part]) for t in range(members)])
    kv_part = tn(normed_one, kv_low)

    def shared(values):
        summed = lax.psum_scatter(values.astype(bf16), "tensor", scatter_dimension=0, tiled=False)
        return lax.psum_scatter(summed, "dp", scatter_dimension=0, tiled=True).astype(f32)

    q_grad, o_grad = shared(q_part), shared(o_part)
    small = jnp.concatenate([kv_part, gain_one_part[:, None], gain_two_part[:, None]], axis=1)
    small = lax.psum_scatter(small, "dp", scatter_dimension=0, tiled=True)
    small = lax.psum(small.astype(bf16), "tensor").astype(f32)
    return (
        output,
        tokens_grad,
        small[:, 2 * kv_width],
        q_grad,
        small[:, :kv_width],
        small[:, kv_width : 2 * kv_width],
        o_grad,
        small[:, 2 * kv_width + 1],
        gate_out,
        up_out,
        down_out,
    )

def body_by_chips(
    tokens,
    expert_ids,
    route_weights,
    attn_gain,
    q_weight,
    k_weight,
    v_weight,
    o_weight,
    moe_gain,
    gate_weight,
    up_weight,
    down_weight,
    cotangent,
):
    members = lax.axis_size("tensor")
    member = lax.axis_index("tensor")
    devices = lax.axis_size("dp")
    own_rows, width = tokens.shape
    rows = own_rows * members
    calls = EXPERTS // 2 // CALL_PAIRS

    gains = jnp.pad(jnp.stack([attn_gain, moe_gain], axis=1), ((0, 0), (0, HD - 2)))
    cosine, sine = doubled_tables(rows)
    square_all, tall_all, grad_all, rank_cols, routes, normed_one, queries, kv_all, mixed, hidden, rows_all, *chunks = front(
        tokens,
        q_weight,
        o_weight,
        k_weight,
        v_weight,
        gains,
        cosine,
        sine,
        cotangent,
        expert_ids.T,
        route_weights.T,
        gate_weight,
        up_weight,
        down_weight,
        members,
        devices,
    )
    packed, (from_x, from_y, far_x, far_y, *after) = chunks[:calls], chunks[calls:]
    near = [(from_x, from_y), *zip(after[0::2], after[1::2])]
    sums, grads, *others = expert_pass(
        rank_cols, routes, rows_all, grad_all, packed, near, (far_x, far_y), members
    )
    plain, added = others[-6:-4], others[-4:-2]
    tokens_grad, moe_moved, parts, *moved = attention_back(
        sums,
        cotangent,
        hidden,
        tokens,
        normed_one,
        queries,
        kv_all,
        mixed,
        square_all,
        tall_all,
        cosine,
        sine,
        grads,
        *added,
        members,
    )
    output, q_grad, o_grad, k_grad, v_grad, gain_grads, x_end, y_end = reduce_small(
        parts, sums, moe_moved, hidden, *added, members, devices
    )
    x_before, y_before, x_last, y_last, x_late, y_late = moved
    gate_out, up_out, down_out = unpack_all(
        grads,
        [(plain[0], x_late), (plain[1], y_late)],
        [(x_before, x_end), (y_before, y_end)],
        (x_last, y_last),
    )
    return (
        output,
        tokens_grad,
        gain_grads[:, 0],
        q_grad,
        k_grad,
        v_grad,
        o_grad,
        gain_grads[:, 1],
        gate_out,
        up_out,
        down_out,
    )


def doubled_tables(rows):
    half = HD // 2
    frequency = np.float32(rope_base) ** -(np.arange(half, dtype=np.float32) * np.float32(2.0 / HD))
    angles = (np.arange(rows) % SEQ).astype(np.float32)[:, None] * frequency
    cosine, sine = np.cos(angles), np.sin(angles)
    return jnp.asarray(np.concatenate([cosine, cosine], axis=1)), jnp.asarray(np.concatenate([-sine, sine], axis=1))


def solution(mesh):
    rows = P(("dp", "tensor"), None)
    experts = P("dp", None, "tensor")
    square = P("dp", "tensor")
    tall = P("dp", None)
    return jax.shard_map(
        body_by_chips if mesh.shape["dp"] == 8 else body_anywhere,
        mesh=mesh,
        in_specs=(
            rows, tall, tall, P("dp"), square, tall, tall, square, P("dp"), experts, experts, experts, rows
        ),
        out_specs=(rows, rows, P("dp"), square, tall, tall, square, P("dp"), experts, experts, experts),
        check_vma=False,
    )
```

```python
import jax
import jax.numpy as jnp
import numpy as np
from jax import lax
from jax.experimental import pallas as pl
from jax.experimental.pallas import tpu as pltpu
from jax.sharding import PartitionSpec as P

KV = 2
HD = 128
EXPERTS = 32
TOPK = 4
SEQ = 1024
BLOCK = 256
CAP = 256
TAIL = 64
CALL_PAIRS = 4
STRAIGHT = 2

eps = 1e-06
rope_base = 1000000.0
negative = -1e30
bf16 = jnp.bfloat16
f32 = jnp.float32


def nn(a, b):
    return jnp.dot(a, b, preferred_element_type=f32)


def nt(a, b):
    return lax.dot_general(a, b, (((1,), (1,)), ((), ())), preferred_element_type=f32)


def tn(a, b):
    return lax.dot_general(a, b, (((0,), (0,)), ((), ())), preferred_element_type=f32)


def rope_tables(positions):
    half = HD // 2
    frequency = rope_base ** (-(jnp.arange(half).astype(f32) * 2.0 / HD))
    angles = positions.astype(f32)[:, None] * frequency[None, :]
    return jnp.cos(angles), jnp.sin(angles)


def rotate(values, cos_table, sin_table):
    rows = values.shape[0]
    heads = values.reshape(rows, -1, 2, HD // 2)
    a, b = heads[:, :, 0], heads[:, :, 1]
    cos_table, sin_table = cos_table[:, None], sin_table[:, None]
    turned = jnp.stack([a * cos_table - b * sin_table, b * cos_table + a * sin_table], axis=2)
    return turned.reshape(rows, -1)


def rms_pieces(x):
    inverse = lax.rsqrt(jnp.mean(x * x, axis=-1, keepdims=True) + eps)
    return inverse, x * inverse


def rms_backward(grad, unit, inverse, gain):
    u = grad * gain
    back = inverse * (u - unit * jnp.mean(u * unit, axis=-1, keepdims=True))
    return back, jnp.sum(grad * unit, axis=0)


def probabilities(q, k, first_row):
    rows, keys = q.shape[0], k.shape[0]
    scores = nt(q, k) * (HD**-0.5)
    q_block = (first_row + lax.broadcasted_iota(jnp.int32, (rows, keys), 0)) // BLOCK
    k_block = lax.broadcasted_iota(jnp.int32, (rows, keys), 1) // BLOCK
    scores = jnp.where(k_block <= q_block, scores, negative)
    raised = jnp.exp(scores - jnp.max(scores, axis=-1, keepdims=True))
    return raised / jnp.sum(raised, axis=-1, keepdims=True)


def attend_forward(first_row, q, k, v):
    rows, width = q.shape
    heads = width // HD
    shared = heads // KV

    def kernel(first_ref, q_ref, k_ref, v_ref, o_ref):
        p = probabilities(q_ref[...], k_ref[...], first_ref[0]).astype(bf16)
        o_ref[...] = nn(p, v_ref[...]).astype(bf16)

    per_head = pl.BlockSpec((rows, HD), lambda h, f: (0, h))
    per_kv = pl.BlockSpec((k.shape[0], HD), lambda h, f: (0, h // shared))
    return pl.pallas_call(
        kernel,
        grid_spec=pltpu.PrefetchScalarGridSpec(
            num_scalar_prefetch=1,
            grid=(heads,),
            in_specs=[per_head, per_kv, per_kv],
            out_specs=per_head,
        ),
        out_shape=jax.ShapeDtypeStruct((rows, width), bf16),
        compiler_params=pltpu.CompilerParams(vmem_limit_bytes=32 * 2**20),
        cost_estimate=pl.CostEstimate(
            flops=4 * rows * width * k.shape[0],
            bytes_accessed=4 * rows * width,
            transcendentals=rows * heads * k.shape[0],
        ),
        name="attend",
    )(first_row, q, k, v)


def attend_backward(first_row, q, k, v, do):
    rows, width = q.shape
    keys = k.shape[0]
    heads = width // HD
    shared = heads // KV

    def kernel(first_ref, q_ref, k_ref, v_ref, do_ref, dq_ref, dk_ref, dv_ref):
        q_now, k_now, v_now, do_now = q_ref[...], k_ref[...], v_ref[...], do_ref[...]
        p = probabilities(q_now, k_now, first_ref[0])
        dp = nt(do_now, v_now)
        ds = (p * (dp - jnp.sum(p * dp, axis=-1, keepdims=True))).astype(bf16)
        dq_ref[...] = nn(ds, k_now) * (HD**-0.5)
        dk = tn(ds, q_now) * (HD**-0.5)
        dv = tn(p.astype(bf16), do_now)
        head = pl.program_id(0)

        @pl.when(lax.rem(head, shared) == 0)
        def _():
            dk_ref[...] = dk
            dv_ref[...] = dv

        @pl.when(lax.rem(head, shared) != 0)
        def _():
            dk_ref[...] += dk
            dv_ref[...] += dv

    per_head = pl.BlockSpec((rows, HD), lambda h, f: (0, h))
    per_kv = pl.BlockSpec((keys, HD), lambda h, f: (0, h // shared))
    return pl.pallas_call(
        kernel,
        grid_spec=pltpu.PrefetchScalarGridSpec(
            num_scalar_prefetch=1,
            grid=(heads,),
            in_specs=[per_head, per_kv, per_kv, per_head],
            out_specs=[per_head, per_kv, per_kv],
        ),
        out_shape=[
            jax.ShapeDtypeStruct((rows, width), f32),
            jax.ShapeDtypeStruct((keys, KV * HD), f32),
            jax.ShapeDtypeStruct((keys, KV * HD), f32),
        ],
        compiler_params=pltpu.CompilerParams(vmem_limit_bytes=32 * 2**20),
        cost_estimate=pl.CostEstimate(
            flops=10 * rows * width * keys,
            bytes_accessed=8 * rows * width,
            transcendentals=rows * heads * keys,
        ),
        name="attend_back",
    )(first_row, q, k, v, do)


def sibling():
    me = lax.axis_index("dp")
    return me + 1 - 2 * lax.rem(me, 2)


def pair_of_experts(expert, place, w, rank_c, routes_ref, x_ref, gy_ref, y_buf, pick_buf, put):
    rows, width = x_ref.shape
    lanes = w.shape[1]
    third = lanes // 3
    low_half = lax.broadcasted_iota(jnp.int32, (CAP, HD), 1) < TAIL
    slot_of = lax.broadcasted_iota(jnp.int32, (rows, CAP), 1).astype(f32)
    slot_at = lax.broadcasted_iota(jnp.int32, (CAP, rows), 0).astype(f32)
    gate_up = [slice(q * third, (q + 1) * third) for q in range(2)]
    down = [slice(2 * third + q * HD, 2 * third + (q + 2) * HD) for q in range(2)]

    def place_of(q):
        return pl.ds(pl.multiple_of((place + q) * CAP, CAP), CAP)

    def rows_of(q):
        hit = slot_at == routes_ref[q, 0:1]
        weight = jnp.sum(jnp.where(hit, routes_ref[q, 1:2], 0.0), axis=1, keepdims=True)
        pick = hit.astype(bf16)
        return nn(pick, x_ref[...]).astype(bf16), (nn(pick, gy_ref[...]) * weight).astype(bf16), weight

    def picked(q):
        column = (lax.broadcasted_iota(jnp.int32, (HD, CAP), 0) == expert + q).astype(bf16)
        pick_buf[:, place_of(q)] = (nn(rank_c[...], column) == slot_of).astype(bf16)

    def unit(gate, up, dact):
        sig = jax.nn.sigmoid(gate)
        silu = gate * sig
        return silu * up, dact * up * sig * (1.0 + gate * (1.0 - sig)), dact * silu

    def middle(q, gu, dact):
        tail = gu[:, 2 * HD :]
        if q == 0:
            d0, d1 = dact[:, :HD], dact[:, HD:]
        else:
            d0, d1 = dact[:, HD:], pltpu.roll(dact[:, :HD], TAIL, 1)
        a0, dg0, du0 = unit(gu[:, :HD], gu[:, HD : 2 * HD], d0)
        a1, dg1, du1 = unit(tail, pltpu.roll(tail, TAIL, 1), d1)
        a1 = jnp.where(low_half, a1, 0.0)
        dgu1 = jnp.where(low_half, dg1, pltpu.roll(du1, TAIL, 1))
        act = [a0, a1] if q == 0 else [pltpu.roll(a1, TAIL, 1), a0]
        act = jnp.concatenate([part.astype(bf16) for part in act], axis=1)
        return act, jnp.concatenate([part.astype(bf16) for part in (dg0, du0, dgu1)], axis=1)

    def ends(q, xe, deo, weight, act, dgu):
        y_buf[place_of(q), :width] = (nt(act, w[:, down[q]]) * weight).astype(bf16)
        y_buf[place_of(q), width:] = nt(dgu, w[:, gate_up[q]]).astype(bf16)
        put(q * third, tn(xe, dgu))
        grad = tn(deo, act)
        put(2 * third + 2 * q * HD, grad[:, :HD] if q == 0 else grad[:, HD:])
        return grad[:, HD:] if q == 0 else grad[:, :HD]

    xe0, deo0, weight0 = rows_of(0)
    first = nn(xe0, w[:, gate_up[0]]), nn(deo0, w[:, down[0]])
    xe1, deo1, weight1 = rows_of(1)
    act0, dgu0 = middle(0, *first)
    second = nn(xe1, w[:, gate_up[1]]), nn(deo1, w[:, down[1]])
    picked(0)
    tail0 = ends(0, xe0, deo0, weight0, act0, dgu0)
    act1, dgu1 = middle(1, *second)
    picked(1)
    tail1 = ends(1, xe1, deo1, weight1, act1, dgu1)
    put(2 * third + HD, tail0 + tail1)


def expert_call(rank_cols, routes, x, gy, weights, sums):
    rows, width = x.shape
    pairs, _, lanes = weights.shape
    blocks = 6
    tile = 2 * width // blocks

    def kernel(rank_c, routes_ref, x_ref, gy_ref, w_ref, sums_in, grad_out, sums_out, y_buf, pick_buf):
        step = pl.program_id(0)

        def put(at, value):
            grad_out[0, :, at : at + value.shape[1]] = value.astype(bf16)

        @pl.when(step < pairs)
        def _():
            pair_of_experts(2 * step, 2 * step, w_ref.at[0], rank_c, routes_ref, x_ref, gy_ref, y_buf, pick_buf, put)

        @pl.when(step >= pairs)
        def _():
            at = pl.ds(pl.multiple_of((step - pairs) * tile, tile), tile)
            sums_out[...] = sums_in[...] + nn(pick_buf[...], y_buf[:, at])

    def held(step):
        return jnp.minimum(step, pairs - 1)

    def block(step):
        return (0, jnp.maximum(step - pairs, 0))

    once = pl.Buffered(1)
    whole = pl.BlockSpec((rows, width), lambda s: (0, 0), pipeline_mode=once)
    of_pair = pl.BlockSpec((1, width, lanes), lambda s: (held(s), 0, 0))
    return pl.pallas_call(
        kernel,
        grid=(pairs + blocks,),
        in_specs=[
            pl.BlockSpec((rows, HD), lambda s: (0, 0), pipeline_mode=once),
            pl.BlockSpec((2, 2, rows), lambda s: (held(s), 0, 0)),
            whole,
            whole,
            of_pair,
            pl.BlockSpec((rows, tile), block),
        ],
        out_specs=[of_pair, pl.BlockSpec((rows, tile), block)],
        scratch_shapes=[pltpu.VMEM((2 * pairs * CAP, 2 * width), bf16), pltpu.VMEM((rows, 2 * pairs * CAP), bf16)],
        out_shape=[
            jax.ShapeDtypeStruct((pairs, width, lanes), bf16),
            jax.ShapeDtypeStruct((rows, 2 * width), f32),
        ],
        compiler_params=pltpu.CompilerParams(vmem_limit_bytes=62 * 10**6),
        name="experts",
    )(rank_cols, routes, x, gy, weights, sums)


def expert_pass(rank_cols, routes, x, gy, packed, near, far, members):
    rows, width = x.shape
    calls = len(packed)
    size, height, lanes = packed[0].shape
    half = size // 2
    pairs = calls * size
    blocks = 6
    tile = 2 * width // blocks
    period = size + blocks
    early = calls - 1
    dma = pltpu.SemaphoreType.DMA
    known = len(near)
    unknown = calls - known
    n_in = 4 + calls + 2 * known + 2

    def kernel(*refs):
        rank_c, routes_ref, x_ref, gy_ref = refs[:4]
        own = refs[4 : 4 + calls]
        near_in = refs[4 + calls : n_in - 2]
        far_in = refs[n_in - 2 : n_in]
        outs = refs[n_in:]
        sums_out, grads = outs[:2]
        near_out, outs = outs[2 : 2 + 2 * unknown], outs[2 + 2 * unknown :]
        far_out = outs[: 2 * early]
        plain_x, plain_y, added_x, added_y, via_x, via_y = outs[2 * early : 6 + 2 * early]
        scratch = outs[6 + 2 * early :]
        w_buf, y_buf, pick_buf, total, kept, leaving, arriving, load_buf, add_buf = scratch[:9]
        local_sem, push_sem, pull_sem, send_sem, recv_sem, keep_sem, load_sem, add_sem = scratch[9:17]
        chip_send, chip_recv, cross_send, cross_recv, straight_send, straight_recv, w_free, g_free = scratch[17:]
        step = pl.program_id(0)
        call, phase = step // period, lax.rem(step, period)
        pair = call * size + phase
        x_side, y_side = chip_neighbours()
        other = {"dp": sibling()}
        near_all = (*near_in, *near_out)
        near_x, near_y = near_all[0::2], near_all[1::2]
        far_all = [far_in, *(far_out[2 * i : 2 * i + 2] for i in range(early))]

        def chip(index, source, target, device):
            return remote(source, target, chip_send.at[index], chip_recv.at[index], {"dp": device})

        forward = []
        for i in range(early):
            forward.append(chip(2 * i, near_x[i + 1].at[:half], far_out[2 * i], y_side))
            forward.append(chip(2 * i + 1, near_y[i + 1].at[half:], far_out[2 * i + 1], x_side))
        fresh = []
        for i in range(unknown):
            fresh.append(chip(2 * early + 2 * i, own[known + i], near_out[2 * i], x_side))
            fresh.append(chip(2 * early + 2 * i + 1, own[known + i], near_out[2 * i + 1], y_side))

        def weights(now, slot, sub):
            chunk, side = sub // 2, sub % 2
            sources = [own[chunk], near_x[chunk], near_y[chunk], far_all[chunk][side]]
            begins = [chunk * size] * 3 + [chunk * size + side * half]
            found = []
            for k, (source, begin) in enumerate(zip(sources, begins)):
                source = source.at[now - begin]
                mine = w_buf.at[slot, pl.ds(2 * k * height, height)]
                found.append(pltpu.make_async_copy(source, mine, local_sem.at[slot, k]))
                theirs = w_buf.at[slot, pl.ds((2 * k + 1) * height, height)]
                found.append(remote(source, theirs, push_sem.at[slot, k], pull_sem.at[slot, k], other))
            return found

        def start(now):
            slot = lax.rem(now, 2)
            for sub in range(2 * calls):

                @pl.when((now >= sub * half) & (now < (sub + 1) * half))
                def _():
                    if sub >= 2:

                        @pl.when(now == sub * half)
                        def _():
                            forward[sub - 2].wait_recv()

                    for copy in weights(now, slot, sub):
                        copy.start()

        def leave(slot):
            return remote(leaving.at[slot], arriving.at[slot], send_sem.at[slot], recv_sem.at[slot], other)

        def keep(now):
            slot = lax.rem(now, 2)
            return pltpu.make_async_copy(kept.at[slot], grads.at[:, now], keep_sem.at[slot])

        def crossing(now, first):
            at = now // size * half + lax.rem(now, size) - (0 if first else half)
            sems = cross_send.at[now], cross_recv.at[now]
            if first:
                return remote(grads.at[3, now], via_x.at[at], *sems, {"dp": x_side})
            return remote(grads.at[3, now], via_y.at[at], *sems, {"dp": y_side})

        def straight(now, first):
            at = now // size * half + lax.rem(now, size) - (0 if first else half)
            sems = straight_send.at[now], straight_recv.at[now]
            if first:
                return remote(grads.at[1, now], plain_x.at[at], *sems, {"dp": x_side})
            return remote(grads.at[2, now], plain_y.at[at], *sems, {"dp": y_side})

        def by_half(now, do):
            for first in (True, False):

                @pl.when((lax.rem(now, size) < half) if first else (lax.rem(now, size) >= half))
                def _():
                    do(first)

        def scatter(now):
            by_half(now, lambda first: crossing(now, first).start())

        def finish(now):
            slot = lax.rem(now, 2)
            leave(slot).wait()
            for k in range(4):
                kept[slot, k] = (kept[slot, k].astype(f32) + arriving[slot, k].astype(f32)).astype(bf16)
            keep(now).start()

        def signal(sem):
            pl.semaphore_signal(sem, inc=1, device_id=other, device_id_type=pl.DeviceIdType.MESH)

        def put(at, value):
            slot = lax.rem(pair, 2)
            for k in range(4):
                for parity, target in enumerate((kept, leaving)):
                    row = (2 * k + parity) * height
                    target[slot, k, :, at : at + value.shape[1]] = value[row : row + height].astype(bf16)

        def loads(now):
            at = now // size * half + lax.rem(now, half)

            def copies(first):
                via, block = (via_x, 2) if first else (via_y, 1)
                return (
                    pltpu.make_async_copy(via.at[at], load_buf.at[0], load_sem.at[0]),
                    pltpu.make_async_copy(grads.at[block, now], load_buf.at[1], load_sem.at[1]),
                )

            return copies

        def stores(now, first):
            at = now // size * half + lax.rem(now, half)
            return pltpu.make_async_copy(add_buf, (added_y if first else added_x).at[at], add_sem)

        @pl.when(step == 0)
        def _():
            barrier = pltpu.get_barrier_semaphore()
            for device in (x_side, y_side, sibling()):
                pl.semaphore_signal(barrier, inc=1, device_id={"dp": device}, device_id_type=pl.DeviceIdType.MESH)
            pl.semaphore_wait(barrier, 3)
            start(step)
            for copy in forward[:2]:
                copy.start()

        @pl.when(phase < size)
        def _():
            @pl.when((pair >= 1) & (pair + 1 < pairs))
            def _():
                signal(w_free)
                pl.semaphore_wait(w_free, 1)

            for i in range(unknown):

                @pl.when(pair == (1 if i == 0 else i * size + 2))
                def _():
                    for copy in fresh[2 * i : 2 * i + 2]:
                        copy.start()

                @pl.when(pair == (i + 1) * size + i)
                def _():
                    for copy in fresh[2 * i : 2 * i + 2]:
                        copy.wait_recv()
                    begin = 2 * (known + i - 1)
                    for copy in forward[begin : begin + 2]:
                        copy.start()

            @pl.when(pair >= early * size)
            def _():
                for i in range(STRAIGHT):
                    now = pair - (early - i) * size
                    by_half(now, lambda first, now=now: straight(now, first).start())

            @pl.when(pair + 1 < pairs)
            def _():
                start(pair + 1)

            @pl.when(pair >= 2)
            def _():
                keep(pair - 2).wait()

            @pl.when(pair == size + 1)
            def _():
                for now in range(size - 1):
                    crossing(now, now < half).start()

            @pl.when((pair > size) & (pair - 2 < early * size))
            def _():
                scatter(pair - 2)

            slot = lax.rem(pair, 2)
            for copy in weights(0, slot, 0):
                copy.wait()
            pair_of_experts(
                2 * pair, 2 * phase, w_buf.at[slot], rank_c, routes_ref, x_ref, gy_ref, y_buf, pick_buf, put
            )

        @pl.when((phase >= 1) & (phase <= size))
        def _():
            finish(pair - 1)

            @pl.when(pair + 1 < pairs)
            def _():
                signal(g_free)

        @pl.when(phase < size)
        def _():
            @pl.when(pair >= 2)
            def _():
                pl.semaphore_wait(g_free, 1)

            leave(lax.rem(pair, 2)).start()

        @pl.when(phase >= size)
        def _():
            block = phase - size
            at = pl.ds(pl.multiple_of(block * tile, tile), tile)
            made = nn(pick_buf[...], y_buf[:, at])

            @pl.when(call == 0)
            def _():
                total[:, at] = made.astype(bf16)

            @pl.when((call > 0) & (call < calls - 1))
            def _():
                total[:, at] = (made + total[:, at].astype(f32)).astype(bf16)

            @pl.when(call == calls - 1)
            def _():
                sums_out[...] = (made + total[:, at].astype(f32)).astype(bf16)

            before = (call - 1) * size + block

            @pl.when((call > 0) & (block >= 2) & (block < size + 2))
            def _():
                by_half(before - 2, lambda first: stores(before - 2, first).wait())

            @pl.when((call > 0) & (block >= 1) & (block < size + 1))
            def _():
                def add_to(first):
                    for copy in loads(before - 1)(first):
                        copy.wait()
                    add_buf[...] = (load_buf[0].astype(f32) + load_buf[1].astype(f32)).astype(bf16)
                    stores(before - 1, first).start()

                by_half(before - 1, add_to)

            @pl.when((call > 0) & (block < size))
            def _():
                def load(first):
                    crossing(before, first).wait_recv()
                    for copy in loads(before)(first):
                        copy.start()

                by_half(before, load)

        @pl.when(step == calls * period - 1)
        def _():
            for now in (pairs - 2, pairs - 1):
                keep(now).wait()
            for copy in (*forward, *fresh):
                copy.wait_send()
            for now in range(early * size):
                first = now % size < half
                crossing(now, first).wait_send()
                if now < STRAIGHT * size:
                    straight(now, first).wait()

    def held(step):
        return step // period * size + jnp.minimum(lax.rem(step, period), size - 1)

    def block(step):
        return (0, jnp.where(step >= (calls - 1) * period + size, step - (calls - 1) * period - size, 0))

    once = pl.Buffered(1)
    whole = pl.BlockSpec((rows, width), lambda s: (0, 0), pipeline_mode=once)
    anywhere = pl.BlockSpec(memory_space=pl.ANY)
    some = jax.ShapeDtypeStruct((early * half, height, lanes), bf16)
    regular = pltpu.SemaphoreType.REGULAR
    return pl.pallas_call(
        kernel,
        grid=(calls * period,),
        in_specs=[
            pl.BlockSpec((rows, HD), lambda s: (0, 0), pipeline_mode=once),
            pl.BlockSpec((2, 2, rows), lambda s: (held(s), 0, 0)),
            whole,
            whole,
        ]
        + [anywhere] * (n_in - 4),
        out_specs=[pl.BlockSpec((rows, tile), block)] + [anywhere] * (7 + 2 * unknown + 2 * early),
        out_shape=[
            jax.ShapeDtypeStruct((rows, 2 * width), bf16),
            jax.ShapeDtypeStruct((4, pairs, height, lanes), bf16),
        ]
        + [jax.ShapeDtypeStruct((size, height, lanes), bf16)] * (2 * unknown)
        + [jax.ShapeDtypeStruct((half, height, lanes), bf16)] * (2 * early)
        + [jax.ShapeDtypeStruct((STRAIGHT * half, height, lanes), bf16)] * 2
        + [some] * 4,
        scratch_shapes=[
            pltpu.VMEM((2, width, lanes), bf16),
            pltpu.VMEM((2 * size * CAP, 2 * width), bf16),
            pltpu.VMEM((rows, 2 * size * CAP), bf16),
            pltpu.VMEM((rows, 2 * width), bf16),
            pltpu.VMEM((2, 4, height, lanes), bf16),
            pltpu.VMEM((2, 4, height, lanes), bf16),
            pltpu.VMEM((2, 4, height, lanes), bf16),
            pltpu.VMEM((2, height, lanes), bf16),
            pltpu.VMEM((height, lanes), bf16),
            dma((2, 4)),
            dma((2, 4)),
            dma((2, 4)),
            dma((2,)),
            dma((2,)),
            dma((2,)),
            dma((2,)),
            dma,
            dma((2 * early + 2 * unknown,)),
            dma((2 * early + 2 * unknown,)),
            dma((early * size,)),
            dma((early * size,)),
            dma((early * size,)),
            dma((early * size,)),
            regular,
            regular,
        ],
        compiler_params=pltpu.CompilerParams(
            vmem_limit_bytes=62 * 10**6, collective_id=1, has_side_effects=True
        ),
        cost_estimate=pl.CostEstimate(flops=2 * 10**11, bytes_accessed=10**8, transcendentals=0),
        name="experts",
    )(rank_cols, routes, x, gy, *packed, *(side for both in near for side in both), *far)


def remote(source, target, send_sem, recv_sem, device):
    return pltpu.make_async_remote_copy(
        src_ref=source,
        dst_ref=target,
        send_sem=send_sem,
        recv_sem=recv_sem,
        device_id=device,
        device_id_type=pl.DeviceIdType.MESH,
    )


def chip_neighbours():
    me = lax.axis_index("dp")
    return me + 2 - 4 * lax.rem(me // 2, 2), me + 4 - 8 * lax.rem(me // 4, 2)


def meet(members, core):
    barrier = pltpu.get_barrier_semaphore()
    z = lax.axis_index("tensor")

    def signal(device):
        pl.semaphore_signal(barrier, inc=1, device_id=device, device_id_type=pl.DeviceIdType.MESH)

    @pl.when(z > 0)
    def _():
        signal({"tensor": z - 1})

    @pl.when(z < members - 1)
    def _():
        signal({"tensor": z + 1})

    for other in (*chip_neighbours(), *([sibling()] if core else [])):
        signal({"dp": other})
    inner = jnp.where((z > 0) & (z < members - 1), 1, 0)
    pl.semaphore_wait(barrier, 3 + inner + (1 if core else 0))


class LineGather:
    def __init__(self, members, at, send, recv):
        self.members, self.at, self.send, self.recv = members, at, send, recv

    def copies(self, hop):
        z, last = lax.axis_index("tensor"), self.members - 1
        up, down = z - hop + 1, z + hop - 1

        def copy(block, way, device):
            return lambda: remote(
                self.at(block), self.at(block), self.send.at[way, hop - 1], self.recv.at[way, hop - 1], {"tensor": device}
            )

        return (
            ((up >= 0) & (z < last), copy(up, 0, z + 1)),
            ((down <= last) & (z > 0), copy(down, 1, z - 1)),
        ), (
            (z - hop >= 0, copy(z - hop, 0, z)),
            (z + hop <= last, copy(z + hop, 1, z)),
        )

    def start(self, hop):
        for present, copy in self.copies(hop)[0]:

            @pl.when(present)
            def _():
                copy().start()

    def arrive(self, hop):
        for present, copy in self.copies(hop)[1]:

            @pl.when(present)
            def _():
                copy().wait_recv()

    def close(self):
        for hop in range(1, self.members):
            for present, copy in self.copies(hop)[0]:

                @pl.when(present)
                def _():
                    copy().wait_send()


class LineSum:
    def __init__(self, members, part, leaving, arriving, send, recv):
        self.members, self.part, self.leaving, self.arriving = members, part, leaving, arriving
        self.send, self.recv = send, recv

    def copy(self, way, hop, device):
        return remote(
            self.leaving.at[way],
            self.arriving.at[way, hop - 1],
            self.send.at[way, hop - 1],
            self.recv.at[way, hop - 1],
            {"tensor": device},
        )

    def ways(self, hop):
        z, last = lax.axis_index("tensor"), self.members - 1
        return (
            (0, z - hop >= 0, z - hop, z < last, z - 1, (z < last) & (z + 1 - hop >= 0)),
            (1, z + hop <= last, z + hop, z > 0, z + 1, (z > 0) & (z - 1 + hop <= last)),
        )

    def start(self, hop, begun=True):
        if hop + 1 < self.members and begun:
            self.leave(hop + 1)
        for way, present, block, behind, device, _ in self.ways(hop):

            @pl.when(present)
            def _():
                self.leaving[way] = self.part(block).astype(bf16)

            if hop + 1 < self.members:

                @pl.when(present & behind)
                def _():
                    both = self.part(block).astype(f32) + self.arriving[way, hop].astype(f32)
                    self.leaving[way] = both.astype(bf16)

            @pl.when(present)
            def _():
                self.copy(way, hop, device).start()

    def arrive(self, hop):
        for way, _, _, _, device, present in self.ways(hop):

            @pl.when(present)
            def _():
                self.copy(way, hop, device).wait_recv()

    def total(self, out):
        z, last = lax.axis_index("tensor"), self.members - 1
        out[...] = self.part(z).astype(f32)
        for way, present in ((0, z < last), (1, z > 0)):

            @pl.when(present)
            def _():
                out[...] += self.arriving[way, 0].astype(f32)

    def leave(self, hop):
        for way, present, _, _, device, _ in self.ways(hop):

            @pl.when(present)
            def _():
                self.copy(way, hop, device).wait_send()

    def close(self):
        self.leave(1)


def swap_blocks(values):
    me = lax.axis_index("dp")
    chip = values.shape[1] // 4
    four = [values[:, i * chip : (i + 1) * chip] for i in range(4)]
    y_side, x_side, core_side = lax.rem(me // 4, 2) == 1, lax.rem(me // 2, 2) == 1, lax.rem(me, 2) == 1
    four = [jnp.where(y_side, four[i ^ 2], four[i]) for i in range(4)]
    four = [jnp.where(x_side, four[i ^ 1], four[i]) for i in range(4)]
    four = [jnp.where(core_side, pltpu.roll(part, chip // 2, 1), part) for part in four]
    return jnp.concatenate(four, axis=1)


def in_vmem(count):
    return [pl.BlockSpec(memory_space=pltpu.VMEM)] * count


def pack_chunk(gate, up, down, begin):
    gate, up, down = (
        jnp.swapaxes(w[:, begin : begin + 2 * CALL_PAIRS, :], 0, 1) for w in (gate, up, down)
    )

    def pair(a, b):
        return [a[:, :HD], b[:, :HD], jnp.concatenate([a[:, HD:], b[:, HD:]], axis=1)]

    def inner(a, b):
        a, b, tails = pair(a, b)
        return [a, tails, b]

    return [
        jnp.concatenate(
            pair(gate[e], up[e]) + pair(gate[e + 1], up[e + 1]) + inner(down[e], down[e + 1]), axis=1
        )
        for e in range(0, 2 * CALL_PAIRS, 2)
    ]


def turn(values, cosine, sine):
    return values * cosine + pltpu.roll(values, HD // 2, 1) * sine


def front(
    tokens, q_weight, o_weight, k_weight, v_weight, gains, cosine, sine, cotangent, ids, route_weights, gate, up, down, members, devices
):
    height, part = q_weight.shape
    own_rows, width = cotangent.shape
    rows = own_rows * members
    kv = 2 * KV * HD
    tall = kv + HD
    lanes = 9 * HD
    calls = EXPERTS // 2 // CALL_PAIRS
    half = CALL_PAIRS // 2
    heads = width // HD
    per_kv = heads // KV
    last = members - 1
    dma = pltpu.SemaphoreType.DMA

    def kernel(*refs):
        x_ref, q_weight_ref, o_ref, k_ref, v_ref, gains_ref, cos_ref, sin_ref, cot_ref = refs[:9]
        ids_ref, weights_ref, gate_ref, up_ref, down_ref = refs[9:14]
        square_all, tall_all, grad_all, rank_cols, routes = refs[14:19]
        normed_ref, q_ref, kv_all, mixed_ref, hidden_ref, rows_all = refs[19:25]
        packed = refs[25 : 25 + calls]
        from_x, from_y, far_x, far_y, next_x, next_y = refs[25 + calls : 31 + calls]
        rest = refs[31 + calls :]
        line_send, line_recv, grad_send, grad_recv, kv_send, kv_recv, row_send, row_recv = rest[:8]
        chip_send, chip_recv, core_send, core_recv = rest[8:]
        me, z = lax.axis_index("dp"), lax.axis_index("tensor")
        x_side, y_side = chip_neighbours()
        diagonal = x_side + y_side - me
        core = sibling()

        def rows_of(device):
            return pl.ds(pl.multiple_of(device * height, 16), height)

        def block_of(ref):
            return lambda block: ref.at[pl.ds(pl.multiple_of(block * own_rows, 16), own_rows)]

        own = pl.ds(pl.multiple_of(z * own_rows, 16), own_rows)

        def pack(call):
            chunk = pack_chunk(gate_ref, up_ref, down_ref, 2 * CALL_PAIRS * call)
            for pair, value in enumerate(chunk):
                packed[call][pair] = value

        def chip(index, source, device, target=None):
            target = source if target is None else target
            return remote(source, target, chip_send.at[index], chip_recv.at[index], {"dp": device})

        def across(index, source):
            return remote(source, source, core_send.at[index], core_recv.at[index], {"dp": core})

        def tall_at(device):
            return tall_all.at[rows_of(device)]

        def square_at(device, side=None):
            span = slice(None) if side is None else slice(side * part, (side + 1) * part)
            return square_all.at[:, rows_of(device), span]

        trades = []

        def trade(index, source):
            trades.append(across(index, source))
            trades[-1].start()

        def there(index, device, of):
            across(index, of(core if device is None else device + core - me)).wait_recv()

        square_all[z, rows_of(me), :part] = q_weight_ref[...]
        square_all[z, rows_of(me), part:] = o_ref[...]
        tall_all[rows_of(me), : kv // 2] = k_ref[...]
        tall_all[rows_of(me), kv // 2 : kv] = v_ref[...]
        tall_all[rows_of(me), kv:] = gains_ref[...]
        line = LineGather(members, lambda block: square_all.at[block, rows_of(me)], line_send, line_recv)
        group = LineGather(members, block_of(grad_all), grad_send, grad_recv)
        kv_line = LineGather(members, block_of(kv_all), kv_send, kv_recv)
        row_line = LineGather(members, block_of(rows_all), row_send, row_recv)
        moves = [
            chip(0, tall_at(me), x_side),
            chip(1, tall_at(me), y_side),
            chip(2, packed[0].at[:half], x_side, from_x.at[:half]),
            chip(3, packed[0].at[:half], y_side, from_y.at[:half]),
            chip(4, square_at(me), x_side),
            chip(5, square_at(me), y_side),
            chip(6, packed[0].at[half:], x_side, from_x.at[half:]),
            chip(7, packed[0].at[half:], y_side, from_y.at[half:]),
            chip(8, tall_at(x_side), y_side),
            chip(9, square_at(x_side, 0), y_side),
            chip(10, square_at(y_side, 1), x_side),
            chip(11, from_x.at[:half], y_side, far_x),
            chip(12, from_y.at[half:], x_side, far_y),
            chip(13, packed[1], x_side, next_x),
            chip(14, packed[1], y_side, next_y),
        ]
        meet(members, True)
        line.start(1)
        for copy in moves[:2]:
            copy.start()
        trade(0, tall_at(me))
        pack(0)
        for index, device in ((0, x_side), (1, y_side)):
            chip(index, tall_at(device), device).wait_recv()
        moves[8].start()
        trade(2, tall_at(x_side))
        trade(3, tall_at(y_side))
        line.arrive(1)
        if last > 1:
            line.start(2)
        grad_all[own, :] = swap_blocks(cot_ref[...]).astype(bf16)
        chip(8, tall_at(diagonal), y_side).wait_recv()
        trade(6, tall_at(diagonal))
        for hop in range(2, members):
            line.arrive(hop)
            if hop < last:
                line.start(hop + 1)
        for copy in moves[4:6]:
            copy.start()
        trade(1, square_at(me))

        for index, device in ((0, None), (2, x_side), (3, y_side), (6, diagonal)):
            there(index, device, tall_at)
        gain_one, gain_two = (jnp.transpose(tall_all[:, kv:].astype(f32))[i : i + 1] for i in range(2))
        cosine, sine = cos_ref[own], sin_ref[own]
        normed_ref[...] = (rms_pieces(x_ref[...].astype(f32))[1] * gain_one).astype(bf16)
        made = nn(normed_ref[...], tall_all[:, :kv])
        for head in range(KV):
            span = slice(head * HD, (head + 1) * HD)
            kv_all[own, span] = turn(made[:, span], cosine, sine).astype(bf16)
        kv_all[own, KV * HD :] = made[:, KV * HD :].astype(bf16)
        kv_line.start(1)

        expert = lax.broadcasted_iota(jnp.int32, (HD, rows), 0)
        weight = jnp.zeros((HD, rows), f32)
        named = jnp.zeros((HD, rows), f32)
        for route in range(ids_ref.shape[0]):
            here = ids_ref[route : route + 1, :] == expert
            named = jnp.where(here, 1.0, named)
            weight = jnp.where(here, weights_ref[route : route + 1, :], weight)
        row = lax.broadcasted_iota(jnp.int32, (rows, rows), 0)
        later = (row < lax.broadcasted_iota(jnp.int32, (rows, rows), 1)).astype(bf16)
        rank = jnp.where(named > 0.0, nn(named.astype(bf16), later), -1.0)
        rank_cols[...] = jnp.transpose(rank).astype(bf16)
        for e in range(EXPERTS):
            routes[e, 0:1, :] = rank[e : e + 1]
            routes[e, 1:2, :] = weight[e : e + 1]
        for call in range(1, calls):
            kv_line_hop = call
            if kv_line_hop < members:
                kv_line.arrive(kv_line_hop)
                if kv_line_hop < last:
                    kv_line.start(kv_line_hop + 1)
            pack(call)
        for hop in range(calls, members):
            kv_line.arrive(hop)
            if hop < last:
                kv_line.start(hop + 1)
        group.start(1)

        for index, device in ((4, x_side), (5, y_side)):
            chip(index, square_at(device), device).wait_recv()
        for copy in moves[9:11]:
            copy.start()
        trade(4, square_at(x_side))
        trade(5, square_at(y_side))
        chip(9, square_at(diagonal, 0), y_side).wait_recv()
        chip(10, square_at(diagonal, 1), x_side).wait_recv()
        trade(7, square_at(diagonal))
        for copy in (*moves[2:4], *moves[6:8]):
            copy.start()
        group.arrive(1)
        if last > 1:
            group.start(2)
        for index, device in ((1, None), (4, x_side), (5, y_side), (7, diagonal)):
            there(index, device, square_at)

        for t in range(members):
            made = nn(normed_ref[...], square_all[t, :, :part])
            for head in range(part // HD):
                span = slice(head * HD, (head + 1) * HD)
                q_ref[:, t * part + head * HD : t * part + (head + 1) * HD] = turn(
                    made[:, span], cosine, sine
                ).astype(bf16)

        def attend(begin, end):
            @pl.loop(begin, end)
            def _(head):
                span = pl.ds(pl.multiple_of(head * HD, HD), HD)
                key_span = pl.ds(pl.multiple_of(head // per_kv * HD, HD), HD)
                value_span = pl.ds(pl.multiple_of((KV + head // per_kv) * HD, HD), HD)
                p = probabilities(q_ref[:, span], kv_all[:, key_span], z * own_rows).astype(bf16)
                mixed_ref[:, span] = nn(p, kv_all[:, value_span]).astype(bf16)

        for copy in moves[13:15]:
            copy.start()
        attend(0, heads // 2)
        for hop in range(2, members):
            group.arrive(hop)
            if hop < last:
                group.start(hop + 1)
            if hop == 2:
                attend(heads // 2, heads)
        if members <= 2:
            attend(heads // 2, heads)
        hidden = x_ref[...].astype(f32)
        for t in range(members):
            hidden += nt(mixed_ref[:, t * part : (t + 1) * part], square_all[t, :, part:])
        hidden_ref[...] = hidden
        rows_all[own, :] = swap_blocks(rms_pieces(hidden)[1] * gain_two).astype(bf16)
        for hop in range(1, members):
            row_line.start(hop)
            if hop == 1:
                for copy in (*moves[2:4], *moves[6:8]):
                    copy.wait_recv()
                for copy in moves[11:13]:
                    copy.start()
            row_line.arrive(hop)
        for copy in moves[11:]:
            copy.wait_recv()
        for copy in moves + trades:
            copy.wait_send()
        for each in (line, group, kv_line, row_line):
            each.close()

    chunk_shape = jax.ShapeDtypeStruct((CALL_PAIRS, height, lanes), bf16)
    half_shape = jax.ShapeDtypeStruct((half, height, lanes), bf16)
    low_rows = jax.ShapeDtypeStruct((own_rows, width), bf16)
    return pl.pallas_call(
        kernel,
        in_specs=in_vmem(14),
        out_specs=in_vmem(11 + calls) + [pl.BlockSpec(memory_space=pl.ANY)] * 6,
        out_shape=[
            jax.ShapeDtypeStruct((members, devices * height, 2 * part), bf16),
            jax.ShapeDtypeStruct((devices * height, tall), bf16),
            jax.ShapeDtypeStruct((rows, width), bf16),
            jax.ShapeDtypeStruct((rows, HD), bf16),
            jax.ShapeDtypeStruct((EXPERTS, 2, rows), f32),
            low_rows,
            low_rows,
            jax.ShapeDtypeStruct((rows, kv), bf16),
            low_rows,
            jax.ShapeDtypeStruct((own_rows, width), f32),
            jax.ShapeDtypeStruct((rows, width), bf16),
        ]
        + [chunk_shape] * (calls + 2)
        + [half_shape] * 2
        + [chunk_shape] * 2,
        scratch_shapes=[dma((2, members - 1))] * 8 + [dma((15,))] * 2 + [dma((8,))] * 2,
        compiler_params=pltpu.CompilerParams(collective_id=2, has_side_effects=True, vmem_limit_bytes=62 * 10**6),
        cost_estimate=pl.CostEstimate(flops=2 * 10**11, bytes_accessed=10**7, transcendentals=0),
        name="front",
    )(
        tokens,
        q_weight,
        o_weight,
        k_weight,
        v_weight,
        gains,
        cosine,
        sine,
        cotangent,
        ids,
        route_weights,
        gate,
        up,
        down,
    )


def gain_rows(tall_ref, kv):
    return jnp.transpose(tall_ref[:, kv:].astype(f32))


def attention_back(
    sums, cotangent, hidden, tokens, normed, q, kv_all, mixed, square, tall, cosine, sine, grads, to_x, to_y, members
):
    own_rows, width = tokens.shape
    rows = own_rows * members
    kv = 2 * KV * HD
    heads = width // HD
    per_kv = heads // KV
    part = width // members
    dma = pltpu.SemaphoreType.DMA

    def kernel(sums_ref, cot_ref, hidden_ref, x_ref, normed_ref, q_ref, kv_ref, mixed_ref, square_ref, tall_ref, *rest):
        cos_ref, sin_ref, grads_ref, to_x_ref, to_y_ref = rest[:5]
        grad_ref, moe_out, parts, x_before, y_before, x_last, y_last, x_late, y_late = rest[5:14]
        do_ref, dq_ref, dkv_ref, total, kv_total, stage, tall_part, back_part = rest[14:22]
        back_leave, back_arrive, moe_leave, moe_arrive, kv_leave, kv_arrive = rest[22:28]
        back_send, back_recv, moe_send, moe_recv, kv_send, kv_recv, stage_sem, part_sem = rest[28:36]
        through, added, added_sem, chip_send, chip_recv = rest[36:]
        z = lax.axis_index("tensor")
        x_side, y_side = chip_neighbours()
        first, second = slice(0, size // 2), slice(size // 2, size)

        def chunk(block, span):
            return grads_ref.at[block, pairs_before + span.start : pairs_before + span.stop]


        def chip(index, source, target, device):
            return remote(source, target, chip_send.at[index], chip_recv.at[index], {"dp": device})

        def sums_of(begin):
            return [
                pltpu.make_async_copy(
                    sums_ref.at[b * own_rows : (b + 1) * own_rows, begin : begin + width], back_part.at[b], part_sem.at[b]
                )
                for b in range(members)
            ]

        loads = sums_of(width) + [
            pltpu.make_async_copy(chunk(1, second), added.at[0], added_sem.at[0]),
            pltpu.make_async_copy(chunk(2, first), added.at[1], added_sem.at[1]),
        ]
        for copy in loads:
            copy.start()
        meet(members, False)
        moves = [
            chip(0, chunk(3, first), through.at[0], x_side),
            chip(1, chunk(3, second), through.at[1], y_side),
            chip(2, to_x_ref.at[:soon], x_before, x_side),
            chip(3, to_y_ref.at[:soon], y_before, y_side),
            chip(4, chunk(1, first), x_last.at[first], x_side),
            chip(5, chunk(2, second), y_last.at[second], y_side),
            chip(6, added.at[0], x_last.at[second], x_side),
            chip(7, added.at[1], y_last.at[first], y_side),
        ]
        for i in range(late):
            begin, here = (i + STRAIGHT) * size, slice(i * size // 2, (i + 1) * size // 2)
            middle = begin + size // 2
            moves.append(chip(8 + 2 * i, grads_ref.at[1, begin:middle], x_late.at[here], x_side))
            moves.append(chip(9 + 2 * i, grads_ref.at[2, middle : begin + size], y_late.at[here], y_side))
        for copy in (*moves[:6], *moves[8:]):
            copy.start()
        own = pl.ds(pl.multiple_of(z * own_rows, 16), own_rows)
        for copy in loads:
            copy.wait()

        def block(ref, span):
            return lambda b: ref[pl.ds(pl.multiple_of(b * own_rows, 16), own_rows), span]

        back = LineSum(members, lambda b: back_part[b], back_leave, back_arrive, back_send, back_recv)
        moe = LineSum(members, lambda b: back_part[b], moe_leave, moe_arrive, moe_send, moe_recv)
        pairs = LineSum(members, block(dkv_ref, slice(None)), kv_leave, kv_arrive, kv_send, kv_recv)
        gains = gain_rows(tall_ref, kv)
        cosine, sine = cos_ref[own], sin_ref[own]
        last = members - 1
        stored = []

        def store(value, at):
            slot = len(stored) % 2
            if len(stored) >= 2:
                stored[-2].wait()
            stage[slot] = value.astype(bf16)
            copy = pltpu.make_async_copy(stage.at[slot], parts.at[:, at : at + part], stage_sem.at[slot])
            copy.start()
            stored.append(copy)

        for hop in range(last, 0, -1):
            back.start(hop)
            back.arrive(hop)
        back.total(total)
        loads = sums_of(0)
        for copy in loads:
            copy.start()
        normed_grad = swap_blocks(total[...])
        inverse, unit = rms_pieces(hidden_ref[...])
        for copy in loads:
            copy.wait()
        if last > 1:
            moe.start(last)
        by_hidden, gain_two = rms_backward(normed_grad, unit, inverse, gains[1:2])
        grad_ref[...] = cot_ref[...] + by_hidden
        low = grad_ref[...].astype(bf16)
        for t in range(members):
            span = slice(t * part, (t + 1) * part)
            do_ref[:, span] = nn(low, square_ref[t, :, part:]).astype(bf16)
            store(tn(low, mixed_ref[:, span]), t * part)
        dkv_ref[...] = jnp.zeros_like(dkv_ref)
        first_row = z * own_rows

        def attend(begin, end):
            @pl.loop(begin, end)
            def _(head):
                span = pl.ds(pl.multiple_of(head * HD, HD), HD)
                key_span = pl.ds(pl.multiple_of(head // per_kv * HD, HD), HD)
                value_span = pl.ds(pl.multiple_of((KV + head // per_kv) * HD, HD), HD)
                q_now, k_now, do_now = q_ref[:, span], kv_ref[:, key_span], do_ref[:, span]
                p = probabilities(q_now, k_now, first_row)
                dp = nt(do_now, kv_ref[:, value_span])
                ds = (p * (dp - jnp.sum(p * dp, axis=-1, keepdims=True))).astype(bf16)
                dq_ref[:, span] = turn(nn(ds, k_now) * (HD**-0.5), cosine, -sine).astype(bf16)
                dkv_ref[:, key_span] += tn(ds, q_now) * (HD**-0.5)
                dkv_ref[:, value_span] += tn(p.astype(bf16), do_now)

        attend(0, heads // 3)
        if last > 1:
            moe.arrive(last)
            if last > 2:
                moe.start(last - 1)
        attend(heads // 3, heads)

        pairs.start(last)

        def query_part(t):
            store(tn(normed_ref[...], dq_ref[:, t * part : (t + 1) * part]), width + t * part)

        def normed_part(t):
            made = nt(dq_ref[:, t * part : (t + 1) * part], square_ref[t, :, :part])
            if t == 0:
                total[...] = made
            else:
                total[...] += made

        for i, copy in enumerate(moves[:2]):
            copy.wait()
            added[1 - i] = (added[1 - i].astype(f32) + through[i].astype(f32)).astype(bf16)
            moves[7 - i].start()
        work = [(do, t) for do in (query_part, normed_part) for t in range(members)]
        share = len(work) // last
        for hop in range(last, 0, -1):
            for do, t in work[: share if hop > 1 else None]:
                do(t)
            work = work[share:]
            pairs.arrive(hop)
            if hop > 1:
                pairs.start(hop - 1)
        for hop in range(last - 1, 1, -1):
            moe.arrive(hop)
            if hop > 2:
                moe.start(hop - 1)
        for way, present in ((0, (z < last) & (z >= 1)), (1, (z > 0) & (z + 1 <= last))):

            @pl.when(present)
            def _():
                moe_out[way] = moe_arrive[way, 1]

            @pl.when(jnp.logical_not(present))
            def _():
                moe_out[way] = jnp.zeros((own_rows, width), bf16)

        pairs.total(kv_total)
        low_kv = [
            turn(kv_total[:, head * HD : (head + 1) * HD], cosine, -sine).astype(bf16) for head in range(KV)
        ] + [kv_total[:, KV * HD :].astype(bf16)]
        low_kv = jnp.concatenate(low_kv, axis=1)
        normed_grad = total[...] + nt(low_kv, tall_ref[:, :kv])
        inverse, unit = rms_pieces(x_ref[...].astype(f32))
        by_tokens, gain_one = rms_backward(normed_grad, unit, inverse, gains[0:1])
        grad_ref[...] += by_tokens
        tall_part[:, :kv] = tn(normed_ref[...], low_kv).astype(bf16)
        row = lax.broadcasted_iota(jnp.int32, (HD, width), 0)
        both = jnp.where(row == 0, gain_one[None], jnp.where(row == 1, gain_two[None], 0.0))
        tall_part[:, kv:] = jnp.transpose(both).astype(bf16)
        tall_copy = pltpu.make_async_copy(tall_part, parts.at[:, 2 * width :], stage_sem.at[2])
        tall_copy.start()
        for line in (back, pairs):
            line.close()
        if last > 1:
            moe.leave(2)
        for copy in (*stored[-2:], tall_copy, *moves[2:]):
            copy.wait()

    hops = (2, members - 1)
    anywhere = pl.BlockSpec(memory_space=pl.ANY)
    _, height, lanes = to_x.shape
    size = CALL_PAIRS
    pairs_before = grads.shape[1] - size
    late = pairs_before // size - STRAIGHT
    soon = to_x.shape[0] - size // 2
    halves = (2, size // 2, height, lanes)
    return pl.pallas_call(
        kernel,
        in_specs=[anywhere] + in_vmem(11) + [anywhere] * 3,
        out_specs=in_vmem(2) + [anywhere] * 7,
        out_shape=[
            jax.ShapeDtypeStruct((own_rows, width), f32),
            jax.ShapeDtypeStruct((2, own_rows, width), bf16),
            jax.ShapeDtypeStruct((width, 2 * width + tall.shape[1]), bf16),
        ]
        + [jax.ShapeDtypeStruct((soon, height, lanes), bf16)] * 2
        + [jax.ShapeDtypeStruct((size, height, lanes), bf16)] * 2
        + [jax.ShapeDtypeStruct((late * size // 2, height, lanes), bf16)] * 2,
        scratch_shapes=[
            pltpu.VMEM((own_rows, width), bf16),
            pltpu.VMEM((own_rows, width), bf16),
            pltpu.VMEM((rows, kv), f32),
            pltpu.VMEM((own_rows, width), f32),
            pltpu.VMEM((own_rows, kv), f32),
            pltpu.VMEM((2, width, part), bf16),
            pltpu.VMEM(tall.shape, bf16),
            pltpu.VMEM((members, own_rows, width), bf16),
            pltpu.VMEM((2, own_rows, width), bf16),
            pltpu.VMEM((*hops, own_rows, width), bf16),
            pltpu.VMEM((2, own_rows, width), bf16),
            pltpu.VMEM((*hops, own_rows, width), bf16),
            pltpu.VMEM((2, own_rows, kv), bf16),
            pltpu.VMEM((*hops, own_rows, kv), bf16),
        ]
        + [dma(hops)] * 6
        + [dma((3,)), dma((members,)), pltpu.VMEM(halves, bf16), pltpu.VMEM(halves, bf16), dma((2,)), dma((8 + 2 * late,)), dma((8 + 2 * late,))],
        compiler_params=pltpu.CompilerParams(collective_id=4, has_side_effects=True, vmem_limit_bytes=62 * 10**6),
        cost_estimate=pl.CostEstimate(flops=10**11, bytes_accessed=10**7, transcendentals=0),
        name="attention_back",
    )(
        sums, cotangent, hidden, tokens, normed, q, kv_all, mixed, square, tall, cosine, sine, grads, to_x, to_y
    )


def reduce_small(parts, sums, moved, hidden, to_x, to_y, members, devices):
    own_rows = hidden.shape[0]
    width = parts.shape[0]
    height = width // devices
    lanes = parts.shape[1]
    tall = lanes - 2 * width
    kv = KV * HD
    part = width // members
    half = height // 2
    groups = (slice(0, width), slice(width, lanes))
    begun = to_x.shape[0] - CALL_PAIRS // 2
    dma = pltpu.SemaphoreType.DMA

    def kernel(parts_ref, sums_ref, to_x_ref, to_y_ref, moved_ref, hidden_ref, *rest):
        out_ref, q_out, o_out, k_out, v_out, gains_out, x_end, y_end = rest[:8]
        rest = rest[8:]
        own, theirs, leave, arrive, blocks, line_leave, line_arrive, tall_all, line_total = rest[:9]
        moe_part, moe_leave, moe_arrive, total_ref = rest[9:13]
        own_sem, core_send, core_recv, chip_send, chip_recv = rest[13:18]
        o_send, o_recv, q_send, q_recv, tall_send, tall_recv, moe_send, moe_recv, part_sem, end_send, end_recv = rest[18:]
        me, z = lax.axis_index("dp"), lax.axis_index("tensor")
        x_side, y_side = chip_neighbours()
        core = sibling()
        chips = [me, x_side, y_side, x_side + y_side - me]
        loads = [
            pltpu.make_async_copy(
                sums_ref.at[b * own_rows : (b + 1) * own_rows, :width], moe_part.at[b], part_sem.at[b]
            )
            for b in range(members)
        ]
        for copy in loads:
            copy.start()

        def rows(device, span):
            return parts_ref.at[pl.ds(pl.multiple_of(device * height, 16), height), span]

        def trade(m, g):
            target = theirs.at[m, :, groups[g]]
            source = rows(chips[m] + core - me, groups[g])
            return remote(source, target, core_send.at[m, g], core_recv.at[m, g], {"dp": core})

        def keep(m, g):
            return pltpu.make_async_copy(rows(chips[m], groups[g]), own.at[m, :, groups[g]], own_sem.at[m, g])

        order = (3, 2, 1, 0)
        for g in range(2):
            for m in order:
                keep(m, g).start()
        meet(members, True)
        for g in range(2):
            for m in order:
                trade(m, g).start()
        moe = LineSum(members, lambda b: moe_part[b], moe_leave, moe_arrive, moe_send, moe_recv)
        if members > 2:
            for way in range(2):
                moe_arrive[way, 1] = moved_ref[way]
        for copy in loads:
            copy.wait()
        moe.start(1, False)

        def both(m, rows, lanes):
            return own[m, rows, lanes].astype(f32) + theirs[m, rows, lanes].astype(f32)

        def chip(index, g, slot, span, device):
            source, target = leave.at[slot, span, groups[g]], arrive.at[slot, span, groups[g]]
            return remote(source, target, chip_send.at[index, g], chip_recv.at[index, g], {"dp": device})

        first, second = slice(0, half), slice(half, height)
        every = slice(0, height)
        far = [[chip(0, g, 0, first, x_side), chip(1, g, 0, second, y_side)] for g in range(2)]
        near = [[chip(2, g, 1, every, x_side), chip(3, g, 2, every, y_side)] for g in range(2)]

        def ready(m, g):
            trade(m, g).wait()
            keep(m, g).wait()

        for g, span in enumerate(groups):
            ready(3, g)
            for copy, part_of in zip(far[g], (first, second)):
                leave[0, part_of, span] = both(3, part_of, span).astype(bf16)
                copy.start()
            for m in order[1:]:
                ready(m, g)
        for g, span in enumerate(groups):
            leave[1, first, span] = both(1, first, span).astype(bf16)
            leave[2, second, span] = both(2, second, span).astype(bf16)
            far[g][1].wait()
            leave[1, second, span] = (both(1, second, span) + arrive[0, second, span].astype(f32)).astype(bf16)
            near[g][0].start()
            far[g][0].wait()
            leave[2, first, span] = (both(2, first, span) + arrive[0, first, span].astype(f32)).astype(bf16)
            near[g][1].start()
        moe.arrive(1)
        moe.total(total_ref)
        out_ref[...] = (hidden_ref[...] + swap_blocks(total_ref[...])).astype(bf16)

        def total(span):
            return both(0, every, span) + arrive[1, :, span].astype(f32) + arrive[2, :, span].astype(f32)

        lines = [
            LineSum(members, lambda b, g=g: blocks[g, b], line_leave.at[g], line_arrive.at[g], send, recv)
            for g, (send, recv) in enumerate(((o_send, o_recv), (q_send, q_recv)))
        ]
        group = LineGather(members, lambda b: tall_all.at[b], tall_send, tall_recv)

        def hop_of(line, hop):
            line.arrive(hop)
            if hop > 1:
                line.start(hop - 1)

        last = members - 1
        for copy in near[0]:
            copy.wait()
        for t in range(members):
            blocks[0, t] = total(slice(t * part, (t + 1) * part))
        lines[0].start(last)
        for copy in near[1]:
            copy.wait()
        ends = [
            remote(source.at[begun:], target, end_send.at[i], end_recv.at[i], {"dp": device})
            for i, (source, target, device) in enumerate(((to_x_ref, x_end, x_side), (to_y_ref, y_end, y_side)))
        ]
        for copy in ends:
            copy.start()
        tall_all[z] = total(slice(2 * width, lanes)).astype(bf16)
        for t in range(members):
            blocks[1, t] = total(slice(width + t * part, width + (t + 1) * part))
        lines[1].start(last)
        group.start(1)
        for hop in range(last, 0, -1):
            hop_of(lines[0], hop)
            hop_of(lines[1], hop)
            group.arrive(members - hop)
            if hop > 1:
                group.start(members - hop + 1)
        lines[0].total(line_total)
        o_out[...] = line_total[...]
        lines[1].total(line_total)
        q_out[...] = line_total[...]
        summed = tall_all[0].astype(f32)
        for t in range(1, members):
            summed += tall_all[t].astype(f32)
        k_out[...] = summed[:, :kv]
        v_out[...] = summed[:, kv : 2 * kv]
        gains_out[...] = summed[:, 2 * kv :]
        for line in (*lines, group, moe):
            line.close()
        for copy in ends:
            copy.wait()

    hops = (2, members - 1)
    return pl.pallas_call(
        kernel,
        in_specs=[pl.BlockSpec(memory_space=pl.ANY)] * 4 + in_vmem(2),
        out_specs=in_vmem(6) + [pl.BlockSpec(memory_space=pl.ANY)] * 2,
        out_shape=[
            jax.ShapeDtypeStruct((own_rows, width), bf16),
            jax.ShapeDtypeStruct((height, part), f32),
            jax.ShapeDtypeStruct((height, part), f32),
            jax.ShapeDtypeStruct((height, kv), f32),
            jax.ShapeDtypeStruct((height, kv), f32),
            jax.ShapeDtypeStruct((height, tall - 2 * kv), f32),
        ]
        + [jax.ShapeDtypeStruct((CALL_PAIRS // 2, *to_x.shape[1:]), bf16)] * 2,
        scratch_shapes=[
            pltpu.VMEM((4, height, lanes), bf16),
            pltpu.VMEM((4, height, lanes), bf16),
            pltpu.VMEM((3, height, lanes), bf16),
            pltpu.VMEM((3, height, lanes), bf16),
            pltpu.VMEM((2, members, height, part), f32),
            pltpu.VMEM((2, 2, height, part), bf16),
            pltpu.VMEM((2, *hops, height, part), bf16),
            pltpu.VMEM((members, height, tall), bf16),
            pltpu.VMEM((height, part), f32),
            pltpu.VMEM((members, own_rows, width), bf16),
            pltpu.VMEM((2, own_rows, width), bf16),
            pltpu.VMEM((*hops, own_rows, width), bf16),
            pltpu.VMEM((own_rows, width), f32),
            dma((4, 2)),
            dma((4, 2)),
            dma((4, 2)),
            dma((4, 2)),
            dma((4, 2)),
        ]
        + [dma(hops)] * 8
        + [dma((members,)), dma((2,)), dma((2,))],
        compiler_params=pltpu.CompilerParams(collective_id=5, has_side_effects=True, vmem_limit_bytes=60 * 2**20),
        cost_estimate=pl.CostEstimate(flops=8 * 10**10, bytes_accessed=10**7, transcendentals=0),
        name="reduce_small",
    )(parts, sums, to_x, to_y, moved, hidden)


def unpack_all(grads, plain, added, last):
    _, pairs, height, lanes = grads.shape
    half = CALL_PAIRS // 2
    units = lanes // 6
    tail = units - HD
    step = 48 if height % 48 == 0 else height
    kinds = (*plain, *added, last[:1], last[1:])
    others = [array for kind in kinds for array in kind]

    def kernel(own, *refs):
        gate, up, down = refs[len(others) :]
        given = iter(refs)
        plain_x, plain_y, added_x, added_y, last_x, last_y = (
            [(ref, i) for _, ref in zip(kind, given) for i in range(ref.shape[0])] for kind in kinds
        )

        def of(kind, at):
            ref, i = kind[at]
            return ref[i].astype(f32)

        for call in range(pairs // CALL_PAIRS):
            found = [[], [], []]
            for turn in range(CALL_PAIRS):
                pair = call * CALL_PAIRS + turn
                at = call * half + turn % half
                if pair >= pairs - CALL_PAIRS:
                    by_x, by_y = of(last_x, turn), of(last_y, turn)
                elif turn < half:
                    by_x, by_y = of(plain_x, at), of(added_y, at)
                else:
                    by_x, by_y = of(added_x, at), of(plain_y, at)
                value = own[0, pair].astype(f32) + by_x + by_y
                tiles = [value[:, i * HD : (i + 1) * HD] for i in range(9)]
                for i, (a, b, both) in enumerate(((0, 1, 2), (3, 4, 5), (6, 8, 7))):
                    left = jnp.concatenate([tiles[a], tiles[both][:, :tail]], axis=1)
                    right = jnp.concatenate([tiles[b], tiles[both][:, tail:]], axis=1)
                    if i < 2:
                        found[0].append(left)
                        found[1].append(right)
                    else:
                        found[2] += [left, right]
            span = slice(2 * CALL_PAIRS * call, 2 * CALL_PAIRS * (call + 1))
            for out, values in zip((gate, up, down), found):
                out[:, span, :] = jnp.swapaxes(jnp.stack(values), 0, 1)

    shape = (height, 2 * pairs, units)
    return pl.pallas_call(
        kernel,
        grid=(height // step,),
        in_specs=[pl.BlockSpec((1, pairs, step, lanes), lambda i: (0, 0, i, 0))]
        + [pl.BlockSpec((other.shape[0], step, lanes), lambda i: (0, i, 0)) for other in others],
        out_specs=[pl.BlockSpec((step, *shape[1:]), lambda i: (i, 0, 0))] * 3,
        out_shape=[jax.ShapeDtypeStruct(shape, f32)] * 3,
        compiler_params=pltpu.CompilerParams(vmem_limit_bytes=48 * 2**20),
        name="unpack",
    )(grads, *others)


def pack(gate, up, down):
    def pair(a, b):
        return jnp.concatenate([a[..., :HD], b[..., :HD], a[..., HD:], b[..., HD:]], axis=-1)

    gate, up, down = (jnp.transpose(w, (1, 0, 2)) for w in (gate, up, down))
    gate_up = pair(gate, up)
    a, b = down[0::2], down[1::2]
    inner = jnp.concatenate([a[..., :HD], a[..., HD:], b[..., HD:], b[..., :HD]], axis=-1)
    return jnp.concatenate([gate_up[0::2], gate_up[1::2], inner], axis=-1)


def unpack(packed):
    n, height, lanes = packed.shape
    third = lanes // 3

    def halves(both):
        tail = third // 2 - HD
        a = jnp.concatenate([both[..., :HD], both[..., 2 * HD : 2 * HD + tail]], axis=-1)
        b = jnp.concatenate([both[..., HD : 2 * HD], both[..., 2 * HD + tail :]], axis=-1)
        return a, b

    def experts(even, odd):
        both = jnp.stack([even, odd], axis=1).reshape(2 * n, height, third // 2)
        return jnp.transpose(both, (1, 0, 2))

    gate0, up0 = halves(packed[..., :third])
    gate1, up1 = halves(packed[..., third : 2 * third])
    down0, down1 = packed[..., 2 * third : 2 * third + third // 2], packed[..., 2 * third + third // 2 :]
    tail = third // 2 - HD
    down1 = jnp.concatenate([down1[..., tail:], down1[..., :tail]], axis=-1)
    return experts(gate0, gate1), experts(up0, up1), experts(down0, down1)


def routes_of(expert_ids, route_weights):
    rows = expert_ids.shape[0]
    lanes = jnp.arange(EXPERTS, dtype=jnp.int32)
    named = expert_ids[:, :, None] == lanes
    member_of = jnp.any(named, axis=1)
    weight_of = jnp.sum(jnp.where(named, route_weights[:, :, None], 0.0), axis=1)
    earlier = jnp.arange(rows)[:, None] > jnp.arange(rows)[None, :]
    rank = jnp.where(member_of, nn(earlier.astype(bf16), member_of.astype(bf16)), -1.0)
    rank_cols = jnp.pad(rank, ((0, 0), (0, HD)), constant_values=-1.0).astype(bf16)
    return rank_cols, jnp.stack([rank.T, weight_of.T], axis=1)


def body_anywhere(
    tokens,
    expert_ids,
    route_weights,
    attn_gain,
    q_weight,
    k_weight,
    v_weight,
    o_weight,
    moe_gain,
    gate_weight,
    up_weight,
    down_weight,
    cotangent,
):
    members = lax.axis_size("tensor")
    member = lax.axis_index("tensor")
    own_rows, width = tokens.shape
    rows = own_rows * members
    pairs = EXPERTS // 2
    calls = pairs // CALL_PAIRS

    packed = [
        pack(*(w[:, 2 * CALL_PAIRS * i : 2 * CALL_PAIRS * (i + 1)] for w in (gate_weight, up_weight, down_weight)))
        for i in range(calls)
    ]
    gathered = [lax.all_gather(own, "dp", axis=1, tiled=True) for own in packed]

    gain_one = lax.all_gather(attn_gain, "dp", axis=0, tiled=True).astype(f32)
    gain_two = lax.all_gather(moe_gain, "dp", axis=0, tiled=True).astype(f32)
    kv_full = lax.all_gather(jnp.concatenate([k_weight, v_weight], axis=1), "dp", axis=0, tiled=True)
    q_full = lax.all_gather(lax.all_gather(q_weight, "dp", axis=0, tiled=True), "tensor", axis=0)
    o_full = lax.all_gather(lax.all_gather(o_weight, "dp", axis=0, tiled=True), "tensor", axis=0)
    kv_width = k_weight.shape[1]

    rank_cols, routes = routes_of(expert_ids, route_weights)

    grad_low = cotangent.astype(bf16)
    grad_all = lax.all_gather(grad_low, "tensor", axis=0, tiled=True)

    x = tokens.astype(f32)
    inverse_one, unit_one = rms_pieces(x)
    normed_one = (unit_one * gain_one).astype(bf16)
    first_row = (member * own_rows).reshape(1)
    cos_table, sin_table = rope_tables(member * own_rows + jnp.arange(own_rows, dtype=jnp.int32))
    kv_own = nn(normed_one, kv_full)
    kv_own = jnp.concatenate(
        [rotate(kv_own[:, :kv_width], cos_table, sin_table), kv_own[:, kv_width:]], axis=1
    ).astype(bf16)
    kv_all = lax.all_gather(kv_own, "tensor", axis=0, tiled=True)
    keys, values = kv_all[:, :kv_width], kv_all[:, kv_width:]
    queries = jnp.concatenate([nn(normed_one, q_full[t]) for t in range(members)], axis=1)
    queries = rotate(queries, cos_table, sin_table).astype(bf16)
    mixed = attend_forward(first_row, queries, keys, values)
    part = width // members
    branch = sum(nt(mixed[:, t * part : (t + 1) * part], o_full[t]) for t in range(members))
    hidden = x + branch
    inverse_two, unit_two = rms_pieces(hidden)
    normed_two = (unit_two * gain_two).astype(bf16)
    rows_all = lax.all_gather(normed_two, "tensor", axis=0, tiled=True)

    sums = jnp.zeros((rows, 2 * width), f32)
    chunks = []
    for call in range(calls):
        some = slice(2 * CALL_PAIRS * call, 2 * CALL_PAIRS * (call + 1))
        columns = slice(2 * CALL_PAIRS * call, 2 * CALL_PAIRS * call + HD)
        grads, sums = expert_call(
            rank_cols[:, columns],
            routes[some],
            rows_all,
            grad_all,
            gathered[call],
            sums,
        )
        chunks.append(grads)
    shares = [
        unpack(lax.psum_scatter(grads, "dp", scatter_dimension=1, tiled=True).astype(f32)) for grads in chunks
    ]
    gate_out, up_out, down_out = (jnp.concatenate(parts, axis=1) for parts in zip(*shares))

    low_sums = sums.astype(bf16)
    normed_grad = lax.psum_scatter(low_sums[:, width:], "tensor", scatter_dimension=0, tiled=True).astype(f32)
    moe_own = lax.psum_scatter(low_sums[:, :width], "tensor", scatter_dimension=0, tiled=True).astype(f32)
    output = (hidden + moe_own).astype(bf16)

    back_two, gain_two_part = rms_backward(normed_grad, unit_two, inverse_two, gain_two)
    hidden_grad = cotangent + back_two
    hidden_low = hidden_grad.astype(bf16)
    mixed_grad = jnp.concatenate([nn(hidden_low, o_full[t]) for t in range(members)], axis=1).astype(bf16)
    o_part = jnp.stack([tn(hidden_low, mixed[:, t * part : (t + 1) * part]) for t in range(members)])
    dq, dk, dv = attend_backward(first_row, queries, keys, values, mixed_grad)
    kv_grad = lax.psum_scatter(
        jnp.concatenate([dk, dv], axis=1).astype(bf16), "tensor", scatter_dimension=0, tiled=True
    ).astype(f32)
    dq_low = rotate(dq, cos_table, -sin_table).astype(bf16)
    kv_low = jnp.concatenate(
        [rotate(kv_grad[:, :kv_width], cos_table, -sin_table), kv_grad[:, kv_width:]], axis=1
    ).astype(bf16)
    normed_one_grad = nt(kv_low, kv_full) + sum(
        nt(dq_low[:, t * part : (t + 1) * part], q_full[t]) for t in range(members)
    )
    back_one, gain_one_part = rms_backward(normed_one_grad, unit_one, inverse_one, gain_one)
    tokens_grad = hidden_grad + back_one
    q_part = jnp.stack([tn(normed_one, dq_low[:, t * part : (t + 1) * part]) for t in range(members)])
    kv_part = tn(normed_one, kv_low)

    def shared(values):
        summed = lax.psum_scatter(values.astype(bf16), "tensor", scatter_dimension=0, tiled=False)
        return lax.psum_scatter(summed, "dp", scatter_dimension=0, tiled=True).astype(f32)

    q_grad, o_grad = shared(q_part), shared(o_part)
    small = jnp.concatenate([kv_part, gain_one_part[:, None], gain_two_part[:, None]], axis=1)
    small = lax.psum_scatter(small, "dp", scatter_dimension=0, tiled=True)
    small = lax.psum(small.astype(bf16), "tensor").astype(f32)
    return (
        output,
        tokens_grad,
        small[:, 2 * kv_width],
        q_grad,
        small[:, :kv_width],
        small[:, kv_width : 2 * kv_width],
        o_grad,
        small[:, 2 * kv_width + 1],
        gate_out,
        up_out,
        down_out,
    )

def body_by_chips(
    tokens,
    expert_ids,
    route_weights,
    attn_gain,
    q_weight,
    k_weight,
    v_weight,
    o_weight,
    moe_gain,
    gate_weight,
    up_weight,
    down_weight,
    cotangent,
):
    members = lax.axis_size("tensor")
    member = lax.axis_index("tensor")
    devices = lax.axis_size("dp")
    own_rows, width = tokens.shape
    rows = own_rows * members
    calls = EXPERTS // 2 // CALL_PAIRS

    gains = jnp.pad(jnp.stack([attn_gain, moe_gain], axis=1), ((0, 0), (0, HD - 2)))
    cosine, sine = doubled_tables(rows)
    square_all, tall_all, grad_all, rank_cols, routes, normed_one, queries, kv_all, mixed, hidden, rows_all, *chunks = front(
        tokens,
        q_weight,
        o_weight,
        k_weight,
        v_weight,
        gains,
        cosine,
        sine,
        cotangent,
        expert_ids.T,
        route_weights.T,
        gate_weight,
        up_weight,
        down_weight,
        members,
        devices,
    )
    packed, (from_x, from_y, far_x, far_y, *after) = chunks[:calls], chunks[calls:]
    near = [(from_x, from_y), *zip(after[0::2], after[1::2])]
    sums, grads, *others = expert_pass(
        rank_cols, routes, rows_all, grad_all, packed, near, (far_x, far_y), members
    )
    plain, added = others[-6:-4], others[-4:-2]
    tokens_grad, moe_moved, parts, *moved = attention_back(
        sums,
        cotangent,
        hidden,
        tokens,
        normed_one,
        queries,
        kv_all,
        mixed,
        square_all,
        tall_all,
        cosine,
        sine,
        grads,
        *added,
        members,
    )
    output, q_grad, o_grad, k_grad, v_grad, gain_grads, x_end, y_end = reduce_small(
        parts, sums, moe_moved, hidden, *added, members, devices
    )
    x_before, y_before, x_last, y_last, x_late, y_late = moved
    gate_out, up_out, down_out = unpack_all(
        grads,
        [(plain[0], x_late), (plain[1], y_late)],
        [(x_before, x_end), (y_before, y_end)],
        (x_last, y_last),
    )
    return (
        output,
        tokens_grad,
        gain_grads[:, 0],
        q_grad,
        k_grad,
        v_grad,
        o_grad,
        gain_grads[:, 1],
        gate_out,
        up_out,
        down_out,
    )


def doubled_tables(rows):
    half = HD // 2
    frequency = np.float32(rope_base) ** -(np.arange(half, dtype=np.float32) * np.float32(2.0 / HD))
    angles = (np.arange(rows) % SEQ).astype(np.float32)[:, None] * frequency
    cosine, sine = np.cos(angles), np.sin(angles)
    return jnp.asarray(np.concatenate([cosine, cosine], axis=1)), jnp.asarray(np.concatenate([-sine, sine], axis=1))


def solution(mesh):
    rows = P(("dp", "tensor"), None)
    experts = P("dp", None, "tensor")
    square = P("dp", "tensor")
    tall = P("dp", None)
    return jax.shard_map(
        body_by_chips if mesh.shape["dp"] == 8 else body_anywhere,
        mesh=mesh,
        in_specs=(
            rows, tall, tall, P("dp"), square, tall, tall, square, P("dp"), experts, experts, experts, rows
        ),
        out_specs=(rows, rows, P("dp"), square, tall, tall, square, P("dp"), experts, experts, experts),
        check_vma=False,
    )
```

```python
import jax
import jax.numpy as jnp
import numpy as np
from jax import lax
from jax.experimental import pallas as pl
from jax.experimental.pallas import tpu as pltpu
from jax.sharding import PartitionSpec as P

KV = 2
HD = 128
EXPERTS = 32
TOPK = 4
SEQ = 1024
BLOCK = 256
CAP = 256
TAIL = 64
CALL_PAIRS = 4
STRAIGHT = 2

eps = 1e-06
rope_base = 1000000.0
negative = -1e30
bf16 = jnp.bfloat16
f32 = jnp.float32


def nn(a, b):
    return jnp.dot(a, b, preferred_element_type=f32)


def nt(a, b):
    return lax.dot_general(a, b, (((1,), (1,)), ((), ())), preferred_element_type=f32)


def tn(a, b):
    return lax.dot_general(a, b, (((0,), (0,)), ((), ())), preferred_element_type=f32)


def rope_tables(positions):
    half = HD // 2
    frequency = rope_base ** (-(jnp.arange(half).astype(f32) * 2.0 / HD))
    angles = positions.astype(f32)[:, None] * frequency[None, :]
    return jnp.cos(angles), jnp.sin(angles)


def rotate(values, cos_table, sin_table):
    rows = values.shape[0]
    heads = values.reshape(rows, -1, 2, HD // 2)
    a, b = heads[:, :, 0], heads[:, :, 1]
    cos_table, sin_table = cos_table[:, None], sin_table[:, None]
    turned = jnp.stack([a * cos_table - b * sin_table, b * cos_table + a * sin_table], axis=2)
    return turned.reshape(rows, -1)


def rms_pieces(x):
    inverse = lax.rsqrt(jnp.mean(x * x, axis=-1, keepdims=True) + eps)
    return inverse, x * inverse


def rms_backward(grad, unit, inverse, gain):
    u = grad * gain
    back = inverse * (u - unit * jnp.mean(u * unit, axis=-1, keepdims=True))
    return back, jnp.sum(grad * unit, axis=0)


def probabilities(q, k, first_row):
    rows, keys = q.shape[0], k.shape[0]
    scores = nt(q, k) * (HD**-0.5)
    q_block = (first_row + lax.broadcasted_iota(jnp.int32, (rows, keys), 0)) // BLOCK
    k_block = lax.broadcasted_iota(jnp.int32, (rows, keys), 1) // BLOCK
    scores = jnp.where(k_block <= q_block, scores, negative)
    raised = jnp.exp(scores - jnp.max(scores, axis=-1, keepdims=True))
    return raised / jnp.sum(raised, axis=-1, keepdims=True)


def attend_forward(first_row, q, k, v):
    rows, width = q.shape
    heads = width // HD
    shared = heads // KV

    def kernel(first_ref, q_ref, k_ref, v_ref, o_ref):
        p = probabilities(q_ref[...], k_ref[...], first_ref[0]).astype(bf16)
        o_ref[...] = nn(p, v_ref[...]).astype(bf16)

    per_head = pl.BlockSpec((rows, HD), lambda h, f: (0, h))
    per_kv = pl.BlockSpec((k.shape[0], HD), lambda h, f: (0, h // shared))
    return pl.pallas_call(
        kernel,
        grid_spec=pltpu.PrefetchScalarGridSpec(
            num_scalar_prefetch=1,
            grid=(heads,),
            in_specs=[per_head, per_kv, per_kv],
            out_specs=per_head,
        ),
        out_shape=jax.ShapeDtypeStruct((rows, width), bf16),
        compiler_params=pltpu.CompilerParams(vmem_limit_bytes=32 * 2**20),
        cost_estimate=pl.CostEstimate(
            flops=4 * rows * width * k.shape[0],
            bytes_accessed=4 * rows * width,
            transcendentals=rows * heads * k.shape[0],
        ),
        name="attend",
    )(first_row, q, k, v)


def attend_backward(first_row, q, k, v, do):
    rows, width = q.shape
    keys = k.shape[0]
    heads = width // HD
    shared = heads // KV

    def kernel(first_ref, q_ref, k_ref, v_ref, do_ref, dq_ref, dk_ref, dv_ref):
        q_now, k_now, v_now, do_now = q_ref[...], k_ref[...], v_ref[...], do_ref[...]
        p = probabilities(q_now, k_now, first_ref[0])
        dp = nt(do_now, v_now)
        ds = (p * (dp - jnp.sum(p * dp, axis=-1, keepdims=True))).astype(bf16)
        dq_ref[...] = nn(ds, k_now) * (HD**-0.5)
        dk = tn(ds, q_now) * (HD**-0.5)
        dv = tn(p.astype(bf16), do_now)
        head = pl.program_id(0)

        @pl.when(lax.rem(head, shared) == 0)
        def _():
            dk_ref[...] = dk
            dv_ref[...] = dv

        @pl.when(lax.rem(head, shared) != 0)
        def _():
            dk_ref[...] += dk
            dv_ref[...] += dv

    per_head = pl.BlockSpec((rows, HD), lambda h, f: (0, h))
    per_kv = pl.BlockSpec((keys, HD), lambda h, f: (0, h // shared))
    return pl.pallas_call(
        kernel,
        grid_spec=pltpu.PrefetchScalarGridSpec(
            num_scalar_prefetch=1,
            grid=(heads,),
            in_specs=[per_head, per_kv, per_kv, per_head],
            out_specs=[per_head, per_kv, per_kv],
        ),
        out_shape=[
            jax.ShapeDtypeStruct((rows, width), f32),
            jax.ShapeDtypeStruct((keys, KV * HD), f32),
            jax.ShapeDtypeStruct((keys, KV * HD), f32),
        ],
        compiler_params=pltpu.CompilerParams(vmem_limit_bytes=32 * 2**20),
        cost_estimate=pl.CostEstimate(
            flops=10 * rows * width * keys,
            bytes_accessed=8 * rows * width,
            transcendentals=rows * heads * keys,
        ),
        name="attend_back",
    )(first_row, q, k, v, do)


def sibling():
    me = lax.axis_index("dp")
    return me + 1 - 2 * lax.rem(me, 2)


def pair_of_experts(expert, place, w, rank_c, routes_ref, x_ref, gy_ref, y_buf, pick_buf, put):
    rows, width = x_ref.shape
    lanes = w.shape[1]
    third = lanes // 3
    low_half = lax.broadcasted_iota(jnp.int32, (CAP, HD), 1) < TAIL
    slot_of = lax.broadcasted_iota(jnp.int32, (rows, CAP), 1).astype(f32)
    slot_at = lax.broadcasted_iota(jnp.int32, (CAP, rows), 0).astype(f32)
    gate_up = [slice(q * third, (q + 1) * third) for q in range(2)]
    down = [slice(2 * third + q * HD, 2 * third + (q + 2) * HD) for q in range(2)]

    def place_of(q):
        return pl.ds(pl.multiple_of((place + q) * CAP, CAP), CAP)

    def rows_of(q):
        hit = slot_at == routes_ref[q, 0:1]
        weight = jnp.sum(jnp.where(hit, routes_ref[q, 1:2], 0.0), axis=1, keepdims=True)
        pick = hit.astype(bf16)
        return nn(pick, x_ref[...]).astype(bf16), (nn(pick, gy_ref[...]) * weight).astype(bf16), weight

    def picked(q):
        column = (lax.broadcasted_iota(jnp.int32, (HD, CAP), 0) == expert + q).astype(bf16)
        pick_buf[:, place_of(q)] = (nn(rank_c[...], column) == slot_of).astype(bf16)

    def unit(gate, up, dact):
        sig = jax.nn.sigmoid(gate)
        silu = gate * sig
        return silu * up, dact * up * sig * (1.0 + gate * (1.0 - sig)), dact * silu

    def middle(q, gu, dact):
        tail = gu[:, 2 * HD :]
        if q == 0:
            d0, d1 = dact[:, :HD], dact[:, HD:]
        else:
            d0, d1 = dact[:, HD:], pltpu.roll(dact[:, :HD], TAIL, 1)
        a0, dg0, du0 = unit(gu[:, :HD], gu[:, HD : 2 * HD], d0)
        a1, dg1, du1 = unit(tail, pltpu.roll(tail, TAIL, 1), d1)
        a1 = jnp.where(low_half, a1, 0.0)
        dgu1 = jnp.where(low_half, dg1, pltpu.roll(du1, TAIL, 1))
        act = [a0, a1] if q == 0 else [pltpu.roll(a1, TAIL, 1), a0]
        act = jnp.concatenate([part.astype(bf16) for part in act], axis=1)
        return act, jnp.concatenate([part.astype(bf16) for part in (dg0, du0, dgu1)], axis=1)

    def ends(q, xe, deo, weight, act, dgu):
        y_buf[place_of(q), :width] = (nt(act, w[:, down[q]]) * weight).astype(bf16)
        y_buf[place_of(q), width:] = nt(dgu, w[:, gate_up[q]]).astype(bf16)
        put(q * third, tn(xe, dgu))
        grad = tn(deo, act)
        put(2 * third + 2 * q * HD, grad[:, :HD] if q == 0 else grad[:, HD:])
        return grad[:, HD:] if q == 0 else grad[:, :HD]

    xe0, deo0, weight0 = rows_of(0)
    first = nn(xe0, w[:, gate_up[0]]), nn(deo0, w[:, down[0]])
    xe1, deo1, weight1 = rows_of(1)
    act0, dgu0 = middle(0, *first)
    second = nn(xe1, w[:, gate_up[1]]), nn(deo1, w[:, down[1]])
    picked(0)
    tail0 = ends(0, xe0, deo0, weight0, act0, dgu0)
    act1, dgu1 = middle(1, *second)
    picked(1)
    tail1 = ends(1, xe1, deo1, weight1, act1, dgu1)
    put(2 * third + HD, tail0 + tail1)


def expert_call(rank_cols, routes, x, gy, weights, sums):
    rows, width = x.shape
    pairs, _, lanes = weights.shape
    blocks = 6
    tile = 2 * width // blocks

    def kernel(rank_c, routes_ref, x_ref, gy_ref, w_ref, sums_in, grad_out, sums_out, y_buf, pick_buf):
        step = pl.program_id(0)

        def put(at, value):
            grad_out[0, :, at : at + value.shape[1]] = value.astype(bf16)

        @pl.when(step < pairs)
        def _():
            pair_of_experts(2 * step, 2 * step, w_ref.at[0], rank_c, routes_ref, x_ref, gy_ref, y_buf, pick_buf, put)

        @pl.when(step >= pairs)
        def _():
            at = pl.ds(pl.multiple_of((step - pairs) * tile, tile), tile)
            sums_out[...] = sums_in[...] + nn(pick_buf[...], y_buf[:, at])

    def held(step):
        return jnp.minimum(step, pairs - 1)

    def block(step):
        return (0, jnp.maximum(step - pairs, 0))

    once = pl.Buffered(1)
    whole = pl.BlockSpec((rows, width), lambda s: (0, 0), pipeline_mode=once)
    of_pair = pl.BlockSpec((1, width, lanes), lambda s: (held(s), 0, 0))
    return pl.pallas_call(
        kernel,
        grid=(pairs + blocks,),
        in_specs=[
            pl.BlockSpec((rows, HD), lambda s: (0, 0), pipeline_mode=once),
            pl.BlockSpec((2, 2, rows), lambda s: (held(s), 0, 0)),
            whole,
            whole,
            of_pair,
            pl.BlockSpec((rows, tile), block),
        ],
        out_specs=[of_pair, pl.BlockSpec((rows, tile), block)],
        scratch_shapes=[pltpu.VMEM((2 * pairs * CAP, 2 * width), bf16), pltpu.VMEM((rows, 2 * pairs * CAP), bf16)],
        out_shape=[
            jax.ShapeDtypeStruct((pairs, width, lanes), bf16),
            jax.ShapeDtypeStruct((rows, 2 * width), f32),
        ],
        compiler_params=pltpu.CompilerParams(vmem_limit_bytes=62 * 10**6),
        name="experts",
    )(rank_cols, routes, x, gy, weights, sums)


def expert_pass(rank_cols, routes, x, gy, packed, near, far, members):
    rows, width = x.shape
    calls = len(packed)
    size, height, lanes = packed[0].shape
    half = size // 2
    pairs = calls * size
    blocks = 6
    tile = 2 * width // blocks
    period = size + blocks
    early = calls - 1
    dma = pltpu.SemaphoreType.DMA
    known = len(near)
    unknown = calls - known
    n_in = 4 + calls + 2 * known + 2

    def kernel(*refs):
        rank_c, routes_ref, x_ref, gy_ref = refs[:4]
        own = refs[4 : 4 + calls]
        near_in = refs[4 + calls : n_in - 2]
        far_in = refs[n_in - 2 : n_in]
        outs = refs[n_in:]
        sums_out, grads = outs[:2]
        near_out, outs = outs[2 : 2 + 2 * unknown], outs[2 + 2 * unknown :]
        far_out = outs[: 2 * early]
        plain_x, plain_y, added_x, added_y, via_x, via_y = outs[2 * early : 6 + 2 * early]
        scratch = outs[6 + 2 * early :]
        w_buf, y_buf, pick_buf, total, kept, leaving, arriving, load_buf, add_buf = scratch[:9]
        local_sem, push_sem, pull_sem, send_sem, recv_sem, keep_sem, load_sem, add_sem = scratch[9:17]
        chip_send, chip_recv, cross_send, cross_recv, straight_send, straight_recv, w_free, g_free = scratch[17:]
        step = pl.program_id(0)
        call, phase = step // period, lax.rem(step, period)
        pair = call * size + phase
        x_side, y_side = chip_neighbours()
        other = {"dp": sibling()}
        near_all = (*near_in, *near_out)
        near_x, near_y = near_all[0::2], near_all[1::2]
        far_all = [far_in, *(far_out[2 * i : 2 * i + 2] for i in range(early))]

        def chip(index, source, target, device):
            return remote(source, target, chip_send.at[index], chip_recv.at[index], {"dp": device})

        forward = []
        for i in range(early):
            forward.append(chip(2 * i, near_x[i + 1].at[:half], far_out[2 * i], y_side))
            forward.append(chip(2 * i + 1, near_y[i + 1].at[half:], far_out[2 * i + 1], x_side))
        fresh = []
        for i in range(unknown):
            fresh.append(chip(2 * early + 2 * i, own[known + i], near_out[2 * i], x_side))
            fresh.append(chip(2 * early + 2 * i + 1, own[known + i], near_out[2 * i + 1], y_side))

        def weights(now, slot, sub):
            chunk, side = sub // 2, sub % 2
            sources = [own[chunk], near_x[chunk], near_y[chunk], far_all[chunk][side]]
            begins = [chunk * size] * 3 + [chunk * size + side * half]
            found = []
            for k, (source, begin) in enumerate(zip(sources, begins)):
                source = source.at[now - begin]
                mine = w_buf.at[slot, pl.ds(2 * k * height, height)]
                found.append(pltpu.make_async_copy(source, mine, local_sem.at[slot, k]))
                theirs = w_buf.at[slot, pl.ds((2 * k + 1) * height, height)]
                found.append(remote(source, theirs, push_sem.at[slot, k], pull_sem.at[slot, k], other))
            return found

        def start(now):
            slot = lax.rem(now, 2)
            for sub in range(2 * calls):

                @pl.when((now >= sub * half) & (now < (sub + 1) * half))
                def _():
                    if sub >= 2:

                        @pl.when(now == sub * half)
                        def _():
                            forward[sub - 2].wait_recv()

                    for copy in weights(now, slot, sub):
                        copy.start()

        def leave(slot):
            return remote(leaving.at[slot], arriving.at[slot], send_sem.at[slot], recv_sem.at[slot], other)

        def keep(now):
            slot = lax.rem(now, 2)
            return pltpu.make_async_copy(kept.at[slot], grads.at[:, now], keep_sem.at[slot])

        def crossing(now, first):
            at = now // size * half + lax.rem(now, size) - (0 if first else half)
            sems = cross_send.at[now], cross_recv.at[now]
            if first:
                return remote(grads.at[3, now], via_x.at[at], *sems, {"dp": x_side})
            return remote(grads.at[3, now], via_y.at[at], *sems, {"dp": y_side})

        def straight(now, first):
            at = now // size * half + lax.rem(now, size) - (0 if first else half)
            sems = straight_send.at[now], straight_recv.at[now]
            if first:
                return remote(grads.at[1, now], plain_x.at[at], *sems, {"dp": x_side})
            return remote(grads.at[2, now], plain_y.at[at], *sems, {"dp": y_side})

        def by_half(now, do):
            for first in (True, False):

                @pl.when((lax.rem(now, size) < half) if first else (lax.rem(now, size) >= half))
                def _():
                    do(first)

        def scatter(now):
            by_half(now, lambda first: crossing(now, first).start())

        def finish(now):
            slot = lax.rem(now, 2)
            leave(slot).wait()
            for k in range(4):
                kept[slot, k] = (kept[slot, k].astype(f32) + arriving[slot, k].astype(f32)).astype(bf16)
            keep(now).start()

        def signal(sem):
            pl.semaphore_signal(sem, inc=1, device_id=other, device_id_type=pl.DeviceIdType.MESH)

        def put(at, value):
            slot = lax.rem(pair, 2)
            for k in range(4):
                for parity, target in enumerate((kept, leaving)):
                    row = (2 * k + parity) * height
                    target[slot, k, :, at : at + value.shape[1]] = value[row : row + height].astype(bf16)

        def loads(now):
            at = now // size * half + lax.rem(now, half)

            def copies(first):
                via, block = (via_x, 2) if first else (via_y, 1)
                return (
                    pltpu.make_async_copy(via.at[at], load_buf.at[0], load_sem.at[0]),
                    pltpu.make_async_copy(grads.at[block, now], load_buf.at[1], load_sem.at[1]),
                )

            return copies

        def stores(now, first):
            at = now // size * half + lax.rem(now, half)
            return pltpu.make_async_copy(add_buf, (added_y if first else added_x).at[at], add_sem)

        @pl.when(step == 0)
        def _():
            barrier = pltpu.get_barrier_semaphore()
            for device in (x_side, y_side, sibling()):
                pl.semaphore_signal(barrier, inc=1, device_id={"dp": device}, device_id_type=pl.DeviceIdType.MESH)
            pl.semaphore_wait(barrier, 3)
            start(step)
            for copy in forward[:2]:
                copy.start()

        @pl.when(phase < size)
        def _():
            @pl.when((pair >= 1) & (pair + 1 < pairs))
            def _():
                signal(w_free)
                pl.semaphore_wait(w_free, 1)

            for i in range(unknown):

                @pl.when(pair == (1 if i == 0 else i * size + 2))
                def _():
                    for copy in fresh[2 * i : 2 * i + 2]:
                        copy.start()

                @pl.when(pair == (i + 1) * size + i)
                def _():
                    for copy in fresh[2 * i : 2 * i + 2]:
                        copy.wait_recv()
                    begin = 2 * (known + i - 1)
                    for copy in forward[begin : begin + 2]:
                        copy.start()

            @pl.when(pair >= early * size)
            def _():
                for i in range(STRAIGHT):
                    now = pair - (early - i) * size
                    by_half(now, lambda first, now=now: straight(now, first).start())

            @pl.when(pair + 1 < pairs)
            def _():
                start(pair + 1)

            @pl.when(pair >= 2)
            def _():
                keep(pair - 2).wait()

            @pl.when(pair == size + 1)
            def _():
                for now in range(size - 1):
                    crossing(now, now < half).start()

            @pl.when((pair > size) & (pair - 2 < early * size))
            def _():
                scatter(pair - 2)

            slot = lax.rem(pair, 2)
            for copy in weights(0, slot, 0):
                copy.wait()
            pair_of_experts(
                2 * pair, 2 * phase, w_buf.at[slot], rank_c, routes_ref, x_ref, gy_ref, y_buf, pick_buf, put
            )

        @pl.when((phase >= 1) & (phase <= size))
        def _():
            finish(pair - 1)

            @pl.when(pair + 1 < pairs)
            def _():
                signal(g_free)

        @pl.when(phase < size)
        def _():
            @pl.when(pair >= 2)
            def _():
                pl.semaphore_wait(g_free, 1)

            leave(lax.rem(pair, 2)).start()

        @pl.when(phase >= size)
        def _():
            block = phase - size
            at = pl.ds(pl.multiple_of(block * tile, tile), tile)
            made = nn(pick_buf[...], y_buf[:, at])

            @pl.when(call == 0)
            def _():
                total[:, at] = made.astype(bf16)

            @pl.when((call > 0) & (call < calls - 1))
            def _():
                total[:, at] = (made + total[:, at].astype(f32)).astype(bf16)

            @pl.when(call == calls - 1)
            def _():
                sums_out[...] = (made + total[:, at].astype(f32)).astype(bf16)

            before = (call - 1) * size + block

            @pl.when((call > 0) & (block >= 2) & (block < size + 2))
            def _():
                by_half(before - 2, lambda first: stores(before - 2, first).wait())

            @pl.when((call > 0) & (block >= 1) & (block < size + 1))
            def _():
                def add_to(first):
                    for copy in loads(before - 1)(first):
                        copy.wait()
                    add_buf[...] = (load_buf[0].astype(f32) + load_buf[1].astype(f32)).astype(bf16)
                    stores(before - 1, first).start()

                by_half(before - 1, add_to)

            @pl.when((call > 0) & (block < size))
            def _():
                def load(first):
                    crossing(before, first).wait_recv()
                    for copy in loads(before)(first):
                        copy.start()

                by_half(before, load)

        @pl.when(step == calls * period - 1)
        def _():
            for now in (pairs - 2, pairs - 1):
                keep(now).wait()
            for copy in (*forward, *fresh):
                copy.wait_send()
            for now in range(early * size):
                first = now % size < half
                crossing(now, first).wait_send()
                if now < STRAIGHT * size:
                    straight(now, first).wait()

    def held(step):
        return step // period * size + jnp.minimum(lax.rem(step, period), size - 1)

    def block(step):
        return (0, jnp.where(step >= (calls - 1) * period + size, step - (calls - 1) * period - size, 0))

    once = pl.Buffered(1)
    whole = pl.BlockSpec((rows, width), lambda s: (0, 0), pipeline_mode=once)
    anywhere = pl.BlockSpec(memory_space=pl.ANY)
    some = jax.ShapeDtypeStruct((early * half, height, lanes), bf16)
    regular = pltpu.SemaphoreType.REGULAR
    return pl.pallas_call(
        kernel,
        grid=(calls * period,),
        in_specs=[
            pl.BlockSpec((rows, HD), lambda s: (0, 0), pipeline_mode=once),
            pl.BlockSpec((2, 2, rows), lambda s: (held(s), 0, 0)),
            whole,
            whole,
        ]
        + [anywhere] * (n_in - 4),
        out_specs=[pl.BlockSpec((rows, tile), block)] + [anywhere] * (7 + 2 * unknown + 2 * early),
        out_shape=[
            jax.ShapeDtypeStruct((rows, 2 * width), bf16),
            jax.ShapeDtypeStruct((4, pairs, height, lanes), bf16),
        ]
        + [jax.ShapeDtypeStruct((size, height, lanes), bf16)] * (2 * unknown)
        + [jax.ShapeDtypeStruct((half, height, lanes), bf16)] * (2 * early)
        + [jax.ShapeDtypeStruct((STRAIGHT * half, height, lanes), bf16)] * 2
        + [some] * 4,
        scratch_shapes=[
            pltpu.VMEM((2, width, lanes), bf16),
            pltpu.VMEM((2 * size * CAP, 2 * width), bf16),
            pltpu.VMEM((rows, 2 * size * CAP), bf16),
            pltpu.VMEM((rows, 2 * width), bf16),
            pltpu.VMEM((2, 4, height, lanes), bf16),
            pltpu.VMEM((2, 4, height, lanes), bf16),
            pltpu.VMEM((2, 4, height, lanes), bf16),
            pltpu.VMEM((2, height, lanes), bf16),
            pltpu.VMEM((height, lanes), bf16),
            dma((2, 4)),
            dma((2, 4)),
            dma((2, 4)),
            dma((2,)),
            dma((2,)),
            dma((2,)),
            dma((2,)),
            dma,
            dma((2 * early + 2 * unknown,)),
            dma((2 * early + 2 * unknown,)),
            dma((early * size,)),
            dma((early * size,)),
            dma((early * size,)),
            dma((early * size,)),
            regular,
            regular,
        ],
        compiler_params=pltpu.CompilerParams(
            vmem_limit_bytes=62 * 10**6, collective_id=1, has_side_effects=True
        ),
        cost_estimate=pl.CostEstimate(flops=2 * 10**11, bytes_accessed=10**8, transcendentals=0),
        name="experts",
    )(rank_cols, routes, x, gy, *packed, *(side for both in near for side in both), *far)


def remote(source, target, send_sem, recv_sem, device):
    return pltpu.make_async_remote_copy(
        src_ref=source,
        dst_ref=target,
        send_sem=send_sem,
        recv_sem=recv_sem,
        device_id=device,
        device_id_type=pl.DeviceIdType.MESH,
    )


def chip_neighbours():
    me = lax.axis_index("dp")
    return me + 2 - 4 * lax.rem(me // 2, 2), me + 4 - 8 * lax.rem(me // 4, 2)


def meet(members, core):
    barrier = pltpu.get_barrier_semaphore()
    z = lax.axis_index("tensor")

    def signal(device):
        pl.semaphore_signal(barrier, inc=1, device_id=device, device_id_type=pl.DeviceIdType.MESH)

    @pl.when(z > 0)
    def _():
        signal({"tensor": z - 1})

    @pl.when(z < members - 1)
    def _():
        signal({"tensor": z + 1})

    for other in (*chip_neighbours(), *([sibling()] if core else [])):
        signal({"dp": other})
    inner = jnp.where((z > 0) & (z < members - 1), 1, 0)
    pl.semaphore_wait(barrier, 3 + inner + (1 if core else 0))


class LineGather:
    def __init__(self, members, at, send, recv):
        self.members, self.at, self.send, self.recv = members, at, send, recv

    def copies(self, hop):
        z, last = lax.axis_index("tensor"), self.members - 1
        up, down = z - hop + 1, z + hop - 1

        def copy(block, way, device):
            return lambda: remote(
                self.at(block), self.at(block), self.send.at[way, hop - 1], self.recv.at[way, hop - 1], {"tensor": device}
            )

        return (
            ((up >= 0) & (z < last), copy(up, 0, z + 1)),
            ((down <= last) & (z > 0), copy(down, 1, z - 1)),
        ), (
            (z - hop >= 0, copy(z - hop, 0, z)),
            (z + hop <= last, copy(z + hop, 1, z)),
        )

    def start(self, hop):
        for present, copy in self.copies(hop)[0]:

            @pl.when(present)
            def _():
                copy().start()

    def arrive(self, hop):
        for present, copy in self.copies(hop)[1]:

            @pl.when(present)
            def _():
                copy().wait_recv()

    def close(self):
        for hop in range(1, self.members):
            for present, copy in self.copies(hop)[0]:

                @pl.when(present)
                def _():
                    copy().wait_send()


class LineSum:
    def __init__(self, members, part, leaving, arriving, send, recv):
        self.members, self.part, self.leaving, self.arriving = members, part, leaving, arriving
        self.send, self.recv = send, recv

    def copy(self, way, hop, device):
        return remote(
            self.leaving.at[way],
            self.arriving.at[way, hop - 1],
            self.send.at[way, hop - 1],
            self.recv.at[way, hop - 1],
            {"tensor": device},
        )

    def ways(self, hop):
        z, last = lax.axis_index("tensor"), self.members - 1
        return (
            (0, z - hop >= 0, z - hop, z < last, z - 1, (z < last) & (z + 1 - hop >= 0)),
            (1, z + hop <= last, z + hop, z > 0, z + 1, (z > 0) & (z - 1 + hop <= last)),
        )

    def start(self, hop, begun=True):
        if hop + 1 < self.members and begun:
            self.leave(hop + 1)
        for way, present, block, behind, device, _ in self.ways(hop):

            @pl.when(present)
            def _():
                self.leaving[way] = self.part(block).astype(bf16)

            if hop + 1 < self.members:

                @pl.when(present & behind)
                def _():
                    both = self.part(block).astype(f32) + self.arriving[way, hop].astype(f32)
                    self.leaving[way] = both.astype(bf16)

            @pl.when(present)
            def _():
                self.copy(way, hop, device).start()

    def arrive(self, hop):
        for way, _, _, _, device, present in self.ways(hop):

            @pl.when(present)
            def _():
                self.copy(way, hop, device).wait_recv()

    def total(self, out):
        z, last = lax.axis_index("tensor"), self.members - 1
        out[...] = self.part(z).astype(f32)
        for way, present in ((0, z < last), (1, z > 0)):

            @pl.when(present)
            def _():
                out[...] += self.arriving[way, 0].astype(f32)

    def leave(self, hop):
        for way, present, _, _, device, _ in self.ways(hop):

            @pl.when(present)
            def _():
                self.copy(way, hop, device).wait_send()

    def close(self):
        self.leave(1)


def swap_blocks(values):
    me = lax.axis_index("dp")
    chip = values.shape[1] // 4
    four = [values[:, i * chip : (i + 1) * chip] for i in range(4)]
    y_side, x_side, core_side = lax.rem(me // 4, 2) == 1, lax.rem(me // 2, 2) == 1, lax.rem(me, 2) == 1
    four = [jnp.where(y_side, four[i ^ 2], four[i]) for i in range(4)]
    four = [jnp.where(x_side, four[i ^ 1], four[i]) for i in range(4)]
    four = [jnp.where(core_side, pltpu.roll(part, chip // 2, 1), part) for part in four]
    return jnp.concatenate(four, axis=1)


def in_vmem(count):
    return [pl.BlockSpec(memory_space=pltpu.VMEM)] * count


def pack_chunk(gate, up, down, begin):
    gate, up, down = (
        jnp.swapaxes(w[:, begin : begin + 2 * CALL_PAIRS, :], 0, 1) for w in (gate, up, down)
    )

    def pair(a, b):
        return [a[:, :HD], b[:, :HD], jnp.concatenate([a[:, HD:], b[:, HD:]], axis=1)]

    def inner(a, b):
        a, b, tails = pair(a, b)
        return [a, tails, b]

    return [
        jnp.concatenate(
            pair(gate[e], up[e]) + pair(gate[e + 1], up[e + 1]) + inner(down[e], down[e + 1]), axis=1
        )
        for e in range(0, 2 * CALL_PAIRS, 2)
    ]


def turn(values, cosine, sine):
    return values * cosine + pltpu.roll(values, HD // 2, 1) * sine


def front(
    tokens, q_weight, o_weight, k_weight, v_weight, gains, cosine, sine, cotangent, ids, route_weights, gate, up, down, members, devices
):
    height, part = q_weight.shape
    own_rows, width = cotangent.shape
    rows = own_rows * members
    kv = 2 * KV * HD
    tall = kv + HD
    lanes = 9 * HD
    calls = EXPERTS // 2 // CALL_PAIRS
    half = CALL_PAIRS // 2
    heads = width // HD
    per_kv = heads // KV
    last = members - 1
    dma = pltpu.SemaphoreType.DMA

    def kernel(*refs):
        x_ref, q_weight_ref, o_ref, k_ref, v_ref, gains_ref, cos_ref, sin_ref, cot_ref = refs[:9]
        ids_ref, weights_ref, gate_ref, up_ref, down_ref = refs[9:14]
        square_all, tall_all, grad_all, rank_cols, routes = refs[14:19]
        normed_ref, q_ref, kv_all, mixed_ref, hidden_ref, rows_all = refs[19:25]
        packed = refs[25 : 25 + calls]
        from_x, from_y, far_x, far_y, next_x, next_y = refs[25 + calls : 31 + calls]
        rest = refs[31 + calls :]
        line_send, line_recv, grad_send, grad_recv, kv_send, kv_recv, row_send, row_recv = rest[:8]
        chip_send, chip_recv, core_send, core_recv = rest[8:]
        me, z = lax.axis_index("dp"), lax.axis_index("tensor")
        x_side, y_side = chip_neighbours()
        diagonal = x_side + y_side - me
        core = sibling()

        def rows_of(device):
            return pl.ds(pl.multiple_of(device * height, 16), height)

        def block_of(ref):
            return lambda block: ref.at[pl.ds(pl.multiple_of(block * own_rows, 16), own_rows)]

        own = pl.ds(pl.multiple_of(z * own_rows, 16), own_rows)

        def pack(call):
            chunk = pack_chunk(gate_ref, up_ref, down_ref, 2 * CALL_PAIRS * call)
            for pair, value in enumerate(chunk):
                packed[call][pair] = value

        def chip(index, source, device, target=None):
            target = source if target is None else target
            return remote(source, target, chip_send.at[index], chip_recv.at[index], {"dp": device})

        def across(index, source):
            return remote(source, source, core_send.at[index], core_recv.at[index], {"dp": core})

        def tall_at(device):
            return tall_all.at[rows_of(device)]

        def square_at(device, side=None):
            span = slice(None) if side is None else slice(side * part, (side + 1) * part)
            return square_all.at[:, rows_of(device), span]

        trades = []

        def trade(index, source):
            trades.append(across(index, source))
            trades[-1].start()

        def there(index, device, of):
            across(index, of(core if device is None else device + core - me)).wait_recv()

        square_all[z, rows_of(me), :part] = q_weight_ref[...]
        square_all[z, rows_of(me), part:] = o_ref[...]
        tall_all[rows_of(me), : kv // 2] = k_ref[...]
        tall_all[rows_of(me), kv // 2 : kv] = v_ref[...]
        tall_all[rows_of(me), kv:] = gains_ref[...]
        line = LineGather(members, lambda block: square_all.at[block, rows_of(me)], line_send, line_recv)
        group = LineGather(members, block_of(grad_all), grad_send, grad_recv)
        kv_line = LineGather(members, block_of(kv_all), kv_send, kv_recv)
        row_line = LineGather(members, block_of(rows_all), row_send, row_recv)
        moves = [
            chip(0, tall_at(me), x_side),
            chip(1, tall_at(me), y_side),
            chip(2, packed[0].at[:half], x_side, from_x.at[:half]),
            chip(3, packed[0].at[:half], y_side, from_y.at[:half]),
            chip(4, square_at(me), x_side),
            chip(5, square_at(me), y_side),
            chip(6, packed[0].at[half:], x_side, from_x.at[half:]),
            chip(7, packed[0].at[half:], y_side, from_y.at[half:]),
            chip(8, tall_at(x_side), y_side),
            chip(9, square_at(x_side, 0), y_side),
            chip(10, square_at(y_side, 1), x_side),
            chip(11, from_x.at[:half], y_side, far_x),
            chip(12, from_y.at[half:], x_side, far_y),
            chip(13, packed[1], x_side, next_x),
            chip(14, packed[1], y_side, next_y),
        ]
        meet(members, True)
        line.start(1)
        for copy in moves[:2]:
            copy.start()
        trade(0, tall_at(me))
        pack(0)
        for index, device in ((0, x_side), (1, y_side)):
            chip(index, tall_at(device), device).wait_recv()
        moves[8].start()
        trade(2, tall_at(x_side))
        trade(3, tall_at(y_side))
        line.arrive(1)
        if last > 1:
            line.start(2)
        grad_all[own, :] = swap_blocks(cot_ref[...]).astype(bf16)
        chip(8, tall_at(diagonal), y_side).wait_recv()
        trade(6, tall_at(diagonal))
        for hop in range(2, members):
            line.arrive(hop)
            if hop < last:
                line.start(hop + 1)
        for copy in moves[4:6]:
            copy.start()
        trade(1, square_at(me))

        for index, device in ((0, None), (2, x_side), (3, y_side), (6, diagonal)):
            there(index, device, tall_at)
        gain_one, gain_two = (jnp.transpose(tall_all[:, kv:].astype(f32))[i : i + 1] for i in range(2))
        cosine, sine = cos_ref[own], sin_ref[own]
        normed_ref[...] = (rms_pieces(x_ref[...].astype(f32))[1] * gain_one).astype(bf16)
        made = nn(normed_ref[...], tall_all[:, :kv])
        for head in range(KV):
            span = slice(head * HD, (head + 1) * HD)
            kv_all[own, span] = turn(made[:, span], cosine, sine).astype(bf16)
        kv_all[own, KV * HD :] = made[:, KV * HD :].astype(bf16)
        kv_line.start(1)

        expert = lax.broadcasted_iota(jnp.int32, (HD, rows), 0)
        weight = jnp.zeros((HD, rows), f32)
        named = jnp.zeros((HD, rows), f32)
        for route in range(ids_ref.shape[0]):
            here = ids_ref[route : route + 1, :] == expert
            named = jnp.where(here, 1.0, named)
            weight = jnp.where(here, weights_ref[route : route + 1, :], weight)
        row = lax.broadcasted_iota(jnp.int32, (rows, rows), 0)
        later = (row < lax.broadcasted_iota(jnp.int32, (rows, rows), 1)).astype(bf16)
        rank = jnp.where(named > 0.0, nn(named.astype(bf16), later), -1.0)
        rank_cols[...] = jnp.transpose(rank).astype(bf16)
        for e in range(EXPERTS):
            routes[e, 0:1, :] = rank[e : e + 1]
            routes[e, 1:2, :] = weight[e : e + 1]
        for call in range(1, calls):
            kv_line_hop = call
            if kv_line_hop < members:
                kv_line.arrive(kv_line_hop)
                if kv_line_hop < last:
                    kv_line.start(kv_line_hop + 1)
            pack(call)
        for hop in range(calls, members):
            kv_line.arrive(hop)
            if hop < last:
                kv_line.start(hop + 1)
        group.start(1)

        for index, device in ((4, x_side), (5, y_side)):
            chip(index, square_at(device), device).wait_recv()
        for copy in moves[9:11]:
            copy.start()
        trade(4, square_at(x_side))
        trade(5, square_at(y_side))
        chip(9, square_at(diagonal, 0), y_side).wait_recv()
        chip(10, square_at(diagonal, 1), x_side).wait_recv()
        trade(7, square_at(diagonal))
        for copy in (*moves[2:4], *moves[6:8]):
            copy.start()
        group.arrive(1)
        if last > 1:
            group.start(2)
        for index, device in ((1, None), (4, x_side), (5, y_side), (7, diagonal)):
            there(index, device, square_at)

        for t in range(members):
            made = nn(normed_ref[...], square_all[t, :, :part])
            for head in range(part // HD):
                span = slice(head * HD, (head + 1) * HD)
                q_ref[:, t * part + head * HD : t * part + (head + 1) * HD] = turn(
                    made[:, span], cosine, sine
                ).astype(bf16)

        def attend(begin, end):
            @pl.loop(begin, end)
            def _(head):
                span = pl.ds(pl.multiple_of(head * HD, HD), HD)
                key_span = pl.ds(pl.multiple_of(head // per_kv * HD, HD), HD)
                value_span = pl.ds(pl.multiple_of((KV + head // per_kv) * HD, HD), HD)
                p = probabilities(q_ref[:, span], kv_all[:, key_span], z * own_rows).astype(bf16)
                mixed_ref[:, span] = nn(p, kv_all[:, value_span]).astype(bf16)

        for copy in moves[13:15]:
            copy.start()
        attend(0, heads // 2)
        for hop in range(2, members):
            group.arrive(hop)
            if hop < last:
                group.start(hop + 1)
            if hop == 2:
                attend(heads // 2, heads)
        if members <= 2:
            attend(heads // 2, heads)
        hidden = x_ref[...].astype(f32)
        for t in range(members):
            hidden += nt(mixed_ref[:, t * part : (t + 1) * part], square_all[t, :, part:])
        hidden_ref[...] = hidden
        rows_all[own, :] = swap_blocks(rms_pieces(hidden)[1] * gain_two).astype(bf16)
        for hop in range(1, members):
            row_line.start(hop)
            if hop == 1:
                for copy in (*moves[2:4], *moves[6:8]):
                    copy.wait_recv()
                for copy in moves[11:13]:
                    copy.start()
            row_line.arrive(hop)
        for copy in moves[11:]:
            copy.wait_recv()
        for copy in moves + trades:
            copy.wait_send()
        for each in (line, group, kv_line, row_line):
            each.close()

    chunk_shape = jax.ShapeDtypeStruct((CALL_PAIRS, height, lanes), bf16)
    half_shape = jax.ShapeDtypeStruct((half, height, lanes), bf16)
    low_rows = jax.ShapeDtypeStruct((own_rows, width), bf16)
    return pl.pallas_call(
        kernel,
        in_specs=in_vmem(14),
        out_specs=in_vmem(11 + calls) + [pl.BlockSpec(memory_space=pl.ANY)] * 6,
        out_shape=[
            jax.ShapeDtypeStruct((members, devices * height, 2 * part), bf16),
            jax.ShapeDtypeStruct((devices * height, tall), bf16),
            jax.ShapeDtypeStruct((rows, width), bf16),
            jax.ShapeDtypeStruct((rows, HD), bf16),
            jax.ShapeDtypeStruct((EXPERTS, 2, rows), f32),
            low_rows,
            low_rows,
            jax.ShapeDtypeStruct((rows, kv), bf16),
            low_rows,
            jax.ShapeDtypeStruct((own_rows, width), f32),
            jax.ShapeDtypeStruct((rows, width), bf16),
        ]
        + [chunk_shape] * (calls + 2)
        + [half_shape] * 2
        + [chunk_shape] * 2,
        scratch_shapes=[dma((2, members - 1))] * 8 + [dma((15,))] * 2 + [dma((8,))] * 2,
        compiler_params=pltpu.CompilerParams(collective_id=2, has_side_effects=True, vmem_limit_bytes=62 * 10**6),
        cost_estimate=pl.CostEstimate(flops=2 * 10**11, bytes_accessed=10**7, transcendentals=0),
        name="front",
    )(
        tokens,
        q_weight,
        o_weight,
        k_weight,
        v_weight,
        gains,
        cosine,
        sine,
        cotangent,
        ids,
        route_weights,
        gate,
        up,
        down,
    )


def gain_rows(tall_ref, kv):
    return jnp.transpose(tall_ref[:, kv:].astype(f32))


def attention_back(
    sums, cotangent, hidden, tokens, normed, q, kv_all, mixed, square, tall, cosine, sine, grads, to_x, to_y, members
):
    own_rows, width = tokens.shape
    rows = own_rows * members
    kv = 2 * KV * HD
    heads = width // HD
    per_kv = heads // KV
    part = width // members
    dma = pltpu.SemaphoreType.DMA

    def kernel(sums_ref, cot_ref, hidden_ref, x_ref, normed_ref, q_ref, kv_ref, mixed_ref, square_ref, tall_ref, *rest):
        cos_ref, sin_ref, grads_ref, to_x_ref, to_y_ref = rest[:5]
        grad_ref, moe_out, parts, x_before, y_before, x_last, y_last, x_late, y_late = rest[5:14]
        do_ref, dq_ref, dkv_ref, total, kv_total, stage, tall_part, back_part = rest[14:22]
        back_leave, back_arrive, moe_leave, moe_arrive, kv_leave, kv_arrive = rest[22:28]
        back_send, back_recv, moe_send, moe_recv, kv_send, kv_recv, stage_sem, part_sem = rest[28:36]
        through, added, added_sem, chip_send, chip_recv = rest[36:]
        z = lax.axis_index("tensor")
        x_side, y_side = chip_neighbours()
        first, second = slice(0, size // 2), slice(size // 2, size)

        def chunk(block, span):
            return grads_ref.at[block, pairs_before + span.start : pairs_before + span.stop]


        def chip(index, source, target, device):
            return remote(source, target, chip_send.at[index], chip_recv.at[index], {"dp": device})

        def sums_of(begin):
            return [
                pltpu.make_async_copy(
                    sums_ref.at[b * own_rows : (b + 1) * own_rows, begin : begin + width], back_part.at[b], part_sem.at[b]
                )
                for b in range(members)
            ]

        loads = sums_of(width) + [
            pltpu.make_async_copy(chunk(1, second), added.at[0], added_sem.at[0]),
            pltpu.make_async_copy(chunk(2, first), added.at[1], added_sem.at[1]),
        ]
        for copy in loads:
            copy.start()
        meet(members, False)
        moves = [
            chip(0, chunk(3, first), through.at[0], x_side),
            chip(1, chunk(3, second), through.at[1], y_side),
            chip(2, to_x_ref.at[:soon], x_before, x_side),
            chip(3, to_y_ref.at[:soon], y_before, y_side),
            chip(4, chunk(1, first), x_last.at[first], x_side),
            chip(5, chunk(2, second), y_last.at[second], y_side),
            chip(6, added.at[0], x_last.at[second], x_side),
            chip(7, added.at[1], y_last.at[first], y_side),
        ]
        for i in range(late):
            begin, here = (i + STRAIGHT) * size, slice(i * size // 2, (i + 1) * size // 2)
            middle = begin + size // 2
            moves.append(chip(8 + 2 * i, grads_ref.at[1, begin:middle], x_late.at[here], x_side))
            moves.append(chip(9 + 2 * i, grads_ref.at[2, middle : begin + size], y_late.at[here], y_side))
        for copy in (*moves[:6], *moves[8:]):
            copy.start()
        own = pl.ds(pl.multiple_of(z * own_rows, 16), own_rows)
        for copy in loads:
            copy.wait()

        def block(ref, span):
            return lambda b: ref[pl.ds(pl.multiple_of(b * own_rows, 16), own_rows), span]

        back = LineSum(members, lambda b: back_part[b], back_leave, back_arrive, back_send, back_recv)
        moe = LineSum(members, lambda b: back_part[b], moe_leave, moe_arrive, moe_send, moe_recv)
        pairs = LineSum(members, block(dkv_ref, slice(None)), kv_leave, kv_arrive, kv_send, kv_recv)
        gains = gain_rows(tall_ref, kv)
        cosine, sine = cos_ref[own], sin_ref[own]
        last = members - 1
        stored = []

        def store(value, at):
            slot = len(stored) % 2
            if len(stored) >= 2:
                stored[-2].wait()
            stage[slot] = value.astype(bf16)
            copy = pltpu.make_async_copy(stage.at[slot], parts.at[:, at : at + part], stage_sem.at[slot])
            copy.start()
            stored.append(copy)

        for hop in range(last, 0, -1):
            back.start(hop)
            back.arrive(hop)
        back.total(total)
        loads = sums_of(0)
        for copy in loads:
            copy.start()
        normed_grad = swap_blocks(total[...])
        inverse, unit = rms_pieces(hidden_ref[...])
        for copy in loads:
            copy.wait()
        if last > 1:
            moe.start(last)
        by_hidden, gain_two = rms_backward(normed_grad, unit, inverse, gains[1:2])
        grad_ref[...] = cot_ref[...] + by_hidden
        low = grad_ref[...].astype(bf16)
        for t in range(members):
            span = slice(t * part, (t + 1) * part)
            do_ref[:, span] = nn(low, square_ref[t, :, part:]).astype(bf16)
            store(tn(low, mixed_ref[:, span]), t * part)
        dkv_ref[...] = jnp.zeros_like(dkv_ref)
        first_row = z * own_rows

        def attend(begin, end):
            @pl.loop(begin, end)
            def _(head):
                span = pl.ds(pl.multiple_of(head * HD, HD), HD)
                key_span = pl.ds(pl.multiple_of(head // per_kv * HD, HD), HD)
                value_span = pl.ds(pl.multiple_of((KV + head // per_kv) * HD, HD), HD)
                q_now, k_now, do_now = q_ref[:, span], kv_ref[:, key_span], do_ref[:, span]
                p = probabilities(q_now, k_now, first_row)
                dp = nt(do_now, kv_ref[:, value_span])
                ds = (p * (dp - jnp.sum(p * dp, axis=-1, keepdims=True))).astype(bf16)
                dq_ref[:, span] = turn(nn(ds, k_now) * (HD**-0.5), cosine, -sine).astype(bf16)
                dkv_ref[:, key_span] += tn(ds, q_now) * (HD**-0.5)
                dkv_ref[:, value_span] += tn(p.astype(bf16), do_now)

        attend(0, heads // 3)
        if last > 1:
            moe.arrive(last)
            if last > 2:
                moe.start(last - 1)
        attend(heads // 3, heads)

        pairs.start(last)

        def query_part(t):
            store(tn(normed_ref[...], dq_ref[:, t * part : (t + 1) * part]), width + t * part)

        def normed_part(t):
            made = nt(dq_ref[:, t * part : (t + 1) * part], square_ref[t, :, :part])
            if t == 0:
                total[...] = made
            else:
                total[...] += made

        for i, copy in enumerate(moves[:2]):
            copy.wait()
            added[1 - i] = (added[1 - i].astype(f32) + through[i].astype(f32)).astype(bf16)
            moves[7 - i].start()
        work = [(do, t) for do in (query_part, normed_part) for t in range(members)]
        share = len(work) // last
        for hop in range(last, 0, -1):
            for do, t in work[: share if hop > 1 else None]:
                do(t)
            work = work[share:]
            pairs.arrive(hop)
            if hop > 1:
                pairs.start(hop - 1)
        for hop in range(last - 1, 1, -1):
            moe.arrive(hop)
            if hop > 2:
                moe.start(hop - 1)
        for way, present in ((0, (z < last) & (z >= 1)), (1, (z > 0) & (z + 1 <= last))):

            @pl.when(present)
            def _():
                moe_out[way] = moe_arrive[way, 1]

            @pl.when(jnp.logical_not(present))
            def _():
                moe_out[way] = jnp.zeros((own_rows, width), bf16)

        pairs.total(kv_total)
        low_kv = [
            turn(kv_total[:, head * HD : (head + 1) * HD], cosine, -sine).astype(bf16) for head in range(KV)
        ] + [kv_total[:, KV * HD :].astype(bf16)]
        low_kv = jnp.concatenate(low_kv, axis=1)
        normed_grad = total[...] + nt(low_kv, tall_ref[:, :kv])
        inverse, unit = rms_pieces(x_ref[...].astype(f32))
        by_tokens, gain_one = rms_backward(normed_grad, unit, inverse, gains[0:1])
        grad_ref[...] += by_tokens
        tall_part[:, :kv] = tn(normed_ref[...], low_kv).astype(bf16)
        row = lax.broadcasted_iota(jnp.int32, (HD, width), 0)
        both = jnp.where(row == 0, gain_one[None], jnp.where(row == 1, gain_two[None], 0.0))
        tall_part[:, kv:] = jnp.transpose(both).astype(bf16)
        tall_copy = pltpu.make_async_copy(tall_part, parts.at[:, 2 * width :], stage_sem.at[2])
        tall_copy.start()
        for line in (back, pairs):
            line.close()
        if last > 1:
            moe.leave(2)
        for copy in (*stored[-2:], tall_copy, *moves[2:]):
            copy.wait()

    hops = (2, members - 1)
    anywhere = pl.BlockSpec(memory_space=pl.ANY)
    _, height, lanes = to_x.shape
    size = CALL_PAIRS
    pairs_before = grads.shape[1] - size
    late = pairs_before // size - STRAIGHT
    soon = to_x.shape[0] - size // 2
    halves = (2, size // 2, height, lanes)
    return pl.pallas_call(
        kernel,
        in_specs=[anywhere] + in_vmem(11) + [anywhere] * 3,
        out_specs=in_vmem(2) + [anywhere] * 7,
        out_shape=[
            jax.ShapeDtypeStruct((own_rows, width), f32),
            jax.ShapeDtypeStruct((2, own_rows, width), bf16),
            jax.ShapeDtypeStruct((width, 2 * width + tall.shape[1]), bf16),
        ]
        + [jax.ShapeDtypeStruct((soon, height, lanes), bf16)] * 2
        + [jax.ShapeDtypeStruct((size, height, lanes), bf16)] * 2
        + [jax.ShapeDtypeStruct((late * size // 2, height, lanes), bf16)] * 2,
        scratch_shapes=[
            pltpu.VMEM((own_rows, width), bf16),
            pltpu.VMEM((own_rows, width), bf16),
            pltpu.VMEM((rows, kv), f32),
            pltpu.VMEM((own_rows, width), f32),
            pltpu.VMEM((own_rows, kv), f32),
            pltpu.VMEM((2, width, part), bf16),
            pltpu.VMEM(tall.shape, bf16),
            pltpu.VMEM((members, own_rows, width), bf16),
            pltpu.VMEM((2, own_rows, width), bf16),
            pltpu.VMEM((*hops, own_rows, width), bf16),
            pltpu.VMEM((2, own_rows, width), bf16),
            pltpu.VMEM((*hops, own_rows, width), bf16),
            pltpu.VMEM((2, own_rows, kv), bf16),
            pltpu.VMEM((*hops, own_rows, kv), bf16),
        ]
        + [dma(hops)] * 6
        + [dma((3,)), dma((members,)), pltpu.VMEM(halves, bf16), pltpu.VMEM(halves, bf16), dma((2,)), dma((8 + 2 * late,)), dma((8 + 2 * late,))],
        compiler_params=pltpu.CompilerParams(collective_id=4, has_side_effects=True, vmem_limit_bytes=62 * 10**6),
        cost_estimate=pl.CostEstimate(flops=10**11, bytes_accessed=10**7, transcendentals=0),
        name="attention_back",
    )(
        sums, cotangent, hidden, tokens, normed, q, kv_all, mixed, square, tall, cosine, sine, grads, to_x, to_y
    )


def reduce_small(parts, sums, moved, hidden, to_x, to_y, members, devices):
    own_rows = hidden.shape[0]
    width = parts.shape[0]
    height = width // devices
    lanes = parts.shape[1]
    tall = lanes - 2 * width
    kv = KV * HD
    part = width // members
    half = height // 2
    groups = (slice(0, width), slice(width, lanes))
    begun = to_x.shape[0] - CALL_PAIRS // 2
    dma = pltpu.SemaphoreType.DMA

    def kernel(parts_ref, sums_ref, to_x_ref, to_y_ref, moved_ref, hidden_ref, *rest):
        out_ref, q_out, o_out, k_out, v_out, gains_out, x_end, y_end = rest[:8]
        rest = rest[8:]
        own, theirs, leave, arrive, blocks, line_leave, line_arrive, tall_all, line_total = rest[:9]
        moe_part, moe_leave, moe_arrive, total_ref = rest[9:13]
        own_sem, core_send, core_recv, chip_send, chip_recv = rest[13:18]
        o_send, o_recv, q_send, q_recv, tall_send, tall_recv, moe_send, moe_recv, part_sem, end_send, end_recv = rest[18:]
        me, z = lax.axis_index("dp"), lax.axis_index("tensor")
        x_side, y_side = chip_neighbours()
        core = sibling()
        chips = [me, x_side, y_side, x_side + y_side - me]
        loads = [
            pltpu.make_async_copy(
                sums_ref.at[b * own_rows : (b + 1) * own_rows, :width], moe_part.at[b], part_sem.at[b]
            )
            for b in range(members)
        ]
        for copy in loads:
            copy.start()

        def rows(device, span):
            return parts_ref.at[pl.ds(pl.multiple_of(device * height, 16), height), span]

        def trade(m, g):
            target = theirs.at[m, :, groups[g]]
            source = rows(chips[m] + core - me, groups[g])
            return remote(source, target, core_send.at[m, g], core_recv.at[m, g], {"dp": core})

        def keep(m, g):
            return pltpu.make_async_copy(rows(chips[m], groups[g]), own.at[m, :, groups[g]], own_sem.at[m, g])

        order = (3, 2, 1, 0)
        for g in range(2):
            for m in order:
                keep(m, g).start()
        meet(members, True)
        for g in range(2):
            for m in order:
                trade(m, g).start()
        moe = LineSum(members, lambda b: moe_part[b], moe_leave, moe_arrive, moe_send, moe_recv)
        if members > 2:
            for way in range(2):
                moe_arrive[way, 1] = moved_ref[way]
        for copy in loads:
            copy.wait()
        moe.start(1, False)

        def both(m, rows, lanes):
            return own[m, rows, lanes].astype(f32) + theirs[m, rows, lanes].astype(f32)

        def chip(index, g, slot, span, device):
            source, target = leave.at[slot, span, groups[g]], arrive.at[slot, span, groups[g]]
            return remote(source, target, chip_send.at[index, g], chip_recv.at[index, g], {"dp": device})

        first, second = slice(0, half), slice(half, height)
        every = slice(0, height)
        far = [[chip(0, g, 0, first, x_side), chip(1, g, 0, second, y_side)] for g in range(2)]
        near = [[chip(2, g, 1, every, x_side), chip(3, g, 2, every, y_side)] for g in range(2)]

        def ready(m, g):
            trade(m, g).wait()
            keep(m, g).wait()

        for g, span in enumerate(groups):
            ready(3, g)
            for copy, part_of in zip(far[g], (first, second)):
                leave[0, part_of, span] = both(3, part_of, span).astype(bf16)
                copy.start()
            for m in order[1:]:
                ready(m, g)
        for g, span in enumerate(groups):
            leave[1, first, span] = both(1, first, span).astype(bf16)
            leave[2, second, span] = both(2, second, span).astype(bf16)
            far[g][1].wait()
            leave[1, second, span] = (both(1, second, span) + arrive[0, second, span].astype(f32)).astype(bf16)
            near[g][0].start()
            far[g][0].wait()
            leave[2, first, span] = (both(2, first, span) + arrive[0, first, span].astype(f32)).astype(bf16)
            near[g][1].start()
        moe.arrive(1)
        moe.total(total_ref)
        out_ref[...] = (hidden_ref[...] + swap_blocks(total_ref[...])).astype(bf16)

        def total(span):
            return both(0, every, span) + arrive[1, :, span].astype(f32) + arrive[2, :, span].astype(f32)

        lines = [
            LineSum(members, lambda b, g=g: blocks[g, b], line_leave.at[g], line_arrive.at[g], send, recv)
            for g, (send, recv) in enumerate(((o_send, o_recv), (q_send, q_recv)))
        ]
        group = LineGather(members, lambda b: tall_all.at[b], tall_send, tall_recv)

        def hop_of(line, hop):
            line.arrive(hop)
            if hop > 1:
                line.start(hop - 1)

        last = members - 1
        for copy in near[0]:
            copy.wait()
        for t in range(members):
            blocks[0, t] = total(slice(t * part, (t + 1) * part))
        lines[0].start(last)
        for copy in near[1]:
            copy.wait()
        ends = [
            remote(source.at[begun:], target, end_send.at[i], end_recv.at[i], {"dp": device})
            for i, (source, target, device) in enumerate(((to_x_ref, x_end, x_side), (to_y_ref, y_end, y_side)))
        ]
        for copy in ends:
            copy.start()
        tall_all[z] = total(slice(2 * width, lanes)).astype(bf16)
        for t in range(members):
            blocks[1, t] = total(slice(width + t * part, width + (t + 1) * part))
        lines[1].start(last)
        group.start(1)
        for hop in range(last, 0, -1):
            hop_of(lines[0], hop)
            hop_of(lines[1], hop)
            group.arrive(members - hop)
            if hop > 1:
                group.start(members - hop + 1)
        lines[0].total(line_total)
        o_out[...] = line_total[...]
        lines[1].total(line_total)
        q_out[...] = line_total[...]
        summed = tall_all[0].astype(f32)
        for t in range(1, members):
            summed += tall_all[t].astype(f32)
        k_out[...] = summed[:, :kv]
        v_out[...] = summed[:, kv : 2 * kv]
        gains_out[...] = summed[:, 2 * kv :]
        for line in (*lines, group, moe):
            line.close()
        for copy in ends:
            copy.wait()

    hops = (2, members - 1)
    return pl.pallas_call(
        kernel,
        in_specs=[pl.BlockSpec(memory_space=pl.ANY)] * 4 + in_vmem(2),
        out_specs=in_vmem(6) + [pl.BlockSpec(memory_space=pl.ANY)] * 2,
        out_shape=[
            jax.ShapeDtypeStruct((own_rows, width), bf16),
            jax.ShapeDtypeStruct((height, part), f32),
            jax.ShapeDtypeStruct((height, part), f32),
            jax.ShapeDtypeStruct((height, kv), f32),
            jax.ShapeDtypeStruct((height, kv), f32),
            jax.ShapeDtypeStruct((height, tall - 2 * kv), f32),
        ]
        + [jax.ShapeDtypeStruct((CALL_PAIRS // 2, *to_x.shape[1:]), bf16)] * 2,
        scratch_shapes=[
            pltpu.VMEM((4, height, lanes), bf16),
            pltpu.VMEM((4, height, lanes), bf16),
            pltpu.VMEM((3, height, lanes), bf16),
            pltpu.VMEM((3, height, lanes), bf16),
            pltpu.VMEM((2, members, height, part), f32),
            pltpu.VMEM((2, 2, height, part), bf16),
            pltpu.VMEM((2, *hops, height, part), bf16),
            pltpu.VMEM((members, height, tall), bf16),
            pltpu.VMEM((height, part), f32),
            pltpu.VMEM((members, own_rows, width), bf16),
            pltpu.VMEM((2, own_rows, width), bf16),
            pltpu.VMEM((*hops, own_rows, width), bf16),
            pltpu.VMEM((own_rows, width), f32),
            dma((4, 2)),
            dma((4, 2)),
            dma((4, 2)),
            dma((4, 2)),
            dma((4, 2)),
        ]
        + [dma(hops)] * 8
        + [dma((members,)), dma((2,)), dma((2,))],
        compiler_params=pltpu.CompilerParams(collective_id=5, has_side_effects=True, vmem_limit_bytes=60 * 2**20),
        cost_estimate=pl.CostEstimate(flops=8 * 10**10, bytes_accessed=10**7, transcendentals=0),
        name="reduce_small",
    )(parts, sums, to_x, to_y, moved, hidden)


def unpack_all(grads, plain, added, last):
    _, pairs, height, lanes = grads.shape
    half = CALL_PAIRS // 2
    units = lanes // 6
    tail = units - HD
    step = 96 if height % 96 == 0 else height
    kinds = (*plain, *added, last[:1], last[1:])
    others = [array for kind in kinds for array in kind]

    def kernel(own, *refs):
        gate, up, down = refs[len(others) :]
        given = iter(refs)
        plain_x, plain_y, added_x, added_y, last_x, last_y = (
            [(ref, i) for _, ref in zip(kind, given) for i in range(ref.shape[0])] for kind in kinds
        )

        def of(kind, at):
            ref, i = kind[at]
            return ref[i].astype(f32)

        for call in range(pairs // CALL_PAIRS):
            found = [[], [], []]
            for turn in range(CALL_PAIRS):
                pair = call * CALL_PAIRS + turn
                at = call * half + turn % half
                if pair >= pairs - CALL_PAIRS:
                    by_x, by_y = of(last_x, turn), of(last_y, turn)
                elif turn < half:
                    by_x, by_y = of(plain_x, at), of(added_y, at)
                else:
                    by_x, by_y = of(added_x, at), of(plain_y, at)
                value = own[0, pair].astype(f32) + by_x + by_y
                tiles = [value[:, i * HD : (i + 1) * HD] for i in range(9)]
                for i, (a, b, both) in enumerate(((0, 1, 2), (3, 4, 5), (6, 8, 7))):
                    left = jnp.concatenate([tiles[a], tiles[both][:, :tail]], axis=1)
                    right = jnp.concatenate([tiles[b], tiles[both][:, tail:]], axis=1)
                    if i < 2:
                        found[0].append(left)
                        found[1].append(right)
                    else:
                        found[2] += [left, right]
            span = slice(2 * CALL_PAIRS * call, 2 * CALL_PAIRS * (call + 1))
            for out, values in zip((gate, up, down), found):
                out[:, span, :] = jnp.swapaxes(jnp.stack(values), 0, 1)

    shape = (height, 2 * pairs, units)
    return pl.pallas_call(
        kernel,
        grid=(height // step,),
        in_specs=[pl.BlockSpec((1, pairs, step, lanes), lambda i: (0, 0, i, 0))]
        + [pl.BlockSpec((other.shape[0], step, lanes), lambda i: (0, i, 0)) for other in others],
        out_specs=[pl.BlockSpec((step, *shape[1:]), lambda i: (i, 0, 0))] * 3,
        out_shape=[jax.ShapeDtypeStruct(shape, f32)] * 3,
        compiler_params=pltpu.CompilerParams(vmem_limit_bytes=62 * 10**6),
        name="unpack",
    )(grads, *others)


def pack(gate, up, down):
    def pair(a, b):
        return jnp.concatenate([a[..., :HD], b[..., :HD], a[..., HD:], b[..., HD:]], axis=-1)

    gate, up, down = (jnp.transpose(w, (1, 0, 2)) for w in (gate, up, down))
    gate_up = pair(gate, up)
    a, b = down[0::2], down[1::2]
    inner = jnp.concatenate([a[..., :HD], a[..., HD:], b[..., HD:], b[..., :HD]], axis=-1)
    return jnp.concatenate([gate_up[0::2], gate_up[1::2], inner], axis=-1)


def unpack(packed):
    n, height, lanes = packed.shape
    third = lanes // 3

    def halves(both):
        tail = third // 2 - HD
        a = jnp.concatenate([both[..., :HD], both[..., 2 * HD : 2 * HD + tail]], axis=-1)
        b = jnp.concatenate([both[..., HD : 2 * HD], both[..., 2 * HD + tail :]], axis=-1)
        return a, b

    def experts(even, odd):
        both = jnp.stack([even, odd], axis=1).reshape(2 * n, height, third // 2)
        return jnp.transpose(both, (1, 0, 2))

    gate0, up0 = halves(packed[..., :third])
    gate1, up1 = halves(packed[..., third : 2 * third])
    down0, down1 = packed[..., 2 * third : 2 * third + third // 2], packed[..., 2 * third + third // 2 :]
    tail = third // 2 - HD
    down1 = jnp.concatenate([down1[..., tail:], down1[..., :tail]], axis=-1)
    return experts(gate0, gate1), experts(up0, up1), experts(down0, down1)


def routes_of(expert_ids, route_weights):
    rows = expert_ids.shape[0]
    lanes = jnp.arange(EXPERTS, dtype=jnp.int32)
    named = expert_ids[:, :, None] == lanes
    member_of = jnp.any(named, axis=1)
    weight_of = jnp.sum(jnp.where(named, route_weights[:, :, None], 0.0), axis=1)
    earlier = jnp.arange(rows)[:, None] > jnp.arange(rows)[None, :]
    rank = jnp.where(member_of, nn(earlier.astype(bf16), member_of.astype(bf16)), -1.0)
    rank_cols = jnp.pad(rank, ((0, 0), (0, HD)), constant_values=-1.0).astype(bf16)
    return rank_cols, jnp.stack([rank.T, weight_of.T], axis=1)


def body_anywhere(
    tokens,
    expert_ids,
    route_weights,
    attn_gain,
    q_weight,
    k_weight,
    v_weight,
    o_weight,
    moe_gain,
    gate_weight,
    up_weight,
    down_weight,
    cotangent,
):
    members = lax.axis_size("tensor")
    member = lax.axis_index("tensor")
    own_rows, width = tokens.shape
    rows = own_rows * members
    pairs = EXPERTS // 2
    calls = pairs // CALL_PAIRS

    packed = [
        pack(*(w[:, 2 * CALL_PAIRS * i : 2 * CALL_PAIRS * (i + 1)] for w in (gate_weight, up_weight, down_weight)))
        for i in range(calls)
    ]
    gathered = [lax.all_gather(own, "dp", axis=1, tiled=True) for own in packed]

    gain_one = lax.all_gather(attn_gain, "dp", axis=0, tiled=True).astype(f32)
    gain_two = lax.all_gather(moe_gain, "dp", axis=0, tiled=True).astype(f32)
    kv_full = lax.all_gather(jnp.concatenate([k_weight, v_weight], axis=1), "dp", axis=0, tiled=True)
    q_full = lax.all_gather(lax.all_gather(q_weight, "dp", axis=0, tiled=True), "tensor", axis=0)
    o_full = lax.all_gather(lax.all_gather(o_weight, "dp", axis=0, tiled=True), "tensor", axis=0)
    kv_width = k_weight.shape[1]

    rank_cols, routes = routes_of(expert_ids, route_weights)

    grad_low = cotangent.astype(bf16)
    grad_all = lax.all_gather(grad_low, "tensor", axis=0, tiled=True)

    x = tokens.astype(f32)
    inverse_one, unit_one = rms_pieces(x)
    normed_one = (unit_one * gain_one).astype(bf16)
    first_row = (member * own_rows).reshape(1)
    cos_table, sin_table = rope_tables(member * own_rows + jnp.arange(own_rows, dtype=jnp.int32))
    kv_own = nn(normed_one, kv_full)
    kv_own = jnp.concatenate(
        [rotate(kv_own[:, :kv_width], cos_table, sin_table), kv_own[:, kv_width:]], axis=1
    ).astype(bf16)
    kv_all = lax.all_gather(kv_own, "tensor", axis=0, tiled=True)
    keys, values = kv_all[:, :kv_width], kv_all[:, kv_width:]
    queries = jnp.concatenate([nn(normed_one, q_full[t]) for t in range(members)], axis=1)
    queries = rotate(queries, cos_table, sin_table).astype(bf16)
    mixed = attend_forward(first_row, queries, keys, values)
    part = width // members
    branch = sum(nt(mixed[:, t * part : (t + 1) * part], o_full[t]) for t in range(members))
    hidden = x + branch
    inverse_two, unit_two = rms_pieces(hidden)
    normed_two = (unit_two * gain_two).astype(bf16)
    rows_all = lax.all_gather(normed_two, "tensor", axis=0, tiled=True)

    sums = jnp.zeros((rows, 2 * width), f32)
    chunks = []
    for call in range(calls):
        some = slice(2 * CALL_PAIRS * call, 2 * CALL_PAIRS * (call + 1))
        columns = slice(2 * CALL_PAIRS * call, 2 * CALL_PAIRS * call + HD)
        grads, sums = expert_call(
            rank_cols[:, columns],
            routes[some],
            rows_all,
            grad_all,
            gathered[call],
            sums,
        )
        chunks.append(grads)
    shares = [
        unpack(lax.psum_scatter(grads, "dp", scatter_dimension=1, tiled=True).astype(f32)) for grads in chunks
    ]
    gate_out, up_out, down_out = (jnp.concatenate(parts, axis=1) for parts in zip(*shares))

    low_sums = sums.astype(bf16)
    normed_grad = lax.psum_scatter(low_sums[:, width:], "tensor", scatter_dimension=0, tiled=True).astype(f32)
    moe_own = lax.psum_scatter(low_sums[:, :width], "tensor", scatter_dimension=0, tiled=True).astype(f32)
    output = (hidden + moe_own).astype(bf16)

    back_two, gain_two_part = rms_backward(normed_grad, unit_two, inverse_two, gain_two)
    hidden_grad = cotangent + back_two
    hidden_low = hidden_grad.astype(bf16)
    mixed_grad = jnp.concatenate([nn(hidden_low, o_full[t]) for t in range(members)], axis=1).astype(bf16)
    o_part = jnp.stack([tn(hidden_low, mixed[:, t * part : (t + 1) * part]) for t in range(members)])
    dq, dk, dv = attend_backward(first_row, queries, keys, values, mixed_grad)
    kv_grad = lax.psum_scatter(
        jnp.concatenate([dk, dv], axis=1).astype(bf16), "tensor", scatter_dimension=0, tiled=True
    ).astype(f32)
    dq_low = rotate(dq, cos_table, -sin_table).astype(bf16)
    kv_low = jnp.concatenate(
        [rotate(kv_grad[:, :kv_width], cos_table, -sin_table), kv_grad[:, kv_width:]], axis=1
    ).astype(bf16)
    normed_one_grad = nt(kv_low, kv_full) + sum(
        nt(dq_low[:, t * part : (t + 1) * part], q_full[t]) for t in range(members)
    )
    back_one, gain_one_part = rms_backward(normed_one_grad, unit_one, inverse_one, gain_one)
    tokens_grad = hidden_grad + back_one
    q_part = jnp.stack([tn(normed_one, dq_low[:, t * part : (t + 1) * part]) for t in range(members)])
    kv_part = tn(normed_one, kv_low)

    def shared(values):
        summed = lax.psum_scatter(values.astype(bf16), "tensor", scatter_dimension=0, tiled=False)
        return lax.psum_scatter(summed, "dp", scatter_dimension=0, tiled=True).astype(f32)

    q_grad, o_grad = shared(q_part), shared(o_part)
    small = jnp.concatenate([kv_part, gain_one_part[:, None], gain_two_part[:, None]], axis=1)
    small = lax.psum_scatter(small, "dp", scatter_dimension=0, tiled=True)
    small = lax.psum(small.astype(bf16), "tensor").astype(f32)
    return (
        output,
        tokens_grad,
        small[:, 2 * kv_width],
        q_grad,
        small[:, :kv_width],
        small[:, kv_width : 2 * kv_width],
        o_grad,
        small[:, 2 * kv_width + 1],
        gate_out,
        up_out,
        down_out,
    )

def body_by_chips(
    tokens,
    expert_ids,
    route_weights,
    attn_gain,
    q_weight,
    k_weight,
    v_weight,
    o_weight,
    moe_gain,
    gate_weight,
    up_weight,
    down_weight,
    cotangent,
):
    members = lax.axis_size("tensor")
    member = lax.axis_index("tensor")
    devices = lax.axis_size("dp")
    own_rows, width = tokens.shape
    rows = own_rows * members
    calls = EXPERTS // 2 // CALL_PAIRS

    gains = jnp.pad(jnp.stack([attn_gain, moe_gain], axis=1), ((0, 0), (0, HD - 2)))
    cosine, sine = doubled_tables(rows)
    square_all, tall_all, grad_all, rank_cols, routes, normed_one, queries, kv_all, mixed, hidden, rows_all, *chunks = front(
        tokens,
        q_weight,
        o_weight,
        k_weight,
        v_weight,
        gains,
        cosine,
        sine,
        cotangent,
        expert_ids.T,
        route_weights.T,
        gate_weight,
        up_weight,
        down_weight,
        members,
        devices,
    )
    packed, (from_x, from_y, far_x, far_y, *after) = chunks[:calls], chunks[calls:]
    near = [(from_x, from_y), *zip(after[0::2], after[1::2])]
    sums, grads, *others = expert_pass(
        rank_cols, routes, rows_all, grad_all, packed, near, (far_x, far_y), members
    )
    plain, added = others[-6:-4], others[-4:-2]
    tokens_grad, moe_moved, parts, *moved = attention_back(
        sums,
        cotangent,
        hidden,
        tokens,
        normed_one,
        queries,
        kv_all,
        mixed,
        square_all,
        tall_all,
        cosine,
        sine,
        grads,
        *added,
        members,
    )
    output, q_grad, o_grad, k_grad, v_grad, gain_grads, x_end, y_end = reduce_small(
        parts, sums, moe_moved, hidden, *added, members, devices
    )
    x_before, y_before, x_last, y_last, x_late, y_late = moved
    gate_out, up_out, down_out = unpack_all(
        grads,
        [(plain[0], x_late), (plain[1], y_late)],
        [(x_before, x_end), (y_before, y_end)],
        (x_last, y_last),
    )
    return (
        output,
        tokens_grad,
        gain_grads[:, 0],
        q_grad,
        k_grad,
        v_grad,
        o_grad,
        gain_grads[:, 1],
        gate_out,
        up_out,
        down_out,
    )


def doubled_tables(rows):
    half = HD // 2
    frequency = np.float32(rope_base) ** -(np.arange(half, dtype=np.float32) * np.float32(2.0 / HD))
    angles = (np.arange(rows) % SEQ).astype(np.float32)[:, None] * frequency
    cosine, sine = np.cos(angles), np.sin(angles)
    return jnp.asarray(np.concatenate([cosine, cosine], axis=1)), jnp.asarray(np.concatenate([-sine, sine], axis=1))


def solution(mesh):
    rows = P(("dp", "tensor"), None)
    experts = P("dp", None, "tensor")
    square = P("dp", "tensor")
    tall = P("dp", None)
    return jax.shard_map(
        body_by_chips if mesh.shape["dp"] == 8 else body_anywhere,
        mesh=mesh,
        in_specs=(
            rows, tall, tall, P("dp"), square, tall, tall, square, P("dp"), experts, experts, experts, rows
        ),
        out_specs=(rows, rows, P("dp"), square, tall, tall, square, P("dp"), experts, experts, experts),
        check_vma=False,
    )
```
